32 devices in a mesh: groups: 2 (over y), ctx: 4 (over z), head: 4 (over x, core).
Axes of the slice: x: 2, y: 2, z: 4, core: 2. Of those that a mesh axis runs over, the one named last changes fastest.
Arguments:
- queries: bfloat16 [1024, 8192], P(('groups', 'ctx'), 'head'), parts along dimension 0, may hold values from -145 to 145
- stretch_keys: bfloat16 [1024, 1024], P(('groups', 'ctx'), 'head'), parts along dimension 0, may hold values from -4.5 to 4.5
- stretch_values: bfloat16 [1024, 1024], P(('groups', 'ctx'), 'head'), parts along dimension 0, may hold values from -4 to 4
- cache_keys: bfloat16 [2048, 1024], P(('groups', 'ctx'), 'head'), parts along dimension 0, may hold values from -4 to 4
- cache_values: bfloat16 [2048, 1024], P(('groups', 'ctx'), 'head'), parts along dimension 0, may hold values from -4 to 4
- prefix_length: int32 [2], P('groups'), parts along dimension 0, may hold values from 256 to 1024
- page_targets: int32 [64], P('groups'), parts along dimension 0, may hold values from 0 to 31, as said below
- pool_keys: bfloat16 [1024, 16, 1024], P(('groups', 'ctx'), None, 'head'), parts along dimension 0, may hold values from -4.5 to 4.5
- pool_values: bfloat16 [1024, 16, 1024], P(('groups', 'ctx'), None, 'head'), parts along dimension 0, may hold values from -4 to 4
- decode_queries: bfloat16 [64, 8192], P(('groups', 'ctx'), 'head'), parts along dimension 0, may hold values from -145 to 145
- page_lists: int32 [64, 32], P(('groups', 'ctx')), parts along dimension 0, may hold values from 0 to 135, as said below
- context_length: int32 [64], P(('groups', 'ctx')), parts along dimension 0, may hold values from 32 to 512
Outputs:
- prefill_attention: bfloat16 [1024, 8192], P(('groups', 'ctx'), 'head'), parts along dimension 0
- decode_attention: bfloat16 [64, 8192], P(('groups', 'ctx'), 'head'), parts along dimension 0
The draws below stay inside these ranges and needn't reach their ends.
There are 2 independent parts, one for each index of `groups`. The reference program is written for one: setup_inputs(seed, part) draws one part's arguments, and reference() takes and returns one part's arrays. A program takes and returns all parts, laid end to end along the dimension named above; each array names one. Nothing has to cross between parts.
Inputs may be any that keep to these rules, and one draw needn't show every extreme that they name: `page_targets`: targets are distinct; every owner receives exactly 8 new pages, and the 8 pages of one index of ctx go to owners 2 at a time, so that exactly 2 of them share each of their owners. `page_lists`: entry 0 of every row names one of the 128 held pages; entry 1 of row r names new slot 128 + (r % 8) % 8.
All inputs are finite; a program needn't handle non-finite values.
Results may differ from the reference program's by a relative error of at most 0.006.
Values may be sent and summed in bfloat16 or wider, within the bound.
No kernel may reach another device: no remote copies, remote signals or barrier semaphores. Data moves between devices by JAX's collectives and lax.ppermute only.
A program may use at most 64 MiB of HBM per device.

```python
import jax
import jax.numpy as jnp
from jax import lax

HEADS = 64
KV_HEADS = 8
HEAD_DIM = 128
TOK_DEV = 128
PAGE = 16
SEND_CAP = 2
POOL = 128
DROWS = 8
MAXP = 32
P_DEV = 8
STRETCH = 512
CACHE = 1024
NEWPAGES = 32
POOLS = 512
ROWS = 32
KW = 1024
N_CTX = 4


def paired_stretch(key):
    key = jax.random.fold_in(key, 101)
    first_key = jax.random.fold_in(key, 0)
    width = KV_HEADS * HEAD_DIM
    base = jnp.clip(jax.random.normal(first_key, (STRETCH // 2, 2, width), jnp.float32), -4.0, 4.0)
    second = base[:, 1]
    return jnp.stack([base[:, 0], second], axis=1).reshape(STRETCH, width)


def paired_pool(key):
    key = jax.random.fold_in(key, 202)
    first_key = jax.random.fold_in(key, 0)
    width = KV_HEADS * HEAD_DIM
    base = jnp.clip(jax.random.normal(first_key, (POOLS, PAGE, width), jnp.float32), -4.0, 4.0)
    second = base[:, 1]
    return base.at[:, 1].set(second)


def row_pages(key):
    key = jax.random.fold_in(key, 303)
    first_key, second_key = jax.random.split(key)
    listed = jax.random.randint(first_key, (ROWS, MAXP), 0, POOL + P_DEV, jnp.int32)
    leading = jax.random.randint(second_key, (ROWS,), 0, POOL, jnp.int32)
    row_ids = jnp.arange(ROWS, dtype=jnp.int32)
    fresh = POOL + row_ids % DROWS % P_DEV
    return listed.at[:, 0].set(leading).at[:, 1].set(fresh)


def draw_stretch_keys(key, part):
    return paired_stretch(key).astype(jnp.bfloat16)


def draw_queries(key, part):
    key = jax.random.fold_in(key, 7)
    first_key = jax.random.fold_in(key, 0)
    base = jnp.clip(jax.random.normal(first_key, (STRETCH, HEADS * HEAD_DIM), jnp.float32), -4.0, 4.0)
    return base.astype(jnp.bfloat16)


def draw_pool_keys(key, part):
    return paired_pool(key).astype(jnp.bfloat16)


def draw_page_lists(key, part):
    return row_pages(key)


def draw_decode_queries(key, part):
    key = jax.random.fold_in(key, 9)
    first_key = jax.random.fold_in(key, 0)
    base = jnp.clip(jax.random.normal(first_key, (ROWS, HEADS * HEAD_DIM), jnp.float32), -4.0, 4.0)
    return base.astype(jnp.bfloat16)


def draw_page_targets(key, part):
    key = jax.random.fold_in(key, 5)
    first_key, second_key, third_key = jax.random.split(key, 3)
    sender_perm = jax.random.permutation(first_key, N_CTX).astype(jnp.int32)
    owner_perm = jax.random.permutation(second_key, N_CTX).astype(jnp.int32)
    slot_perm = jax.random.permutation(third_key, P_DEV).astype(jnp.int32)
    senders = jnp.arange(N_CTX, dtype=jnp.int32)[:, None]
    page_ids = jnp.arange(P_DEV, dtype=jnp.int32)[None, :]
    owners = owner_perm[(sender_perm[senders] + page_ids // SEND_CAP) % N_CTX]
    targets = owners * P_DEV + slot_perm[page_ids]
    return targets.reshape(N_CTX * P_DEV).astype(jnp.int32)


def place_ends(values, stream_key, least, high):
    longest = values.shape.index(max(values.shape))
    spots = []
    for shift in (0, 1):
        where = [jax.random.randint(jax.random.fold_in(stream_key, axis), (), 0, length) for axis, length in enumerate(values.shape)]
        where[longest] = (where[longest] + shift) % values.shape[longest]
        spots.append(tuple(where))
    return values.at[spots[0]].set(least).at[spots[1]].set(high)


def shard_levels(rng, extent, shards, low, high):
    def one(position, parts):
        heights = jax.random.uniform(jax.random.fold_in(jax.random.fold_in(rng, 6), position), (parts,), jnp.float32, low / len(shards), high / len(shards))
        return jnp.repeat(jnp.exp(heights), extent[position] // parts).reshape((-1,) + (1,) * (len(extent) - position - 1))

    factor_of = one(*shards[0])
    for cut in shards[1:]:
        factor_of = factor_of * one(*cut)
    return factor_of


def scatter_about(rng, extent, scale, reach, cuts=(), kind=jnp.bfloat16):
    gain = shard_levels(rng, extent, cuts, -0.22, 0.18) if cuts else 1.0
    result = jax.random.normal(rng, extent, jnp.float32) * scale * gain
    return jnp.minimum(jnp.maximum(result, -reach), reach).astype(kind)


def setup_inputs(seed: int = 0, part: int = 0) -> dict:
    streams_of = jax.random.split(jax.random.key(seed), 13)
    part_keys = jax.random.split(jax.random.fold_in(streams_of[12], part), 13)
    return {
        "queries": draw_queries(jax.random.fold_in(jax.random.fold_in(streams_of[12], part), 71), part),
        "stretch_keys": draw_stretch_keys(jax.random.fold_in(jax.random.fold_in(streams_of[12], part), 71), part),
        "stretch_values": scatter_about(part_keys[2], (STRETCH, KW), 1.0, 4.0, ((0, 4), (1, 4))),
        "cache_keys": scatter_about(part_keys[3], (CACHE, KW), 1.0, 4.0, ((0, 4), (1, 4))),
        "cache_values": scatter_about(part_keys[4], (CACHE, KW), 1.0, 4.0, ((0, 4), (1, 4))),
        "prefix_length": jax.random.randint(part_keys[5], (1,), CACHE // 4, CACHE + 1).astype(jnp.int32),
        "page_targets": draw_page_targets(jax.random.fold_in(jax.random.fold_in(streams_of[12], part), 71), part),
        "pool_keys": draw_pool_keys(jax.random.fold_in(jax.random.fold_in(streams_of[12], part), 71), part),
        "pool_values": scatter_about(part_keys[8], (POOLS, PAGE, KW), 1.0, 4.0, ((0, 4), (2, 4))),
        "decode_queries": draw_decode_queries(jax.random.fold_in(jax.random.fold_in(streams_of[12], part), 71), part),
        "page_lists": draw_page_lists(jax.random.fold_in(jax.random.fold_in(streams_of[12], part), 71), part),
        "context_length": place_ends(jax.random.randint(part_keys[11], (ROWS,), 2 * PAGE, MAXP * PAGE + 1), jax.random.fold_in(part_keys[11], 1), 2 * PAGE, MAXP * PAGE).astype(jnp.int32),
    }


def prefill_block(block, queries, joined_keys, joined_values, prefix_length):
    group_size = HEADS // KV_HEADS
    query_rows = lax.dynamic_slice_in_dim(queries, block * TOK_DEV, TOK_DEV, 0).astype(jnp.float32)
    query_rows = query_rows.reshape(TOK_DEV, KV_HEADS, group_size, HEAD_DIM)
    scores = jnp.einsum("tkgd,nkd->tkgn", query_rows, joined_keys) * (HEAD_DIM ** -0.5)
    positions = block * TOK_DEV + jnp.arange(TOK_DEV, dtype=jnp.int32)
    cache_seen = jnp.broadcast_to(jnp.arange(CACHE, dtype=jnp.int32)[None, :] < prefix_length[0], (TOK_DEV, CACHE))
    stretch_seen = jnp.arange(STRETCH, dtype=jnp.int32)[None, :] <= positions[:, None]
    visible = jnp.concatenate([cache_seen, stretch_seen], axis=1)[:, None, None, :]
    masked = jnp.where(visible, scores, jnp.float32(-1e30))
    highest = jnp.max(masked, axis=-1, keepdims=True)
    weights = jnp.where(visible, jnp.exp(masked - highest), jnp.float32(0.0))
    total = jnp.sum(weights, axis=-1)
    rounded = lax.optimization_barrier(weights.astype(jnp.bfloat16)).astype(jnp.float32)
    mixed = jnp.einsum("tkgn,nkd->tkgd", rounded, joined_values) / total[..., None]
    return mixed.reshape(TOK_DEV, HEADS * HEAD_DIM).astype(jnp.bfloat16)


def decode_owner(inputs):
    extended, owner_queries, owner_lists, owner_lengths = inputs
    group_size = HEADS // KV_HEADS
    span = MAXP * PAGE
    gathered = extended[:, owner_lists].astype(jnp.float32)
    key_heads = gathered[0].reshape(DROWS, span, KV_HEADS, HEAD_DIM)
    value_heads = gathered[1].reshape(DROWS, span, KV_HEADS, HEAD_DIM)
    query_heads = owner_queries.astype(jnp.float32).reshape(DROWS, KV_HEADS, group_size, HEAD_DIM)
    scores = jnp.einsum("rkgd,rnkd->rkgn", query_heads, key_heads) * (HEAD_DIM ** -0.5)
    visible = (jnp.arange(span, dtype=jnp.int32)[None, :] < owner_lengths[:, None])[:, None, None, :]
    masked = jnp.where(visible, scores, jnp.float32(-1e30))
    highest = jnp.max(masked, axis=-1, keepdims=True)
    weights = jnp.where(visible, jnp.exp(masked - highest), jnp.float32(0.0))
    total = jnp.sum(weights, axis=-1)
    rounded = lax.optimization_barrier(weights.astype(jnp.bfloat16)).astype(jnp.float32)
    mixed = jnp.einsum("rkgn,rnkd->rkgd", rounded, value_heads) / total[..., None]
    return mixed.reshape(DROWS, HEADS * HEAD_DIM).astype(jnp.bfloat16)


def reference(queries, stretch_keys, stretch_values, cache_keys, cache_values, prefix_length, page_targets, pool_keys, pool_values, decode_queries, page_lists, context_length):
    joined_keys = jnp.concatenate([cache_keys, stretch_keys], axis=0).astype(jnp.float32).reshape(-1, KV_HEADS, HEAD_DIM)
    joined_values = jnp.concatenate([cache_values, stretch_values], axis=0).astype(jnp.float32).reshape(-1, KV_HEADS, HEAD_DIM)
    blocks = jnp.arange(N_CTX, dtype=jnp.int32)
    prefill = lax.map(lambda block: prefill_block(block, queries, joined_keys, joined_values, prefix_length), blocks)
    prefill = prefill.reshape(STRETCH, HEADS * HEAD_DIM)
    width = KV_HEADS * HEAD_DIM
    page_data = jnp.stack([stretch_keys, stretch_values]).reshape(2, NEWPAGES, PAGE, width)
    placed = jnp.zeros((2, NEWPAGES, PAGE, width), jnp.bfloat16).at[:, page_targets].set(page_data)
    held = jnp.stack([pool_keys, pool_values]).reshape(2, N_CTX, POOL, PAGE, width)
    extended = jnp.concatenate([held, placed.reshape(2, N_CTX, P_DEV, PAGE, width)], axis=2)
    extended = jnp.transpose(extended, (1, 0, 2, 3, 4))
    decoded = lax.map(decode_owner, (extended, decode_queries.reshape(N_CTX, DROWS, HEADS * HEAD_DIM), page_lists.reshape(N_CTX, DROWS, MAXP), context_length.reshape(N_CTX, DROWS)))
    return prefill, decoded.reshape(ROWS, HEADS * HEAD_DIM)
```

```python
import functools

import jax
import jax.numpy as jnp
from jax import lax
from jax.experimental import pallas as pl
from jax.experimental.pallas import tpu as pltpu
from jax.sharding import PartitionSpec as P

HEADS = 64
KV_HEADS = 8
HEAD_DIM = 128
GROUP = HEADS // KV_HEADS
PAGE = 16
P_DEV = 8
EXP2_SCALE = HEAD_DIM ** (-0.5) * 1.4426950408889634
HIDDEN = -1e30
VMEM_BYTES = 48 * 1024 * 1024

VMEM = pl.BlockSpec(memory_space=pltpu.VMEM)
SMEM = pl.BlockSpec(memory_space=pltpu.SMEM)


def absorb(qt_ref, high_ref, total_ref, accum_ref, keys, values, seen_of):
    kv_local, _, rows = qt_ref.shape
    width = min(2 * (rows // GROUP), rows)
    for head in range(kv_local):
        feats = slice(head * HEAD_DIM, (head + 1) * HEAD_DIM)
        key_head = keys[:, feats]
        value_head = values[:, feats].T
        for start in range(0, rows, width):
            cols = slice(start, start + width)
            scores = jnp.dot(key_head, qt_ref[head, :, cols], preferred_element_type=jnp.float32)
            if seen_of is not None:
                scores = jnp.where(seen_of(scores.shape), scores, jnp.float32(HIDDEN))
            old_high = high_ref[head, :, cols]
            high = jnp.maximum(old_high, jnp.max(scores, axis=0, keepdims=True))
            weights = jnp.exp2((scores - high) * EXP2_SCALE)
            decay = jnp.exp2((old_high - high) * EXP2_SCALE)
            high_ref[head, :, cols] = high
            total_ref[head, :, cols] = total_ref[head, :, cols] * decay + jnp.sum(
                weights, axis=0, keepdims=True
            )
            accum_ref[head, :, cols] = accum_ref[head, :, cols] * decay + jnp.dot(
                value_head, weights.astype(jnp.bfloat16), preferred_element_type=jnp.float32
            )


def cache_seen(first, limit):
    def seen(shape):
        return lax.broadcasted_iota(jnp.int32, shape, 0) + first < limit

    return seen


def own_kernel(
    own_ref, limit_ref, q_ref, sk_ref, sv_ref, ck_ref, cv_ref, qt_ref, high_ref, total_ref, accum_ref
):
    kv_local = qt_ref.shape[0]
    tokens = q_ref.shape[0]
    for head in range(kv_local):
        for sub in range(GROUP):
            col = (head * GROUP + sub) * HEAD_DIM
            qt_ref[head, :, sub * tokens : (sub + 1) * tokens] = q_ref[:, col : col + HEAD_DIM].T
    high_ref[...] = jnp.full_like(high_ref, HIDDEN)
    total_ref[...] = jnp.zeros_like(total_ref)
    accum_ref[...] = jnp.zeros_like(accum_ref)

    def causal(shape):
        token = lax.rem(lax.broadcasted_iota(jnp.int32, shape, 1), tokens)
        return lax.broadcasted_iota(jnp.int32, shape, 0) <= token

    absorb(qt_ref, high_ref, total_ref, accum_ref, sk_ref[...], sv_ref[...], causal)
    first = own_ref[0] * ck_ref.shape[0]

    @pl.when(first < limit_ref[0])
    def _():
        absorb(
            qt_ref, high_ref, total_ref, accum_ref, ck_ref[...], cv_ref[...],
            cache_seen(first, limit_ref[0]),
        )


def step_kernel(step, count, *refs):
    own_ref, limit_ref, qt_ref, up_s, up_c, down_c, high_in, total_in, accum_in = refs[:9]
    last = step == count - 1
    if last:
        out_ref, high_ref, total_ref, accum_ref = refs[9:]
    else:
        high_ref, total_ref, accum_ref = refs[9:]
    high_ref[...] = high_in[...]
    total_ref[...] = total_in[...]
    accum_ref[...] = accum_in[...]
    own = own_ref[0]
    limit = limit_ref[0]
    s_rows = up_s.shape[0] // 2
    c_rows = up_c.shape[0] // 2

    @pl.when(own >= step)
    def _():
        absorb(qt_ref, high_ref, total_ref, accum_ref, up_s[:s_rows], up_s[s_rows:], None)
        first = (own - step) * c_rows

        @pl.when(first < limit)
        def _():
            absorb(
                qt_ref, high_ref, total_ref, accum_ref, up_c[:c_rows], up_c[c_rows:],
                cache_seen(first, limit),
            )

    down_first = (own + step) * c_rows

    @pl.when((own + step < count) & (down_first < limit))
    def _():
        absorb(
            qt_ref, high_ref, total_ref, accum_ref, down_c[:c_rows], down_c[c_rows:],
            cache_seen(down_first, limit),
        )

    if last:
        kv_local = qt_ref.shape[0]
        tokens = out_ref.shape[0]
        for head in range(kv_local):
            for sub in range(GROUP):
                cols = slice(sub * tokens, (sub + 1) * tokens)
                col = (head * GROUP + sub) * HEAD_DIM
                mixed = accum_ref[head, :, cols] / total_ref[head, :, cols]
                out_ref[:, col : col + HEAD_DIM] = mixed.T.astype(jnp.bfloat16)


def decode_kernel(count, *refs):
    own_ref, slots_ref, q_ref, lists_ref, length_ref, pool_k, pool_v, own_s = refs[:8]
    ups = refs[8 : 8 + count - 1]
    downs = refs[8 + count - 1 : 8 + 2 * (count - 1)]
    out_ref = refs[-1]
    own = own_ref[0]
    rows, width = q_ref.shape
    heads = width // HEAD_DIM
    kv_local = heads // GROUP
    span = lists_ref.shape[1]
    lists = lists_ref[...]
    lengths = length_ref[...]

    queries = q_ref[...].astype(jnp.float32)
    stacked = []
    for head in range(heads):
        piece = queries[:, head * HEAD_DIM : (head + 1) * HEAD_DIM]
        blank = jnp.zeros_like(piece)
        stacked.append(
            jnp.concatenate([piece if kv == head // GROUP else blank for kv in range(kv_local)], axis=1)
        )
    wide_queries = jnp.concatenate(stacked, axis=0).astype(jnp.bfloat16)

    def copies(slot):
        tokens = slot.shape[1]
        offset = lax.rem(lax.broadcasted_iota(jnp.int32, (rows, tokens), 1), PAGE)
        tally = jnp.zeros((rows, tokens), jnp.float32)
        for entry in range(span):
            hit = (slot == lists[:, entry : entry + 1]) & (offset < lengths - entry * PAGE)
            tally = tally + jnp.where(hit, jnp.float32(1.0), jnp.float32(0.0))
        return tally

    parts = []

    def add_part(keys, values, slot):
        scores = lax.dot_general(
            wide_queries, keys, (((1,), (1,)), ((), ())), preferred_element_type=jnp.float32
        )
        tally = copies(slot)[None]
        scores = scores.reshape(heads, rows, -1)
        scores = jnp.where(tally > 0, scores, jnp.float32(HIDDEN))
        parts.append((scores, tally, values))

    held = pool_k.shape[0] * PAGE
    held_slot = lax.broadcasted_iota(jnp.int32, (rows, held), 1) // PAGE
    add_part(pool_k[...].reshape(held, -1), pool_v[...].reshape(held, -1), held_slot)
    s_rows = own_s.shape[0] // 2

    def add_shard(ref, shard):
        valid = (shard >= 0) & (shard < count)
        index = jnp.clip(shard, 0, count - 1)
        slot = jnp.where(valid, slots_ref[pl.ds(index, 1), :], -1)
        add_part(ref[:s_rows], ref[s_rows:], jnp.broadcast_to(slot, (rows, s_rows)))

    add_shard(own_s, own)
    for step in range(1, count):
        add_shard(ups[step - 1], own - step)
        add_shard(downs[step - 1], own + step)

    high = functools.reduce(
        jnp.maximum, [jnp.max(scores, axis=-1, keepdims=True) for scores, _, _ in parts]
    )
    total = 0.0
    mixed = 0.0
    for scores, tally, values in parts:
        weights = jnp.exp2((scores - high) * EXP2_SCALE) * tally
        total = total + jnp.sum(weights, axis=-1, keepdims=True)
        mixed = mixed + jnp.dot(
            weights.reshape(heads * rows, -1).astype(jnp.bfloat16),
            values,
            preferred_element_type=jnp.float32,
        )
    for head in range(heads):
        kv = head // GROUP
        piece = mixed[head * rows : (head + 1) * rows, kv * HEAD_DIM : (kv + 1) * HEAD_DIM]
        out_ref[:, head * HEAD_DIM : (head + 1) * HEAD_DIM] = (piece / total[head]).astype(jnp.bfloat16)


def per_device(
    count,
    queries,
    stretch_keys,
    stretch_values,
    cache_keys,
    cache_values,
    prefix_length,
    page_targets,
    pool_keys,
    pool_values,
    decode_queries,
    page_lists,
    context_length,
):
    own = lax.axis_index("ctx")
    own_array = jnp.full((1,), own, jnp.int32)
    tokens, width = queries.shape
    kv_local = stretch_keys.shape[1] // HEAD_DIM
    rows = GROUP * tokens
    f32 = jnp.float32
    params = pltpu.CompilerParams(vmem_limit_bytes=VMEM_BYTES)

    upward = [(i, i + 1) for i in range(count - 1)]
    downward = [(i + 1, i) for i in range(count - 1)]
    own_s = jnp.concatenate([stretch_keys, stretch_values], axis=0)
    own_c = jnp.concatenate([cache_keys, cache_values], axis=0)
    up_s, up_c, down_s, down_c = [own_s], [own_c], [own_s], [own_c]
    for _ in range(1, count):
        up_s.append(lax.ppermute(up_s[-1], "ctx", upward))
        down_s.append(lax.ppermute(down_s[-1], "ctx", downward))
        up_c.append(lax.ppermute(up_c[-1], "ctx", upward))
        down_c.append(lax.ppermute(down_c[-1], "ctx", downward))

    state_shapes = (
        jax.ShapeDtypeStruct((kv_local, 1, rows), f32),
        jax.ShapeDtypeStruct((kv_local, 1, rows), f32),
        jax.ShapeDtypeStruct((kv_local, HEAD_DIM, rows), f32),
    )

    def cost(keys):
        pairs = kv_local * rows * keys
        return pl.CostEstimate(
            flops=4 * pairs * HEAD_DIM, bytes_accessed=4 * rows * kv_local * HEAD_DIM, transcendentals=pairs
        )

    c_rows = cache_keys.shape[0]
    qt, *state = pl.pallas_call(
        own_kernel,
        out_shape=(jax.ShapeDtypeStruct((kv_local, HEAD_DIM, rows), jnp.bfloat16),) + state_shapes,
        in_specs=[SMEM, SMEM] + [VMEM] * 5,
        out_specs=(VMEM,) * 4,
        compiler_params=params,
        cost_estimate=cost(c_rows + tokens),
        name="own_shard",
    )(own_array, prefix_length, queries, stretch_keys, stretch_values, cache_keys, cache_values)

    prefill = None
    for step in range(1, count):
        last = step == count - 1
        outs = state_shapes
        if last:
            outs = jax.ShapeDtypeStruct((tokens, width), jnp.bfloat16)
        results = pl.pallas_call(
            functools.partial(step_kernel, step, count),
            out_shape=outs,
            in_specs=[SMEM, SMEM] + [VMEM] * 7,
            out_specs=VMEM if last else (VMEM,) * 3,
            scratch_shapes=[pltpu.VMEM(s.shape, s.dtype) for s in state_shapes] if last else [],
            compiler_params=params,
            cost_estimate=cost(c_rows + tokens),
            name="shards_at_" + str(step),
        )(own_array, prefix_length, qt, up_s[step], up_c[step], down_c[step], *state)
        if last:
            prefill = results
        else:
            state = results

    slots = jnp.where(page_targets // P_DEV == own, pool_keys.shape[0] + page_targets % P_DEV, -1)
    slots = jnp.repeat(slots, PAGE).reshape(count, tokens)
    decoded = pl.pallas_call(
        functools.partial(decode_kernel, count),
        out_shape=jax.ShapeDtypeStruct(decode_queries.shape, jnp.bfloat16),
        in_specs=[SMEM] + [VMEM] * (7 + 2 * (count - 1)),
        out_specs=VMEM,
        compiler_params=params,
        cost_estimate=pl.CostEstimate(
            flops=4 * 128 * 2048 * 256, bytes_accessed=4 * pool_keys.size, transcendentals=128 * 2560
        ),
        name="decode_rows",
    )(
        own_array, slots, decode_queries, page_lists, context_length.reshape(-1, 1),
        pool_keys, pool_values, own_s, *up_s[1:], *down_s[1:],
    )
    return (prefill, decoded)


def solution(mesh):
    in_specs = (
        P(("groups", "ctx"), "head"),
        P(("groups", "ctx"), "head"),
        P(("groups", "ctx"), "head"),
        P(("groups", "ctx"), "head"),
        P(("groups", "ctx"), "head"),
        P("groups"),
        P("groups"),
        P(("groups", "ctx"), None, "head"),
        P(("groups", "ctx"), None, "head"),
        P(("groups", "ctx"), "head"),
        P(("groups", "ctx"), None),
        P(("groups", "ctx")),
    )
    out_specs = (P(("groups", "ctx"), "head"), P(("groups", "ctx"), "head"))
    return jax.shard_map(
        functools.partial(per_device, mesh.shape["ctx"]),
        mesh=mesh,
        in_specs=in_specs,
        out_specs=out_specs,
        check_vma=False,
    )
```

```python
import functools

import jax
import jax.numpy as jnp
from jax import lax
from jax.experimental import pallas as pl
from jax.experimental.pallas import tpu as pltpu
from jax.sharding import PartitionSpec as P

HEADS = 64
KV_HEADS = 8
HEAD_DIM = 128
GROUP = HEADS // KV_HEADS
PAGE = 16
P_DEV = 8
EXP2_SCALE = HEAD_DIM ** (-0.5) * 1.4426950408889634
HIDDEN = -1e30
VMEM_BYTES = 48 * 1024 * 1024

VMEM = pl.BlockSpec(memory_space=pltpu.VMEM)
SMEM = pl.BlockSpec(memory_space=pltpu.SMEM)


def attend(qt_ref, head, cols, keys, values_t, seen, state):
    scores = jnp.dot(keys, qt_ref[head, :, cols], preferred_element_type=jnp.float32)
    scores = jnp.where(seen, scores, jnp.float32(HIDDEN))
    high = jnp.max(scores, axis=0, keepdims=True)
    if state is not None:
        old_high, old_total, old_accum = state
        high = jnp.maximum(high, old_high)
    weights = jnp.exp2((scores - high) * EXP2_SCALE)
    total = jnp.sum(weights, axis=0, keepdims=True)
    accum = jnp.dot(values_t, weights.astype(jnp.bfloat16), preferred_element_type=jnp.float32)
    if state is not None:
        decay = jnp.exp2((old_high - high) * EXP2_SCALE)
        total = total + old_total * decay
        accum = accum + old_accum * decay
    return high, total, accum


def near_kernel(
    own_ref, limit_ref, q_ref, stretch_ref, cache_ref, qt_ref, high_ref, total_ref, accum_ref
):
    kv_local, _, rows = qt_ref.shape
    count, s_rows, _ = stretch_ref.shape
    s_rows = s_rows // 2
    c_rows = cache_ref.shape[0] // 2
    tokens = q_ref.shape[0]
    own = own_ref[0]
    for head in range(kv_local):
        for sub in range(GROUP):
            col = (head * GROUP + sub) * HEAD_DIM
            qt_ref[head, :, sub * tokens : (sub + 1) * tokens] = q_ref[:, col : col + HEAD_DIM].T
    width = min(2 * tokens, rows)
    keys_all = count * s_rows + c_rows
    place = lax.broadcasted_iota(jnp.int32, (keys_all, width), 0)
    token = lax.rem(lax.broadcasted_iota(jnp.int32, (keys_all, width), 1), tokens)
    held = place - count * s_rows
    seen = ((held < 0) & (place <= own * tokens + token)) | (
        (held >= 0) & (held < limit_ref[0] - own * c_rows)
    )
    for head in range(kv_local):
        feats = slice(head * HEAD_DIM, (head + 1) * HEAD_DIM)
        keys = jnp.concatenate(
            [stretch_ref[shard, :s_rows, feats] for shard in range(count)] + [cache_ref[:c_rows, feats]], axis=0
        )
        values = jnp.concatenate(
            [stretch_ref[shard, s_rows:, feats] for shard in range(count)] + [cache_ref[c_rows:, feats]], axis=0
        )
        values_t = values.T
        for start in range(0, rows, width):
            cols = slice(start, start + width)
            high, total, accum = attend(qt_ref, head, cols, keys, values_t, seen, None)
            high_ref[head, :, cols] = high
            total_ref[head, :, cols] = total
            accum_ref[head, :, cols] = accum


def far_kernel(count, own_ref, limit_ref, qt_ref, cache_ref, high_ref, total_ref, accum_ref, out_ref):
    kv_local, _, rows = qt_ref.shape
    c_rows = cache_ref.shape[1] // 2
    tokens = out_ref.shape[0]
    width = min(2 * tokens, rows)
    own = own_ref[0]
    limit = limit_ref[0]
    shards = [lax.rem(own + hop, count) for hop in range(1, count)]
    place = lax.broadcasted_iota(jnp.int32, (c_rows, width), 0)
    seen = jnp.concatenate([place < limit - shard * c_rows for shard in shards], axis=0)
    for head in range(kv_local):
        feats = slice(head * HEAD_DIM, (head + 1) * HEAD_DIM)
        keys = jnp.concatenate([cache_ref[shard, :c_rows, feats] for shard in shards], axis=0)
        values_t = jnp.concatenate([cache_ref[shard, c_rows:, feats] for shard in shards], axis=0).T
        for start in range(0, rows, width):
            cols = slice(start, start + width)
            state = (high_ref[head, :, cols], total_ref[head, :, cols], accum_ref[head, :, cols])
            _, total, accum = attend(qt_ref, head, cols, keys, values_t, seen, state)
            mixed = accum / total
            for piece in range(width // tokens):
                col = (head * GROUP + start // tokens + piece) * HEAD_DIM
                out_ref[:, col : col + HEAD_DIM] = (
                    mixed[:, piece * tokens : (piece + 1) * tokens].T.astype(jnp.bfloat16)
                )


def decode_kernel(slots_ref, q_ref, lists_ref, length_ref, pool_k, pool_v, stretch_ref, out_ref):
    rows, q_width = q_ref.shape
    heads = q_width // HEAD_DIM
    kv_local = heads // GROUP
    span = lists_ref.shape[1]
    lists = lists_ref[...]
    lengths = length_ref[...]

    queries = q_ref[...].astype(jnp.float32)
    stacked = []
    for head in range(heads):
        piece = queries[:, head * HEAD_DIM : (head + 1) * HEAD_DIM]
        blank = jnp.zeros_like(piece)
        stacked.append(
            jnp.concatenate([piece if kv == head // GROUP else blank for kv in range(kv_local)], axis=1)
        )
    wide_queries = jnp.concatenate(stacked, axis=0).astype(jnp.bfloat16)

    def copies(slot):
        tokens = slot.shape[1]
        offset = lax.rem(lax.broadcasted_iota(jnp.int32, (rows, tokens), 1), PAGE)
        tally = jnp.zeros((rows, tokens), jnp.float32)
        for entry in range(span):
            hit = (slot == lists[:, entry : entry + 1]) & (offset < lengths - entry * PAGE)
            tally = tally + jnp.where(hit, jnp.float32(1.0), jnp.float32(0.0))
        return tally

    parts = []

    def add_part(keys, values, slot):
        scores = lax.dot_general(
            wide_queries, keys, (((1,), (1,)), ((), ())), preferred_element_type=jnp.float32
        )
        tally = copies(slot)[None]
        scores = scores.reshape(heads, rows, -1)
        scores = jnp.where(tally > 0, scores, jnp.float32(HIDDEN))
        parts.append((scores, tally, values))

    held = pool_k.shape[0] * PAGE
    held_slot = lax.broadcasted_iota(jnp.int32, (rows, held), 1) // PAGE
    add_part(pool_k[...].reshape(held, -1), pool_v[...].reshape(held, -1), held_slot)
    count, s_rows, kv_width = stretch_ref.shape
    s_rows = s_rows // 2
    fresh = count * s_rows
    add_part(
        stretch_ref[:, :s_rows, :].reshape(fresh, kv_width),
        stretch_ref[:, s_rows:, :].reshape(fresh, kv_width),
        jnp.broadcast_to(slots_ref[...], (rows, fresh)),
    )

    high = functools.reduce(
        jnp.maximum, [jnp.max(scores, axis=-1, keepdims=True) for scores, _, _ in parts]
    )
    total = 0.0
    mixed = 0.0
    for scores, tally, values in parts:
        weights = jnp.exp2((scores - high) * EXP2_SCALE) * tally
        total = total + jnp.sum(weights, axis=-1, keepdims=True)
        mixed = mixed + jnp.dot(
            weights.reshape(heads * rows, -1).astype(jnp.bfloat16),
            values,
            preferred_element_type=jnp.float32,
        )
    for head in range(heads):
        kv = head // GROUP
        piece = mixed[head * rows : (head + 1) * rows, kv * HEAD_DIM : (kv + 1) * HEAD_DIM]
        out_ref[:, head * HEAD_DIM : (head + 1) * HEAD_DIM] = (piece / total[head]).astype(jnp.bfloat16)


def per_device(
    count,
    queries,
    stretch_keys,
    stretch_values,
    cache_keys,
    cache_values,
    prefix_length,
    page_targets,
    pool_keys,
    pool_values,
    decode_queries,
    page_lists,
    context_length,
):
    own = lax.axis_index("ctx")
    own_array = jnp.full((1,), own, jnp.int32)
    tokens, width = queries.shape
    kv_local = stretch_keys.shape[1] // HEAD_DIM
    rows = GROUP * tokens
    c_rows = cache_keys.shape[0]
    f32 = jnp.float32
    params = pltpu.CompilerParams(vmem_limit_bytes=VMEM_BYTES)

    own_c = jnp.concatenate([cache_keys, cache_values], axis=0)
    own_s = jnp.concatenate([stretch_keys, stretch_values], axis=0)
    all_c = lax.all_gather(own_c, "ctx", axis=0, tiled=True).reshape(count, 2 * c_rows, -1)
    all_s = lax.all_gather(own_s, "ctx", axis=0, tiled=True).reshape(count, 2 * tokens, -1)

    def cost(keys):
        pairs = kv_local * rows * keys
        return pl.CostEstimate(
            flops=4 * pairs * HEAD_DIM, bytes_accessed=4 * rows * kv_local * HEAD_DIM, transcendentals=pairs
        )

    qt, high, total, accum = pl.pallas_call(
        near_kernel,
        out_shape=(
            jax.ShapeDtypeStruct((kv_local, HEAD_DIM, rows), jnp.bfloat16),
            jax.ShapeDtypeStruct((kv_local, 1, rows), f32),
            jax.ShapeDtypeStruct((kv_local, 1, rows), f32),
            jax.ShapeDtypeStruct((kv_local, HEAD_DIM, rows), f32),
        ),
        in_specs=[SMEM, SMEM] + [VMEM] * 3,
        out_specs=(VMEM,) * 4,
        compiler_params=params,
        cost_estimate=cost(count * tokens + c_rows),
        name="stretch_and_own_cache",
    )(own_array, prefix_length, queries, all_s, own_c)

    slots = jnp.where(page_targets // P_DEV == own, pool_keys.shape[0] + page_targets % P_DEV, -1)
    slots = jnp.repeat(slots, PAGE).reshape(1, -1)
    decoded = pl.pallas_call(
        decode_kernel,
        out_shape=jax.ShapeDtypeStruct(decode_queries.shape, jnp.bfloat16),
        in_specs=[VMEM] * 7,
        out_specs=VMEM,
        compiler_params=params,
        cost_estimate=pl.CostEstimate(
            flops=4 * 128 * 2048 * 256, bytes_accessed=4 * pool_keys.size, transcendentals=128 * 2560
        ),
        name="decode_rows",
    )(
        slots, decode_queries, page_lists, context_length.reshape(-1, 1),
        pool_keys, pool_values, all_s,
    )

    prefill = pl.pallas_call(
        functools.partial(far_kernel, count),
        out_shape=jax.ShapeDtypeStruct((tokens, width), jnp.bfloat16),
        in_specs=[SMEM, SMEM] + [VMEM] * 5,
        out_specs=VMEM,
        compiler_params=params,
        cost_estimate=cost((count - 1) * c_rows),
        name="other_cache_shards",
    )(own_array, prefix_length, qt, all_c, high, total, accum)
    return (prefill, decoded)


def solution(mesh):
    in_specs = (
        P(("groups", "ctx"), "head"),
        P(("groups", "ctx"), "head"),
        P(("groups", "ctx"), "head"),
        P(("groups", "ctx"), "head"),
        P(("groups", "ctx"), "head"),
        P("groups"),
        P("groups"),
        P(("groups", "ctx"), None, "head"),
        P(("groups", "ctx"), None, "head"),
        P(("groups", "ctx"), "head"),
        P(("groups", "ctx"), None),
        P(("groups", "ctx")),
    )
    out_specs = (P(("groups", "ctx"), "head"), P(("groups", "ctx"), "head"))
    return jax.shard_map(
        functools.partial(per_device, mesh.shape["ctx"]),
        mesh=mesh,
        in_specs=in_specs,
        out_specs=out_specs,
        check_vma=False,
    )
```

```python
import functools

import jax
import jax.numpy as jnp
from jax import lax
from jax.experimental import pallas as pl
from jax.experimental.pallas import tpu as pltpu
from jax.sharding import PartitionSpec as P

HEADS = 64
KV_HEADS = 8
HEAD_DIM = 128
GROUP = HEADS // KV_HEADS
PAGE = 16
P_DEV = 8
EXP2_SCALE = HEAD_DIM ** (-0.5) * 1.4426950408889634
HIDDEN = -1e30
VMEM_BYTES = 48 * 1024 * 1024

VMEM = pl.BlockSpec(memory_space=pltpu.VMEM)
SMEM = pl.BlockSpec(memory_space=pltpu.SMEM)


def attend(qt_ref, head, cols, keys, values_t, state):
    tokens = keys.shape[1] - HEAD_DIM
    queries = qt_ref[head, :, cols]
    place = lax.broadcasted_iota(jnp.int32, (tokens, queries.shape[1]), 0)
    token = lax.rem(lax.broadcasted_iota(jnp.int32, (tokens, queries.shape[1]), 1), tokens)
    pick = jnp.where(place == token, jnp.float32(1.0), jnp.float32(0.0)).astype(jnp.bfloat16)
    queries = jnp.concatenate([queries, pick], axis=0)
    scores = jnp.dot(keys, queries, preferred_element_type=jnp.float32)
    high = jnp.max(scores, axis=0, keepdims=True)
    if state is not None:
        old_high, old_total, old_accum = state
        high = jnp.maximum(high, old_high)
    weights = jnp.exp2((scores - high) * EXP2_SCALE)
    total = jnp.sum(weights, axis=0, keepdims=True)
    accum = jnp.dot(values_t, weights.astype(jnp.bfloat16), preferred_element_type=jnp.float32)
    if state is not None:
        decay = jnp.exp2((old_high - high) * EXP2_SCALE)
        total = total + old_total * decay
        accum = accum + old_accum * decay
    return high, total, accum


def hidden(seen):
    return jnp.where(seen, jnp.float32(0.0), jnp.float32(HIDDEN)).astype(jnp.bfloat16)


def shard_mask(shard, own, limit, tokens, keys):
    c_rows = keys - tokens
    place = lax.broadcasted_iota(jnp.int32, (keys, tokens), 0)
    token = lax.broadcasted_iota(jnp.int32, (keys, tokens), 1)
    stretch = place - token <= (own - shard) * tokens
    cached = place - tokens < limit - shard * c_rows
    return hidden(((place < tokens) & stretch) | ((place >= tokens) & cached))


def wide_queries(q_ref, kv_local):
    heads = q_ref.shape[1] // HEAD_DIM
    queries = q_ref[...].astype(jnp.float32)
    stacked = []
    for head in range(heads):
        piece = queries[:, head * HEAD_DIM : (head + 1) * HEAD_DIM]
        blank = jnp.zeros_like(piece)
        stacked.append(
            jnp.concatenate([piece if kv == head // GROUP else blank for kv in range(kv_local)], axis=1)
        )
    return jnp.concatenate(stacked, axis=0).astype(jnp.bfloat16)


def decode_attend(queries, lists, lengths, parts, state):
    rows, span = lists.shape
    heads = queries.shape[0] // rows
    done = []
    for keys, values, slot in parts:
        tokens = slot.shape[1]
        offset = lax.rem(lax.broadcasted_iota(jnp.int32, (rows, tokens), 1), PAGE)
        tally = jnp.zeros((rows, tokens), jnp.float32)
        for entry in range(span):
            hit = (slot == lists[:, entry : entry + 1]) & (offset < lengths - entry * PAGE)
            tally = tally + jnp.where(hit, jnp.float32(1.0), jnp.float32(0.0))
        tally = tally[None]
        scores = lax.dot_general(
            queries, keys, (((1,), (1,)), ((), ())), preferred_element_type=jnp.float32
        ).reshape(heads, rows, tokens)
        done.append((jnp.where(tally > 0, scores, jnp.float32(HIDDEN)), tally, values))
    highs = [jnp.max(scores, axis=-1, keepdims=True) for scores, _, _ in done]
    if state is not None:
        old_high, old_total, old_mixed = state
        highs.append(old_high)
    high = functools.reduce(jnp.maximum, highs)
    total, mixed = 0.0, 0.0
    if state is not None:
        decay = jnp.exp2((old_high - high) * EXP2_SCALE)
        total = old_total * decay
        mixed = old_mixed * decay
    for scores, tally, values in done:
        weights = jnp.exp2((scores - high) * EXP2_SCALE) * tally
        total = total + jnp.sum(weights, axis=-1, keepdims=True)
        mixed = mixed + jnp.dot(
            weights.reshape(heads * rows, -1).astype(jnp.bfloat16),
            values,
            preferred_element_type=jnp.float32,
        ).reshape(heads, rows, -1)
    return high, total, mixed


def own_kernel(own_ref, limit_ref, q_ref, shard_ref, qt_ref, high_ref, total_ref, accum_ref):
    kv_local, _, rows = qt_ref.shape
    tokens = q_ref.shape[0]
    for head in range(kv_local):
        for sub in range(GROUP):
            col = (head * GROUP + sub) * HEAD_DIM
            qt_ref[head, :, sub * tokens : (sub + 1) * tokens] = q_ref[:, col : col + HEAD_DIM].T
    half = shard_ref.shape[0] // 2
    width = min(2 * tokens, rows)
    mask = shard_mask(own_ref[0], own_ref[0], limit_ref[0], tokens, half)
    for head in range(kv_local):
        feats = slice(head * HEAD_DIM, (head + 1) * HEAD_DIM)
        keys = jnp.concatenate([shard_ref[:half, feats], mask], axis=1)
        values_t = shard_ref[half:, feats].T
        for start in range(0, rows, width):
            cols = slice(start, start + width)
            high, total, accum = attend(qt_ref, head, cols, keys, values_t, None)
            high_ref[head, :, cols] = high
            total_ref[head, :, cols] = total
            accum_ref[head, :, cols] = accum


def held_kernel(
    own_ref, q_ref, lists_ref, length_ref, slots_ref, pool_k, pool_v, shard_ref,
    wide_ref, high_ref, total_ref, mixed_ref,
):
    rows = q_ref.shape[0]
    tokens = slots_ref.shape[1]
    half, kv_width = shard_ref.shape
    half = half // 2
    held = pool_k.shape[0] * PAGE
    queries = wide_queries(q_ref, kv_width // HEAD_DIM)
    wide_ref[...] = queries
    held_slot = lax.broadcasted_iota(jnp.int32, (rows, held), 1) // PAGE
    own_slot = jnp.broadcast_to(slots_ref[pl.ds(own_ref[0], 1), :], (rows, tokens))
    parts = [
        (pool_k[...].reshape(held, kv_width), pool_v[...].reshape(held, kv_width), held_slot),
        (shard_ref[:tokens], shard_ref[half : half + tokens], own_slot),
    ]
    high_ref[...], total_ref[...], mixed_ref[...] = decode_attend(
        queries, lists_ref[...], length_ref[...], parts, None
    )


def hop_kernel(count, hops, last, *refs):
    own_ref, limit_ref, qt_ref, wide_ref, lists_ref, length_ref, slots_ref = refs[:7]
    shard_refs = refs[7 : 7 + len(hops)]
    high_in, total_in, accum_in, dec_high, dec_total, dec_mixed = refs[7 + len(hops) : 13 + len(hops)]
    outs = refs[13 + len(hops) :]
    own = own_ref[0]
    limit = limit_ref[0]
    kv_local, _, rows = qt_ref.shape
    tokens = slots_ref.shape[1]
    half = shard_refs[0].shape[0] // 2
    width = min(2 * tokens, rows)
    shards = [lax.rem(own + hop + count, count) for hop in hops]

    dec_rows = lists_ref.shape[0]
    parts = [
        (
            ref[:tokens],
            ref[half : half + tokens],
            jnp.broadcast_to(slots_ref[pl.ds(shard, 1), :], (dec_rows, tokens)),
        )
        for shard, ref in zip(shards, shard_refs)
    ]
    state = (dec_high[...], dec_total[...], dec_mixed[...])
    state = decode_attend(wide_ref[...], lists_ref[...], length_ref[...], parts, state)
    if last:
        _, total, mixed = state
        for head in range(kv_local * GROUP):
            kv = head // GROUP
            piece = mixed[head, :, kv * HEAD_DIM : (kv + 1) * HEAD_DIM] / total[head]
            outs[1][:, head * HEAD_DIM : (head + 1) * HEAD_DIM] = piece.astype(jnp.bfloat16)
    else:
        outs[3][...], outs[4][...], outs[5][...] = state

    mask = jnp.concatenate([shard_mask(shard, own, limit, tokens, half) for shard in shards], axis=0)
    for head in range(kv_local):
        feats = slice(head * HEAD_DIM, (head + 1) * HEAD_DIM)
        keys = jnp.concatenate([ref[:half, feats] for ref in shard_refs], axis=0)
        keys = jnp.concatenate([keys, mask], axis=1)
        values_t = jnp.concatenate([ref[half:, feats] for ref in shard_refs], axis=0).T
        for start in range(0, rows, width):
            cols = slice(start, start + width)
            state = (high_in[head, :, cols], total_in[head, :, cols], accum_in[head, :, cols])
            high, total, accum = attend(qt_ref, head, cols, keys, values_t, state)
            if last:
                mixed = (accum / total).astype(jnp.bfloat16)
                for piece in range(width // tokens):
                    col = (head * GROUP + start // tokens + piece) * HEAD_DIM
                    outs[0][:, col : col + HEAD_DIM] = mixed[:, piece * tokens : (piece + 1) * tokens].T
            else:
                outs[0][head, :, cols] = high
                outs[1][head, :, cols] = total
                outs[2][head, :, cols] = accum


def per_device(
    count,
    queries,
    stretch_keys,
    stretch_values,
    cache_keys,
    cache_values,
    prefix_length,
    page_targets,
    pool_keys,
    pool_values,
    decode_queries,
    page_lists,
    context_length,
):
    own = lax.axis_index("ctx")
    own_array = jnp.full((1,), own, jnp.int32)
    tokens, width = queries.shape
    kv_width = stretch_keys.shape[1]
    kv_local = kv_width // HEAD_DIM
    rows = GROUP * tokens
    heads = kv_local * GROUP
    dec_rows = decode_queries.shape[0]
    half = tokens + cache_keys.shape[0]
    f32 = jnp.float32
    params = pltpu.CompilerParams(vmem_limit_bytes=VMEM_BYTES)

    up_pairs = [(i, (i + 1) % count) for i in range(count)]
    down_pairs = [(i, (i - 1) % count) for i in range(count)]
    shard = jnp.concatenate([stretch_keys, cache_keys, stretch_values, cache_values], axis=0)
    ups, downs = [shard], [shard]
    for hop in range(1, count // 2 + 1):
        ups.append(lax.ppermute(ups[-1], "ctx", up_pairs))
        if hop <= (count - 1) // 2:
            downs.append(lax.ppermute(downs[-1], "ctx", down_pairs))

    def cost(keys):
        pairs = kv_local * rows * keys
        return pl.CostEstimate(
            flops=4 * pairs * HEAD_DIM, bytes_accessed=4 * rows * kv_local * HEAD_DIM, transcendentals=pairs
        )

    state_shapes = (
        jax.ShapeDtypeStruct((kv_local, 1, rows), f32),
        jax.ShapeDtypeStruct((kv_local, 1, rows), f32),
        jax.ShapeDtypeStruct((kv_local, HEAD_DIM, rows), f32),
    )
    dec_shapes = (
        jax.ShapeDtypeStruct((heads, dec_rows, 1), f32),
        jax.ShapeDtypeStruct((heads, dec_rows, 1), f32),
        jax.ShapeDtypeStruct((heads, dec_rows, kv_width), f32),
    )
    qt, *state = pl.pallas_call(
        own_kernel,
        out_shape=(jax.ShapeDtypeStruct((kv_local, HEAD_DIM, rows), jnp.bfloat16),) + state_shapes,
        in_specs=[SMEM, SMEM, VMEM, VMEM],
        out_specs=(VMEM,) * 4,
        compiler_params=params,
        cost_estimate=cost(half),
        name="own_shard",
    )(own_array, prefix_length, queries, shard)

    slots = jnp.where(page_targets // P_DEV == own, pool_keys.shape[0] + page_targets % P_DEV, -1)
    slots = jnp.repeat(slots, PAGE).reshape(count, tokens)
    lengths = context_length.reshape(-1, 1)
    wide, *dec_state = pl.pallas_call(
        held_kernel,
        out_shape=(jax.ShapeDtypeStruct((heads * dec_rows, kv_width), jnp.bfloat16),) + dec_shapes,
        in_specs=[SMEM] + [VMEM] * 7,
        out_specs=(VMEM,) * 4,
        compiler_params=params,
        cost_estimate=pl.CostEstimate(
            flops=4 * 128 * 2048 * 256, bytes_accessed=4 * pool_keys.size, transcendentals=128 * 2560
        ),
        name="decode_held_pages",
    )(own_array, decode_queries, page_lists, lengths, slots, pool_keys, pool_values, shard)

    for hop in range(1, count // 2 + 1):
        last = hop == count // 2
        hops, shards = [-hop], [ups[hop]]
        if hop < len(downs):
            hops.append(hop)
            shards.append(downs[hop])
        out_shape = state_shapes + dec_shapes
        if last:
            out_shape = (
                jax.ShapeDtypeStruct((tokens, width), jnp.bfloat16),
                jax.ShapeDtypeStruct(decode_queries.shape, jnp.bfloat16),
            )
        results = pl.pallas_call(
            functools.partial(hop_kernel, count, hops, last),
            out_shape=out_shape,
            in_specs=[SMEM, SMEM] + [VMEM] * (11 + len(hops)),
            out_specs=(VMEM,) * len(out_shape),
            compiler_params=params,
            cost_estimate=cost(half * len(hops)),
            name="shards_" + str(hop) + "_away",
        )(
            own_array, prefix_length, qt, wide, page_lists, lengths, slots,
            *shards, *state, *dec_state,
        )
        if last:
            return tuple(results)
        state, dec_state = results[:3], results[3:]


def solution(mesh):
    in_specs = (
        P(("groups", "ctx"), "head"),
        P(("groups", "ctx"), "head"),
        P(("groups", "ctx"), "head"),
        P(("groups", "ctx"), "head"),
        P(("groups", "ctx"), "head"),
        P("groups"),
        P("groups"),
        P(("groups", "ctx"), None, "head"),
        P(("groups", "ctx"), None, "head"),
        P(("groups", "ctx"), "head"),
        P(("groups", "ctx"), None),
        P(("groups", "ctx")),
    )
    out_specs = (P(("groups", "ctx"), "head"), P(("groups", "ctx"), "head"))
    return jax.shard_map(
        functools.partial(per_device, mesh.shape["ctx"]),
        mesh=mesh,
        in_specs=in_specs,
        out_specs=out_specs,
        check_vma=False,
    )
```

```python
import functools

import jax
import jax.numpy as jnp
from jax import lax
from jax.experimental import pallas as pl
from jax.experimental.pallas import tpu as pltpu
from jax.sharding import PartitionSpec as P

HEADS = 64
KV_HEADS = 8
HEAD_DIM = 128
GROUP = HEADS // KV_HEADS
PAGE = 16
P_DEV = 8
EXP2_SCALE = HEAD_DIM ** (-0.5) * 1.4426950408889634
HIDDEN = -1e30
VMEM_BYTES = 48 * 1024 * 1024

VMEM = pl.BlockSpec(memory_space=pltpu.VMEM)
SMEM = pl.BlockSpec(memory_space=pltpu.SMEM)


def attend(qt_ref, head, cols, keys, values_t, state):
    tokens = keys.shape[1] - HEAD_DIM
    queries = qt_ref[head, :, cols]
    place = lax.broadcasted_iota(jnp.int32, (tokens, queries.shape[1]), 0)
    token = lax.rem(lax.broadcasted_iota(jnp.int32, (tokens, queries.shape[1]), 1), tokens)
    pick = jnp.where(place == token, jnp.float32(1.0), jnp.float32(0.0)).astype(jnp.bfloat16)
    queries = jnp.concatenate([queries, pick], axis=0)
    scores = jnp.dot(keys, queries, preferred_element_type=jnp.float32)
    high = jnp.max(scores, axis=0, keepdims=True)
    if state is not None:
        old_high, old_total, old_accum = state
        high = jnp.maximum(high, old_high)
    weights = jnp.exp2((scores - high) * EXP2_SCALE)
    total = jnp.sum(weights, axis=0, keepdims=True)
    accum = jnp.dot(values_t, weights.astype(jnp.bfloat16), preferred_element_type=jnp.float32)
    if state is not None:
        decay = jnp.exp2((old_high - high) * EXP2_SCALE)
        total = total + old_total * decay
        accum = accum + old_accum * decay
    return high, total, accum


def hidden(seen):
    return jnp.where(seen, jnp.float32(0.0), jnp.float32(HIDDEN)).astype(jnp.bfloat16)


def shard_mask(shard, own, limit, tokens, keys):
    c_rows = keys - tokens
    place = lax.broadcasted_iota(jnp.int32, (keys, tokens), 0)
    token = lax.broadcasted_iota(jnp.int32, (keys, tokens), 1)
    stretch = place - token <= (own - shard) * tokens
    cached = place - tokens < limit - shard * c_rows
    return hidden(((place < tokens) & stretch) | ((place >= tokens) & cached))


def wide_queries(q_ref, kv_local):
    heads = q_ref.shape[1] // HEAD_DIM
    queries = q_ref[...].astype(jnp.float32)
    stacked = []
    for head in range(heads):
        piece = queries[:, head * HEAD_DIM : (head + 1) * HEAD_DIM]
        blank = jnp.zeros_like(piece)
        stacked.append(
            jnp.concatenate([piece if kv == head // GROUP else blank for kv in range(kv_local)], axis=1)
        )
    return jnp.concatenate(stacked, axis=0).astype(jnp.bfloat16)


def decode_attend(queries, lists, lengths, parts, state):
    rows, span = lists.shape
    heads = queries.shape[0] // rows
    done = []
    for keys, values, slot in parts:
        tokens = slot.shape[1]
        offset = lax.rem(lax.broadcasted_iota(jnp.int32, (rows, tokens), 1), PAGE)
        tally = jnp.zeros((rows, tokens), jnp.float32)
        for entry in range(span):
            hit = (slot == lists[:, entry : entry + 1]) & (offset < lengths - entry * PAGE)
            tally = tally + jnp.where(hit, jnp.float32(1.0), jnp.float32(0.0))
        tally = tally[None]
        scores = lax.dot_general(
            queries, keys, (((1,), (1,)), ((), ())), preferred_element_type=jnp.float32
        ).reshape(heads, rows, tokens)
        done.append((jnp.where(tally > 0, scores, jnp.float32(HIDDEN)), tally, values))
    highs = [jnp.max(scores, axis=-1, keepdims=True) for scores, _, _ in done]
    if state is not None:
        old_high, old_total, old_mixed = state
        highs.append(old_high)
    high = functools.reduce(jnp.maximum, highs)
    total, mixed = 0.0, 0.0
    if state is not None:
        decay = jnp.exp2((old_high - high) * EXP2_SCALE)
        total = old_total * decay
        mixed = old_mixed * decay
    for scores, tally, values in done:
        weights = jnp.exp2((scores - high) * EXP2_SCALE) * tally
        total = total + jnp.sum(weights, axis=-1, keepdims=True)
        mixed = mixed + jnp.dot(
            weights.reshape(heads * rows, -1).astype(jnp.bfloat16),
            values,
            preferred_element_type=jnp.float32,
        ).reshape(heads, rows, -1)
    return high, total, mixed


def own_kernel(own_ref, limit_ref, q_ref, shard_ref, qt_ref, high_ref, total_ref, accum_ref):
    kv_local, _, rows = qt_ref.shape
    tokens = q_ref.shape[0]
    for head in range(kv_local):
        for sub in range(GROUP):
            col = (head * GROUP + sub) * HEAD_DIM
            qt_ref[head, :, sub * tokens : (sub + 1) * tokens] = q_ref[:, col : col + HEAD_DIM].T
    half = shard_ref.shape[0] // 2
    width = min(2 * tokens, rows)
    mask = shard_mask(own_ref[0], own_ref[0], limit_ref[0], tokens, half)
    for head in range(kv_local):
        feats = slice(head * HEAD_DIM, (head + 1) * HEAD_DIM)
        keys = jnp.concatenate([shard_ref[:half, feats], mask], axis=1)
        values_t = shard_ref[half:, feats].T
        for start in range(0, rows, width):
            cols = slice(start, start + width)
            high, total, accum = attend(qt_ref, head, cols, keys, values_t, None)
            high_ref[head, :, cols] = high
            total_ref[head, :, cols] = total
            accum_ref[head, :, cols] = accum


def held_kernel(
    own_ref, q_ref, lists_ref, length_ref, slots_ref, pool_k, pool_v, shard_ref,
    wide_ref, high_ref, total_ref, mixed_ref,
):
    rows = q_ref.shape[0]
    tokens = slots_ref.shape[1]
    half, kv_width = shard_ref.shape
    half = half // 2
    held = pool_k.shape[0] * PAGE
    queries = wide_queries(q_ref, kv_width // HEAD_DIM)
    wide_ref[...] = queries
    held_slot = lax.broadcasted_iota(jnp.int32, (rows, held), 1) // PAGE
    own_slot = jnp.broadcast_to(slots_ref[pl.ds(own_ref[0], 1), :], (rows, tokens))
    parts = [
        (pool_k[...].reshape(held, kv_width), pool_v[...].reshape(held, kv_width), held_slot),
        (shard_ref[:tokens], shard_ref[half : half + tokens], own_slot),
    ]
    high_ref[...], total_ref[...], mixed_ref[...] = decode_attend(
        queries, lists_ref[...], length_ref[...], parts, None
    )


def hop_kernel(count, hops, last, *refs):
    own_ref, limit_ref, qt_ref, wide_ref, lists_ref, length_ref, slots_ref = refs[:7]
    shard_refs = refs[7 : 7 + len(hops)]
    high_in, total_in, accum_in, dec_high, dec_total, dec_mixed = refs[7 + len(hops) : 13 + len(hops)]
    outs = refs[13 + len(hops) :]
    own = own_ref[0]
    limit = limit_ref[0]
    kv_local, _, rows = qt_ref.shape
    tokens = slots_ref.shape[1]
    half = shard_refs[0].shape[0] // 2
    width = min(2 * tokens, rows)
    shards = [lax.rem(own + hop + count, count) for hop in hops]

    dec_rows = lists_ref.shape[0]
    parts = [
        (
            ref[:tokens],
            ref[half : half + tokens],
            jnp.broadcast_to(slots_ref[pl.ds(shard, 1), :], (dec_rows, tokens)),
        )
        for shard, ref in zip(shards, shard_refs)
    ]
    state = (dec_high[...], dec_total[...], dec_mixed[...])
    state = decode_attend(wide_ref[...], lists_ref[...], length_ref[...], parts, state)
    if last:
        _, total, mixed = state
        for head in range(kv_local * GROUP):
            kv = head // GROUP
            piece = mixed[head, :, kv * HEAD_DIM : (kv + 1) * HEAD_DIM] / total[head]
            outs[1][:, head * HEAD_DIM : (head + 1) * HEAD_DIM] = piece.astype(jnp.bfloat16)
    else:
        outs[3][...], outs[4][...], outs[5][...] = state

    mask = jnp.concatenate([shard_mask(shard, own, limit, tokens, half) for shard in shards], axis=0)
    for head in range(kv_local):
        feats = slice(head * HEAD_DIM, (head + 1) * HEAD_DIM)
        keys = jnp.concatenate([ref[:half, feats] for ref in shard_refs], axis=0)
        keys = jnp.concatenate([keys, mask], axis=1)
        values_t = jnp.concatenate([ref[half:, feats] for ref in shard_refs], axis=0).T
        for start in range(0, rows, width):
            cols = slice(start, start + width)
            state = (high_in[head, :, cols], total_in[head, :, cols], accum_in[head, :, cols])
            high, total, accum = attend(qt_ref, head, cols, keys, values_t, state)
            if last:
                mixed = (accum / total).astype(jnp.bfloat16)
                for piece in range(width // tokens):
                    col = (head * GROUP + start // tokens + piece) * HEAD_DIM
                    outs[0][:, col : col + HEAD_DIM] = mixed[:, piece * tokens : (piece + 1) * tokens].T
            else:
                outs[0][head, :, cols] = high
                outs[1][head, :, cols] = total
                outs[2][head, :, cols] = accum


def per_device(
    count,
    queries,
    stretch_keys,
    stretch_values,
    cache_keys,
    cache_values,
    prefix_length,
    page_targets,
    pool_keys,
    pool_values,
    decode_queries,
    page_lists,
    context_length,
):
    own = lax.axis_index("ctx")
    own_array = jnp.full((1,), own, jnp.int32)
    tokens, width = queries.shape
    kv_width = stretch_keys.shape[1]
    kv_local = kv_width // HEAD_DIM
    rows = GROUP * tokens
    heads = kv_local * GROUP
    dec_rows = decode_queries.shape[0]
    half = tokens + cache_keys.shape[0]
    f32 = jnp.float32
    params = pltpu.CompilerParams(vmem_limit_bytes=VMEM_BYTES)

    up_pairs = [(i, (i + 1) % count) for i in range(count)]
    down_pairs = [(i, (i - 1) % count) for i in range(count)]
    shard = jnp.concatenate([stretch_keys, cache_keys, stretch_values, cache_values], axis=0)
    ups = [shard, lax.ppermute(shard, "ctx", up_pairs)]
    downs = [shard, lax.ppermute(shard, "ctx", down_pairs)]

    def cost(keys):
        pairs = kv_local * rows * keys
        return pl.CostEstimate(
            flops=4 * pairs * HEAD_DIM, bytes_accessed=4 * rows * kv_local * HEAD_DIM, transcendentals=pairs
        )

    state_shapes = (
        jax.ShapeDtypeStruct((kv_local, 1, rows), f32),
        jax.ShapeDtypeStruct((kv_local, 1, rows), f32),
        jax.ShapeDtypeStruct((kv_local, HEAD_DIM, rows), f32),
    )
    dec_shapes = (
        jax.ShapeDtypeStruct((heads, dec_rows, 1), f32),
        jax.ShapeDtypeStruct((heads, dec_rows, 1), f32),
        jax.ShapeDtypeStruct((heads, dec_rows, kv_width), f32),
    )
    qt, *state = pl.pallas_call(
        own_kernel,
        out_shape=(jax.ShapeDtypeStruct((kv_local, HEAD_DIM, rows), jnp.bfloat16),) + state_shapes,
        in_specs=[SMEM, SMEM, VMEM, VMEM],
        out_specs=(VMEM,) * 4,
        compiler_params=params,
        cost_estimate=cost(half),
        name="own_shard",
    )(own_array, prefix_length, queries, shard)

    slots = jnp.where(page_targets // P_DEV == own, pool_keys.shape[0] + page_targets % P_DEV, -1)
    slots = jnp.repeat(slots, PAGE).reshape(count, tokens)
    lengths = context_length.reshape(-1, 1)
    wide, *dec_state = pl.pallas_call(
        held_kernel,
        out_shape=(jax.ShapeDtypeStruct((heads * dec_rows, kv_width), jnp.bfloat16),) + dec_shapes,
        in_specs=[SMEM] + [VMEM] * 7,
        out_specs=(VMEM,) * 4,
        compiler_params=params,
        cost_estimate=pl.CostEstimate(
            flops=4 * 128 * 2048 * 256, bytes_accessed=4 * pool_keys.size, transcendentals=128 * 2560
        ),
        name="decode_held_pages",
    )(own_array, decode_queries, page_lists, lengths, slots, pool_keys, pool_values, shard)

    ups[1], state, dec_state = lax.optimization_barrier((ups[1], state, dec_state))
    for hop in range(2, count // 2 + 1):
        ups.append(lax.ppermute(ups[-1], "ctx", up_pairs))
        if hop <= (count - 1) // 2:
            downs.append(lax.ppermute(downs[-1], "ctx", down_pairs))

    for hop in range(1, count // 2 + 1):
        last = hop == count // 2
        hops, shards = [-hop], [ups[hop]]
        if hop < len(downs):
            hops.append(hop)
            shards.append(downs[hop])
        out_shape = state_shapes + dec_shapes
        if last:
            out_shape = (
                jax.ShapeDtypeStruct((tokens, width), jnp.bfloat16),
                jax.ShapeDtypeStruct(decode_queries.shape, jnp.bfloat16),
            )
        results = pl.pallas_call(
            functools.partial(hop_kernel, count, hops, last),
            out_shape=out_shape,
            in_specs=[SMEM, SMEM] + [VMEM] * (11 + len(hops)),
            out_specs=(VMEM,) * len(out_shape),
            compiler_params=params,
            cost_estimate=cost(half * len(hops)),
            name="shards_" + str(hop) + "_away",
        )(
            own_array, prefix_length, qt, wide, page_lists, lengths, slots,
            *shards, *state, *dec_state,
        )
        if last:
            return tuple(results)
        state, dec_state = results[:3], results[3:]


def solution(mesh):
    in_specs = (
        P(("groups", "ctx"), "head"),
        P(("groups", "ctx"), "head"),
        P(("groups", "ctx"), "head"),
        P(("groups", "ctx"), "head"),
        P(("groups", "ctx"), "head"),
        P("groups"),
        P("groups"),
        P(("groups", "ctx"), None, "head"),
        P(("groups", "ctx"), None, "head"),
        P(("groups", "ctx"), "head"),
        P(("groups", "ctx"), None),
        P(("groups", "ctx")),
    )
    out_specs = (P(("groups", "ctx"), "head"), P(("groups", "ctx"), "head"))
    return jax.shard_map(
        functools.partial(per_device, mesh.shape["ctx"]),
        mesh=mesh,
        in_specs=in_specs,
        out_specs=out_specs,
        check_vma=False,
    )
```

```python
import functools

import jax
import jax.numpy as jnp
from jax import lax
from jax.experimental import pallas as pl
from jax.experimental.pallas import tpu as pltpu
from jax.sharding import PartitionSpec as P

HEADS = 64
KV_HEADS = 8
HEAD_DIM = 128
GROUP = HEADS // KV_HEADS
PAGE = 16
P_DEV = 8
EXP2_SCALE = HEAD_DIM ** (-0.5) * 1.4426950408889634
HIDDEN = -1e30
VMEM_BYTES = 48 * 1024 * 1024

VMEM = pl.BlockSpec(memory_space=pltpu.VMEM)
SMEM = pl.BlockSpec(memory_space=pltpu.SMEM)
HBM = pl.BlockSpec(memory_space=pltpu.HBM)


def attend(qt_ref, cols, keys, values_t, state):
    tokens = keys.shape[1] - HEAD_DIM
    queries = qt_ref[:, cols]
    place = lax.broadcasted_iota(jnp.int32, (tokens, queries.shape[1]), 0)
    token = lax.rem(lax.broadcasted_iota(jnp.int32, (tokens, queries.shape[1]), 1), tokens)
    pick = jnp.where(place == token, jnp.float32(1.0), jnp.float32(0.0)).astype(jnp.bfloat16)
    queries = jnp.concatenate([queries, pick], axis=0)
    scores = jnp.dot(keys, queries, preferred_element_type=jnp.float32)
    high = jnp.max(scores, axis=0, keepdims=True)
    if state is not None:
        old_high, old_total, old_accum = state
        high = jnp.maximum(high, old_high)
    weights = jnp.exp2((scores - high) * EXP2_SCALE)
    total = jnp.sum(weights, axis=0, keepdims=True)
    accum = jnp.dot(values_t, weights.astype(jnp.bfloat16), preferred_element_type=jnp.float32)
    if state is not None:
        decay = jnp.exp2((old_high - high) * EXP2_SCALE)
        total = total + old_total * decay
        accum = accum + old_accum * decay
    return high, total, accum


def hidden(seen):
    return jnp.where(seen, jnp.float32(0.0), jnp.float32(HIDDEN)).astype(jnp.bfloat16)


def shard_mask(shard, own, limit, tokens, keys):
    c_rows = keys - tokens
    place = lax.broadcasted_iota(jnp.int32, (keys, tokens), 0)
    token = lax.broadcasted_iota(jnp.int32, (keys, tokens), 1)
    stretch = place - token <= (own - shard) * tokens
    cached = place - tokens < limit - shard * c_rows
    return hidden(((place < tokens) & stretch) | ((place >= tokens) & cached))


def slot_row(targets_ref, shard, own, tokens, pool):
    page = lax.broadcasted_iota(jnp.int32, (1, tokens), 1) // PAGE
    slots = jnp.full((1, tokens), -1, jnp.int32)
    for index in range(tokens // PAGE):
        target = targets_ref[shard * (tokens // PAGE) + index]
        slot = jnp.where(target // P_DEV == own, pool + target % P_DEV, -1)
        slots = jnp.where(page == index, slot, slots)
    return slots


def length_column(length_ref):
    rows = length_ref.shape[0]
    place = lax.broadcasted_iota(jnp.int32, (rows, 1), 0)
    lengths = jnp.zeros((rows, 1), jnp.int32)
    for row in range(rows):
        lengths = jnp.where(place == row, length_ref[row], lengths)
    return lengths


def tally_of(lists, lengths, slot):
    rows, span = lists.shape
    tokens = slot.shape[1]
    slot = jnp.broadcast_to(slot, (rows, tokens))
    offset = lax.rem(lax.broadcasted_iota(jnp.int32, (rows, tokens), 1), PAGE)
    tally = jnp.zeros((rows, tokens), jnp.float32)
    for entry in range(span):
        hit = (slot == lists[:, entry : entry + 1]) & (offset < lengths - entry * PAGE)
        tally = tally + jnp.where(hit, jnp.float32(1.0), jnp.float32(0.0))
    return tally[None]


def decode_attend(queries, parts, state):
    done = []
    for keys, values, tally in parts:
        scores = lax.dot_general(
            queries, keys, (((1,), (1,)), ((), ())), preferred_element_type=jnp.float32
        ).reshape(-1, tally.shape[1], tally.shape[2])
        done.append((jnp.where(tally > 0, scores, jnp.float32(HIDDEN)), tally, values))
    highs = [jnp.max(scores, axis=-1, keepdims=True) for scores, _, _ in done]
    if state is not None:
        old_high, old_total, old_mixed = state
        highs.append(old_high)
    high = functools.reduce(jnp.maximum, highs)
    total, mixed = 0.0, 0.0
    if state is not None:
        decay = jnp.exp2((old_high - high) * EXP2_SCALE)
        total = old_total * decay
        mixed = old_mixed * decay
    for scores, tally, values in done:
        weights = jnp.exp2((scores - high) * EXP2_SCALE) * tally
        total = total + jnp.sum(weights, axis=-1, keepdims=True)
        mixed = mixed + jnp.dot(
            weights.reshape(queries.shape[0], -1).astype(jnp.bfloat16),
            values,
            preferred_element_type=jnp.float32,
        ).reshape(high.shape[0], high.shape[1], -1)
    return high, total, mixed


def pack_kernel(sk_ref, ck_ref, sv_ref, cv_ref, *refs):
    outs, sems = refs[:-1], refs[-1]
    copies = []
    for head, out_ref in enumerate(outs):
        feats = pl.ds(head * HEAD_DIM, HEAD_DIM)
        start = 0
        for place, ref in enumerate((sk_ref, ck_ref, sv_ref, cv_ref)):
            rows = ref.shape[0]
            copies.append(
                pltpu.make_async_copy(
                    ref.at[:, feats], out_ref.at[pl.ds(start, rows), :], sems.at[head, place]
                )
            )
            start += rows
    for copy in copies:
        copy.start()
    for copy in copies:
        copy.wait()


def own_kernel(kv_local, own_ref, limit_ref, q_ref, *refs):
    shard_refs, outs = refs[:kv_local], refs[kv_local:]
    tokens = q_ref.shape[0]
    rows = GROUP * tokens
    half = shard_refs[0].shape[0] // 2
    width = min(2 * tokens, rows)
    mask = shard_mask(own_ref[0], own_ref[0], limit_ref[0], tokens, half)
    for head in range(kv_local):
        qt_ref, high_ref, total_ref, accum_ref = outs[4 * head : 4 * head + 4]
        for sub in range(GROUP):
            col = (head * GROUP + sub) * HEAD_DIM
            qt_ref[:, sub * tokens : (sub + 1) * tokens] = q_ref[:, col : col + HEAD_DIM].T
        keys = jnp.concatenate([shard_refs[head][:half], mask], axis=1)
        values_t = shard_refs[head][half:].T
        for start in range(0, rows, width):
            cols = slice(start, start + width)
            high, total, accum = attend(qt_ref, cols, keys, values_t, None)
            high_ref[:, cols] = high
            total_ref[:, cols] = total
            accum_ref[:, cols] = accum


def held_kernel(kv_local, own_ref, targets_ref, length_ref, q_ref, lists_ref, pool_k, pool_v, *refs):
    shard_refs = refs[:kv_local]
    outs = refs[kv_local:-3]
    keys_ref, values_ref, sems = refs[-3:]
    copies = []
    for place, (source, target) in enumerate(((pool_k, keys_ref), (pool_v, values_ref))):
        pages = source.shape[0] // 2
        for part in range(2):
            span = pl.ds(part * pages, pages)
            copies.append(pltpu.make_async_copy(source.at[span], target.at[span], sems.at[place, part]))
    for copy in copies:
        copy.start()
    dec_rows = q_ref.shape[0]
    half = shard_refs[0].shape[0] // 2
    pool = keys_ref.shape[0]
    held = pool * PAGE
    tokens = PAGE * P_DEV
    own = own_ref[0]
    lists = lists_ref[...]
    lengths = length_column(length_ref)
    held_tally = tally_of(lists, lengths, lax.broadcasted_iota(jnp.int32, (1, held), 1) // PAGE)
    own_tally = tally_of(lists, lengths, slot_row(targets_ref, own, own, tokens, pool))
    queries = q_ref[...].astype(jnp.float32)
    for head in range(kv_local):
        pieces = [
            queries[:, (head * GROUP + sub) * HEAD_DIM : (head * GROUP + sub + 1) * HEAD_DIM]
            for sub in range(GROUP)
        ]
        outs[4 * head][...] = jnp.concatenate(pieces, axis=0).astype(jnp.bfloat16)
    for copy in copies:
        copy.wait()
    for head in range(kv_local):
        feats = slice(head * HEAD_DIM, (head + 1) * HEAD_DIM)
        rows_ref, high_ref, total_ref, mixed_ref = outs[4 * head : 4 * head + 4]
        parts = [
            (keys_ref[:, :, feats].reshape(held, -1), values_ref[:, :, feats].reshape(held, -1), held_tally),
            (shard_refs[head][:tokens], shard_refs[head][half : half + tokens], own_tally),
        ]
        high_ref[...], total_ref[...], mixed_ref[...] = decode_attend(rows_ref[...], parts, None)


def hop_kernel(count, hops, pool, last, first_out, *refs):
    own_ref, limit_ref, targets_ref, length_ref, lists_ref = refs[:5]
    shard_refs = refs[5 : 5 + len(hops)]
    qt_ref, high_in, total_in, accum_in, dec_q, dec_high, dec_total, dec_mixed = refs[5 + len(hops) : 13 + len(hops)]
    outs = refs[first_out:]
    own = own_ref[0]
    limit = limit_ref[0]
    rows = qt_ref.shape[1]
    tokens = rows // GROUP
    half = shard_refs[0].shape[0] // 2
    width = min(2 * tokens, rows)
    shards = [lax.rem(own + hop + count, count) for hop in hops]

    lists = lists_ref[...]
    lengths = length_column(length_ref)
    parts = [
        (
            ref[:tokens],
            ref[half : half + tokens],
            tally_of(lists, lengths, slot_row(targets_ref, shard, own, tokens, pool)),
        )
        for shard, ref in zip(shards, shard_refs)
    ]
    state = decode_attend(dec_q[...], parts, (dec_high[...], dec_total[...], dec_mixed[...]))
    if last:
        _, total, mixed = state
        for sub in range(GROUP):
            outs[1][:, sub * HEAD_DIM : (sub + 1) * HEAD_DIM] = (mixed[sub] / total[sub]).astype(jnp.bfloat16)
    else:
        outs[3][...], outs[4][...], outs[5][...] = state

    mask = jnp.concatenate([shard_mask(shard, own, limit, tokens, half) for shard in shards], axis=0)
    keys = jnp.concatenate([jnp.concatenate([ref[:half] for ref in shard_refs], axis=0), mask], axis=1)
    values_t = jnp.concatenate([ref[half:] for ref in shard_refs], axis=0).T
    for start in range(0, rows, width):
        cols = slice(start, start + width)
        state = (high_in[:, cols], total_in[:, cols], accum_in[:, cols])
        high, total, accum = attend(qt_ref, cols, keys, values_t, state)
        if last:
            mixed = (accum * (1.0 / total)).astype(jnp.bfloat16)
            for piece in range(width // tokens):
                col = (start // tokens + piece) * HEAD_DIM
                outs[0][:, col : col + HEAD_DIM] = mixed[:, piece * tokens : (piece + 1) * tokens].T
        else:
            outs[0][:, cols] = high
            outs[1][:, cols] = total
            outs[2][:, cols] = accum


def per_device(
    count,
    queries,
    stretch_keys,
    stretch_values,
    cache_keys,
    cache_values,
    prefix_length,
    page_targets,
    pool_keys,
    pool_values,
    decode_queries,
    page_lists,
    context_length,
):
    own = lax.axis_index("ctx")
    own_array = jnp.full((1,), own, jnp.int32)
    tokens, width = queries.shape
    kv_local = stretch_keys.shape[1] // HEAD_DIM
    rows = GROUP * tokens
    dec_rows = decode_queries.shape[0]
    half = tokens + cache_keys.shape[0]
    pool = pool_keys.shape[0]
    f32, bf16 = jnp.float32, jnp.bfloat16
    params = pltpu.CompilerParams(vmem_limit_bytes=VMEM_BYTES)
    up_pairs = [(i, (i + 1) % count) for i in range(count)]
    down_pairs = [(i, (i - 1) % count) for i in range(count)]
    shape = jax.ShapeDtypeStruct

    def cost(keys):
        pairs = rows * keys
        return pl.CostEstimate(
            flops=4 * pairs * HEAD_DIM, bytes_accessed=4 * rows * HEAD_DIM, transcendentals=pairs
        )

    shard = pl.pallas_call(
        pack_kernel,
        out_shape=(shape((2 * half, HEAD_DIM), bf16),) * kv_local,
        in_specs=[HBM] * 4,
        out_specs=(HBM,) * kv_local,
        scratch_shapes=[pltpu.SemaphoreType.DMA((kv_local, 4))],
        name="pack_own_shard",
    )(stretch_keys, cache_keys, stretch_values, cache_values)

    ups = [list(shard), [lax.ppermute(piece, "ctx", up_pairs) for piece in shard]]

    state_shapes = (shape((1, rows), f32), shape((1, rows), f32), shape((HEAD_DIM, rows), f32))
    dec_shapes = (
        shape((GROUP, dec_rows, 1), f32),
        shape((GROUP, dec_rows, 1), f32),
        shape((GROUP, dec_rows, HEAD_DIM), f32),
    )
    results = pl.pallas_call(
        functools.partial(own_kernel, kv_local),
        out_shape=((shape((HEAD_DIM, rows), bf16),) + state_shapes) * kv_local,
        in_specs=[SMEM, SMEM] + [VMEM] * (1 + kv_local),
        out_specs=(VMEM,) * (4 * kv_local),
        compiler_params=params,
        cost_estimate=cost(half * kv_local),
        name="own_shard",
    )(own_array, prefix_length, queries, *shard)
    states = [list(results[4 * head : 4 * head + 4]) for head in range(kv_local)]

    sent_down, states = lax.optimization_barrier((list(shard), states))
    downs = [sent_down, [lax.ppermute(piece, "ctx", down_pairs) for piece in sent_down]]

    results = pl.pallas_call(
        functools.partial(held_kernel, kv_local),
        out_shape=((shape((GROUP * dec_rows, HEAD_DIM), bf16),) + dec_shapes) * kv_local,
        in_specs=[SMEM] * 3 + [VMEM] * 2 + [HBM] * 2 + [VMEM] * kv_local,
        out_specs=(VMEM,) * (4 * kv_local),
        scratch_shapes=[
            pltpu.VMEM(pool_keys.shape, bf16),
            pltpu.VMEM(pool_values.shape, bf16),
            pltpu.SemaphoreType.DMA((2, 2)),
        ],
        compiler_params=params,
        cost_estimate=pl.CostEstimate(
            flops=4 * 128 * 2048 * 256, bytes_accessed=4 * pool_keys.size, transcendentals=128 * 2560
        ),
        name="decode_held_pages",
    )(
        own_array, page_targets, context_length, decode_queries, page_lists, pool_keys, pool_values, *shard
    )
    dec_states = [list(results[4 * head : 4 * head + 4]) for head in range(kv_local)]

    for head in range(kv_local):
        ups[1][head], dec_states[head] = lax.optimization_barrier((ups[1][head], dec_states[head]))
    for hop in range(2, count // 2 + 1):
        ups.append([lax.ppermute(piece, "ctx", up_pairs) for piece in ups[-1]])
        if hop <= (count - 1) // 2:
            downs.append([lax.ppermute(piece, "ctx", down_pairs) for piece in downs[-1]])

    outputs = None
    for hop in range(1, count // 2 + 1):
        last = hop == count // 2
        hops = [-hop] + ([hop] if hop < len(downs) else [])
        for head in range(kv_local):
            operands = [own_array, prefix_length, page_targets, context_length, page_lists, ups[hop][head]]
            if hop < len(downs):
                operands.append(downs[hop][head])
            operands += states[head] + dec_states[head]
            in_specs = [SMEM] * 4 + [VMEM] * (len(operands) - 4)
            options = {}
            if last:
                out_shape = (shape((tokens, width), bf16), shape(decode_queries.shape, bf16))
                out_specs = (
                    pl.BlockSpec((tokens, rows), lambda step, head=head: (0, head)),
                    pl.BlockSpec((dec_rows, GROUP * HEAD_DIM), lambda step, head=head: (0, head)),
                )
                options["grid"] = (1,)
                if outputs is not None:
                    options["input_output_aliases"] = {len(operands): 0, len(operands) + 1: 1}
                    operands += list(outputs)
                    in_specs += [pl.BlockSpec(memory_space=pl.ANY)] * 2
            else:
                out_shape = state_shapes + dec_shapes
                out_specs = (VMEM,) * len(out_shape)
            results = pl.pallas_call(
                functools.partial(hop_kernel, count, hops, pool, last, len(operands)),
                out_shape=out_shape,
                in_specs=in_specs,
                out_specs=out_specs,
                compiler_params=params,
                cost_estimate=cost(half * len(hops)),
                name="head_" + str(head) + "_shards_" + str(hop) + "_away",
                **options,
            )(*operands)
            if last:
                outputs = results
            else:
                states[head][1:] = results[:3]
                dec_states[head][1:] = results[3:]
    return tuple(outputs)


def solution(mesh):
    in_specs = (
        P(("groups", "ctx"), "head"),
        P(("groups", "ctx"), "head"),
        P(("groups", "ctx"), "head"),
        P(("groups", "ctx"), "head"),
        P(("groups", "ctx"), "head"),
        P("groups"),
        P("groups"),
        P(("groups", "ctx"), None, "head"),
        P(("groups", "ctx"), None, "head"),
        P(("groups", "ctx"), "head"),
        P(("groups", "ctx"), None),
        P(("groups", "ctx")),
    )
    out_specs = (P(("groups", "ctx"), "head"), P(("groups", "ctx"), "head"))
    return jax.shard_map(
        functools.partial(per_device, mesh.shape["ctx"]),
        mesh=mesh,
        in_specs=in_specs,
        out_specs=out_specs,
        check_vma=False,
    )
```

```python
import functools

import jax
import jax.numpy as jnp
from jax import lax
from jax.experimental import pallas as pl
from jax.experimental.pallas import tpu as pltpu
from jax.sharding import PartitionSpec as P

HEADS = 64
KV_HEADS = 8
HEAD_DIM = 128
GROUP = HEADS // KV_HEADS
PAGE = 16
P_DEV = 8
EXP2_SCALE = HEAD_DIM ** (-0.5) * 1.4426950408889634
HIDDEN = -1e30
VMEM_BYTES = 48 * 1024 * 1024

VMEM = pl.BlockSpec(memory_space=pltpu.VMEM)
SMEM = pl.BlockSpec(memory_space=pltpu.SMEM)
HBM = pl.BlockSpec(memory_space=pltpu.HBM)


def attend(qt_ref, cols, keys, values_t, state):
    tokens = keys.shape[1] - HEAD_DIM
    queries = qt_ref[:, cols]
    place = lax.broadcasted_iota(jnp.int32, (tokens, queries.shape[1]), 0)
    token = lax.rem(lax.broadcasted_iota(jnp.int32, (tokens, queries.shape[1]), 1), tokens)
    pick = jnp.where(place == token, jnp.float32(1.0), jnp.float32(0.0)).astype(jnp.bfloat16)
    queries = jnp.concatenate([queries, pick], axis=0)
    scores = jnp.dot(keys, queries, preferred_element_type=jnp.float32)
    high = jnp.max(scores, axis=0, keepdims=True)
    if state is not None:
        old_high, old_total, old_accum = state
        high = jnp.maximum(high, old_high)
    weights = jnp.exp2((scores - high) * EXP2_SCALE)
    total = jnp.sum(weights, axis=0, keepdims=True)
    accum = jnp.dot(values_t, weights.astype(jnp.bfloat16), preferred_element_type=jnp.float32)
    if state is not None:
        decay = jnp.exp2((old_high - high) * EXP2_SCALE)
        total = total + old_total * decay
        accum = accum + old_accum * decay
    return high, total, accum


def hidden(seen):
    return jnp.where(seen, jnp.float32(0.0), jnp.float32(HIDDEN)).astype(jnp.bfloat16)


def stretch_mask(shard, own, tokens):
    place = lax.broadcasted_iota(jnp.int32, (tokens, tokens), 0)
    token = lax.broadcasted_iota(jnp.int32, (tokens, tokens), 1)
    return hidden(place - token <= (own - shard) * tokens)


def cache_mask(shard, limit, c_rows, tokens):
    place = lax.broadcasted_iota(jnp.int32, (c_rows, tokens), 0)
    return hidden(place < limit - shard * c_rows)


def slot_row(targets_ref, shard, own, tokens, pool):
    page = lax.broadcasted_iota(jnp.int32, (1, tokens), 1) // PAGE
    slots = jnp.full((1, tokens), -1, jnp.int32)
    for index in range(tokens // PAGE):
        target = targets_ref[shard * (tokens // PAGE) + index]
        slot = jnp.where(target // P_DEV == own, pool + target % P_DEV, -1)
        slots = jnp.where(page == index, slot, slots)
    return slots


def length_column(length_ref):
    rows = length_ref.shape[0]
    place = lax.broadcasted_iota(jnp.int32, (rows, 1), 0)
    lengths = jnp.zeros((rows, 1), jnp.int32)
    for row in range(rows):
        lengths = jnp.where(place == row, length_ref[row], lengths)
    return lengths


def tally_of(lists, lengths, slot):
    rows, span = lists.shape
    tokens = slot.shape[1]
    slot = jnp.broadcast_to(slot, (rows, tokens))
    offset = lax.rem(lax.broadcasted_iota(jnp.int32, (rows, tokens), 1), PAGE)
    tally = jnp.zeros((rows, tokens), jnp.float32)
    for entry in range(span):
        hit = (slot == lists[:, entry : entry + 1]) & (offset < lengths - entry * PAGE)
        tally = tally + jnp.where(hit, jnp.float32(1.0), jnp.float32(0.0))
    return tally[None]


def shard_of(own, hop, count):
    return lax.rem(own + hop + count, count)


def own_kernel(own_ref, limit_ref, q_ref, stretch_ref, cache_ref, qt_ref, high_ref, total_ref, accum_ref):
    kv_local, _, rows = qt_ref.shape
    tokens = q_ref.shape[0]
    c_rows = cache_ref.shape[0] // 2
    width = min(2 * tokens, rows)
    own = own_ref[0]
    mask = jnp.concatenate(
        [stretch_mask(own, own, tokens), cache_mask(own, limit_ref[0], c_rows, tokens)], axis=0
    )
    for head in range(kv_local):
        for sub in range(GROUP):
            col = (head * GROUP + sub) * HEAD_DIM
            qt_ref[head, :, sub * tokens : (sub + 1) * tokens] = q_ref[:, col : col + HEAD_DIM].T
        feats = slice(head * HEAD_DIM, (head + 1) * HEAD_DIM)
        keys = jnp.concatenate([stretch_ref[:tokens, feats], cache_ref[:c_rows, feats]], axis=0)
        keys = jnp.concatenate([keys, mask], axis=1)
        values_t = jnp.concatenate([stretch_ref[tokens:, feats], cache_ref[c_rows:, feats]], axis=0).T
        for start in range(0, rows, width):
            cols = slice(start, start + width)
            high, total, accum = attend(qt_ref.at[head], cols, keys, values_t, None)
            high_ref[head, :, cols] = high
            total_ref[head, :, cols] = total
            accum_ref[head, :, cols] = accum


def hop_kernel(count, stretch_hops, hop, last, own_ref, limit_ref, qt_ref, high_in, total_in, accum_in, *refs):
    stretch_refs, refs = refs[: len(stretch_hops)], refs[len(stretch_hops) :]
    cache_ref, outs = refs[0], refs[1:]
    own = own_ref[0]
    kv_local, _, rows = qt_ref.shape
    tokens = rows // GROUP
    c_rows = cache_ref.shape[0] // 2
    width = min(2 * tokens, rows)
    masks = [stretch_mask(shard_of(own, far, count), own, tokens) for far in stretch_hops]
    masks.append(cache_mask(shard_of(own, hop, count), limit_ref[0], c_rows, tokens))
    mask = jnp.concatenate(masks, axis=0)
    for head in range(kv_local):
        feats = slice(head * HEAD_DIM, (head + 1) * HEAD_DIM)
        keys = [ref[:tokens, feats] for ref in stretch_refs] + [cache_ref[:c_rows, feats]]
        values = [ref[tokens:, feats] for ref in stretch_refs] + [cache_ref[c_rows:, feats]]
        keys = jnp.concatenate([jnp.concatenate(keys, axis=0), mask], axis=1)
        values_t = jnp.concatenate(values, axis=0).T
        for start in range(0, rows, width):
            cols = slice(start, start + width)
            state = (high_in[head, :, cols], total_in[head, :, cols], accum_in[head, :, cols])
            high, total, accum = attend(qt_ref.at[head], cols, keys, values_t, state)
            if last:
                mixed = (accum * (1.0 / total)).astype(jnp.bfloat16)
                for piece in range(width // tokens):
                    col = (head * GROUP + start // tokens + piece) * HEAD_DIM
                    outs[0][:, col : col + HEAD_DIM] = mixed[:, piece * tokens : (piece + 1) * tokens].T
            else:
                outs[0][head, :, cols] = high
                outs[1][head, :, cols] = total
                outs[2][head, :, cols] = accum


def decode_kernel(count, hops, own_ref, targets_ref, length_ref, q_ref, lists_ref, pool_k, pool_v, *refs):
    stretch_refs, out_ref = refs[:-1], refs[-1]
    rows, q_width = q_ref.shape
    heads = q_width // HEAD_DIM
    kv_local = heads // GROUP
    pool = pool_k.shape[0]
    held = pool * PAGE
    tokens = stretch_refs[0].shape[0] // 2
    own = own_ref[0]
    lists = lists_ref[...]
    lengths = length_column(length_ref)

    queries = q_ref[...].astype(jnp.float32)
    stacked = []
    for head in range(heads):
        piece = queries[:, head * HEAD_DIM : (head + 1) * HEAD_DIM]
        blank = jnp.zeros_like(piece)
        stacked.append(
            jnp.concatenate([piece if kv == head // GROUP else blank for kv in range(kv_local)], axis=1)
        )
    wide = jnp.concatenate(stacked, axis=0).astype(jnp.bfloat16)

    parts = [(pool_k[...].reshape(held, -1), pool_v[...].reshape(held, -1))]
    slots = [lax.broadcasted_iota(jnp.int32, (1, held), 1) // PAGE]
    for hop, ref in zip(hops, stretch_refs):
        parts.append((ref[:tokens], ref[tokens:]))
        slots.append(slot_row(targets_ref, shard_of(own, hop, count), own, tokens, pool))
    done = []
    for (keys, values), slot in zip(parts, slots):
        scores = lax.dot_general(wide, keys, (((1,), (1,)), ((), ())), preferred_element_type=jnp.float32)
        tally = tally_of(lists, lengths, slot)
        scores = scores.reshape(heads, rows, -1)
        done.append((jnp.where(tally > 0, scores, jnp.float32(HIDDEN)), tally, values))
    high = functools.reduce(
        jnp.maximum, [jnp.max(scores, axis=-1, keepdims=True) for scores, _, _ in done]
    )
    total, mixed = 0.0, 0.0
    for scores, tally, values in done:
        weights = jnp.exp2((scores - high) * EXP2_SCALE) * tally
        total = total + jnp.sum(weights, axis=-1, keepdims=True)
        mixed = mixed + jnp.dot(
            weights.reshape(heads * rows, -1).astype(jnp.bfloat16),
            values,
            preferred_element_type=jnp.float32,
        )
    for head in range(heads):
        kv = head // GROUP
        piece = mixed[head * rows : (head + 1) * rows, kv * HEAD_DIM : (kv + 1) * HEAD_DIM]
        out_ref[:, head * HEAD_DIM : (head + 1) * HEAD_DIM] = (piece / total[head]).astype(jnp.bfloat16)


def per_device(
    count,
    queries,
    stretch_keys,
    stretch_values,
    cache_keys,
    cache_values,
    prefix_length,
    page_targets,
    pool_keys,
    pool_values,
    decode_queries,
    page_lists,
    context_length,
):
    own = lax.axis_index("ctx")
    own_array = jnp.full((1,), own, jnp.int32)
    tokens, width = queries.shape
    kv_local = stretch_keys.shape[1] // HEAD_DIM
    rows = GROUP * tokens
    c_rows = cache_keys.shape[0]
    f32 = jnp.float32
    params = pltpu.CompilerParams(vmem_limit_bytes=VMEM_BYTES)
    up_pairs = [(i, (i + 1) % count) for i in range(count)]
    down_pairs = [(i, (i - 1) % count) for i in range(count)]
    ups, downs = count // 2, (count - 1) // 2

    def send(array, hop):
        return lax.ppermute(array, "ctx", up_pairs if hop < 0 else down_pairs)

    def cost(keys):
        pairs = kv_local * rows * keys
        return pl.CostEstimate(
            flops=4 * pairs * HEAD_DIM, bytes_accessed=4 * rows * kv_local * HEAD_DIM, transcendentals=pairs
        )

    stretch = {0: jnp.concatenate([stretch_keys, stretch_values], axis=0)}
    cache = {0: jnp.concatenate([cache_keys, cache_values], axis=0)}
    stretch[-1] = send(stretch[0], -1)
    stretch[1] = send(stretch[0], 1)
    cache[-1] = send(cache[0], -1)

    state_shapes = (
        jax.ShapeDtypeStruct((kv_local, 1, rows), f32),
        jax.ShapeDtypeStruct((kv_local, 1, rows), f32),
        jax.ShapeDtypeStruct((kv_local, HEAD_DIM, rows), f32),
    )
    qt, *state = pl.pallas_call(
        own_kernel,
        out_shape=(jax.ShapeDtypeStruct((kv_local, HEAD_DIM, rows), jnp.bfloat16),) + state_shapes,
        in_specs=[SMEM, SMEM] + [VMEM] * 3,
        out_specs=(VMEM,) * 4,
        compiler_params=params,
        cost_estimate=cost(tokens + c_rows),
        name="own_shard",
    )(own_array, prefix_length, queries, stretch[0], cache[0])

    stretch[-1], state = lax.optimization_barrier((stretch[-1], state))
    for far in range(2, ups + 1):
        stretch[-far] = send(stretch[1 - far], -1)
        if far <= downs:
            stretch[far] = send(stretch[far - 1], 1)
    later, state = lax.optimization_barrier((cache[0], state))
    cache[1] = send(later, 1)

    hops = sorted(stretch)
    decoded = pl.pallas_call(
        functools.partial(decode_kernel, count, hops),
        out_shape=jax.ShapeDtypeStruct(decode_queries.shape, jnp.bfloat16),
        in_specs=[SMEM] * 3 + [VMEM] * (4 + len(hops)),
        out_specs=VMEM,
        compiler_params=params,
        cost_estimate=pl.CostEstimate(
            flops=4 * 128 * 2560 * 256, bytes_accessed=4 * pool_keys.size, transcendentals=128 * 2560
        ),
        name="decode_rows",
    )(
        own_array, page_targets, context_length, decode_queries, page_lists, pool_keys, pool_values,
        *[stretch[hop] for hop in hops],
    )

    cache[-1], decoded = lax.optimization_barrier((cache[-1], decoded))
    order = [-1, 1]
    for far in range(2, ups + 1):
        cache[-far] = send(cache[1 - far], -1)
        order.append(-far)
        if far <= downs:
            cache[far] = send(cache[far - 1], 1)
            order.append(far)

    for place, hop in enumerate(order):
        last = place == len(order) - 1
        stretch_hops = [far for far in hops if far != 0] if place == 0 else []
        out_shape = (jax.ShapeDtypeStruct((tokens, width), jnp.bfloat16),) if last else state_shapes
        state = pl.pallas_call(
            functools.partial(hop_kernel, count, stretch_hops, hop, last),
            out_shape=out_shape,
            in_specs=[SMEM, SMEM] + [VMEM] * (5 + len(stretch_hops)),
            out_specs=(VMEM,) * len(out_shape),
            compiler_params=params,
            cost_estimate=cost(c_rows + tokens * len(stretch_hops)),
            name="hop_kernel_" + str(place),
        )(own_array, prefix_length, qt, *state, *[stretch[far] for far in stretch_hops], cache[hop])
    return (state[0], decoded)


def solution(mesh):
    in_specs = (
        P(("groups", "ctx"), "head"),
        P(("groups", "ctx"), "head"),
        P(("groups", "ctx"), "head"),
        P(("groups", "ctx"), "head"),
        P(("groups", "ctx"), "head"),
        P("groups"),
        P("groups"),
        P(("groups", "ctx"), None, "head"),
        P(("groups", "ctx"), None, "head"),
        P(("groups", "ctx"), "head"),
        P(("groups", "ctx"), None),
        P(("groups", "ctx")),
    )
    out_specs = (P(("groups", "ctx"), "head"), P(("groups", "ctx"), "head"))
    return jax.shard_map(
        functools.partial(per_device, mesh.shape["ctx"]),
        mesh=mesh,
        in_specs=in_specs,
        out_specs=out_specs,
        check_vma=False,
    )
```

```python
import functools

import jax
import jax.numpy as jnp
from jax import lax
from jax.experimental import pallas as pl
from jax.experimental.pallas import tpu as pltpu
from jax.sharding import PartitionSpec as P

HEADS = 64
KV_HEADS = 8
HEAD_DIM = 128
GROUP = HEADS // KV_HEADS
PAGE = 16
P_DEV = 8
EXP2_SCALE = HEAD_DIM ** (-0.5) * 1.4426950408889634
HIDDEN = -1e30
VMEM_BYTES = 48 * 1024 * 1024

VMEM = pl.BlockSpec(memory_space=pltpu.VMEM)
SMEM = pl.BlockSpec(memory_space=pltpu.SMEM)
HBM = pl.BlockSpec(memory_space=pltpu.HBM)


def attend(qt_ref, cols, keys, values_t, state):
    tokens = keys.shape[1] - HEAD_DIM
    queries = qt_ref[:, cols]
    place = lax.broadcasted_iota(jnp.int32, (tokens, queries.shape[1]), 0)
    token = lax.rem(lax.broadcasted_iota(jnp.int32, (tokens, queries.shape[1]), 1), tokens)
    pick = jnp.where(place == token, jnp.float32(1.0), jnp.float32(0.0)).astype(jnp.bfloat16)
    queries = jnp.concatenate([queries, pick], axis=0)
    scores = jnp.dot(keys, queries, preferred_element_type=jnp.float32)
    high = jnp.max(scores, axis=0, keepdims=True)
    if state is not None:
        old_high, old_total, old_accum = state
        high = jnp.maximum(high, old_high)
    weights = jnp.exp2((scores - high) * EXP2_SCALE)
    total = jnp.sum(weights, axis=0, keepdims=True)
    accum = jnp.dot(values_t, weights.astype(jnp.bfloat16), preferred_element_type=jnp.float32)
    if state is not None:
        decay = jnp.exp2((old_high - high) * EXP2_SCALE)
        total = total + old_total * decay
        accum = accum + old_accum * decay
    return high, total, accum


def hidden(seen):
    return jnp.where(seen, jnp.float32(0.0), jnp.float32(HIDDEN)).astype(jnp.bfloat16)


def stretch_mask(shard, own, tokens):
    place = lax.broadcasted_iota(jnp.int32, (tokens, tokens), 0)
    token = lax.broadcasted_iota(jnp.int32, (tokens, tokens), 1)
    return hidden(place - token <= (own - shard) * tokens)


def cache_mask(shard, limit, c_rows, tokens):
    place = lax.broadcasted_iota(jnp.int32, (c_rows, tokens), 0)
    return hidden(place < limit - shard * c_rows)


def slot_row(targets_ref, shard, own, tokens, pool):
    page = lax.broadcasted_iota(jnp.int32, (1, tokens), 1) // PAGE
    slots = jnp.full((1, tokens), -1, jnp.int32)
    for index in range(tokens // PAGE):
        target = targets_ref[shard * (tokens // PAGE) + index]
        slot = jnp.where(target // P_DEV == own, pool + target % P_DEV, -1)
        slots = jnp.where(page == index, slot, slots)
    return slots


def length_column(length_ref):
    rows = length_ref.shape[0]
    place = lax.broadcasted_iota(jnp.int32, (rows, 1), 0)
    lengths = jnp.zeros((rows, 1), jnp.int32)
    for row in range(rows):
        lengths = jnp.where(place == row, length_ref[row], lengths)
    return lengths


def tally_of(lists, lengths, slot):
    rows, span = lists.shape
    tokens = slot.shape[1]
    slot = jnp.broadcast_to(slot, (rows, tokens))
    offset = lax.rem(lax.broadcasted_iota(jnp.int32, (rows, tokens), 1), PAGE)
    tally = jnp.zeros((rows, tokens), jnp.float32)
    for entry in range(span):
        hit = (slot == lists[:, entry : entry + 1]) & (offset < lengths - entry * PAGE)
        tally = tally + jnp.where(hit, jnp.float32(1.0), jnp.float32(0.0))
    return tally[None]


def shard_of(own, hop, count):
    return lax.rem(own + hop + count, count)


def wide_queries(q_ref, kv_local):
    heads = q_ref.shape[1] // HEAD_DIM
    queries = q_ref[...].astype(jnp.float32)
    stacked = []
    for head in range(heads):
        piece = queries[:, head * HEAD_DIM : (head + 1) * HEAD_DIM]
        blank = jnp.zeros_like(piece)
        stacked.append(
            jnp.concatenate([piece if kv == head // GROUP else blank for kv in range(kv_local)], axis=1)
        )
    return jnp.concatenate(stacked, axis=0).astype(jnp.bfloat16)


def decode_attend(queries, parts, state):
    done = []
    for keys, values, tally in parts:
        scores = lax.dot_general(
            queries, keys, (((1,), (1,)), ((), ())), preferred_element_type=jnp.float32
        ).reshape(-1, tally.shape[1], tally.shape[2])
        done.append((jnp.where(tally > 0, scores, jnp.float32(HIDDEN)), tally, values))
    highs = [jnp.max(scores, axis=-1, keepdims=True) for scores, _, _ in done]
    if state is not None:
        old_high, old_total, old_mixed = state
        highs.append(old_high)
    high = functools.reduce(jnp.maximum, highs)
    total, mixed = 0.0, 0.0
    if state is not None:
        decay = jnp.exp2((old_high - high) * EXP2_SCALE)
        total = old_total * decay
        mixed = old_mixed * decay
    for scores, tally, values in done:
        weights = jnp.exp2((scores - high) * EXP2_SCALE) * tally
        total = total + jnp.sum(weights, axis=-1, keepdims=True)
        mixed = mixed + jnp.dot(
            weights.reshape(queries.shape[0], -1).astype(jnp.bfloat16),
            values,
            preferred_element_type=jnp.float32,
        ).reshape(high.shape[0], high.shape[1], -1)
    return high, total, mixed


def pack_kernel(sk_ref, sv_ref, cv_ref, ck_ref, out_ref, sems):
    copies, start = [], 0
    for place, ref in enumerate((sk_ref, sv_ref, cv_ref, ck_ref)):
        span = pl.ds(start, ref.shape[0])
        copies.append(pltpu.make_async_copy(ref, out_ref.at[span], sems.at[place]))
        start += ref.shape[0]
    for copy in copies:
        copy.start()
    for copy in copies:
        copy.wait()


def own_kernel(
    count, hops, own_ref, limit_ref, q_ref, shard_ref,
    qt_ref, near_ref, far_ref, high_ref, total_ref, accum_ref,
):
    kv_local, _, rows = qt_ref.shape
    tokens = q_ref.shape[0]
    c_rows = far_ref.shape[1]
    cached = 2 * tokens + c_rows
    width = min(2 * tokens, rows)
    own = own_ref[0]
    limit = limit_ref[0]
    for place, hop in enumerate(hops):
        shard = shard_of(own, hop, count)
        near_ref[place] = stretch_mask(shard, own, tokens)
        far_ref[place] = cache_mask(shard, limit, c_rows, tokens)
    mask = jnp.concatenate([stretch_mask(own, own, tokens), cache_mask(own, limit, c_rows, tokens)], axis=0)
    for head in range(kv_local):
        for sub in range(GROUP):
            col = (head * GROUP + sub) * HEAD_DIM
            qt_ref[head, :, sub * tokens : (sub + 1) * tokens] = q_ref[:, col : col + HEAD_DIM].T
        feats = slice(head * HEAD_DIM, (head + 1) * HEAD_DIM)
        keys = jnp.concatenate([shard_ref[:tokens, feats], shard_ref[cached:, feats]], axis=0)
        keys = jnp.concatenate([keys, mask], axis=1)
        values_t = shard_ref[tokens:cached, feats].T
        for start in range(0, rows, width):
            cols = slice(start, start + width)
            high, total, accum = attend(qt_ref.at[head], cols, keys, values_t, None)
            high_ref[head, :, cols] = high
            total_ref[head, :, cols] = total
            accum_ref[head, :, cols] = accum


def held_kernel(
    own_ref, targets_ref, length_ref, q_ref, lists_ref, pool_k, pool_v, rest_ref,
    wide_ref, high_ref, total_ref, mixed_ref,
):
    kv_width = rest_ref.shape[1]
    pool = pool_k.shape[0]
    held = pool * PAGE
    tokens = PAGE * P_DEV
    own = own_ref[0]
    lists = lists_ref[...]
    lengths = length_column(length_ref)
    wide_ref[...] = wide_queries(q_ref, kv_width // HEAD_DIM)
    held_slot = lax.broadcasted_iota(jnp.int32, (1, held), 1) // PAGE
    own_slot = slot_row(targets_ref, own, own, tokens, pool)
    parts = [
        (
            pool_k[...].reshape(held, kv_width),
            pool_v[...].reshape(held, kv_width),
            tally_of(lists, lengths, held_slot),
        ),
        (rest_ref[:tokens], rest_ref[tokens : 2 * tokens], tally_of(lists, lengths, own_slot)),
    ]
    high_ref[...], total_ref[...], mixed_ref[...] = decode_attend(wide_ref[...], parts, None)


def hop_kernel(places, qt_ref, near_ref, far_ref, high_in, total_in, accum_in, *refs):
    shard_refs, outs = refs[: len(places)], refs[len(places) :]
    kv_local, _, rows = qt_ref.shape
    tokens = rows // GROUP
    cached = 2 * tokens + far_ref.shape[1]
    width = min(2 * tokens, rows)
    for head in range(kv_local):
        feats = slice(head * HEAD_DIM, (head + 1) * HEAD_DIM)
        keys, values, masks = [], [], []
        for place, shard_ref in zip(places, shard_refs):
            keys += [shard_ref[:tokens, feats], shard_ref[cached:, feats]]
            masks += [near_ref[place], far_ref[place]]
            values.append(shard_ref[tokens:cached, feats])
        keys = jnp.concatenate([jnp.concatenate(keys, axis=0), jnp.concatenate(masks, axis=0)], axis=1)
        values_t = jnp.concatenate(values, axis=0).T
        for start in range(0, rows, width):
            cols = slice(start, start + width)
            state = (high_in[head, :, cols], total_in[head, :, cols], accum_in[head, :, cols])
            high, total, accum = attend(qt_ref.at[head], cols, keys, values_t, state)
            outs[0][head, :, cols] = high
            outs[1][head, :, cols] = total
            outs[2][head, :, cols] = accum


def fresh_kernel(count, hops, pool, place, own_ref, targets_ref, length_ref, lists_ref, *refs):
    rest_refs, refs = refs[: len(hops)], refs[len(hops) :]
    wide_ref, dec_high, dec_total, dec_mixed, qt_ref, near_ref, high_in, total_in, accum_in = refs[:9]
    dec_out, high_ref, total_ref, accum_ref = refs[9:]
    kv_local, _, rows = qt_ref.shape
    tokens = rows // GROUP
    width = min(2 * tokens, rows)
    own = own_ref[0]
    lists = lists_ref[...]
    lengths = length_column(length_ref)
    parts = []
    for hop, ref in zip(hops, rest_refs):
        slot = slot_row(targets_ref, shard_of(own, hop, count), own, tokens, pool)
        parts.append((ref[:tokens], ref[tokens : 2 * tokens], tally_of(lists, lengths, slot)))
    _, total, mixed = decode_attend(wide_ref[...], parts, (dec_high[...], dec_total[...], dec_mixed[...]))
    for head in range(kv_local * GROUP):
        kv = head // GROUP
        piece = mixed[head, :, kv * HEAD_DIM : (kv + 1) * HEAD_DIM] / total[head]
        dec_out[:, head * HEAD_DIM : (head + 1) * HEAD_DIM] = piece.astype(jnp.bfloat16)
    for head in range(kv_local):
        feats = slice(head * HEAD_DIM, (head + 1) * HEAD_DIM)
        keys = jnp.concatenate([rest_refs[place][:tokens, feats], near_ref[place]], axis=1)
        values_t = rest_refs[place][tokens : 2 * tokens, feats].T
        for start in range(0, rows, width):
            cols = slice(start, start + width)
            state = (high_in[head, :, cols], total_in[head, :, cols], accum_in[head, :, cols])
            high, total, accum = attend(qt_ref.at[head], cols, keys, values_t, state)
            high_ref[head, :, cols] = high
            total_ref[head, :, cols] = total
            accum_ref[head, :, cols] = accum


def last_kernel(
    place, qt_ref, far_ref, high_in, total_in, accum_in, ck_ref, rest_ref, out_ref, result_ref, sems
):
    kv_local, _, rows = qt_ref.shape
    tokens = rows // GROUP
    width = min(2 * tokens, rows)
    copies = []
    for head in range(kv_local):
        feats = slice(head * HEAD_DIM, (head + 1) * HEAD_DIM)
        keys = jnp.concatenate([ck_ref[:, feats], far_ref[place]], axis=1)
        values_t = rest_ref[2 * tokens :, feats].T
        for start in range(0, rows, width):
            cols = slice(start, start + width)
            state = (high_in[head, :, cols], total_in[head, :, cols], accum_in[head, :, cols])
            _, total, accum = attend(qt_ref.at[head], cols, keys, values_t, state)
            mixed = (accum * (1.0 / total)).astype(jnp.bfloat16)
            first = (head * GROUP + start // tokens) * HEAD_DIM
            for piece in range(width // tokens):
                col = first + piece * HEAD_DIM
                result_ref[:, col : col + HEAD_DIM] = mixed[:, piece * tokens : (piece + 1) * tokens].T
            span = pl.ds(first, width // tokens * HEAD_DIM)
            copy = pltpu.make_async_copy(result_ref.at[:, span], out_ref.at[:, span], sems.at[len(copies)])
            copy.start()
            copies.append(copy)
    for copy in copies:
        copy.wait()


def per_device(
    count,
    queries,
    stretch_keys,
    stretch_values,
    cache_keys,
    cache_values,
    prefix_length,
    page_targets,
    pool_keys,
    pool_values,
    decode_queries,
    page_lists,
    context_length,
):
    own = lax.axis_index("ctx")
    own_array = jnp.full((1,), own, jnp.int32)
    tokens, width = queries.shape
    kv_width = stretch_keys.shape[1]
    kv_local = kv_width // HEAD_DIM
    rows = GROUP * tokens
    heads = kv_local * GROUP
    dec_rows = decode_queries.shape[0]
    c_rows = cache_keys.shape[0]
    pool = pool_keys.shape[0]
    f32, bf16 = jnp.float32, jnp.bfloat16
    shape = jax.ShapeDtypeStruct
    params = pltpu.CompilerParams(vmem_limit_bytes=VMEM_BYTES)
    up_pairs = [(i, (i + 1) % count) for i in range(count)]
    down_pairs = [(i, (i - 1) % count) for i in range(count)]
    hops = []
    for far in range(1, count // 2 + 1):
        hops += [-far, far] if far <= (count - 1) // 2 else [-far]

    def send(array, hop):
        return lax.ppermute(array, "ctx", up_pairs if hop < 0 else down_pairs)

    def cost(keys):
        pairs = kv_local * rows * keys
        return pl.CostEstimate(
            flops=4 * pairs * HEAD_DIM, bytes_accessed=4 * rows * kv_local * HEAD_DIM, transcendentals=pairs
        )

    parts = (stretch_keys, stretch_values, cache_values, cache_keys)
    packed = pl.pallas_call(
        pack_kernel,
        out_shape=shape((2 * tokens + 2 * c_rows, kv_width), bf16),
        in_specs=[HBM] * 4,
        out_specs=HBM,
        scratch_shapes=[pltpu.SemaphoreType.DMA((4,))],
        name="pack_own_shard",
    )(*parts)
    shard = {0: packed}
    for hop in hops[:2]:
        shard[hop] = send(shard[0], hop)

    state_shapes = (
        shape((kv_local, 1, rows), f32),
        shape((kv_local, 1, rows), f32),
        shape((kv_local, HEAD_DIM, rows), f32),
    )
    qt, near, far, *state = pl.pallas_call(
        functools.partial(own_kernel, count, hops),
        out_shape=(
            shape((kv_local, HEAD_DIM, rows), bf16),
            shape((count - 1, tokens, tokens), bf16),
            shape((count - 1, c_rows, tokens), bf16),
        )
        + state_shapes,
        in_specs=[SMEM, SMEM] + [VMEM] * 2,
        out_specs=(VMEM,) * 6,
        compiler_params=params,
        cost_estimate=cost(tokens + c_rows),
        name="own_shard",
    )(own_array, prefix_length, queries, shard[0])

    wide, *dec_state = pl.pallas_call(
        held_kernel,
        out_shape=(
            shape((heads * dec_rows, kv_width), bf16),
            shape((heads, dec_rows, 1), f32),
            shape((heads, dec_rows, 1), f32),
            shape((heads, dec_rows, kv_width), f32),
        ),
        in_specs=[SMEM] * 3 + [VMEM] * 5,
        out_specs=(VMEM,) * 4,
        compiler_params=params,
        cost_estimate=pl.CostEstimate(
            flops=4 * 128 * 2048 * 256, bytes_accessed=4 * pool_keys.size, transcendentals=128 * 2048
        ),
        name="decode_held_pages",
    )(own_array, page_targets, context_length, decode_queries, page_lists, pool_keys, pool_values, shard[0])

    shard[-1], state, dec_state = lax.optimization_barrier((shard[-1], state, dec_state))
    for hop in hops[2:-1]:
        shard[hop] = send(shard[hop + 1 if hop < 0 else hop - 1], hop)
    hop = hops[-1]
    nearer = shard[hop + 1 if hop < 0 else hop - 1]
    last_rest = send(nearer[: 2 * tokens + c_rows], hop)
    last_keys = send(nearer[2 * tokens + c_rows :], hop)

    for first in range(0, len(hops) - 1, 2):
        places = list(range(first, min(first + 2, len(hops) - 1)))
        state = pl.pallas_call(
            functools.partial(hop_kernel, places),
            out_shape=state_shapes,
            in_specs=[VMEM] * (6 + len(places)),
            out_specs=(VMEM,) * 3,
            compiler_params=params,
            cost_estimate=cost((c_rows + tokens) * len(places)),
            name="whole_shards_" + str(first),
        )(qt, near, far, *state, *[shard[hops[place]] for place in places])

    final = len(hops) - 1
    decoded, *state = pl.pallas_call(
        functools.partial(fresh_kernel, count, hops, pool, final),
        out_shape=(shape(decode_queries.shape, bf16),) + state_shapes,
        in_specs=[SMEM] * 3 + [VMEM] * (10 + len(hops)),
        out_specs=(VMEM,) * 4,
        compiler_params=params,
        cost_estimate=cost(tokens),
        name="new_pages_and_last_stretch",
    )(
        own_array, page_targets, context_length, page_lists, *[shard[hop] for hop in hops[:-1]], last_rest,
        wide, *dec_state, qt, near, *state,
    )

    prefill = pl.pallas_call(
        functools.partial(last_kernel, final),
        out_shape=shape((tokens, width), bf16),
        in_specs=[VMEM] * 7,
        out_specs=HBM,
        scratch_shapes=[
            pltpu.VMEM((tokens, width), bf16),
            pltpu.SemaphoreType.DMA((kv_local * max(GROUP // 2, 1),)),
        ],
        compiler_params=params,
        cost_estimate=cost(c_rows),
        name="last_cached_keys",
    )(qt, far, *state, last_keys, last_rest)
    return (prefill, decoded)


def solution(mesh):
    in_specs = (
        P(("groups", "ctx"), "head"),
        P(("groups", "ctx"), "head"),
        P(("groups", "ctx"), "head"),
        P(("groups", "ctx"), "head"),
        P(("groups", "ctx"), "head"),
        P("groups"),
        P("groups"),
        P(("groups", "ctx"), None, "head"),
        P(("groups", "ctx"), None, "head"),
        P(("groups", "ctx"), "head"),
        P(("groups", "ctx"), None),
        P(("groups", "ctx")),
    )
    out_specs = (P(("groups", "ctx"), "head"), P(("groups", "ctx"), "head"))
    return jax.shard_map(
        functools.partial(per_device, mesh.shape["ctx"]),
        mesh=mesh,
        in_specs=in_specs,
        out_specs=out_specs,
        check_vma=False,
    )
```

```python
import functools

import jax
import jax.numpy as jnp
from jax import lax
from jax.experimental import pallas as pl
from jax.experimental.pallas import tpu as pltpu
from jax.sharding import PartitionSpec as P

HEADS = 64
KV_HEADS = 8
HEAD_DIM = 128
GROUP = HEADS // KV_HEADS
PAGE = 16
P_DEV = 8
EXP2_SCALE = HEAD_DIM ** (-0.5) * 1.4426950408889634
HIDDEN = -1e30
VMEM_BYTES = 48 * 1024 * 1024

VMEM = pl.BlockSpec(memory_space=pltpu.VMEM)
SMEM = pl.BlockSpec(memory_space=pltpu.SMEM)
HBM = pl.BlockSpec(memory_space=pltpu.HBM)


def scores_of(qt_ref, head, cols, keys):
    return jnp.dot(keys, qt_ref[head, :, cols], preferred_element_type=jnp.float32)


def soften(scores, old):
    high = jnp.max(scores, axis=0, keepdims=True)
    if old is None:
        weights = jnp.exp2((scores - high) * EXP2_SCALE)
        return weights.astype(jnp.bfloat16), high, jnp.sum(weights, axis=0, keepdims=True), None
    old_high, old_total = old
    high = jnp.maximum(high, old_high)
    decay = jnp.exp2((old_high - high) * EXP2_SCALE)
    weights = jnp.exp2((scores - high) * EXP2_SCALE)
    total = old_total * decay + jnp.sum(weights, axis=0, keepdims=True)
    return weights.astype(jnp.bfloat16), high, total, decay


def walk(blocks, first, second):
    ahead = first(blocks[0])
    for place, block in enumerate(blocks):
        current = ahead
        if place + 1 < len(blocks):
            ahead = first(blocks[place + 1])
        second(block, current)


def blocks_of(qt_ref):
    kv_local, _, rows = qt_ref.shape
    width = min(2 * (rows // GROUP), rows)
    return [(head, slice(start, start + width)) for head in range(kv_local) for start in range(0, rows, width)]


def attend(qt_ref, keys, values_t, old, new):
    high_ref, total_ref, accum_ref = new

    def second(block, scores):
        head, cols = block
        before = None if old is None else (old[0][head, :, cols], old[1][head, :, cols])
        weights, high, total, decay = soften(scores, before)
        accum = jnp.dot(values_t[head], weights, preferred_element_type=jnp.float32)
        if old is not None:
            accum = accum + old[2][head, :, cols] * decay
        high_ref[head, :, cols] = high
        total_ref[head, :, cols] = total
        accum_ref[head, :, cols] = accum

    walk(blocks_of(qt_ref), lambda block: scores_of(qt_ref, block[0], block[1], keys[block[0]]), second)


def hidden(seen):
    return jnp.where(seen, jnp.float32(0.0), jnp.float32(HIDDEN)).astype(jnp.bfloat16)


def stretch_mask(shard, own, tokens):
    place = lax.broadcasted_iota(jnp.int32, (tokens, tokens), 0)
    token = lax.broadcasted_iota(jnp.int32, (tokens, tokens), 1)
    return hidden(place - token <= (own - shard) * tokens)


def cache_mask(shard, limit, c_rows, tokens):
    place = lax.broadcasted_iota(jnp.int32, (c_rows, tokens), 0)
    return hidden(place < limit - shard * c_rows)


def slot_row(targets_ref, shard, own, tokens, pool):
    page = lax.broadcasted_iota(jnp.int32, (1, tokens), 1) // PAGE
    slots = jnp.full((1, tokens), -1, jnp.int32)
    for index in range(tokens // PAGE):
        target = targets_ref[shard * (tokens // PAGE) + index]
        slot = jnp.where(target // P_DEV == own, pool + target % P_DEV, -1)
        slots = jnp.where(page == index, slot, slots)
    return slots


def length_column(length_ref):
    rows = length_ref.shape[0]
    place = lax.broadcasted_iota(jnp.int32, (rows, 1), 0)
    lengths = jnp.zeros((rows, 1), jnp.int32)
    for row in range(rows):
        lengths = jnp.where(place == row, length_ref[row], lengths)
    return lengths


def tally_of(lists, lengths, slot):
    rows, span = lists.shape
    tokens = slot.shape[1]
    slot = jnp.broadcast_to(slot, (rows, tokens))
    offset = lax.rem(lax.broadcasted_iota(jnp.int32, (rows, tokens), 1), PAGE)
    tally = jnp.zeros((rows, tokens), jnp.float32)
    for entry in range(span):
        hit = (slot == lists[:, entry : entry + 1]) & (offset < lengths - entry * PAGE)
        tally = tally + jnp.where(hit, jnp.float32(1.0), jnp.float32(0.0))
    return tally[None]


def shard_of(own, hop, count):
    return lax.rem(own + hop + count, count)


def wide_queries(q_ref, kv_local):
    heads = q_ref.shape[1] // HEAD_DIM
    queries = q_ref[...].astype(jnp.float32)
    stacked = []
    for head in range(heads):
        piece = queries[:, head * HEAD_DIM : (head + 1) * HEAD_DIM]
        blank = jnp.zeros_like(piece)
        stacked.append(
            jnp.concatenate([piece if kv == head // GROUP else blank for kv in range(kv_local)], axis=1)
        )
    return jnp.concatenate(stacked, axis=0).astype(jnp.bfloat16)


def decode_attend(queries, parts, state):
    done = []
    for keys, values, tally in parts:
        scores = lax.dot_general(
            queries, keys, (((1,), (1,)), ((), ())), preferred_element_type=jnp.float32
        ).reshape(-1, tally.shape[1], tally.shape[2])
        done.append((jnp.where(tally > 0, scores, jnp.float32(HIDDEN)), tally, values))
    highs = [jnp.max(scores, axis=-1, keepdims=True) for scores, _, _ in done]
    if state is not None:
        old_high, old_total, old_mixed = state
        highs.append(old_high)
    high = functools.reduce(jnp.maximum, highs)
    total, mixed = 0.0, 0.0
    if state is not None:
        decay = jnp.exp2((old_high - high) * EXP2_SCALE)
        total = old_total * decay
        mixed = old_mixed * decay
    for scores, tally, values in done:
        weights = jnp.exp2((scores - high) * EXP2_SCALE) * tally
        total = total + jnp.sum(weights, axis=-1, keepdims=True)
        mixed = mixed + jnp.dot(
            weights.reshape(queries.shape[0], -1).astype(jnp.bfloat16),
            values,
            preferred_element_type=jnp.float32,
        ).reshape(high.shape[0], high.shape[1], -1)
    return high, total, mixed


def features(head):
    return slice(head * HEAD_DIM, (head + 1) * HEAD_DIM)


def shard_parts(ref, tokens, c_rows):
    return slice(0, tokens + c_rows), slice(tokens + c_rows, 2 * (tokens + c_rows))


def own_kernel(
    count, hops, own_ref, limit_ref, q_ref, shard_ref,
    qt_ref, near_ref, far_ref, high_ref, total_ref, accum_ref,
):
    kv_local, _, rows = qt_ref.shape
    tokens = q_ref.shape[0]
    c_rows = far_ref.shape[1]
    own = own_ref[0]
    limit = limit_ref[0]
    place = lax.broadcasted_iota(jnp.int32, (tokens, tokens), 0)
    token = lax.broadcasted_iota(jnp.int32, (tokens, tokens), 1)
    pick = jnp.where(place == token, jnp.float32(1.0), jnp.float32(0.0)).astype(jnp.bfloat16)
    for head in range(kv_local):
        for sub in range(GROUP):
            cols = slice(sub * tokens, (sub + 1) * tokens)
            qt_ref[head, :HEAD_DIM, cols] = q_ref[:, features(head * GROUP + sub)].T
            qt_ref[head, HEAD_DIM:, cols] = pick
    for place, hop in enumerate(hops):
        shard = shard_of(own, hop, count)
        near_ref[place] = stretch_mask(shard, own, tokens)
        far_ref[place] = cache_mask(shard, limit, c_rows, tokens)
    mask = jnp.concatenate([stretch_mask(own, own, tokens), cache_mask(own, limit, c_rows, tokens)], axis=0)
    key_rows, value_rows = shard_parts(shard_ref, tokens, c_rows)
    keys = [jnp.concatenate([shard_ref[key_rows, features(head)], mask], axis=1) for head in range(kv_local)]
    values_t = [shard_ref[value_rows, features(head)].T for head in range(kv_local)]
    attend(qt_ref, keys, values_t, None, (high_ref, total_ref, accum_ref))


def held_kernel(
    own_ref, targets_ref, length_ref, q_ref, lists_ref, pool_k, pool_v, rest_ref,
    wide_ref, high_ref, total_ref, mixed_ref,
):
    kv_width = rest_ref.shape[1]
    pool = pool_k.shape[0]
    held = pool * PAGE
    tokens = PAGE * P_DEV
    half = rest_ref.shape[0] // 2
    own = own_ref[0]
    lists = lists_ref[...]
    lengths = length_column(length_ref)
    wide_ref[...] = wide_queries(q_ref, kv_width // HEAD_DIM)
    held_slot = lax.broadcasted_iota(jnp.int32, (1, held), 1) // PAGE
    own_slot = slot_row(targets_ref, own, own, tokens, pool)
    parts = [
        (
            pool_k[...].reshape(held, kv_width),
            pool_v[...].reshape(held, kv_width),
            tally_of(lists, lengths, held_slot),
        ),
        (rest_ref[:tokens], rest_ref[half : half + tokens], tally_of(lists, lengths, own_slot)),
    ]
    high_ref[...], total_ref[...], mixed_ref[...] = decode_attend(wide_ref[...], parts, None)


def hop_kernel(places, qt_ref, near_ref, far_ref, high_in, total_in, accum_in, *refs):
    shard_refs, outs = refs[: len(places)], refs[len(places) :]
    tokens, c_rows = near_ref.shape[1], far_ref.shape[1]
    mask = jnp.concatenate([ref[place] for place in places for ref in (near_ref, far_ref)], axis=0)
    keys, values_t = [], []
    for head in range(qt_ref.shape[0]):
        pieces, values = [], []
        for ref in shard_refs:
            key_rows, value_rows = shard_parts(ref, tokens, c_rows)
            pieces.append(ref[key_rows, features(head)])
            values.append(ref[value_rows, features(head)])
        keys.append(jnp.concatenate([jnp.concatenate(pieces, axis=0), mask], axis=1))
        values_t.append(jnp.concatenate(values, axis=0).T)
    attend(qt_ref, keys, values_t, (high_in, total_in, accum_in), outs)


def fresh_kernel(count, hops, pool, final, own_ref, targets_ref, length_ref, lists_ref, *refs):
    shard_refs, refs = refs[: len(hops)], refs[len(hops) :]
    wide_ref, dec_high, dec_total, dec_mixed, qt_ref, near_ref, far_ref, high_in, total_in, accum_in = refs[:10]
    dec_out, weights_ref, total_ref, accum_ref = refs[10:]
    kv_local = qt_ref.shape[0]
    tokens, c_rows = near_ref.shape[1], far_ref.shape[1]
    half = tokens + c_rows
    last_ref = shard_refs[final]
    mask = jnp.concatenate([near_ref[final], far_ref[final]], axis=0)
    keys = [jnp.concatenate([last_ref[:half, features(head)], mask], axis=1) for head in range(kv_local)]
    values_t = [last_ref[half : half + tokens, features(head)].T for head in range(kv_local)]

    def second(block, scores):
        head, cols = block
        before = (high_in[head, :, cols], total_in[head, :, cols])
        weights, _, total, decay = soften(scores, before)
        weights_ref[head, :, cols] = weights[tokens:]
        total_ref[head, :, cols] = total
        accum_ref[head, :, cols] = accum_in[head, :, cols] * decay + jnp.dot(
            values_t[head], weights[:tokens], preferred_element_type=jnp.float32
        )

    walk(blocks_of(qt_ref), lambda block: scores_of(qt_ref, block[0], block[1], keys[block[0]]), second)

    own = own_ref[0]
    lists = lists_ref[...]
    lengths = length_column(length_ref)
    parts = []
    for hop, ref in zip(hops, shard_refs):
        slot = slot_row(targets_ref, shard_of(own, hop, count), own, tokens, pool)
        parts.append((ref[:tokens], ref[half : half + tokens], tally_of(lists, lengths, slot)))
    _, total, mixed = decode_attend(wide_ref[...], parts, (dec_high[...], dec_total[...], dec_mixed[...]))
    for head in range(kv_local * GROUP):
        piece = mixed[head, :, features(head // GROUP)] / total[head]
        dec_out[:, features(head)] = piece.astype(jnp.bfloat16)


def last_kernel(weights_ref, total_ref, accum_ref, values_ref, out_ref, result_ref, sems):
    tokens = result_ref.shape[0]
    values_t = [values_ref[:, features(head)].T for head in range(weights_ref.shape[0])]
    copies = []

    def first(block):
        head, cols = block
        return jnp.dot(values_t[head], weights_ref[head, :, cols], preferred_element_type=jnp.float32)

    def second(block, mixed):
        head, cols = block
        mixed = mixed + accum_ref[head, :, cols]
        mixed = (mixed * (1.0 / total_ref[head, :, cols])).astype(jnp.bfloat16)
        start = (head * GROUP + cols.start // tokens) * HEAD_DIM
        pieces = (cols.stop - cols.start) // tokens
        for piece in range(pieces):
            col = start + piece * HEAD_DIM
            result_ref[:, col : col + HEAD_DIM] = mixed[:, piece * tokens : (piece + 1) * tokens].T
        span = pl.ds(start, pieces * HEAD_DIM)
        copy = pltpu.make_async_copy(result_ref.at[:, span], out_ref.at[:, span], sems.at[len(copies)])
        copy.start()
        copies.append(copy)

    walk(blocks_of(weights_ref), first, second)
    for copy in copies:
        copy.wait()


def per_device(
    count,
    queries,
    stretch_keys,
    stretch_values,
    cache_keys,
    cache_values,
    prefix_length,
    page_targets,
    pool_keys,
    pool_values,
    decode_queries,
    page_lists,
    context_length,
):
    own = lax.axis_index("ctx")
    own_array = jnp.full((1,), own, jnp.int32)
    tokens, width = queries.shape
    kv_width = stretch_keys.shape[1]
    kv_local = kv_width // HEAD_DIM
    rows = GROUP * tokens
    heads = kv_local * GROUP
    dec_rows = decode_queries.shape[0]
    c_rows = cache_keys.shape[0]
    pool = pool_keys.shape[0]
    f32, bf16 = jnp.float32, jnp.bfloat16
    shape = jax.ShapeDtypeStruct
    params = pltpu.CompilerParams(vmem_limit_bytes=VMEM_BYTES)
    up_pairs = [(i, (i + 1) % count) for i in range(count)]
    down_pairs = [(i, (i - 1) % count) for i in range(count)]
    hops = []
    for far in range(1, count // 2 + 1):
        hops += [-far, far] if far <= (count - 1) // 2 else [-far]

    def send(array, hop):
        return lax.ppermute(array, "ctx", up_pairs if hop < 0 else down_pairs)

    def cost(keys):
        pairs = kv_local * rows * keys
        return pl.CostEstimate(
            flops=4 * pairs * HEAD_DIM, bytes_accessed=4 * rows * kv_local * HEAD_DIM, transcendentals=pairs
        )

    half = tokens + c_rows
    shard = {0: jnp.concatenate([stretch_keys, cache_keys, stretch_values, cache_values], axis=0)}
    for hop in hops[:2]:
        shard[hop] = send(shard[0], hop)

    state_shapes = (
        shape((kv_local, 1, rows), f32),
        shape((kv_local, 1, rows), f32),
        shape((kv_local, HEAD_DIM, rows), f32),
    )
    qt, near, far, *state = pl.pallas_call(
        functools.partial(own_kernel, count, hops),
        out_shape=(
            shape((kv_local, HEAD_DIM + tokens, rows), bf16),
            shape((count - 1, tokens, tokens), bf16),
            shape((count - 1, c_rows, tokens), bf16),
        )
        + state_shapes,
        in_specs=[SMEM, SMEM] + [VMEM] * 2,
        out_specs=(VMEM,) * 6,
        compiler_params=params,
        cost_estimate=cost(tokens + c_rows),
        name="own_shard",
    )(own_array, prefix_length, queries, shard[0])

    wide, *dec_state = pl.pallas_call(
        held_kernel,
        out_shape=(
            shape((heads * dec_rows, kv_width), bf16),
            shape((heads, dec_rows, 1), f32),
            shape((heads, dec_rows, 1), f32),
            shape((heads, dec_rows, kv_width), f32),
        ),
        in_specs=[SMEM] * 3 + [VMEM] * 5,
        out_specs=(VMEM,) * 4,
        compiler_params=params,
        cost_estimate=pl.CostEstimate(
            flops=4 * 128 * 2048 * 256, bytes_accessed=4 * pool_keys.size, transcendentals=128 * 2048
        ),
        name="decode_held_pages",
    )(own_array, page_targets, context_length, decode_queries, page_lists, pool_keys, pool_values, shard[0])

    shard[-1], state, dec_state = lax.optimization_barrier((shard[-1], state, dec_state))
    for hop in hops[2:-1]:
        shard[hop] = send(shard[hop + 1 if hop < 0 else hop - 1], hop)
    hop = hops[-1]
    nearer = shard[hop + 1 if hop < 0 else hop - 1]
    last_rest = send(nearer[: half + tokens], hop)
    last_values = send(nearer[half + tokens :], hop)

    for first in range(0, len(hops) - 1, 2):
        places = list(range(first, min(first + 2, len(hops) - 1)))
        state = pl.pallas_call(
            functools.partial(hop_kernel, places),
            out_shape=state_shapes,
            in_specs=[VMEM] * (6 + len(places)),
            out_specs=(VMEM,) * 3,
            compiler_params=params,
            cost_estimate=cost((c_rows + tokens) * len(places)),
            name="whole_shards_" + str(first),
        )(qt, near, far, *state, *[shard[hops[place]] for place in places])

    final = len(hops) - 1
    decoded, weights, total, accum = pl.pallas_call(
        functools.partial(fresh_kernel, count, hops, pool, final),
        out_shape=(
            shape(decode_queries.shape, bf16),
            shape((kv_local, c_rows, rows), bf16),
            shape((kv_local, 1, rows), f32),
            shape((kv_local, HEAD_DIM, rows), f32),
        ),
        in_specs=[SMEM] * 3 + [VMEM] * (11 + len(hops)),
        out_specs=(VMEM,) * 4,
        compiler_params=params,
        cost_estimate=cost(half),
        name="new_pages_and_last_scores",
    )(
        own_array, page_targets, context_length, page_lists, *[shard[hop] for hop in hops[:-1]], last_rest,
        wide, *dec_state, qt, near, far, *state,
    )

    prefill = pl.pallas_call(
        last_kernel,
        out_shape=shape((tokens, width), bf16),
        in_specs=[VMEM] * 4,
        out_specs=HBM,
        scratch_shapes=[
            pltpu.VMEM((tokens, width), bf16),
            pltpu.SemaphoreType.DMA((kv_local * max(GROUP // 2, 1),)),
        ],
        compiler_params=params,
        cost_estimate=cost(c_rows // 2),
        name="last_values",
    )(weights, total, accum, last_values)
    return (prefill, decoded)


def solution(mesh):
    in_specs = (
        P(("groups", "ctx"), "head"),
        P(("groups", "ctx"), "head"),
        P(("groups", "ctx"), "head"),
        P(("groups", "ctx"), "head"),
        P(("groups", "ctx"), "head"),
        P("groups"),
        P("groups"),
        P(("groups", "ctx"), None, "head"),
        P(("groups", "ctx"), None, "head"),
        P(("groups", "ctx"), "head"),
        P(("groups", "ctx"), None),
        P(("groups", "ctx")),
    )
    out_specs = (P(("groups", "ctx"), "head"), P(("groups", "ctx"), "head"))
    return jax.shard_map(
        functools.partial(per_device, mesh.shape["ctx"]),
        mesh=mesh,
        in_specs=in_specs,
        out_specs=out_specs,
        check_vma=False,
    )
```

```python
import functools

import jax
import jax.numpy as jnp
from jax import lax
from jax.experimental import pallas as pl
from jax.experimental.pallas import tpu as pltpu
from jax.sharding import PartitionSpec as P

HEADS = 64
KV_HEADS = 8
HEAD_DIM = 128
GROUP = HEADS // KV_HEADS
PAGE = 16
P_DEV = 8
SEND_CAP = 2
EXP2_SCALE = HEAD_DIM ** (-0.5) * 1.4426950408889634
HIDDEN = -1e30
VMEM_BYTES = 48 * 1024 * 1024

VMEM = pl.BlockSpec(memory_space=pltpu.VMEM)
SMEM = pl.BlockSpec(memory_space=pltpu.SMEM)
HBM = pl.BlockSpec(memory_space=pltpu.HBM)


def scores_of(qt_ref, head, cols, keys):
    return jnp.dot(keys, qt_ref[head, :, cols], preferred_element_type=jnp.float32)


def soften(scores, old):
    high = jnp.max(scores, axis=0, keepdims=True)
    if old is None:
        weights = jnp.exp2((scores - high) * EXP2_SCALE)
        return weights.astype(jnp.bfloat16), high, jnp.sum(weights, axis=0, keepdims=True), None
    old_high, old_total = old
    high = jnp.maximum(high, old_high)
    decay = jnp.exp2((old_high - high) * EXP2_SCALE)
    weights = jnp.exp2((scores - high) * EXP2_SCALE)
    total = old_total * decay + jnp.sum(weights, axis=0, keepdims=True)
    return weights.astype(jnp.bfloat16), high, total, decay


def walk(blocks, first, second):
    ahead = first(blocks[0])
    for place, block in enumerate(blocks):
        current = ahead
        if place + 1 < len(blocks):
            ahead = first(blocks[place + 1])
        second(block, current)


def blocks_of(qt_ref):
    kv_local, _, rows = qt_ref.shape
    width = min(2 * (rows // GROUP), rows)
    return [(head, slice(start, start + width)) for head in range(kv_local) for start in range(0, rows, width)]


def attend(qt_ref, keys, values_t, old, new):
    high_ref, total_ref, accum_ref = new

    def second(block, scores):
        head, cols = block
        before = None if old is None else (old[0][head, :, cols], old[1][head, :, cols])
        weights, high, total, decay = soften(scores, before)
        accum = jnp.dot(values_t[head], weights, preferred_element_type=jnp.float32)
        if old is not None:
            accum = accum + old[2][head, :, cols] * decay
        high_ref[head, :, cols] = high
        total_ref[head, :, cols] = total
        accum_ref[head, :, cols] = accum

    walk(blocks_of(qt_ref), lambda block: scores_of(qt_ref, block[0], block[1], keys[block[0]]), second)


def hidden(seen):
    return jnp.where(seen, jnp.float32(0.0), jnp.float32(HIDDEN)).astype(jnp.bfloat16)


def stretch_mask(shard, own, tokens):
    place = lax.broadcasted_iota(jnp.int32, (tokens, tokens), 0)
    token = lax.broadcasted_iota(jnp.int32, (tokens, tokens), 1)
    return hidden(place - token <= (own - shard) * tokens)


def cache_mask(shard, limit, c_rows, tokens):
    place = lax.broadcasted_iota(jnp.int32, (c_rows, tokens), 0)
    return hidden(place < limit - shard * c_rows)


def slot_row(targets_ref, shard, own, tokens, pool):
    page = lax.broadcasted_iota(jnp.int32, (1, tokens), 1) // PAGE
    slots = jnp.full((1, tokens), -1, jnp.int32)
    for index in range(tokens // PAGE):
        target = targets_ref[shard * (tokens // PAGE) + index]
        slot = jnp.where(lax.div(target, P_DEV) == own, pool + lax.rem(target, P_DEV), -1)
        slots = jnp.where(page == index, slot, slots)
    return slots


def sent_pages(targets_ref, shard, owner, pages):
    one, two = jnp.int32(-1), jnp.int32(-1)
    for index in range(pages):
        hit = lax.div(targets_ref[shard * pages + index], P_DEV) == owner
        two = jnp.where(hit & (one >= 0) & (two < 0), index, two)
        one = jnp.where(hit & (one < 0), index, one)
    return one, two


def sent_slots(targets_ref, shard, owner, pages, pool):
    place = lax.broadcasted_iota(jnp.int32, (1, SEND_CAP * PAGE), 1)
    slots = []
    for index in sent_pages(targets_ref, shard, owner, pages):
        target = targets_ref[shard * pages + jnp.maximum(index, 0)]
        slots.append(jnp.where(index >= 0, pool + lax.rem(target, P_DEV), -1))
    return jnp.where(place < PAGE, slots[0], slots[1])


def length_column(length_ref):
    rows = length_ref.shape[0]
    place = lax.broadcasted_iota(jnp.int32, (rows, 1), 0)
    lengths = jnp.zeros((rows, 1), jnp.int32)
    for row in range(rows):
        lengths = jnp.where(place == row, length_ref[row], lengths)
    return lengths


def tally_of(lists, lengths, slot):
    rows, span = lists.shape
    tokens = slot.shape[1]
    slot = jnp.broadcast_to(slot, (rows, tokens))
    offset = lax.rem(lax.broadcasted_iota(jnp.int32, (rows, tokens), 1), PAGE)
    tally = jnp.zeros((rows, tokens), jnp.float32)
    for entry in range(span):
        hit = (slot == lists[:, entry : entry + 1]) & (offset < lengths - entry * PAGE)
        tally = tally + jnp.where(hit, jnp.float32(1.0), jnp.float32(0.0))
    return tally[None]


def shard_of(own, hop, count):
    return lax.rem(own + hop + count, count)


def wide_queries(q_ref, kv_local):
    heads = q_ref.shape[1] // HEAD_DIM
    queries = q_ref[...].astype(jnp.float32)
    stacked = []
    for head in range(heads):
        piece = queries[:, head * HEAD_DIM : (head + 1) * HEAD_DIM]
        blank = jnp.zeros_like(piece)
        stacked.append(
            jnp.concatenate([piece if kv == head // GROUP else blank for kv in range(kv_local)], axis=1)
        )
    return jnp.concatenate(stacked, axis=0).astype(jnp.bfloat16)


def decode_attend(queries, parts, state):
    done = []
    for keys, values, tally in parts:
        scores = lax.dot_general(
            queries, keys, (((1,), (1,)), ((), ())), preferred_element_type=jnp.float32
        ).reshape(-1, tally.shape[1], tally.shape[2])
        done.append((jnp.where(tally > 0, scores, jnp.float32(HIDDEN)), tally, values))
    highs = [jnp.max(scores, axis=-1, keepdims=True) for scores, _, _ in done]
    if state is not None:
        old_high, old_total, old_mixed = state
        highs.append(old_high)
    high = functools.reduce(jnp.maximum, highs)
    total, mixed = 0.0, 0.0
    if state is not None:
        decay = jnp.exp2((old_high - high) * EXP2_SCALE)
        total = old_total * decay
        mixed = old_mixed * decay
    for scores, tally, values in done:
        weights = jnp.exp2((scores - high) * EXP2_SCALE) * tally
        total = total + jnp.sum(weights, axis=-1, keepdims=True)
        mixed = mixed + jnp.dot(
            weights.reshape(queries.shape[0], -1).astype(jnp.bfloat16),
            values,
            preferred_element_type=jnp.float32,
        ).reshape(high.shape[0], high.shape[1], -1)
    return high, total, mixed


def features(head):
    return slice(head * HEAD_DIM, (head + 1) * HEAD_DIM)


def shard_parts(ref, tokens, c_rows):
    return slice(0, tokens + c_rows), slice(tokens + c_rows, 2 * (tokens + c_rows))


def own_kernel(
    count, hops, own_ref, limit_ref, targets_ref, q_ref, shard_ref,
    qt_ref, near_ref, far_ref, pick_ref, high_ref, total_ref, accum_ref,
):
    kv_local, _, rows = qt_ref.shape
    tokens = q_ref.shape[0]
    c_rows = far_ref.shape[1]
    own = own_ref[0]
    limit = limit_ref[0]
    place = lax.broadcasted_iota(jnp.int32, (tokens, tokens), 0)
    token = lax.broadcasted_iota(jnp.int32, (tokens, tokens), 1)
    pick = jnp.where(place == token, jnp.float32(1.0), jnp.float32(0.0)).astype(jnp.bfloat16)
    for head in range(kv_local):
        for sub in range(GROUP):
            cols = slice(sub * tokens, (sub + 1) * tokens)
            qt_ref[head, :HEAD_DIM, cols] = q_ref[:, features(head * GROUP + sub)].T
            qt_ref[head, HEAD_DIM:, cols] = pick
    for place, hop in enumerate(hops):
        shard = shard_of(own, hop, count)
        near_ref[place] = stretch_mask(shard, own, tokens)
        far_ref[place] = cache_mask(shard, limit, c_rows, tokens)
    onward = 1 if hops[-1] < 0 else -1
    pages = tokens // PAGE
    one, two = sent_pages(
        targets_ref, shard_of(own, hops[-1] + onward, count), shard_of(own, onward, count), pages
    )
    row = lax.broadcasted_iota(jnp.int32, pick_ref.shape, 0)
    token = lax.broadcasted_iota(jnp.int32, pick_ref.shape, 1)
    sent = ((row < PAGE) & (one >= 0) & (token == row + one * PAGE)) | (
        (row >= PAGE) & (two >= 0) & (token == row + (two - 1) * PAGE)
    )
    pick_ref[...] = jnp.where(sent, jnp.float32(1.0), jnp.float32(0.0)).astype(jnp.bfloat16)
    mask = jnp.concatenate([stretch_mask(own, own, tokens), cache_mask(own, limit, c_rows, tokens)], axis=0)
    key_rows, value_rows = shard_parts(shard_ref, tokens, c_rows)
    keys = [jnp.concatenate([shard_ref[key_rows, features(head)], mask], axis=1) for head in range(kv_local)]
    values_t = [shard_ref[value_rows, features(head)].T for head in range(kv_local)]
    attend(qt_ref, keys, values_t, None, (high_ref, total_ref, accum_ref))


def held_kernel(
    own_ref, targets_ref, length_ref, q_ref, lists_ref, pool_k, pool_v, rest_ref,
    wide_ref, high_ref, total_ref, mixed_ref,
):
    kv_width = rest_ref.shape[1]
    pool = pool_k.shape[0]
    held = pool * PAGE
    tokens = PAGE * P_DEV
    half = rest_ref.shape[0] // 2
    own = own_ref[0]
    lists = lists_ref[...]
    lengths = length_column(length_ref)
    wide_ref[...] = wide_queries(q_ref, kv_width // HEAD_DIM)
    held_slot = lax.broadcasted_iota(jnp.int32, (1, held), 1) // PAGE
    own_slot = slot_row(targets_ref, own, own, tokens, pool)
    parts = [
        (
            pool_k[...].reshape(held, kv_width),
            pool_v[...].reshape(held, kv_width),
            tally_of(lists, lengths, held_slot),
        ),
        (rest_ref[:tokens], rest_ref[half : half + tokens], tally_of(lists, lengths, own_slot)),
    ]
    high_ref[...], total_ref[...], mixed_ref[...] = decode_attend(wide_ref[...], parts, None)


def hop_kernel(places, qt_ref, near_ref, far_ref, high_in, total_in, accum_in, *refs):
    shard_refs, outs = refs[: len(places)], refs[len(places) :]
    tokens, c_rows = near_ref.shape[1], far_ref.shape[1]
    mask = jnp.concatenate([ref[place] for place in places for ref in (near_ref, far_ref)], axis=0)
    keys, values_t = [], []
    for head in range(qt_ref.shape[0]):
        pieces, values = [], []
        for ref in shard_refs:
            key_rows, value_rows = shard_parts(ref, tokens, c_rows)
            pieces.append(ref[key_rows, features(head)])
            values.append(ref[value_rows, features(head)])
        keys.append(jnp.concatenate([jnp.concatenate(pieces, axis=0), mask], axis=1))
        values_t.append(jnp.concatenate(values, axis=0).T)
    attend(qt_ref, keys, values_t, (high_in, total_in, accum_in), outs)


def split_kernel(pick_ref, shard_ref, first_ref, stretch_ref, values_ref):
    tokens = pick_ref.shape[1]
    half = shard_ref.shape[0] // 2
    c_rows = half - tokens
    first_ref[:c_rows] = shard_ref[tokens:half]
    sent = pick_ref.shape[0]
    for place, start in enumerate((0, half)):
        rows = jnp.dot(pick_ref[...], shard_ref[start : start + tokens], preferred_element_type=jnp.float32)
        first_ref[c_rows + place * sent : c_rows + (place + 1) * sent] = rows.astype(jnp.bfloat16)
        stretch_ref[place * tokens : (place + 1) * tokens] = shard_ref[start : start + tokens]
    values_ref[...] = shard_ref[half + tokens :]


def pages_kernel(count, hops, tokens, pool, own_ref, targets_ref, length_ref, lists_ref, *refs):
    shard_refs, refs = refs[: len(hops)], refs[len(hops) :]
    wide_ref, dec_high, dec_total, dec_mixed, dec_out = refs
    own = own_ref[0]
    pages = tokens // PAGE
    lists = lists_ref[...]
    lengths = length_column(length_ref)
    parts = []
    for hop, ref in zip(hops[:-1], shard_refs):
        half = ref.shape[0] // 2
        slot = slot_row(targets_ref, shard_of(own, hop, count), own, tokens, pool)
        parts.append((ref[:tokens], ref[half : half + tokens], tally_of(lists, lengths, slot)))
    ref = shard_refs[-1]
    sent = SEND_CAP * PAGE
    start = ref.shape[0] - 2 * sent
    slot = sent_slots(targets_ref, shard_of(own, hops[-1], count), own, pages, pool)
    parts.append((ref[start : start + sent], ref[start + sent :], tally_of(lists, lengths, slot)))
    _, total, mixed = decode_attend(wide_ref[...], parts, (dec_high[...], dec_total[...], dec_mixed[...]))
    for head in range(dec_high.shape[0]):
        piece = mixed[head, :, features(head // GROUP)] / total[head]
        dec_out[:, features(head)] = piece.astype(jnp.bfloat16)


def score_kernel(
    final, qt_ref, near_ref, far_ref, high_in, total_in, accum_in, first_ref, stretch_ref,
    weights_ref, total_ref, accum_ref,
):
    kv_local = qt_ref.shape[0]
    tokens, c_rows = near_ref.shape[1], far_ref.shape[1]
    mask = jnp.concatenate([near_ref[final], far_ref[final]], axis=0)
    keys, values_t = [], []
    for head in range(kv_local):
        pieces = [stretch_ref[:tokens, features(head)], first_ref[:c_rows, features(head)]]
        keys.append(jnp.concatenate([jnp.concatenate(pieces, axis=0), mask], axis=1))
        values_t.append(stretch_ref[tokens:, features(head)].T)

    def second(block, scores):
        head, cols = block
        before = (high_in[head, :, cols], total_in[head, :, cols])
        weights, _, total, decay = soften(scores, before)
        weights_ref[head, :, cols] = weights[tokens:]
        total_ref[head, :, cols] = total
        accum_ref[head, :, cols] = accum_in[head, :, cols] * decay + jnp.dot(
            values_t[head], weights[:tokens], preferred_element_type=jnp.float32
        )

    walk(blocks_of(qt_ref), lambda block: scores_of(qt_ref, block[0], block[1], keys[block[0]]), second)


def last_kernel(weights_ref, total_ref, accum_ref, values_ref, out_ref, result_ref, sems):
    tokens = result_ref.shape[0]
    values_t = [values_ref[:, features(head)].T for head in range(weights_ref.shape[0])]
    copies = []

    def first(block):
        head, cols = block
        return jnp.dot(values_t[head], weights_ref[head, :, cols], preferred_element_type=jnp.float32)

    def second(block, mixed):
        head, cols = block
        mixed = mixed + accum_ref[head, :, cols]
        mixed = (mixed * (1.0 / total_ref[head, :, cols])).astype(jnp.bfloat16)
        start = (head * GROUP + cols.start // tokens) * HEAD_DIM
        pieces = (cols.stop - cols.start) // tokens
        for piece in range(pieces):
            col = start + piece * HEAD_DIM
            result_ref[:, col : col + HEAD_DIM] = mixed[:, piece * tokens : (piece + 1) * tokens].T
        span = pl.ds(start, pieces * HEAD_DIM)
        copy = pltpu.make_async_copy(result_ref.at[:, span], out_ref.at[:, span], sems.at[len(copies)])
        copy.start()
        copies.append(copy)

    walk(blocks_of(weights_ref), first, second)
    for copy in copies:
        copy.wait()


def per_device(
    count,
    queries,
    stretch_keys,
    stretch_values,
    cache_keys,
    cache_values,
    prefix_length,
    page_targets,
    pool_keys,
    pool_values,
    decode_queries,
    page_lists,
    context_length,
):
    own = lax.axis_index("ctx")
    own_array = jnp.full((1,), own, jnp.int32)
    tokens, width = queries.shape
    kv_width = stretch_keys.shape[1]
    kv_local = kv_width // HEAD_DIM
    rows = GROUP * tokens
    heads = kv_local * GROUP
    dec_rows = decode_queries.shape[0]
    c_rows = cache_keys.shape[0]
    pool = pool_keys.shape[0]
    f32, bf16 = jnp.float32, jnp.bfloat16
    shape = jax.ShapeDtypeStruct
    params = pltpu.CompilerParams(vmem_limit_bytes=VMEM_BYTES)
    up_pairs = [(i, (i + 1) % count) for i in range(count)]
    down_pairs = [(i, (i - 1) % count) for i in range(count)]
    hops = []
    for far in range(1, count // 2 + 1):
        hops += [-far, far] if far <= (count - 1) // 2 else [-far]

    def send(array, hop):
        return lax.ppermute(array, "ctx", up_pairs if hop < 0 else down_pairs)

    def cost(keys):
        pairs = kv_local * rows * keys
        return pl.CostEstimate(
            flops=4 * pairs * HEAD_DIM, bytes_accessed=4 * rows * kv_local * HEAD_DIM, transcendentals=pairs
        )

    half = tokens + c_rows
    low = jnp.array(-jnp.inf, bf16)
    spread, start = [], 0
    for part in (stretch_keys, cache_keys, stretch_values, cache_values):
        end = 2 * half - start - part.shape[0]
        spread.append(lax.pad(part, low, ((start, end, 0), (0, 0, 0))))
        start += part.shape[0]
    shard = {0: functools.reduce(jnp.maximum, spread)}
    for hop in hops[:2]:
        shard[hop] = send(shard[0], hop)

    state_shapes = (
        shape((kv_local, 1, rows), f32),
        shape((kv_local, 1, rows), f32),
        shape((kv_local, HEAD_DIM, rows), f32),
    )
    qt, near, far, pick, *state = pl.pallas_call(
        functools.partial(own_kernel, count, hops),
        out_shape=(
            shape((kv_local, HEAD_DIM + tokens, rows), bf16),
            shape((count - 1, tokens, tokens), bf16),
            shape((count - 1, c_rows, tokens), bf16),
            shape((SEND_CAP * PAGE, tokens), bf16),
        )
        + state_shapes,
        in_specs=[SMEM] * 3 + [VMEM] * 2,
        out_specs=(VMEM,) * 7,
        compiler_params=params,
        cost_estimate=cost(tokens + c_rows),
        name="own_shard",
    )(own_array, prefix_length, page_targets, queries, shard[0])

    wide, *dec_state = pl.pallas_call(
        held_kernel,
        out_shape=(
            shape((heads * dec_rows, kv_width), bf16),
            shape((heads, dec_rows, 1), f32),
            shape((heads, dec_rows, 1), f32),
            shape((heads, dec_rows, kv_width), f32),
        ),
        in_specs=[SMEM] * 3 + [VMEM] * 5,
        out_specs=(VMEM,) * 4,
        compiler_params=params,
        cost_estimate=pl.CostEstimate(
            flops=4 * 128 * 2048 * 256, bytes_accessed=4 * pool_keys.size, transcendentals=128 * 2048
        ),
        name="decode_held_pages",
    )(own_array, page_targets, context_length, decode_queries, page_lists, pool_keys, pool_values, shard[0])

    shard[-1], state, dec_state = lax.optimization_barrier((shard[-1], state, dec_state))
    for hop in hops[2:-1]:
        shard[hop] = send(shard[hop + 1 if hop < 0 else hop - 1], hop)
    hop = hops[-1]
    nearer = shard[hop + 1 if hop < 0 else hop - 1]
    pieces = pl.pallas_call(
        split_kernel,
        out_shape=(
            shape((c_rows + 2 * SEND_CAP * PAGE, kv_width), bf16),
            shape((2 * tokens, kv_width), bf16),
            shape((c_rows, kv_width), bf16),
        ),
        in_specs=[VMEM] * 2,
        out_specs=(VMEM,) * 3,
        compiler_params=params,
        name="pieces_to_send_on",
    )(pick, nearer)
    last_keys = send(pieces[0], hop)
    if 2 * hop == -count:
        pairs = [(i - 1, i) for i in range(count // 2, count)]
        pairs += [(i, i) for i in range(count // 2 - 1)] + [(count - 1, count // 2 - 1)]
        last_stretch = lax.ppermute(pieces[1], "ctx", pairs)
    else:
        last_stretch = send(pieces[1], hop)
    last_values = send(pieces[2], hop)

    for first in range(0, len(hops) - 1, 2):
        places = list(range(first, min(first + 2, len(hops) - 1)))
        state = pl.pallas_call(
            functools.partial(hop_kernel, places),
            out_shape=state_shapes,
            in_specs=[VMEM] * (6 + len(places)),
            out_specs=(VMEM,) * 3,
            compiler_params=params,
            cost_estimate=cost((c_rows + tokens) * len(places)),
            name="whole_shards_" + str(first),
        )(qt, near, far, *state, *[shard[hops[place]] for place in places])

    final = len(hops) - 1
    decoded = pl.pallas_call(
        functools.partial(pages_kernel, count, hops, tokens, pool),
        out_shape=shape(decode_queries.shape, bf16),
        in_specs=[SMEM] * 3 + [VMEM] * (5 + len(hops)),
        out_specs=VMEM,
        compiler_params=params,
        cost_estimate=cost(tokens),
        name="decode_new_pages",
    )(
        own_array, page_targets, context_length, page_lists, *[shard[hop] for hop in hops[:-1]], last_keys,
        wide, *dec_state,
    )

    weights, total, accum = pl.pallas_call(
        functools.partial(score_kernel, final),
        out_shape=(shape((kv_local, c_rows, rows), bf16),) + state_shapes[1:],
        in_specs=[VMEM] * 8,
        out_specs=(VMEM,) * 3,
        compiler_params=params,
        cost_estimate=cost(half),
        name="last_scores",
    )(qt, near, far, *state, last_keys, last_stretch)

    prefill = pl.pallas_call(
        last_kernel,
        out_shape=shape((tokens, width), bf16),
        in_specs=[VMEM] * 4,
        out_specs=HBM,
        scratch_shapes=[
            pltpu.VMEM((tokens, width), bf16),
            pltpu.SemaphoreType.DMA((kv_local * max(GROUP // 2, 1),)),
        ],
        compiler_params=params,
        cost_estimate=cost(c_rows // 2),
        name="last_values",
    )(weights, total, accum, last_values)
    return (prefill, decoded)


def solution(mesh):
    in_specs = (
        P(("groups", "ctx"), "head"),
        P(("groups", "ctx"), "head"),
        P(("groups", "ctx"), "head"),
        P(("groups", "ctx"), "head"),
        P(("groups", "ctx"), "head"),
        P("groups"),
        P("groups"),
        P(("groups", "ctx"), None, "head"),
        P(("groups", "ctx"), None, "head"),
        P(("groups", "ctx"), "head"),
        P(("groups", "ctx"), None),
        P(("groups", "ctx")),
    )
    out_specs = (P(("groups", "ctx"), "head"), P(("groups", "ctx"), "head"))
    return jax.shard_map(
        functools.partial(per_device, mesh.shape["ctx"]),
        mesh=mesh,
        in_specs=in_specs,
        out_specs=out_specs,
        check_vma=False,
    )
```

```python
import functools

import jax
import jax.numpy as jnp
from jax import lax
from jax.experimental import pallas as pl
from jax.experimental.pallas import tpu as pltpu
from jax.sharding import PartitionSpec as P

HEADS = 64
KV_HEADS = 8
HEAD_DIM = 128
GROUP = HEADS // KV_HEADS
PAGE = 16
P_DEV = 8
SEND_CAP = 2
EXP2_SCALE = HEAD_DIM ** (-0.5) * 1.4426950408889634
HIDDEN = -1e30
VMEM_BYTES = 48 * 1024 * 1024

VMEM = pl.BlockSpec(memory_space=pltpu.VMEM)
SMEM = pl.BlockSpec(memory_space=pltpu.SMEM)
HBM = pl.BlockSpec(memory_space=pltpu.HBM)


def scores_of(qt_ref, head, cols, keys):
    return jnp.dot(keys, qt_ref[head, :, cols], preferred_element_type=jnp.float32)


def soften(scores, old):
    high = jnp.max(scores, axis=0, keepdims=True)
    if old is None:
        weights = jnp.exp2((scores - high) * EXP2_SCALE)
        return weights.astype(jnp.bfloat16), high, jnp.sum(weights, axis=0, keepdims=True), None
    old_high, old_total = old
    high = jnp.maximum(high, old_high)
    decay = jnp.exp2((old_high - high) * EXP2_SCALE)
    weights = jnp.exp2((scores - high) * EXP2_SCALE)
    total = old_total * decay + jnp.sum(weights, axis=0, keepdims=True)
    return weights.astype(jnp.bfloat16), high, total, decay


def walk(blocks, first, second):
    ahead = first(blocks[0])
    for place, block in enumerate(blocks):
        current = ahead
        if place + 1 < len(blocks):
            ahead = first(blocks[place + 1])
        second(block, current)


def blocks_of(qt_ref):
    kv_local, _, rows = qt_ref.shape
    width = min(2 * (rows // GROUP), rows)
    return [(head, slice(start, start + width)) for head in range(kv_local) for start in range(0, rows, width)]


def attend(qt_ref, keys, values_t, old, new):
    high_ref, total_ref, accum_ref = new

    def second(block, scores):
        head, cols = block
        before = None if old is None else (old[0][head, :, cols], old[1][head, :, cols])
        weights, high, total, decay = soften(scores, before)
        accum = jnp.dot(values_t[head], weights, preferred_element_type=jnp.float32)
        if old is not None:
            accum = accum + old[2][head, :, cols] * decay
        high_ref[head, :, cols] = high
        total_ref[head, :, cols] = total
        accum_ref[head, :, cols] = accum

    walk(blocks_of(qt_ref), lambda block: scores_of(qt_ref, block[0], block[1], keys[block[0]]), second)


def hidden(seen):
    return jnp.where(seen, jnp.float32(0.0), jnp.float32(HIDDEN)).astype(jnp.bfloat16)


def stretch_mask(shard, own, tokens):
    place = lax.broadcasted_iota(jnp.int32, (tokens, tokens), 0)
    token = lax.broadcasted_iota(jnp.int32, (tokens, tokens), 1)
    return hidden(place - token <= (own - shard) * tokens)


def cache_mask(shard, limit, c_rows, tokens):
    place = lax.broadcasted_iota(jnp.int32, (c_rows, tokens), 0)
    return hidden(place < limit - shard * c_rows)


def slot_row(targets_ref, shard, own, tokens, pool):
    page = lax.broadcasted_iota(jnp.int32, (1, tokens), 1) // PAGE
    slots = jnp.full((1, tokens), -1, jnp.int32)
    for index in range(tokens // PAGE):
        target = targets_ref[shard * (tokens // PAGE) + index]
        slot = jnp.where(lax.div(target, P_DEV) == own, pool + lax.rem(target, P_DEV), -1)
        slots = jnp.where(page == index, slot, slots)
    return slots


def sent_pages(targets_ref, shard, owner, pages):
    one, two = jnp.int32(-1), jnp.int32(-1)
    for index in range(pages):
        hit = lax.div(targets_ref[shard * pages + index], P_DEV) == owner
        two = jnp.where(hit & (one >= 0) & (two < 0), index, two)
        one = jnp.where(hit & (one < 0), index, one)
    return one, two


def sent_slots(targets_ref, shard, owner, pages, pool):
    place = lax.broadcasted_iota(jnp.int32, (1, SEND_CAP * PAGE), 1)
    slots = []
    for index in sent_pages(targets_ref, shard, owner, pages):
        target = targets_ref[shard * pages + jnp.maximum(index, 0)]
        slots.append(jnp.where(index >= 0, pool + lax.rem(target, P_DEV), -1))
    return jnp.where(place < PAGE, slots[0], slots[1])


def length_column(length_ref):
    rows = length_ref.shape[0]
    place = lax.broadcasted_iota(jnp.int32, (rows, 1), 0)
    lengths = jnp.zeros((rows, 1), jnp.int32)
    for row in range(rows):
        lengths = jnp.where(place == row, length_ref[row], lengths)
    return lengths


def tally_of(lists, lengths, slot):
    rows, span = lists.shape
    tokens = slot.shape[1]
    slot = jnp.broadcast_to(slot, (rows, tokens))
    offset = lax.rem(lax.broadcasted_iota(jnp.int32, (rows, tokens), 1), PAGE)
    tally = jnp.zeros((rows, tokens), jnp.float32)
    for entry in range(span):
        hit = (slot == lists[:, entry : entry + 1]) & (offset < lengths - entry * PAGE)
        tally = tally + jnp.where(hit, jnp.float32(1.0), jnp.float32(0.0))
    return tally[None]


def shard_of(own, hop, count):
    return lax.rem(own + hop + count, count)


def wide_queries(q_ref, kv_local):
    heads = q_ref.shape[1] // HEAD_DIM
    queries = q_ref[...].astype(jnp.float32)
    stacked = []
    for head in range(heads):
        piece = queries[:, head * HEAD_DIM : (head + 1) * HEAD_DIM]
        blank = jnp.zeros_like(piece)
        stacked.append(
            jnp.concatenate([piece if kv == head // GROUP else blank for kv in range(kv_local)], axis=1)
        )
    return jnp.concatenate(stacked, axis=0).astype(jnp.bfloat16)


def decode_attend(queries, parts, state):
    done = []
    for keys, values, tally in parts:
        scores = lax.dot_general(
            queries, keys, (((1,), (1,)), ((), ())), preferred_element_type=jnp.float32
        ).reshape(-1, tally.shape[1], tally.shape[2])
        done.append((jnp.where(tally > 0, scores, jnp.float32(HIDDEN)), tally, values))
    highs = [jnp.max(scores, axis=-1, keepdims=True) for scores, _, _ in done]
    if state is not None:
        old_high, old_total, old_mixed = state
        highs.append(old_high)
    high = functools.reduce(jnp.maximum, highs)
    total, mixed = 0.0, 0.0
    if state is not None:
        decay = jnp.exp2((old_high - high) * EXP2_SCALE)
        total = old_total * decay
        mixed = old_mixed * decay
    for scores, tally, values in done:
        weights = jnp.exp2((scores - high) * EXP2_SCALE) * tally
        total = total + jnp.sum(weights, axis=-1, keepdims=True)
        mixed = mixed + jnp.dot(
            weights.reshape(queries.shape[0], -1).astype(jnp.bfloat16),
            values,
            preferred_element_type=jnp.float32,
        ).reshape(high.shape[0], high.shape[1], -1)
    return high, total, mixed


def features(head):
    return slice(head * HEAD_DIM, (head + 1) * HEAD_DIM)


def shard_parts(ref, tokens, c_rows):
    return slice(0, tokens + c_rows), slice(tokens + c_rows, 2 * (tokens + c_rows))


def own_kernel(
    count, hops, own_ref, limit_ref, targets_ref, q_ref, shard_ref,
    qt_ref, near_ref, far_ref, pick_ref, high_ref, total_ref, accum_ref,
):
    kv_local, _, rows = qt_ref.shape
    tokens = q_ref.shape[0]
    c_rows = far_ref.shape[1]
    own = own_ref[0]
    limit = limit_ref[0]
    place = lax.broadcasted_iota(jnp.int32, (tokens, tokens), 0)
    token = lax.broadcasted_iota(jnp.int32, (tokens, tokens), 1)
    pick = jnp.where(place == token, jnp.float32(1.0), jnp.float32(0.0)).astype(jnp.bfloat16)
    for head in range(kv_local):
        for sub in range(GROUP):
            cols = slice(sub * tokens, (sub + 1) * tokens)
            qt_ref[head, :HEAD_DIM, cols] = q_ref[:, features(head * GROUP + sub)].T
            qt_ref[head, HEAD_DIM:, cols] = pick
    for place, hop in enumerate(hops):
        shard = shard_of(own, hop, count)
        near_ref[place] = stretch_mask(shard, own, tokens)
        far_ref[place] = cache_mask(shard, limit, c_rows, tokens)
    onward = 1 if hops[-1] < 0 else -1
    pages = tokens // PAGE
    one, two = sent_pages(
        targets_ref, shard_of(own, hops[-1] + onward, count), shard_of(own, onward, count), pages
    )
    row = lax.broadcasted_iota(jnp.int32, pick_ref.shape, 0)
    token = lax.broadcasted_iota(jnp.int32, pick_ref.shape, 1)
    sent = ((row < PAGE) & (one >= 0) & (token == row + one * PAGE)) | (
        (row >= PAGE) & (two >= 0) & (token == row + (two - 1) * PAGE)
    )
    pick_ref[...] = jnp.where(sent, jnp.float32(1.0), jnp.float32(0.0)).astype(jnp.bfloat16)
    mask = jnp.concatenate([stretch_mask(own, own, tokens), cache_mask(own, limit, c_rows, tokens)], axis=0)
    key_rows, value_rows = shard_parts(shard_ref, tokens, c_rows)
    keys = [jnp.concatenate([shard_ref[key_rows, features(head)], mask], axis=1) for head in range(kv_local)]
    values_t = [shard_ref[value_rows, features(head)].T for head in range(kv_local)]
    attend(qt_ref, keys, values_t, None, (high_ref, total_ref, accum_ref))


def held_kernel(
    own_ref, targets_ref, length_ref, q_ref, lists_ref, pool_k, pool_v, rest_ref,
    wide_ref, high_ref, total_ref, mixed_ref,
):
    kv_width = rest_ref.shape[1]
    pool = pool_k.shape[0]
    held = pool * PAGE
    tokens = PAGE * P_DEV
    half = rest_ref.shape[0] // 2
    own = own_ref[0]
    lists = lists_ref[...]
    lengths = length_column(length_ref)
    wide_ref[...] = wide_queries(q_ref, kv_width // HEAD_DIM)
    held_slot = lax.broadcasted_iota(jnp.int32, (1, held), 1) // PAGE
    own_slot = slot_row(targets_ref, own, own, tokens, pool)
    parts = [
        (
            pool_k[...].reshape(held, kv_width),
            pool_v[...].reshape(held, kv_width),
            tally_of(lists, lengths, held_slot),
        ),
        (rest_ref[:tokens], rest_ref[half : half + tokens], tally_of(lists, lengths, own_slot)),
    ]
    high_ref[...], total_ref[...], mixed_ref[...] = decode_attend(wide_ref[...], parts, None)


def hop_kernel(places, qt_ref, near_ref, far_ref, high_in, total_in, accum_in, *refs):
    shard_refs, outs = refs[: len(places)], refs[len(places) :]
    tokens, c_rows = near_ref.shape[1], far_ref.shape[1]
    mask = jnp.concatenate([ref[place] for place in places for ref in (near_ref, far_ref)], axis=0)
    keys, values_t = [], []
    for head in range(qt_ref.shape[0]):
        pieces, values = [], []
        for ref in shard_refs:
            key_rows, value_rows = shard_parts(ref, tokens, c_rows)
            pieces.append(ref[key_rows, features(head)])
            values.append(ref[value_rows, features(head)])
        keys.append(jnp.concatenate([jnp.concatenate(pieces, axis=0), mask], axis=1))
        values_t.append(jnp.concatenate(values, axis=0).T)
    attend(qt_ref, keys, values_t, (high_in, total_in, accum_in), outs)


def split_kernel(pick_ref, shard_ref, first_ref, stretch_ref, values_ref):
    tokens = pick_ref.shape[1]
    half = shard_ref.shape[0] // 2
    c_rows = half - tokens
    first_ref[:c_rows] = shard_ref[tokens:half]
    sent = pick_ref.shape[0]
    for place, start in enumerate((0, half)):
        rows = jnp.dot(pick_ref[...], shard_ref[start : start + tokens], preferred_element_type=jnp.float32)
        first_ref[c_rows + place * sent : c_rows + (place + 1) * sent] = rows.astype(jnp.bfloat16)
        stretch_ref[place * tokens : (place + 1) * tokens] = shard_ref[start : start + tokens]
    values_ref[...] = shard_ref[half + tokens :]


def pages_kernel(count, hops, tokens, pool, own_ref, targets_ref, length_ref, lists_ref, *refs):
    shard_refs, refs = refs[: len(hops)], refs[len(hops) :]
    wide_ref, dec_high, dec_total, dec_mixed, dec_out = refs
    own = own_ref[0]
    pages = tokens // PAGE
    lists = lists_ref[...]
    lengths = length_column(length_ref)
    parts = []
    for hop, ref in zip(hops[:-1], shard_refs):
        half = ref.shape[0] // 2
        slot = slot_row(targets_ref, shard_of(own, hop, count), own, tokens, pool)
        parts.append((ref[:tokens], ref[half : half + tokens], tally_of(lists, lengths, slot)))
    ref = shard_refs[-1]
    sent = SEND_CAP * PAGE
    start = ref.shape[0] - 2 * sent
    slot = sent_slots(targets_ref, shard_of(own, hops[-1], count), own, pages, pool)
    parts.append((ref[start : start + sent], ref[start + sent :], tally_of(lists, lengths, slot)))
    _, total, mixed = decode_attend(wide_ref[...], parts, (dec_high[...], dec_total[...], dec_mixed[...]))
    for head in range(dec_high.shape[0]):
        piece = mixed[head, :, features(head // GROUP)] / total[head]
        dec_out[:, features(head)] = piece.astype(jnp.bfloat16)


def score_kernel(
    final, qt_ref, near_ref, far_ref, high_in, total_in, accum_in, first_ref, stretch_ref,
    weights_ref, total_ref, accum_ref,
):
    kv_local = qt_ref.shape[0]
    tokens, c_rows = near_ref.shape[1], far_ref.shape[1]
    mask = jnp.concatenate([near_ref[final], far_ref[final]], axis=0)
    keys, values_t = [], []
    for head in range(kv_local):
        pieces = [stretch_ref[:tokens, features(head)], first_ref[:c_rows, features(head)]]
        keys.append(jnp.concatenate([jnp.concatenate(pieces, axis=0), mask], axis=1))
        values_t.append(stretch_ref[tokens:, features(head)].T)

    def second(block, scores):
        head, cols = block
        before = (high_in[head, :, cols], total_in[head, :, cols])
        weights, _, total, decay = soften(scores, before)
        weights_ref[head, :, cols] = weights[tokens:]
        total_ref[head, :, cols] = total
        accum_ref[head, :, cols] = accum_in[head, :, cols] * decay + jnp.dot(
            values_t[head], weights[:tokens], preferred_element_type=jnp.float32
        )

    walk(blocks_of(qt_ref), lambda block: scores_of(qt_ref, block[0], block[1], keys[block[0]]), second)


def last_kernel(weights_ref, total_ref, accum_ref, values_ref, out_ref, result_ref, sems):
    tokens = result_ref.shape[0]
    values_t = [values_ref[:, features(head)].T for head in range(weights_ref.shape[0])]
    copies = []

    def first(block):
        head, cols = block
        return jnp.dot(values_t[head], weights_ref[head, :, cols], preferred_element_type=jnp.float32)

    def second(block, mixed):
        head, cols = block
        mixed = mixed + accum_ref[head, :, cols]
        mixed = (mixed * (1.0 / total_ref[head, :, cols])).astype(jnp.bfloat16)
        start = (head * GROUP + cols.start // tokens) * HEAD_DIM
        pieces = (cols.stop - cols.start) // tokens
        for piece in range(pieces):
            col = start + piece * HEAD_DIM
            result_ref[:, col : col + HEAD_DIM] = mixed[:, piece * tokens : (piece + 1) * tokens].T
        span = pl.ds(start, pieces * HEAD_DIM)
        copy = pltpu.make_async_copy(result_ref.at[:, span], out_ref.at[:, span], sems.at[len(copies)])
        copy.start()
        copies.append(copy)

    walk(blocks_of(weights_ref), first, second)
    for copy in copies:
        copy.wait()


def per_device(
    count,
    queries,
    stretch_keys,
    stretch_values,
    cache_keys,
    cache_values,
    prefix_length,
    page_targets,
    pool_keys,
    pool_values,
    decode_queries,
    page_lists,
    context_length,
):
    own = lax.axis_index("ctx")
    own_array = jnp.full((1,), own, jnp.int32)
    tokens, width = queries.shape
    kv_width = stretch_keys.shape[1]
    kv_local = kv_width // HEAD_DIM
    rows = GROUP * tokens
    heads = kv_local * GROUP
    dec_rows = decode_queries.shape[0]
    c_rows = cache_keys.shape[0]
    pool = pool_keys.shape[0]
    f32, bf16 = jnp.float32, jnp.bfloat16
    shape = jax.ShapeDtypeStruct
    params = pltpu.CompilerParams(vmem_limit_bytes=VMEM_BYTES)
    up_pairs = [(i, (i + 1) % count) for i in range(count)]
    down_pairs = [(i, (i - 1) % count) for i in range(count)]
    hops = []
    for far in range(1, count // 2 + 1):
        hops += [-far, far] if far <= (count - 1) // 2 else [-far]

    def send(array, hop):
        return lax.ppermute(array, "ctx", up_pairs if hop < 0 else down_pairs)

    def cost(keys):
        pairs = kv_local * rows * keys
        return pl.CostEstimate(
            flops=4 * pairs * HEAD_DIM, bytes_accessed=4 * rows * kv_local * HEAD_DIM, transcendentals=pairs
        )

    half = tokens + c_rows
    low = jnp.array(-jnp.inf, bf16)
    spread, start = [], 0
    for part in (stretch_keys, cache_keys, stretch_values, cache_values):
        end = 2 * half - start - part.shape[0]
        spread.append(lax.pad(part, low, ((start, end, 0), (0, 0, 0))))
        start += part.shape[0]
    shard = {0: functools.reduce(jnp.maximum, spread)}
    shard[-1] = send(shard[0], -1)

    state_shapes = (
        shape((kv_local, 1, rows), f32),
        shape((kv_local, 1, rows), f32),
        shape((kv_local, HEAD_DIM, rows), f32),
    )
    qt, near, far, pick, *state = pl.pallas_call(
        functools.partial(own_kernel, count, hops),
        out_shape=(
            shape((kv_local, HEAD_DIM + tokens, rows), bf16),
            shape((count - 1, tokens, tokens), bf16),
            shape((count - 1, c_rows, tokens), bf16),
            shape((SEND_CAP * PAGE, tokens), bf16),
        )
        + state_shapes,
        in_specs=[SMEM] * 3 + [VMEM] * 2,
        out_specs=(VMEM,) * 7,
        compiler_params=params,
        cost_estimate=cost(tokens + c_rows),
        name="own_shard",
    )(own_array, prefix_length, page_targets, queries, shard[0])

    if 1 in hops:
        sent_down, state = lax.optimization_barrier((shard[0], state))
        shard[1] = send(sent_down, 1)

    wide, *dec_state = pl.pallas_call(
        held_kernel,
        out_shape=(
            shape((heads * dec_rows, kv_width), bf16),
            shape((heads, dec_rows, 1), f32),
            shape((heads, dec_rows, 1), f32),
            shape((heads, dec_rows, kv_width), f32),
        ),
        in_specs=[SMEM] * 3 + [VMEM] * 5,
        out_specs=(VMEM,) * 4,
        compiler_params=params,
        cost_estimate=pl.CostEstimate(
            flops=4 * 128 * 2048 * 256, bytes_accessed=4 * pool_keys.size, transcendentals=128 * 2048
        ),
        name="decode_held_pages",
    )(own_array, page_targets, context_length, decode_queries, page_lists, pool_keys, pool_values, shard[0])

    shard[-1], state, dec_state = lax.optimization_barrier((shard[-1], state, dec_state))
    for hop in hops[2:-1]:
        shard[hop] = send(shard[hop + 1 if hop < 0 else hop - 1], hop)
    hop = hops[-1]
    nearer = shard[hop + 1 if hop < 0 else hop - 1]
    pieces = pl.pallas_call(
        split_kernel,
        out_shape=(
            shape((c_rows + 2 * SEND_CAP * PAGE, kv_width), bf16),
            shape((2 * tokens, kv_width), bf16),
            shape((c_rows, kv_width), bf16),
        ),
        in_specs=[VMEM] * 2,
        out_specs=(VMEM,) * 3,
        compiler_params=params,
        name="pieces_to_send_on",
    )(pick, nearer)
    last_keys = send(pieces[0], hop)
    if 2 * hop == -count:
        pairs = [(i - 1, i) for i in range(count // 2, count)]
        pairs += [(i, i) for i in range(count // 2 - 1)] + [(count - 1, count // 2 - 1)]
        last_stretch = lax.ppermute(pieces[1], "ctx", pairs)
    else:
        last_stretch = send(pieces[1], hop)
    last_values = send(pieces[2], hop)

    for first in range(len(hops) - 1):
        places = [first]
        state = pl.pallas_call(
            functools.partial(hop_kernel, places),
            out_shape=state_shapes,
            in_specs=[VMEM] * (6 + len(places)),
            out_specs=(VMEM,) * 3,
            compiler_params=params,
            cost_estimate=cost((c_rows + tokens) * len(places)),
            name="whole_shards_" + str(first),
        )(qt, near, far, *state, *[shard[hops[place]] for place in places])

    final = len(hops) - 1
    decoded = pl.pallas_call(
        functools.partial(pages_kernel, count, hops, tokens, pool),
        out_shape=shape(decode_queries.shape, bf16),
        in_specs=[SMEM] * 3 + [VMEM] * (5 + len(hops)),
        out_specs=VMEM,
        compiler_params=params,
        cost_estimate=cost(tokens),
        name="decode_new_pages",
    )(
        own_array, page_targets, context_length, page_lists, *[shard[hop] for hop in hops[:-1]], last_keys,
        wide, *dec_state,
    )

    weights, total, accum = pl.pallas_call(
        functools.partial(score_kernel, final),
        out_shape=(shape((kv_local, c_rows, rows), bf16),) + state_shapes[1:],
        in_specs=[VMEM] * 8,
        out_specs=(VMEM,) * 3,
        compiler_params=params,
        cost_estimate=cost(half),
        name="last_scores",
    )(qt, near, far, *state, last_keys, last_stretch)

    prefill = pl.pallas_call(
        last_kernel,
        out_shape=shape((tokens, width), bf16),
        in_specs=[VMEM] * 4,
        out_specs=HBM,
        scratch_shapes=[
            pltpu.VMEM((tokens, width), bf16),
            pltpu.SemaphoreType.DMA((kv_local * max(GROUP // 2, 1),)),
        ],
        compiler_params=params,
        cost_estimate=cost(c_rows // 2),
        name="last_values",
    )(weights, total, accum, last_values)
    return (prefill, decoded)


def solution(mesh):
    in_specs = (
        P(("groups", "ctx"), "head"),
        P(("groups", "ctx"), "head"),
        P(("groups", "ctx"), "head"),
        P(("groups", "ctx"), "head"),
        P(("groups", "ctx"), "head"),
        P("groups"),
        P("groups"),
        P(("groups", "ctx"), None, "head"),
        P(("groups", "ctx"), None, "head"),
        P(("groups", "ctx"), "head"),
        P(("groups", "ctx"), None),
        P(("groups", "ctx")),
    )
    out_specs = (P(("groups", "ctx"), "head"), P(("groups", "ctx"), "head"))
    return jax.shard_map(
        functools.partial(per_device, mesh.shape["ctx"]),
        mesh=mesh,
        in_specs=in_specs,
        out_specs=out_specs,
        check_vma=False,
    )
```

```python
import functools

import jax
import jax.numpy as jnp
from jax import lax
from jax.experimental import pallas as pl
from jax.experimental.pallas import tpu as pltpu
from jax.sharding import PartitionSpec as P

HEADS = 64
KV_HEADS = 8
HEAD_DIM = 128
GROUP = HEADS // KV_HEADS
PAGE = 16
P_DEV = 8
SEND_CAP = 2
EXP2_SCALE = HEAD_DIM ** (-0.5) * 1.4426950408889634
HIDDEN = -1e30
VMEM_BYTES = 48 * 1024 * 1024

VMEM = pl.BlockSpec(memory_space=pltpu.VMEM)
SMEM = pl.BlockSpec(memory_space=pltpu.SMEM)
HBM = pl.BlockSpec(memory_space=pltpu.HBM)


def scores_of(qt_ref, head, cols, keys):
    return jnp.dot(keys, qt_ref[head, :, cols], preferred_element_type=jnp.float32)


def soften(scores, old):
    high = jnp.max(scores, axis=0, keepdims=True)
    if old is None:
        weights = jnp.exp2((scores - high) * EXP2_SCALE)
        return weights.astype(jnp.bfloat16), high, jnp.sum(weights, axis=0, keepdims=True), None
    old_high, old_total = old
    high = jnp.maximum(high, old_high)
    decay = jnp.exp2((old_high - high) * EXP2_SCALE)
    weights = jnp.exp2((scores - high) * EXP2_SCALE)
    total = old_total * decay + jnp.sum(weights, axis=0, keepdims=True)
    return weights.astype(jnp.bfloat16), high, total, decay


def walk(blocks, first, second):
    ahead = first(blocks[0])
    for place, block in enumerate(blocks):
        current = ahead
        if place + 1 < len(blocks):
            ahead = first(blocks[place + 1])
        second(block, current)


def blocks_of(qt_ref):
    kv_local, _, rows = qt_ref.shape
    width = min(2 * (rows // GROUP), rows)
    return [(head, slice(start, start + width)) for head in range(kv_local) for start in range(0, rows, width)]


def attend(qt_ref, keys, values_t, old, new):
    high_ref, total_ref, accum_ref = new

    def second(block, scores):
        head, cols = block
        before = None if old is None else (old[0][head, :, cols], old[1][head, :, cols])
        weights, high, total, decay = soften(scores, before)
        accum = jnp.dot(values_t[head], weights, preferred_element_type=jnp.float32)
        if old is not None:
            accum = accum + old[2][head, :, cols] * decay
        high_ref[head, :, cols] = high
        total_ref[head, :, cols] = total
        accum_ref[head, :, cols] = accum

    walk(blocks_of(qt_ref), lambda block: scores_of(qt_ref, block[0], block[1], keys[block[0]]), second)


def hidden(seen):
    return jnp.where(seen, jnp.float32(0.0), jnp.float32(HIDDEN)).astype(jnp.bfloat16)


def stretch_mask(shard, own, tokens):
    place = lax.broadcasted_iota(jnp.int32, (tokens, tokens), 0)
    token = lax.broadcasted_iota(jnp.int32, (tokens, tokens), 1)
    return hidden(place - token <= (own - shard) * tokens)


def cache_mask(shard, limit, c_rows, tokens):
    place = lax.broadcasted_iota(jnp.int32, (c_rows, tokens), 0)
    return hidden(place < limit - shard * c_rows)


def slot_row(targets_ref, shard, own, tokens, pool):
    page = lax.broadcasted_iota(jnp.int32, (1, tokens), 1) // PAGE
    slots = jnp.full((1, tokens), -1, jnp.int32)
    for index in range(tokens // PAGE):
        target = targets_ref[shard * (tokens // PAGE) + index]
        slot = jnp.where(lax.div(target, P_DEV) == own, pool + lax.rem(target, P_DEV), -1)
        slots = jnp.where(page == index, slot, slots)
    return slots


def sent_pages(targets_ref, shard, owner, pages):
    one, two = jnp.int32(-1), jnp.int32(-1)
    for index in range(pages):
        hit = lax.div(targets_ref[shard * pages + index], P_DEV) == owner
        two = jnp.where(hit & (one >= 0) & (two < 0), index, two)
        one = jnp.where(hit & (one < 0), index, one)
    return one, two


def sent_slots(targets_ref, shard, owner, pages, pool):
    place = lax.broadcasted_iota(jnp.int32, (1, SEND_CAP * PAGE), 1)
    slots = []
    for index in sent_pages(targets_ref, shard, owner, pages):
        target = targets_ref[shard * pages + jnp.maximum(index, 0)]
        slots.append(jnp.where(index >= 0, pool + lax.rem(target, P_DEV), -1))
    return jnp.where(place < PAGE, slots[0], slots[1])


def length_column(length_ref):
    rows = length_ref.shape[0]
    place = lax.broadcasted_iota(jnp.int32, (rows, 1), 0)
    lengths = jnp.zeros((rows, 1), jnp.int32)
    for row in range(rows):
        lengths = jnp.where(place == row, length_ref[row], lengths)
    return lengths


def tally_of(lists, lengths, slot):
    rows, span = lists.shape
    tokens = slot.shape[1]
    slot = jnp.broadcast_to(slot, (rows, tokens))
    offset = lax.rem(lax.broadcasted_iota(jnp.int32, (rows, tokens), 1), PAGE)
    tally = jnp.zeros((rows, tokens), jnp.float32)
    for entry in range(span):
        hit = (slot == lists[:, entry : entry + 1]) & (offset < lengths - entry * PAGE)
        tally = tally + jnp.where(hit, jnp.float32(1.0), jnp.float32(0.0))
    return tally[None]


def shard_of(own, hop, count):
    return lax.rem(own + hop + count, count)


def wide_queries(q_ref, kv_local):
    heads = q_ref.shape[1] // HEAD_DIM
    queries = q_ref[...].astype(jnp.float32)
    stacked = []
    for head in range(heads):
        piece = queries[:, head * HEAD_DIM : (head + 1) * HEAD_DIM]
        blank = jnp.zeros_like(piece)
        stacked.append(
            jnp.concatenate([piece if kv == head // GROUP else blank for kv in range(kv_local)], axis=1)
        )
    return jnp.concatenate(stacked, axis=0).astype(jnp.bfloat16)


def decode_attend(queries, parts, state):
    done = []
    for keys, values, tally in parts:
        scores = lax.dot_general(
            queries, keys, (((1,), (1,)), ((), ())), preferred_element_type=jnp.float32
        ).reshape(-1, tally.shape[1], tally.shape[2])
        done.append((jnp.where(tally > 0, scores, jnp.float32(HIDDEN)), tally, values))
    highs = [jnp.max(scores, axis=-1, keepdims=True) for scores, _, _ in done]
    if state is not None:
        old_high, old_total, old_mixed = state
        highs.append(old_high)
    high = functools.reduce(jnp.maximum, highs)
    total, mixed = 0.0, 0.0
    if state is not None:
        decay = jnp.exp2((old_high - high) * EXP2_SCALE)
        total = old_total * decay
        mixed = old_mixed * decay
    for scores, tally, values in done:
        weights = jnp.exp2((scores - high) * EXP2_SCALE) * tally
        total = total + jnp.sum(weights, axis=-1, keepdims=True)
        mixed = mixed + jnp.dot(
            weights.reshape(queries.shape[0], -1).astype(jnp.bfloat16),
            values,
            preferred_element_type=jnp.float32,
        ).reshape(high.shape[0], high.shape[1], -1)
    return high, total, mixed


def features(head):
    return slice(head * HEAD_DIM, (head + 1) * HEAD_DIM)


def shard_parts(ref, tokens, c_rows):
    return slice(0, tokens + c_rows), slice(tokens + c_rows, 2 * (tokens + c_rows))


def own_kernel(
    count, hops, own_ref, limit_ref, targets_ref, q_ref, shard_ref,
    qt_ref, near_ref, far_ref, pick_ref, high_ref, total_ref, accum_ref,
):
    kv_local, _, rows = qt_ref.shape
    tokens = q_ref.shape[0]
    c_rows = far_ref.shape[1]
    own = own_ref[0]
    limit = limit_ref[0]
    place = lax.broadcasted_iota(jnp.int32, (tokens, tokens), 0)
    token = lax.broadcasted_iota(jnp.int32, (tokens, tokens), 1)
    pick = jnp.where(place == token, jnp.float32(1.0), jnp.float32(0.0)).astype(jnp.bfloat16)
    for head in range(kv_local):
        for sub in range(GROUP):
            cols = slice(sub * tokens, (sub + 1) * tokens)
            qt_ref[head, :HEAD_DIM, cols] = q_ref[:, features(head * GROUP + sub)].T
            qt_ref[head, HEAD_DIM:, cols] = pick
    for place, hop in enumerate(hops):
        shard = shard_of(own, hop, count)
        near_ref[place] = stretch_mask(shard, own, tokens)
        far_ref[place] = cache_mask(shard, limit, c_rows, tokens)
    onward = 1 if hops[-1] < 0 else -1
    pages = tokens // PAGE
    one, two = sent_pages(
        targets_ref, shard_of(own, hops[-1] + onward, count), shard_of(own, onward, count), pages
    )
    row = lax.broadcasted_iota(jnp.int32, pick_ref.shape, 0)
    token = lax.broadcasted_iota(jnp.int32, pick_ref.shape, 1)
    sent = ((row < PAGE) & (one >= 0) & (token == row + one * PAGE)) | (
        (row >= PAGE) & (two >= 0) & (token == row + (two - 1) * PAGE)
    )
    pick_ref[...] = jnp.where(sent, jnp.float32(1.0), jnp.float32(0.0)).astype(jnp.bfloat16)
    mask = jnp.concatenate([stretch_mask(own, own, tokens), cache_mask(own, limit, c_rows, tokens)], axis=0)
    key_rows, value_rows = shard_parts(shard_ref, tokens, c_rows)
    keys = [jnp.concatenate([shard_ref[key_rows, features(head)], mask], axis=1) for head in range(kv_local)]
    values_t = [shard_ref[value_rows, features(head)].T for head in range(kv_local)]
    attend(qt_ref, keys, values_t, None, (high_ref, total_ref, accum_ref))


def held_kernel(
    own_ref, targets_ref, length_ref, q_ref, lists_ref, pool_k, pool_v, rest_ref,
    wide_ref, high_ref, total_ref, mixed_ref,
):
    kv_width = rest_ref.shape[1]
    pool = pool_k.shape[0]
    held = pool * PAGE
    tokens = PAGE * P_DEV
    half = rest_ref.shape[0] // 2
    own = own_ref[0]
    lists = lists_ref[...]
    lengths = length_column(length_ref)
    wide_ref[...] = wide_queries(q_ref, kv_width // HEAD_DIM)
    held_slot = lax.broadcasted_iota(jnp.int32, (1, held), 1) // PAGE
    own_slot = slot_row(targets_ref, own, own, tokens, pool)
    parts = [
        (
            pool_k[...].reshape(held, kv_width),
            pool_v[...].reshape(held, kv_width),
            tally_of(lists, lengths, held_slot),
        ),
        (rest_ref[:tokens], rest_ref[half : half + tokens], tally_of(lists, lengths, own_slot)),
    ]
    high_ref[...], total_ref[...], mixed_ref[...] = decode_attend(wide_ref[...], parts, None)


def hop_kernel(places, qt_ref, near_ref, far_ref, high_in, total_in, accum_in, *refs):
    shard_refs, outs = refs[: len(places)], refs[len(places) :]
    tokens, c_rows = near_ref.shape[1], far_ref.shape[1]
    mask = jnp.concatenate([ref[place] for place in places for ref in (near_ref, far_ref)], axis=0)
    keys, values_t = [], []
    for head in range(qt_ref.shape[0]):
        pieces, values = [], []
        for ref in shard_refs:
            key_rows, value_rows = shard_parts(ref, tokens, c_rows)
            pieces.append(ref[key_rows, features(head)])
            values.append(ref[value_rows, features(head)])
        keys.append(jnp.concatenate([jnp.concatenate(pieces, axis=0), mask], axis=1))
        values_t.append(jnp.concatenate(values, axis=0).T)
    attend(qt_ref, keys, values_t, (high_in, total_in, accum_in), outs)


def split_kernel(pick_ref, shard_ref, first_ref, stretch_ref, values_ref):
    tokens = pick_ref.shape[1]
    half = shard_ref.shape[0] // 2
    c_rows = half - tokens
    first_ref[:c_rows] = shard_ref[tokens:half]
    sent = pick_ref.shape[0]
    for place, start in enumerate((0, half)):
        rows = jnp.dot(pick_ref[...], shard_ref[start : start + tokens], preferred_element_type=jnp.float32)
        first_ref[c_rows + place * sent : c_rows + (place + 1) * sent] = rows.astype(jnp.bfloat16)
        stretch_ref[place * tokens : (place + 1) * tokens] = shard_ref[start : start + tokens]
    values_ref[...] = shard_ref[half + tokens :]


def pages_kernel(count, hops, tokens, pool, own_ref, targets_ref, length_ref, lists_ref, *refs):
    shard_refs, refs = refs[: len(hops)], refs[len(hops) :]
    wide_ref, dec_high, dec_total, dec_mixed, dec_out = refs
    own = own_ref[0]
    pages = tokens // PAGE
    lists = lists_ref[...]
    lengths = length_column(length_ref)
    parts = []
    for hop, ref in zip(hops[:-1], shard_refs):
        half = ref.shape[0] // 2
        slot = slot_row(targets_ref, shard_of(own, hop, count), own, tokens, pool)
        parts.append((ref[:tokens], ref[half : half + tokens], tally_of(lists, lengths, slot)))
    ref = shard_refs[-1]
    sent = SEND_CAP * PAGE
    start = ref.shape[0] - 2 * sent
    slot = sent_slots(targets_ref, shard_of(own, hops[-1], count), own, pages, pool)
    parts.append((ref[start : start + sent], ref[start + sent :], tally_of(lists, lengths, slot)))
    _, total, mixed = decode_attend(wide_ref[...], parts, (dec_high[...], dec_total[...], dec_mixed[...]))
    for head in range(dec_high.shape[0]):
        piece = mixed[head, :, features(head // GROUP)] / total[head]
        dec_out[:, features(head)] = piece.astype(jnp.bfloat16)


def score_kernel(
    final, qt_ref, near_ref, far_ref, high_in, total_in, accum_in, first_ref, stretch_ref,
    weights_ref, total_ref, accum_ref,
):
    kv_local = qt_ref.shape[0]
    tokens, c_rows = near_ref.shape[1], far_ref.shape[1]
    mask = jnp.concatenate([near_ref[final], far_ref[final]], axis=0)
    keys, values_t = [], []
    for head in range(kv_local):
        pieces = [stretch_ref[:tokens, features(head)], first_ref[:c_rows, features(head)]]
        keys.append(jnp.concatenate([jnp.concatenate(pieces, axis=0), mask], axis=1))
        values_t.append(stretch_ref[tokens:, features(head)].T)

    def second(block, scores):
        head, cols = block
        before = (high_in[head, :, cols], total_in[head, :, cols])
        weights, _, total, decay = soften(scores, before)
        weights_ref[head, :, cols] = weights[tokens:]
        total_ref[head, :, cols] = total
        accum_ref[head, :, cols] = accum_in[head, :, cols] * decay + jnp.dot(
            values_t[head], weights[:tokens], preferred_element_type=jnp.float32
        )

    walk(blocks_of(qt_ref), lambda block: scores_of(qt_ref, block[0], block[1], keys[block[0]]), second)


def last_kernel(weights_ref, total_ref, accum_ref, values_ref, out_ref, result_ref, sems):
    tokens = result_ref.shape[0]
    values_t = [values_ref[:, features(head)].T for head in range(weights_ref.shape[0])]
    copies = []

    def first(block):
        head, cols = block
        return jnp.dot(values_t[head], weights_ref[head, :, cols], preferred_element_type=jnp.float32)

    def second(block, mixed):
        head, cols = block
        mixed = mixed + accum_ref[head, :, cols]
        mixed = (mixed * (1.0 / total_ref[head, :, cols])).astype(jnp.bfloat16)
        start = (head * GROUP + cols.start // tokens) * HEAD_DIM
        pieces = (cols.stop - cols.start) // tokens
        for piece in range(pieces):
            col = start + piece * HEAD_DIM
            result_ref[:, col : col + HEAD_DIM] = mixed[:, piece * tokens : (piece + 1) * tokens].T
        span = pl.ds(start, pieces * HEAD_DIM)
        copy = pltpu.make_async_copy(result_ref.at[:, span], out_ref.at[:, span], sems.at[len(copies)])
        copy.start()
        copies.append(copy)

    walk(blocks_of(weights_ref), first, second)
    for copy in copies:
        copy.wait()


def per_device(
    count,
    queries,
    stretch_keys,
    stretch_values,
    cache_keys,
    cache_values,
    prefix_length,
    page_targets,
    pool_keys,
    pool_values,
    decode_queries,
    page_lists,
    context_length,
):
    own = lax.axis_index("ctx")
    own_array = jnp.full((1,), own, jnp.int32)
    tokens, width = queries.shape
    kv_width = stretch_keys.shape[1]
    kv_local = kv_width // HEAD_DIM
    rows = GROUP * tokens
    heads = kv_local * GROUP
    dec_rows = decode_queries.shape[0]
    c_rows = cache_keys.shape[0]
    pool = pool_keys.shape[0]
    f32, bf16 = jnp.float32, jnp.bfloat16
    shape = jax.ShapeDtypeStruct
    params = pltpu.CompilerParams(vmem_limit_bytes=VMEM_BYTES)
    up_pairs = [(i, (i + 1) % count) for i in range(count)]
    down_pairs = [(i, (i - 1) % count) for i in range(count)]
    hops = []
    for far in range(1, count // 2 + 1):
        hops += [-far, far] if far <= (count - 1) // 2 else [-far]

    def send(array, hop):
        return lax.ppermute(array, "ctx", up_pairs if hop < 0 else down_pairs)

    def cost(keys):
        pairs = kv_local * rows * keys
        return pl.CostEstimate(
            flops=4 * pairs * HEAD_DIM, bytes_accessed=4 * rows * kv_local * HEAD_DIM, transcendentals=pairs
        )

    half = tokens + c_rows
    low = jnp.array(-jnp.inf, bf16)
    spread, start = [], 0
    for part in (stretch_keys, cache_keys, stretch_values, cache_values):
        end = 2 * half - start - part.shape[0]
        spread.append(lax.pad(part, low, ((start, end, 0), (0, 0, 0))))
        start += part.shape[0]
    shard = {0: functools.reduce(jnp.maximum, spread)}
    shard[-1] = send(shard[0], -1)

    state_shapes = (
        shape((kv_local, 1, rows), f32),
        shape((kv_local, 1, rows), f32),
        shape((kv_local, HEAD_DIM, rows), f32),
    )
    qt, near, far, pick, *state = pl.pallas_call(
        functools.partial(own_kernel, count, hops),
        out_shape=(
            shape((kv_local, HEAD_DIM + tokens, rows), bf16),
            shape((count - 1, tokens, tokens), bf16),
            shape((count - 1, c_rows, tokens), bf16),
            shape((SEND_CAP * PAGE, tokens), bf16),
        )
        + state_shapes,
        in_specs=[SMEM] * 3 + [VMEM] * 2,
        out_specs=(VMEM,) * 7,
        compiler_params=params,
        cost_estimate=cost(tokens + c_rows),
        name="own_shard",
    )(own_array, prefix_length, page_targets, queries, shard[0])

    wide, *dec_state = pl.pallas_call(
        held_kernel,
        out_shape=(
            shape((heads * dec_rows, kv_width), bf16),
            shape((heads, dec_rows, 1), f32),
            shape((heads, dec_rows, 1), f32),
            shape((heads, dec_rows, kv_width), f32),
        ),
        in_specs=[SMEM] * 3 + [VMEM] * 5,
        out_specs=(VMEM,) * 4,
        compiler_params=params,
        cost_estimate=pl.CostEstimate(
            flops=4 * 128 * 2048 * 256, bytes_accessed=4 * pool_keys.size, transcendentals=128 * 2048
        ),
        name="decode_held_pages",
    )(own_array, page_targets, context_length, decode_queries, page_lists, pool_keys, pool_values, shard[0])

    if 1 in hops:
        sent_down, state, dec_state = lax.optimization_barrier((shard[0], state, dec_state))
        shard[1] = send(sent_down, 1)
    shard[-1], state, dec_state = lax.optimization_barrier((shard[-1], state, dec_state))
    for hop in hops[2:-1]:
        shard[hop] = send(shard[hop + 1 if hop < 0 else hop - 1], hop)
    hop = hops[-1]
    nearer = shard[hop + 1 if hop < 0 else hop - 1]
    pieces = pl.pallas_call(
        split_kernel,
        out_shape=(
            shape((c_rows + 2 * SEND_CAP * PAGE, kv_width), bf16),
            shape((2 * tokens, kv_width), bf16),
            shape((c_rows, kv_width), bf16),
        ),
        in_specs=[VMEM] * 2,
        out_specs=(VMEM,) * 3,
        compiler_params=params,
        name="pieces_to_send_on",
    )(pick, nearer)
    last_keys = send(pieces[0], hop)
    if 2 * hop == -count:
        pairs = [(i - 1, i) for i in range(count // 2, count)]
        pairs += [(i, i) for i in range(count // 2 - 1)] + [(count - 1, count // 2 - 1)]
        last_stretch = lax.ppermute(pieces[1], "ctx", pairs)
    else:
        last_stretch = send(pieces[1], hop)
    last_values = send(pieces[2], hop)

    for first in range(len(hops) - 1):
        places = [first]
        state = pl.pallas_call(
            functools.partial(hop_kernel, places),
            out_shape=state_shapes,
            in_specs=[VMEM] * (6 + len(places)),
            out_specs=(VMEM,) * 3,
            compiler_params=params,
            cost_estimate=cost((c_rows + tokens) * len(places)),
            name="whole_shards_" + str(first),
        )(qt, near, far, *state, *[shard[hops[place]] for place in places])

    final = len(hops) - 1
    decoded = pl.pallas_call(
        functools.partial(pages_kernel, count, hops, tokens, pool),
        out_shape=shape(decode_queries.shape, bf16),
        in_specs=[SMEM] * 3 + [VMEM] * (5 + len(hops)),
        out_specs=VMEM,
        compiler_params=params,
        cost_estimate=cost(tokens),
        name="decode_new_pages",
    )(
        own_array, page_targets, context_length, page_lists, *[shard[hop] for hop in hops[:-1]], last_keys,
        wide, *dec_state,
    )

    weights, total, accum = pl.pallas_call(
        functools.partial(score_kernel, final),
        out_shape=(shape((kv_local, c_rows, rows), bf16),) + state_shapes[1:],
        in_specs=[VMEM] * 8,
        out_specs=(VMEM,) * 3,
        compiler_params=params,
        cost_estimate=cost(half),
        name="last_scores",
    )(qt, near, far, *state, last_keys, last_stretch)

    prefill = pl.pallas_call(
        last_kernel,
        out_shape=shape((tokens, width), bf16),
        in_specs=[VMEM] * 4,
        out_specs=HBM,
        scratch_shapes=[
            pltpu.VMEM((tokens, width), bf16),
            pltpu.SemaphoreType.DMA((kv_local * max(GROUP // 2, 1),)),
        ],
        compiler_params=params,
        cost_estimate=cost(c_rows // 2),
        name="last_values",
    )(weights, total, accum, last_values)
    return (prefill, decoded)


def solution(mesh):
    in_specs = (
        P(("groups", "ctx"), "head"),
        P(("groups", "ctx"), "head"),
        P(("groups", "ctx"), "head"),
        P(("groups", "ctx"), "head"),
        P(("groups", "ctx"), "head"),
        P("groups"),
        P("groups"),
        P(("groups", "ctx"), None, "head"),
        P(("groups", "ctx"), None, "head"),
        P(("groups", "ctx"), "head"),
        P(("groups", "ctx"), None),
        P(("groups", "ctx")),
    )
    out_specs = (P(("groups", "ctx"), "head"), P(("groups", "ctx"), "head"))
    return jax.shard_map(
        functools.partial(per_device, mesh.shape["ctx"]),
        mesh=mesh,
        in_specs=in_specs,
        out_specs=out_specs,
        check_vma=False,
    )
```

```python
import functools

import jax
import jax.numpy as jnp
from jax import lax
from jax.experimental import pallas as pl
from jax.experimental.pallas import tpu as pltpu
from jax.sharding import PartitionSpec as P

HEADS = 64
KV_HEADS = 8
HEAD_DIM = 128
GROUP = HEADS // KV_HEADS
PAGE = 16
P_DEV = 8
SEND_CAP = 2
EXP2_SCALE = HEAD_DIM ** (-0.5) * 1.4426950408889634
HIDDEN = -1e30
VMEM_BYTES = 48 * 1024 * 1024

VMEM = pl.BlockSpec(memory_space=pltpu.VMEM)
SMEM = pl.BlockSpec(memory_space=pltpu.SMEM)
HBM = pl.BlockSpec(memory_space=pltpu.HBM)


def scores_of(qt_ref, head, cols, keys):
    return jnp.dot(keys, qt_ref[head, :, cols], preferred_element_type=jnp.float32)


def soften(scores, old):
    high = jnp.max(scores, axis=0, keepdims=True)
    if old is None:
        weights = jnp.exp2((scores - high) * EXP2_SCALE)
        return weights.astype(jnp.bfloat16), high, jnp.sum(weights, axis=0, keepdims=True), None
    old_high, old_total = old
    high = jnp.maximum(high, old_high)
    decay = jnp.exp2((old_high - high) * EXP2_SCALE)
    weights = jnp.exp2((scores - high) * EXP2_SCALE)
    total = old_total * decay + jnp.sum(weights, axis=0, keepdims=True)
    return weights.astype(jnp.bfloat16), high, total, decay


def walk(blocks, first, second):
    ahead = first(blocks[0])
    for place, block in enumerate(blocks):
        current = ahead
        if place + 1 < len(blocks):
            ahead = first(blocks[place + 1])
        second(block, current)


def blocks_of(qt_ref):
    kv_local, _, rows = qt_ref.shape
    width = min(2 * (rows // GROUP), rows)
    return [(head, slice(start, start + width)) for head in range(kv_local) for start in range(0, rows, width)]


def attend(qt_ref, keys, values_t, old, new):
    high_ref, total_ref, accum_ref = new

    def second(block, scores):
        head, cols = block
        before = None if old is None else (old[0][head, :, cols], old[1][head, :, cols])
        weights, high, total, decay = soften(scores, before)
        accum = jnp.dot(values_t[head], weights, preferred_element_type=jnp.float32)
        if old is not None:
            accum = accum + old[2][head, :, cols] * decay
        high_ref[head, :, cols] = high
        total_ref[head, :, cols] = total
        accum_ref[head, :, cols] = accum

    walk(blocks_of(qt_ref), lambda block: scores_of(qt_ref, block[0], block[1], keys[block[0]]), second)


def hidden(seen):
    return jnp.where(seen, jnp.float32(0.0), jnp.float32(HIDDEN)).astype(jnp.bfloat16)


def stretch_mask(shard, own, tokens):
    place = lax.broadcasted_iota(jnp.int32, (tokens, tokens), 0)
    token = lax.broadcasted_iota(jnp.int32, (tokens, tokens), 1)
    return hidden(place - token <= (own - shard) * tokens)


def cache_mask(shard, limit, c_rows, tokens):
    place = lax.broadcasted_iota(jnp.int32, (c_rows, tokens), 0)
    return hidden(place < limit - shard * c_rows)


def slot_row(targets_ref, shard, own, tokens, pool):
    page = lax.broadcasted_iota(jnp.int32, (1, tokens), 1) // PAGE
    slots = jnp.full((1, tokens), -1, jnp.int32)
    for index in range(tokens // PAGE):
        target = targets_ref[shard * (tokens // PAGE) + index]
        slot = jnp.where(lax.div(target, P_DEV) == own, pool + lax.rem(target, P_DEV), -1)
        slots = jnp.where(page == index, slot, slots)
    return slots


def sent_pages(targets_ref, shard, owner, pages):
    one, two = jnp.int32(-1), jnp.int32(-1)
    for index in range(pages):
        hit = lax.div(targets_ref[shard * pages + index], P_DEV) == owner
        two = jnp.where(hit & (one >= 0) & (two < 0), index, two)
        one = jnp.where(hit & (one < 0), index, one)
    return one, two


def sent_slots(targets_ref, shard, owner, pages, pool):
    place = lax.broadcasted_iota(jnp.int32, (1, SEND_CAP * PAGE), 1)
    slots = []
    for index in sent_pages(targets_ref, shard, owner, pages):
        target = targets_ref[shard * pages + jnp.maximum(index, 0)]
        slots.append(jnp.where(index >= 0, pool + lax.rem(target, P_DEV), -1))
    return jnp.where(place < PAGE, slots[0], slots[1])


def length_column(length_ref):
    rows = length_ref.shape[0]
    place = lax.broadcasted_iota(jnp.int32, (rows, 1), 0)
    lengths = jnp.zeros((rows, 1), jnp.int32)
    for row in range(rows):
        lengths = jnp.where(place == row, length_ref[row], lengths)
    return lengths


def tally_of(lists, lengths, slot):
    rows, span = lists.shape
    tokens = slot.shape[1]
    slot = jnp.broadcast_to(slot, (rows, tokens))
    offset = lax.rem(lax.broadcasted_iota(jnp.int32, (rows, tokens), 1), PAGE)
    tally = jnp.zeros((rows, tokens), jnp.float32)
    for entry in range(span):
        hit = (slot == lists[:, entry : entry + 1]) & (offset < lengths - entry * PAGE)
        tally = tally + jnp.where(hit, jnp.float32(1.0), jnp.float32(0.0))
    return tally[None]


def shard_of(own, hop, count):
    return lax.rem(own + hop + count, count)


def wide_queries(q_ref, kv_local):
    heads = q_ref.shape[1] // HEAD_DIM
    queries = q_ref[...].astype(jnp.float32)
    stacked = []
    for head in range(heads):
        piece = queries[:, head * HEAD_DIM : (head + 1) * HEAD_DIM]
        blank = jnp.zeros_like(piece)
        stacked.append(
            jnp.concatenate([piece if kv == head // GROUP else blank for kv in range(kv_local)], axis=1)
        )
    return jnp.concatenate(stacked, axis=0).astype(jnp.bfloat16)


def decode_attend(queries, parts, state):
    done = []
    for keys, values, tally in parts:
        scores = lax.dot_general(
            queries, keys, (((1,), (1,)), ((), ())), preferred_element_type=jnp.float32
        ).reshape(-1, tally.shape[1], tally.shape[2])
        done.append((jnp.where(tally > 0, scores, jnp.float32(HIDDEN)), tally, values))
    highs = [jnp.max(scores, axis=-1, keepdims=True) for scores, _, _ in done]
    if state is not None:
        old_high, old_total, old_mixed = state
        highs.append(old_high)
    high = functools.reduce(jnp.maximum, highs)
    total, mixed = 0.0, 0.0
    if state is not None:
        decay = jnp.exp2((old_high - high) * EXP2_SCALE)
        total = old_total * decay
        mixed = old_mixed * decay
    for scores, tally, values in done:
        weights = jnp.exp2((scores - high) * EXP2_SCALE) * tally
        total = total + jnp.sum(weights, axis=-1, keepdims=True)
        mixed = mixed + jnp.dot(
            weights.reshape(queries.shape[0], -1).astype(jnp.bfloat16),
            values,
            preferred_element_type=jnp.float32,
        ).reshape(high.shape[0], high.shape[1], -1)
    return high, total, mixed


def features(head):
    return slice(head * HEAD_DIM, (head + 1) * HEAD_DIM)


def shard_parts(ref, tokens, c_rows):
    return slice(0, tokens + c_rows), slice(tokens + c_rows, 2 * (tokens + c_rows))


def own_kernel(
    count, hops, own_ref, limit_ref, targets_ref, q_ref, shard_ref,
    qt_ref, near_ref, far_ref, pick_ref, high_ref, total_ref, accum_ref,
):
    kv_local, _, rows = qt_ref.shape
    tokens = q_ref.shape[0]
    c_rows = far_ref.shape[1]
    own = own_ref[0]
    limit = limit_ref[0]
    place = lax.broadcasted_iota(jnp.int32, (tokens, tokens), 0)
    token = lax.broadcasted_iota(jnp.int32, (tokens, tokens), 1)
    pick = jnp.where(place == token, jnp.float32(1.0), jnp.float32(0.0)).astype(jnp.bfloat16)
    for head in range(kv_local):
        for sub in range(GROUP):
            cols = slice(sub * tokens, (sub + 1) * tokens)
            qt_ref[head, :HEAD_DIM, cols] = q_ref[:, features(head * GROUP + sub)].T
            qt_ref[head, HEAD_DIM:, cols] = pick
    for place, hop in enumerate(hops):
        shard = shard_of(own, hop, count)
        near_ref[place] = stretch_mask(shard, own, tokens)
        far_ref[place] = cache_mask(shard, limit, c_rows, tokens)
    onward = 1 if hops[-1] < 0 else -1
    pages = tokens // PAGE
    one, two = sent_pages(
        targets_ref, shard_of(own, hops[-1] + onward, count), shard_of(own, onward, count), pages
    )
    row = lax.broadcasted_iota(jnp.int32, pick_ref.shape, 0)
    token = lax.broadcasted_iota(jnp.int32, pick_ref.shape, 1)
    sent = ((row < PAGE) & (one >= 0) & (token == row + one * PAGE)) | (
        (row >= PAGE) & (two >= 0) & (token == row + (two - 1) * PAGE)
    )
    pick_ref[...] = jnp.where(sent, jnp.float32(1.0), jnp.float32(0.0)).astype(jnp.bfloat16)
    mask = jnp.concatenate([stretch_mask(own, own, tokens), cache_mask(own, limit, c_rows, tokens)], axis=0)
    key_rows, value_rows = shard_parts(shard_ref, tokens, c_rows)
    keys = [jnp.concatenate([shard_ref[key_rows, features(head)], mask], axis=1) for head in range(kv_local)]
    values_t = [shard_ref[value_rows, features(head)].T for head in range(kv_local)]
    attend(qt_ref, keys, values_t, None, (high_ref, total_ref, accum_ref))


def held_kernel(
    own_ref, targets_ref, length_ref, q_ref, lists_ref, pool_k, pool_v, rest_ref,
    wide_ref, high_ref, total_ref, mixed_ref,
):
    kv_width = rest_ref.shape[1]
    pool = pool_k.shape[0]
    held = pool * PAGE
    tokens = PAGE * P_DEV
    half = rest_ref.shape[0] // 2
    own = own_ref[0]
    lists = lists_ref[...]
    lengths = length_column(length_ref)
    wide_ref[...] = wide_queries(q_ref, kv_width // HEAD_DIM)
    held_slot = lax.broadcasted_iota(jnp.int32, (1, held), 1) // PAGE
    own_slot = slot_row(targets_ref, own, own, tokens, pool)
    parts = [
        (
            pool_k[...].reshape(held, kv_width),
            pool_v[...].reshape(held, kv_width),
            tally_of(lists, lengths, held_slot),
        ),
        (rest_ref[:tokens], rest_ref[half : half + tokens], tally_of(lists, lengths, own_slot)),
    ]
    high_ref[...], total_ref[...], mixed_ref[...] = decode_attend(wide_ref[...], parts, None)


def hop_kernel(places, qt_ref, near_ref, far_ref, high_in, total_in, accum_in, *refs):
    shard_refs, outs = refs[: len(places)], refs[len(places) :]
    tokens, c_rows = near_ref.shape[1], far_ref.shape[1]
    mask = jnp.concatenate([ref[place] for place in places for ref in (near_ref, far_ref)], axis=0)
    keys, values_t = [], []
    for head in range(qt_ref.shape[0]):
        pieces, values = [], []
        for ref in shard_refs:
            key_rows, value_rows = shard_parts(ref, tokens, c_rows)
            pieces.append(ref[key_rows, features(head)])
            values.append(ref[value_rows, features(head)])
        keys.append(jnp.concatenate([jnp.concatenate(pieces, axis=0), mask], axis=1))
        values_t.append(jnp.concatenate(values, axis=0).T)
    attend(qt_ref, keys, values_t, (high_in, total_in, accum_in), outs)


def split_kernel(pick_ref, shard_ref, keys_ref, stretch_ref, values_ref, pages_ref):
    tokens = pick_ref.shape[1]
    half = shard_ref.shape[0] // 2
    sent = pick_ref.shape[0]
    for place, start in enumerate((0, half)):
        stretch_ref[place * tokens : (place + 1) * tokens] = shard_ref[start : start + tokens]
        rows = jnp.dot(pick_ref[...], shard_ref[start : start + tokens], preferred_element_type=jnp.float32)
        pages_ref[place * sent : (place + 1) * sent] = rows.astype(jnp.bfloat16)
    keys_ref[...] = shard_ref[tokens:half]
    values_ref[...] = shard_ref[half + tokens :]


def pages_kernel(count, hops, tokens, pool, own_ref, targets_ref, length_ref, lists_ref, *refs):
    shard_refs, refs = refs[: len(hops) + 1], refs[len(hops) + 1 :]
    wide_ref, dec_high, dec_total, dec_mixed, dec_out = refs
    own = own_ref[0]
    pages = tokens // PAGE
    lists = lists_ref[...]
    lengths = length_column(length_ref)
    parts = []
    for hop, ref in zip(hops[:-1], shard_refs):
        half = ref.shape[0] // 2
        slot = slot_row(targets_ref, shard_of(own, hop, count), own, tokens, pool)
        parts.append((ref[:tokens], ref[half : half + tokens], tally_of(lists, lengths, slot)))
    stretch_ref, pages_ref = shard_refs[-2:]
    shard = shard_of(own, hops[-1], count)
    attended = shard < own
    slot = jnp.where(attended, slot_row(targets_ref, shard, own, tokens, pool), -1)
    parts.append((stretch_ref[:tokens], stretch_ref[tokens:], tally_of(lists, lengths, slot)))
    sent = pages_ref.shape[0] // 2
    slot = jnp.where(attended, -1, sent_slots(targets_ref, shard, own, pages, pool))
    parts.append((pages_ref[:sent], pages_ref[sent:], tally_of(lists, lengths, slot)))
    _, total, mixed = decode_attend(wide_ref[...], parts, (dec_high[...], dec_total[...], dec_mixed[...]))
    for head in range(dec_high.shape[0]):
        piece = mixed[head, :, features(head // GROUP)] / total[head]
        dec_out[:, features(head)] = piece.astype(jnp.bfloat16)


def score_kernel(
    final, qt_ref, near_ref, far_ref, high_in, total_in, accum_in, keys_ref, stretch_ref,
    weights_ref, total_ref, accum_ref,
):
    kv_local = qt_ref.shape[0]
    tokens, c_rows = near_ref.shape[1], far_ref.shape[1]
    mask = jnp.concatenate([near_ref[final], far_ref[final]], axis=0)
    keys, values_t = [], []
    for head in range(kv_local):
        pieces = [stretch_ref[:tokens, features(head)], keys_ref[:, features(head)]]
        keys.append(jnp.concatenate([jnp.concatenate(pieces, axis=0), mask], axis=1))
        values_t.append(stretch_ref[tokens:, features(head)].T)

    def second(block, scores):
        head, cols = block
        before = (high_in[head, :, cols], total_in[head, :, cols])
        weights, _, total, decay = soften(scores, before)
        weights_ref[head, :, cols] = weights[tokens:]
        total_ref[head, :, cols] = total
        accum_ref[head, :, cols] = accum_in[head, :, cols] * decay + jnp.dot(
            values_t[head], weights[:tokens], preferred_element_type=jnp.float32
        )

    walk(blocks_of(qt_ref), lambda block: scores_of(qt_ref, block[0], block[1], keys[block[0]]), second)


def last_kernel(weights_ref, total_ref, accum_ref, values_ref, out_ref, result_ref, sems):
    tokens = result_ref.shape[0]
    values_t = [values_ref[:, features(head)].T for head in range(weights_ref.shape[0])]
    copies = []

    def first(block):
        head, cols = block
        return jnp.dot(values_t[head], weights_ref[head, :, cols], preferred_element_type=jnp.float32)

    def second(block, mixed):
        head, cols = block
        mixed = mixed + accum_ref[head, :, cols]
        mixed = (mixed * (1.0 / total_ref[head, :, cols])).astype(jnp.bfloat16)
        start = (head * GROUP + cols.start // tokens) * HEAD_DIM
        pieces = (cols.stop - cols.start) // tokens
        for piece in range(pieces):
            col = start + piece * HEAD_DIM
            result_ref[:, col : col + HEAD_DIM] = mixed[:, piece * tokens : (piece + 1) * tokens].T
        span = pl.ds(start, pieces * HEAD_DIM)
        copy = pltpu.make_async_copy(result_ref.at[:, span], out_ref.at[:, span], sems.at[len(copies)])
        copy.start()
        copies.append(copy)

    walk(blocks_of(weights_ref), first, second)
    for copy in copies:
        copy.wait()


def per_device(
    count,
    queries,
    stretch_keys,
    stretch_values,
    cache_keys,
    cache_values,
    prefix_length,
    page_targets,
    pool_keys,
    pool_values,
    decode_queries,
    page_lists,
    context_length,
):
    own = lax.axis_index("ctx")
    own_array = jnp.full((1,), own, jnp.int32)
    tokens, width = queries.shape
    kv_width = stretch_keys.shape[1]
    kv_local = kv_width // HEAD_DIM
    rows = GROUP * tokens
    heads = kv_local * GROUP
    dec_rows = decode_queries.shape[0]
    c_rows = cache_keys.shape[0]
    pool = pool_keys.shape[0]
    f32, bf16 = jnp.float32, jnp.bfloat16
    shape = jax.ShapeDtypeStruct
    params = pltpu.CompilerParams(vmem_limit_bytes=VMEM_BYTES)
    up_pairs = [(i, (i + 1) % count) for i in range(count)]
    down_pairs = [(i, (i - 1) % count) for i in range(count)]
    hops = []
    for far in range(1, count // 2 + 1):
        hops += [-far, far] if far <= (count - 1) // 2 else [-far]

    def send(array, hop):
        return lax.ppermute(array, "ctx", up_pairs if hop < 0 else down_pairs)

    def cost(keys):
        pairs = kv_local * rows * keys
        return pl.CostEstimate(
            flops=4 * pairs * HEAD_DIM, bytes_accessed=4 * rows * kv_local * HEAD_DIM, transcendentals=pairs
        )

    half = tokens + c_rows
    low = jnp.array(-jnp.inf, bf16)
    spread, start = [], 0
    for part in (stretch_keys, cache_keys, stretch_values, cache_values):
        end = 2 * half - start - part.shape[0]
        spread.append(lax.pad(part, low, ((start, end, 0), (0, 0, 0))))
        start += part.shape[0]
    shard = {0: functools.reduce(jnp.maximum, spread)}
    shard[-1] = send(shard[0], -1)

    state_shapes = (
        shape((kv_local, 1, rows), f32),
        shape((kv_local, 1, rows), f32),
        shape((kv_local, HEAD_DIM, rows), f32),
    )
    qt, near, far, pick, *state = pl.pallas_call(
        functools.partial(own_kernel, count, hops),
        out_shape=(
            shape((kv_local, HEAD_DIM + tokens, rows), bf16),
            shape((count - 1, tokens, tokens), bf16),
            shape((count - 1, c_rows, tokens), bf16),
            shape((SEND_CAP * PAGE, tokens), bf16),
        )
        + state_shapes,
        in_specs=[SMEM] * 3 + [VMEM] * 2,
        out_specs=(VMEM,) * 7,
        compiler_params=params,
        cost_estimate=cost(tokens + c_rows),
        name="own_shard",
    )(own_array, prefix_length, page_targets, queries, shard[0])

    wide, *dec_state = pl.pallas_call(
        held_kernel,
        out_shape=(
            shape((heads * dec_rows, kv_width), bf16),
            shape((heads, dec_rows, 1), f32),
            shape((heads, dec_rows, 1), f32),
            shape((heads, dec_rows, kv_width), f32),
        ),
        in_specs=[SMEM] * 3 + [VMEM] * 5,
        out_specs=(VMEM,) * 4,
        compiler_params=params,
        cost_estimate=pl.CostEstimate(
            flops=4 * 128 * 2048 * 256, bytes_accessed=4 * pool_keys.size, transcendentals=128 * 2048
        ),
        name="decode_held_pages",
    )(own_array, page_targets, context_length, decode_queries, page_lists, pool_keys, pool_values, shard[0])

    if 1 in hops:
        sent_down, state, dec_state = lax.optimization_barrier((shard[0], state, dec_state))
        shard[1] = send(sent_down, 1)
    shard[-1], state, dec_state = lax.optimization_barrier((shard[-1], state, dec_state))
    for hop in hops[2:-1]:
        shard[hop] = send(shard[hop + 1 if hop < 0 else hop - 1], hop)
    hop = hops[-1]
    nearer = shard[hop + 1 if hop < 0 else hop - 1]
    pieces = pl.pallas_call(
        split_kernel,
        out_shape=(
            shape((c_rows, kv_width), bf16),
            shape((2 * tokens, kv_width), bf16),
            shape((c_rows, kv_width), bf16),
            shape((2 * SEND_CAP * PAGE, kv_width), bf16),
        ),
        in_specs=[VMEM] * 2,
        out_specs=(VMEM,) * 4,
        compiler_params=params,
        name="pieces_to_send_on",
    )(pick, nearer)
    last_keys = send(pieces[0], hop)
    attending, others = [], []
    for pair in up_pairs if hop < 0 else down_pairs:
        (attending if (pair[1] + hop) % count < pair[1] else others).append(pair)
    last_stretch = lax.ppermute(pieces[1], "ctx", attending)
    last_pages = lax.ppermute(pieces[3], "ctx", others)
    last_values = send(pieces[2], hop)

    for first in range(len(hops) - 1):
        places = [first]
        state = pl.pallas_call(
            functools.partial(hop_kernel, places),
            out_shape=state_shapes,
            in_specs=[VMEM] * (6 + len(places)),
            out_specs=(VMEM,) * 3,
            compiler_params=params,
            cost_estimate=cost((c_rows + tokens) * len(places)),
            name="whole_shards_" + str(first),
        )(qt, near, far, *state, *[shard[hops[place]] for place in places])

    final = len(hops) - 1
    decoded = pl.pallas_call(
        functools.partial(pages_kernel, count, hops, tokens, pool),
        out_shape=shape(decode_queries.shape, bf16),
        in_specs=[SMEM] * 3 + [VMEM] * (6 + len(hops)),
        out_specs=VMEM,
        compiler_params=params,
        cost_estimate=cost(tokens),
        name="decode_new_pages",
    )(
        own_array, page_targets, context_length, page_lists, *[shard[hop] for hop in hops[:-1]], last_stretch, last_pages,
        wide, *dec_state,
    )

    decoded, state = lax.optimization_barrier((decoded, state))
    weights, total, accum = pl.pallas_call(
        functools.partial(score_kernel, final),
        out_shape=(shape((kv_local, c_rows, rows), bf16),) + state_shapes[1:],
        in_specs=[VMEM] * 8,
        out_specs=(VMEM,) * 3,
        compiler_params=params,
        cost_estimate=cost(half),
        name="last_scores",
    )(qt, near, far, *state, last_keys, last_stretch)

    prefill = pl.pallas_call(
        last_kernel,
        out_shape=shape((tokens, width), bf16),
        in_specs=[VMEM] * 4,
        out_specs=HBM,
        scratch_shapes=[
            pltpu.VMEM((tokens, width), bf16),
            pltpu.SemaphoreType.DMA((kv_local * max(GROUP // 2, 1),)),
        ],
        compiler_params=params,
        cost_estimate=cost(c_rows // 2),
        name="last_values",
    )(weights, total, accum, last_values)
    return (prefill, decoded)


def solution(mesh):
    in_specs = (
        P(("groups", "ctx"), "head"),
        P(("groups", "ctx"), "head"),
        P(("groups", "ctx"), "head"),
        P(("groups", "ctx"), "head"),
        P(("groups", "ctx"), "head"),
        P("groups"),
        P("groups"),
        P(("groups", "ctx"), None, "head"),
        P(("groups", "ctx"), None, "head"),
        P(("groups", "ctx"), "head"),
        P(("groups", "ctx"), None),
        P(("groups", "ctx")),
    )
    out_specs = (P(("groups", "ctx"), "head"), P(("groups", "ctx"), "head"))
    return jax.shard_map(
        functools.partial(per_device, mesh.shape["ctx"]),
        mesh=mesh,
        in_specs=in_specs,
        out_specs=out_specs,
        check_vma=False,
    )
```

```python
import functools

import jax
import jax.numpy as jnp
from jax import lax
from jax.experimental import pallas as pl
from jax.experimental.pallas import tpu as pltpu
from jax.sharding import PartitionSpec as P

HEADS = 64
KV_HEADS = 8
HEAD_DIM = 128
GROUP = HEADS // KV_HEADS
PAGE = 16
P_DEV = 8
SEND_CAP = 2
EXP2_SCALE = HEAD_DIM ** (-0.5) * 1.4426950408889634
HIDDEN = -1e30
VMEM_BYTES = 48 * 1024 * 1024

VMEM = pl.BlockSpec(memory_space=pltpu.VMEM)
SMEM = pl.BlockSpec(memory_space=pltpu.SMEM)
HBM = pl.BlockSpec(memory_space=pltpu.HBM)


def scores_of(qt_ref, head, cols, keys):
    return jnp.dot(keys, qt_ref[head, :, cols], preferred_element_type=jnp.float32)


def soften(scores, old):
    high = jnp.max(scores, axis=0, keepdims=True)
    if old is None:
        weights = jnp.exp2((scores - high) * EXP2_SCALE)
        return weights.astype(jnp.bfloat16), high, jnp.sum(weights, axis=0, keepdims=True), None
    old_high, old_total = old
    high = jnp.maximum(high, old_high)
    decay = jnp.exp2((old_high - high) * EXP2_SCALE)
    weights = jnp.exp2((scores - high) * EXP2_SCALE)
    total = old_total * decay + jnp.sum(weights, axis=0, keepdims=True)
    return weights.astype(jnp.bfloat16), high, total, decay


def walk(blocks, first, second):
    ahead = first(blocks[0])
    for place, block in enumerate(blocks):
        current = ahead
        if place + 1 < len(blocks):
            ahead = first(blocks[place + 1])
        second(block, current)


def blocks_of(qt_ref):
    kv_local, _, rows = qt_ref.shape
    width = min(2 * (rows // GROUP), rows)
    return [(head, slice(start, start + width)) for head in range(kv_local) for start in range(0, rows, width)]


def attend(qt_ref, keys, values_t, old, new):
    high_ref, total_ref, accum_ref = new

    def second(block, scores):
        head, cols = block
        before = None if old is None else (old[0][head, :, cols], old[1][head, :, cols])
        weights, high, total, decay = soften(scores, before)
        accum = jnp.dot(values_t[head], weights, preferred_element_type=jnp.float32)
        if old is not None:
            accum = accum + old[2][head, :, cols] * decay
        high_ref[head, :, cols] = high
        total_ref[head, :, cols] = total
        accum_ref[head, :, cols] = accum

    walk(blocks_of(qt_ref), lambda block: scores_of(qt_ref, block[0], block[1], keys[block[0]]), second)


def hidden(seen):
    return jnp.where(seen, jnp.float32(0.0), jnp.float32(HIDDEN)).astype(jnp.bfloat16)


def stretch_mask(shard, own, tokens):
    place = lax.broadcasted_iota(jnp.int32, (tokens, tokens), 0)
    token = lax.broadcasted_iota(jnp.int32, (tokens, tokens), 1)
    return hidden(place - token <= (own - shard) * tokens)


def cache_mask(shard, limit, c_rows, tokens):
    place = lax.broadcasted_iota(jnp.int32, (c_rows, tokens), 0)
    return hidden(place < limit - shard * c_rows)


def entries_of(count):
    entries = [(kind, hop) for hop in range(1, count - 2) for kind in "ud"]
    return entries + [("f", count - 2), ("x", count - 1)]


def source_of(entry, own, count):
    kind, hop = entry
    nothing = 2 * count
    below, above = own - hop, own + hop
    if kind == "u":
        return jnp.where(below >= 0, below, nothing)
    if kind == "d":
        return jnp.where(above < count, above, nothing)
    return jnp.where(below >= 0, below, jnp.where(above < count, above, nothing))


def sent_pages(targets_ref, shard, owner, pages):
    one, two = jnp.int32(-1), jnp.int32(-1)
    for index in range(pages):
        hit = lax.div(targets_ref[shard * pages + index], P_DEV) == owner
        two = jnp.where(hit & (one >= 0) & (two < 0), index, two)
        one = jnp.where(hit & (one < 0), index, one)
    return one, two


def shard_slots(targets_ref, shard, own, count, pages, pool):
    first = jnp.minimum(shard, count - 1) * pages
    slots = []
    for index in range(pages):
        target = targets_ref[first + index]
        mine = (shard < count) & (lax.div(target, P_DEV) == own)
        slots.append(jnp.where(mine, pool + lax.rem(target, P_DEV), -1))
    return slots


def sent_slots(targets_ref, shard, own, count, pages, pool):
    held = jnp.minimum(shard, count - 1)
    slots = []
    for index in sent_pages(targets_ref, held, own, pages):
        target = targets_ref[held * pages + jnp.maximum(index, 0)]
        slots.append(jnp.where((shard < count) & (index >= 0), pool + lax.rem(target, P_DEV), -1))
    return slots


def slot_row(slots):
    page = lax.broadcasted_iota(jnp.int32, (1, len(slots) * PAGE), 1) // PAGE
    row = jnp.full(page.shape, -1, jnp.int32)
    for index, slot in enumerate(slots):
        row = jnp.where(page == index, slot, row)
    return row


def length_column(length_ref):
    rows = length_ref.shape[0]
    place = lax.broadcasted_iota(jnp.int32, (rows, 1), 0)
    lengths = jnp.zeros((rows, 1), jnp.int32)
    for row in range(rows):
        lengths = jnp.where(place == row, length_ref[row], lengths)
    return lengths


def tally_of(lists, lengths, slot):
    rows, span = lists.shape
    tokens = slot.shape[1]
    slot = jnp.broadcast_to(slot, (rows, tokens))
    offset = lax.rem(lax.broadcasted_iota(jnp.int32, (rows, tokens), 1), PAGE)
    tally = jnp.zeros((rows, tokens), jnp.float32)
    for entry in range(span):
        hit = (slot == lists[:, entry : entry + 1]) & (offset < lengths - entry * PAGE)
        tally = tally + jnp.where(hit, jnp.float32(1.0), jnp.float32(0.0))
    return tally[None]


def wide_queries(q_ref, kv_local):
    heads = q_ref.shape[1] // HEAD_DIM
    queries = q_ref[...].astype(jnp.float32)
    stacked = []
    for head in range(heads):
        piece = queries[:, head * HEAD_DIM : (head + 1) * HEAD_DIM]
        blank = jnp.zeros_like(piece)
        stacked.append(
            jnp.concatenate([piece if kv == head // GROUP else blank for kv in range(kv_local)], axis=1)
        )
    return jnp.concatenate(stacked, axis=0).astype(jnp.bfloat16)


def decode_attend(queries, parts, state):
    done = []
    for keys, values, tally in parts:
        scores = lax.dot_general(
            queries, keys, (((1,), (1,)), ((), ())), preferred_element_type=jnp.float32
        ).reshape(-1, tally.shape[1], tally.shape[2])
        done.append((jnp.where(tally > 0, scores, jnp.float32(HIDDEN)), tally, values))
    highs = [jnp.max(scores, axis=-1, keepdims=True) for scores, _, _ in done]
    if state is not None:
        old_high, old_total, old_mixed = state
        highs.append(old_high)
    high = functools.reduce(jnp.maximum, highs)
    total, mixed = 0.0, 0.0
    if state is not None:
        decay = jnp.exp2((old_high - high) * EXP2_SCALE)
        total = old_total * decay
        mixed = old_mixed * decay
    for scores, tally, values in done:
        weights = jnp.exp2((scores - high) * EXP2_SCALE) * tally
        total = total + jnp.sum(weights, axis=-1, keepdims=True)
        mixed = mixed + jnp.dot(
            weights.reshape(queries.shape[0], -1).astype(jnp.bfloat16),
            values,
            preferred_element_type=jnp.float32,
        ).reshape(high.shape[0], high.shape[1], -1)
    return high, total, mixed


def features(head):
    return slice(head * HEAD_DIM, (head + 1) * HEAD_DIM)


def shard_parts(ref, tokens, c_rows):
    return slice(0, tokens + c_rows), slice(tokens + c_rows, 2 * (tokens + c_rows))


def page_kernel(count, own_ref, targets_ref, shard_ref, *outs):
    tokens = P_DEV * PAGE
    half = shard_ref.shape[0] // 2
    c_rows = half - tokens
    own = own_ref[0]
    sent = SEND_CAP * PAGE
    row = lax.broadcasted_iota(jnp.int32, (sent, tokens), 0)
    token = lax.broadcasted_iota(jnp.int32, (sent, tokens), 1)
    for index, out_ref in enumerate(outs):
        hop = index + 1
        one, two = sent_pages(targets_ref, own, own - hop, P_DEV)
        picked = ((row < PAGE) & (one >= 0) & (token == row + one * PAGE)) | (
            (row >= PAGE) & (two >= 0) & (token == row + (two - 1) * PAGE)
        )
        pick = jnp.where(picked, jnp.float32(1.0), jnp.float32(0.0)).astype(jnp.bfloat16)
        first = out_ref.shape[0] - 2 * sent
        if first:
            out_ref[:c_rows] = shard_ref[tokens:half]
            out_ref[c_rows:first] = shard_ref[half + tokens :]
        for place, start in enumerate((0, half)):
            rows = jnp.dot(pick, shard_ref[start : start + tokens], preferred_element_type=jnp.float32)
            out_ref[first + place * sent : first + (place + 1) * sent] = rows.astype(jnp.bfloat16)


def own_kernel(
    count, own_ref, limit_ref, q_ref, shard_ref,
    qt_ref, near_ref, far_ref, high_ref, total_ref, accum_ref,
):
    kv_local, _, rows = qt_ref.shape
    tokens = q_ref.shape[0]
    c_rows = far_ref.shape[1]
    own = own_ref[0]
    limit = limit_ref[0]
    place = lax.broadcasted_iota(jnp.int32, (tokens, tokens), 0)
    token = lax.broadcasted_iota(jnp.int32, (tokens, tokens), 1)
    pick = jnp.where(place == token, jnp.float32(1.0), jnp.float32(0.0)).astype(jnp.bfloat16)
    for head in range(kv_local):
        for sub in range(GROUP):
            cols = slice(sub * tokens, (sub + 1) * tokens)
            qt_ref[head, :HEAD_DIM, cols] = q_ref[:, features(head * GROUP + sub)].T
            qt_ref[head, HEAD_DIM:, cols] = pick
    for index, entry in enumerate(entries_of(count)):
        shard = source_of(entry, own, count)
        near_ref[index] = stretch_mask(shard, own, tokens)
        far_ref[index] = cache_mask(shard, limit, c_rows, tokens)
    mask = jnp.concatenate([stretch_mask(own, own, tokens), cache_mask(own, limit, c_rows, tokens)], axis=0)
    key_rows, value_rows = shard_parts(shard_ref, tokens, c_rows)
    keys = [jnp.concatenate([shard_ref[key_rows, features(head)], mask], axis=1) for head in range(kv_local)]
    values_t = [shard_ref[value_rows, features(head)].T for head in range(kv_local)]
    attend(qt_ref, keys, values_t, None, (high_ref, total_ref, accum_ref))


def held_kernel(
    own_ref, targets_ref, length_ref, q_ref, lists_ref, pool_k, pool_v, rest_ref,
    wide_ref, high_ref, total_ref, mixed_ref,
):
    kv_width = rest_ref.shape[1]
    pool = pool_k.shape[0]
    held = pool * PAGE
    tokens = PAGE * P_DEV
    half = rest_ref.shape[0] // 2
    own = own_ref[0]
    lists = lists_ref[...]
    lengths = length_column(length_ref)
    wide_ref[...] = wide_queries(q_ref, kv_width // HEAD_DIM)
    held_slot = lax.broadcasted_iota(jnp.int32, (1, held), 1) // PAGE
    count = targets_ref.shape[0] // P_DEV
    own_slot = slot_row(shard_slots(targets_ref, own, own, count, P_DEV, pool))
    parts = [
        (
            pool_k[...].reshape(held, kv_width),
            pool_v[...].reshape(held, kv_width),
            tally_of(lists, lengths, held_slot),
        ),
        (rest_ref[:tokens], rest_ref[half : half + tokens], tally_of(lists, lengths, own_slot)),
    ]
    high_ref[...], total_ref[...], mixed_ref[...] = decode_attend(wide_ref[...], parts, None)


def hop_kernel(index, kind, qt_ref, near_ref, far_ref, high_in, total_in, accum_in, ref, *outs):
    tokens, c_rows = near_ref.shape[1], far_ref.shape[1]
    mask = far_ref[index] if kind == "d" else jnp.concatenate([near_ref[index], far_ref[index]], axis=0)
    keys, values_t = [], []
    rows = c_rows if kind == "d" else tokens + c_rows
    for head in range(qt_ref.shape[0]):
        keys.append(jnp.concatenate([ref[:rows, features(head)], mask], axis=1))
        values_t.append(ref[rows : 2 * rows, features(head)].T)
    attend(qt_ref, keys, values_t, (high_in, total_in, accum_in), outs)


def split_kernel(shard_ref, keys_ref, stretch_ref, values_ref):
    c_rows = keys_ref.shape[0]
    tokens = stretch_ref.shape[0] // 2
    half = tokens + c_rows
    for place, start in enumerate((0, half)):
        stretch_ref[place * tokens : (place + 1) * tokens] = shard_ref[start : start + tokens]
    keys_ref[...] = shard_ref[tokens:half]
    values_ref[...] = shard_ref[half + tokens :]


def pages_kernel(count, pool, own_ref, targets_ref, length_ref, lists_ref, *refs):
    whole_refs, refs = refs[: count - 2], refs[count - 2 :]
    last_ref, refs = refs[0], refs[1:]
    page_refs, refs = refs[: count - 2], refs[count - 2 :]
    wide_ref, dec_high, dec_total, dec_mixed, dec_out = refs
    tokens = P_DEV * PAGE
    own = own_ref[0]
    lists = lists_ref[...]
    lengths = length_column(length_ref)
    whole = [("u", hop) for hop in range(1, count - 2)] + [("x", count - 1), ("u", count - 2)]
    keys, values, slots = [], [], []
    for entry, ref in zip(whole, (*whole_refs, last_ref)):
        half = ref.shape[0] // 2
        keys.append(ref[:tokens])
        values.append(ref[half : half + tokens])
        shard = source_of(entry, own, count)
        slots += shard_slots(targets_ref, shard, own, count, P_DEV, pool)
    parts = [(keys, values, slots)]
    keys, values, slots = [], [], []
    sent = SEND_CAP * PAGE
    for hop, ref in enumerate(page_refs, 1):
        first = ref.shape[0] - 2 * sent
        keys.append(ref[first : first + sent])
        values.append(ref[first + sent :])
        shard = source_of(("d", hop), own, count)
        slots += sent_slots(targets_ref, shard, own, count, P_DEV, pool)
    parts.append((keys, values, slots))
    parts = [
        (
            jnp.concatenate(keys, axis=0),
            jnp.concatenate(values, axis=0),
            tally_of(lists, lengths, slot_row(slots)),
        )
        for keys, values, slots in parts
    ]
    _, total, mixed = decode_attend(wide_ref[...], parts, (dec_high[...], dec_total[...], dec_mixed[...]))
    for head in range(dec_high.shape[0]):
        piece = mixed[head, :, features(head // GROUP)] / total[head]
        dec_out[:, features(head)] = piece.astype(jnp.bfloat16)


def score_kernel(
    index, qt_ref, near_ref, far_ref, high_in, total_in, accum_in, keys_ref, stretch_ref, down_ref,
    weights_ref, total_ref, accum_ref,
):
    kv_local = qt_ref.shape[0]
    tokens, c_rows = near_ref.shape[1], far_ref.shape[1]
    mask = jnp.concatenate([near_ref[index], far_ref[index]], axis=0)
    keys, values_t = [], []
    for head in range(kv_local):
        cached = keys_ref[:, features(head)] + down_ref[:c_rows, features(head)]
        pieces = jnp.concatenate([stretch_ref[:tokens, features(head)], cached], axis=0)
        keys.append(jnp.concatenate([pieces, mask], axis=1))
        values_t.append(stretch_ref[tokens:, features(head)].T)

    def second(block, scores):
        head, cols = block
        before = (high_in[head, :, cols], total_in[head, :, cols])
        weights, _, total, decay = soften(scores, before)
        weights_ref[head, :, cols] = weights[tokens:]
        total_ref[head, :, cols] = total
        accum_ref[head, :, cols] = accum_in[head, :, cols] * decay + jnp.dot(
            values_t[head], weights[:tokens], preferred_element_type=jnp.float32
        )

    walk(blocks_of(qt_ref), lambda block: scores_of(qt_ref, block[0], block[1], keys[block[0]]), second)


def last_kernel(weights_ref, total_ref, accum_ref, values_ref, down_ref, out_ref, result_ref, sems):
    tokens = result_ref.shape[0]
    c_rows = values_ref.shape[0]
    values_t = [
        (values_ref[:, features(head)] + down_ref[c_rows : 2 * c_rows, features(head)]).T
        for head in range(weights_ref.shape[0])
    ]
    copies = []

    def first(block):
        head, cols = block
        return jnp.dot(values_t[head], weights_ref[head, :, cols], preferred_element_type=jnp.float32)

    def second(block, mixed):
        head, cols = block
        mixed = mixed + accum_ref[head, :, cols]
        mixed = (mixed * (1.0 / total_ref[head, :, cols])).astype(jnp.bfloat16)
        start = (head * GROUP + cols.start // tokens) * HEAD_DIM
        pieces = (cols.stop - cols.start) // tokens
        for piece in range(pieces):
            col = start + piece * HEAD_DIM
            result_ref[:, col : col + HEAD_DIM] = mixed[:, piece * tokens : (piece + 1) * tokens].T
        span = pl.ds(start, pieces * HEAD_DIM)
        copy = pltpu.make_async_copy(result_ref.at[:, span], out_ref.at[:, span], sems.at[len(copies)])
        copy.start()
        copies.append(copy)

    walk(blocks_of(weights_ref), first, second)
    for copy in copies:
        copy.wait()


def per_device(
    count,
    queries,
    stretch_keys,
    stretch_values,
    cache_keys,
    cache_values,
    prefix_length,
    page_targets,
    pool_keys,
    pool_values,
    decode_queries,
    page_lists,
    context_length,
):
    own = lax.axis_index("ctx")
    own_array = jnp.full((1,), own, jnp.int32)
    tokens, width = queries.shape
    kv_width = stretch_keys.shape[1]
    kv_local = kv_width // HEAD_DIM
    rows = GROUP * tokens
    heads = kv_local * GROUP
    dec_rows = decode_queries.shape[0]
    c_rows = cache_keys.shape[0]
    pool = pool_keys.shape[0]
    f32, bf16 = jnp.float32, jnp.bfloat16
    shape = jax.ShapeDtypeStruct
    params = pltpu.CompilerParams(vmem_limit_bytes=VMEM_BYTES)
    half = tokens + c_rows
    page_rows = 2 * SEND_CAP * PAGE
    entries = entries_of(count)
    final = count - 2

    def send(array, pairs):
        return lax.ppermute(array, "ctx", pairs)

    def rising(hop):
        return [(i, i + 1) for i in range(hop - 1, count - 1)]

    def falling(hop):
        return [(i, i - 1) for i in range(1, count - hop + 1)]

    def cost(keys):
        pairs = kv_local * rows * keys
        return pl.CostEstimate(
            flops=4 * pairs * HEAD_DIM, bytes_accessed=4 * rows * kv_local * HEAD_DIM, transcendentals=pairs
        )

    low = jnp.array(-jnp.inf, bf16)
    spread, start = [], 0
    for part in (stretch_keys, cache_keys, stretch_values, cache_values):
        end = 2 * half - start - part.shape[0]
        spread.append(lax.pad(part, low, ((start, end, 0), (0, 0, 0))))
        start += part.shape[0]
    shard = functools.reduce(jnp.maximum, spread)
    ups = {1: send(shard, rising(1))}

    wide_rows = 2 * c_rows + page_rows
    going = pl.pallas_call(
        functools.partial(page_kernel, count),
        out_shape=tuple(
            shape((wide_rows if hop == 1 else page_rows, kv_width), bf16) for hop in range(1, count - 1)
        ),
        in_specs=[SMEM] * 2 + [VMEM],
        out_specs=(VMEM,) * (count - 2),
        compiler_params=params,
        name="pages_to_send_down",
    )(own_array, page_targets, shard)
    downs = {1: send(going[0], falling(1))}
    pages = {
        hop: send(going[hop - 1], [(i, i - hop) for i in range(hop, count)]) for hop in range(2, count - 1)
    }

    state_shapes = (
        shape((kv_local, 1, rows), f32),
        shape((kv_local, 1, rows), f32),
        shape((kv_local, HEAD_DIM, rows), f32),
    )
    qt, near, far, *state = pl.pallas_call(
        functools.partial(own_kernel, count),
        out_shape=(
            shape((kv_local, HEAD_DIM + tokens, rows), bf16),
            shape((len(entries), tokens, tokens), bf16),
            shape((len(entries), c_rows, tokens), bf16),
        )
        + state_shapes,
        in_specs=[SMEM] * 2 + [VMEM] * 2,
        out_specs=(VMEM,) * 6,
        compiler_params=params,
        cost_estimate=cost(tokens + c_rows),
        name="own_shard",
    )(own_array, prefix_length, queries, shard)

    wide, *dec_state = pl.pallas_call(
        held_kernel,
        out_shape=(
            shape((heads * dec_rows, kv_width), bf16),
            shape((heads, dec_rows, 1), f32),
            shape((heads, dec_rows, 1), f32),
            shape((heads, dec_rows, kv_width), f32),
        ),
        in_specs=[SMEM] * 3 + [VMEM] * 5,
        out_specs=(VMEM,) * 4,
        compiler_params=params,
        cost_estimate=pl.CostEstimate(
            flops=4 * 128 * 2048 * 256, bytes_accessed=4 * pool_keys.size, transcendentals=128 * 2048
        ),
        name="decode_held_pages",
    )(own_array, page_targets, context_length, decode_queries, page_lists, pool_keys, pool_values, shard)

    pages, state, dec_state = lax.optimization_barrier((pages, state, dec_state))
    later, state, dec_state = lax.optimization_barrier((shard, state, dec_state))
    across = send(later, [(0, count - 1), (count - 1, 0)])
    ups[1], state = lax.optimization_barrier((ups[1], state))
    pages[1] = downs[1]
    for hop in range(2, final):
        ups[hop] = send(ups[hop - 1], rising(hop))
        downs[hop] = send(downs[hop - 1][: 2 * c_rows], falling(hop))

    pieces = pl.pallas_call(
        split_kernel,
        out_shape=(
            shape((c_rows, kv_width), bf16),
            shape((2 * tokens, kv_width), bf16),
            shape((c_rows, kv_width), bf16),
        ),
        in_specs=[VMEM],
        out_specs=(VMEM,) * 3,
        compiler_params=params,
        name="pieces_to_send_on",
    )(ups[final - 1])
    pieces, downs[final - 1] = lax.optimization_barrier((pieces, downs[final - 1]))
    last_keys, last_stretch, last_values = [send(piece, rising(final)) for piece in pieces]
    last_down = send(downs[final - 1][: 2 * c_rows], falling(final))

    for index, entry in enumerate(entries):
        kind, hop = entry
        if kind == "f":
            continue
        received = {"u": ups.get(hop), "d": downs.get(hop), "x": across}[kind]
        state = pl.pallas_call(
            functools.partial(hop_kernel, index, kind),
            out_shape=state_shapes,
            in_specs=[VMEM] * 7,
            out_specs=(VMEM,) * 3,
            compiler_params=params,
            cost_estimate=cost(c_rows if kind == "d" else half),
            name="entry_" + kind + str(hop),
        )(qt, near, far, *state, received)

    decoded = pl.pallas_call(
        functools.partial(pages_kernel, count, pool),
        out_shape=shape(decode_queries.shape, bf16),
        in_specs=[SMEM] * 3 + [VMEM] * (5 + (count - 1) + (count - 2)),
        out_specs=VMEM,
        compiler_params=params,
        cost_estimate=cost(tokens),
        name="decode_new_pages",
    )(
        own_array, page_targets, context_length, page_lists,
        *[ups[hop] for hop in range(1, final)], across, last_stretch,
        *[pages[hop] for hop in range(1, count - 1)],
        wide, *dec_state,
    )

    decoded, state = lax.optimization_barrier((decoded, state))
    weights, total, accum = pl.pallas_call(
        functools.partial(score_kernel, len(entries) - 2),
        out_shape=(shape((kv_local, c_rows, rows), bf16),) + state_shapes[1:],
        in_specs=[VMEM] * 9,
        out_specs=(VMEM,) * 3,
        compiler_params=params,
        cost_estimate=cost(half),
        name="last_scores",
    )(qt, near, far, *state, last_keys, last_stretch, last_down)

    prefill = pl.pallas_call(
        last_kernel,
        out_shape=shape((tokens, width), bf16),
        in_specs=[VMEM] * 5,
        out_specs=HBM,
        scratch_shapes=[
            pltpu.VMEM((tokens, width), bf16),
            pltpu.SemaphoreType.DMA((kv_local * max(GROUP // 2, 1),)),
        ],
        compiler_params=params,
        cost_estimate=cost(c_rows // 2),
        name="last_values",
    )(weights, total, accum, last_values, last_down)
    return (prefill, decoded)


def solution(mesh):
    in_specs = (
        P(("groups", "ctx"), "head"),
        P(("groups", "ctx"), "head"),
        P(("groups", "ctx"), "head"),
        P(("groups", "ctx"), "head"),
        P(("groups", "ctx"), "head"),
        P("groups"),
        P("groups"),
        P(("groups", "ctx"), None, "head"),
        P(("groups", "ctx"), None, "head"),
        P(("groups", "ctx"), "head"),
        P(("groups", "ctx"), None),
        P(("groups", "ctx")),
    )
    out_specs = (P(("groups", "ctx"), "head"), P(("groups", "ctx"), "head"))
    return jax.shard_map(
        functools.partial(per_device, mesh.shape["ctx"]),
        mesh=mesh,
        in_specs=in_specs,
        out_specs=out_specs,
        check_vma=False,
    )
```

```python
import functools

import jax
import jax.numpy as jnp
from jax import lax
from jax.experimental import pallas as pl
from jax.experimental.pallas import tpu as pltpu
from jax.sharding import PartitionSpec as P

HEADS = 64
KV_HEADS = 8
HEAD_DIM = 128
GROUP = HEADS // KV_HEADS
PAGE = 16
P_DEV = 8
SEND_CAP = 2
EXP2_SCALE = HEAD_DIM ** (-0.5) * 1.4426950408889634
HIDDEN = -1e30
VMEM_BYTES = 48 * 1024 * 1024

VMEM = pl.BlockSpec(memory_space=pltpu.VMEM)
SMEM = pl.BlockSpec(memory_space=pltpu.SMEM)
HBM = pl.BlockSpec(memory_space=pltpu.HBM)


def scores_of(qt_ref, head, cols, keys):
    return jnp.dot(keys, qt_ref[head, :, cols], preferred_element_type=jnp.float32)


def soften(scores, old):
    high = jnp.max(scores, axis=0, keepdims=True)
    if old is None:
        weights = jnp.exp2((scores - high) * EXP2_SCALE)
        return weights.astype(jnp.bfloat16), high, jnp.sum(weights, axis=0, keepdims=True), None
    old_high, old_total = old
    high = jnp.maximum(high, old_high)
    decay = jnp.exp2((old_high - high) * EXP2_SCALE)
    weights = jnp.exp2((scores - high) * EXP2_SCALE)
    total = old_total * decay + jnp.sum(weights, axis=0, keepdims=True)
    return weights.astype(jnp.bfloat16), high, total, decay


def walk(blocks, first, second):
    ahead = first(blocks[0])
    for place, block in enumerate(blocks):
        current = ahead
        if place + 1 < len(blocks):
            ahead = first(blocks[place + 1])
        second(block, current)


def blocks_of(qt_ref):
    kv_local, _, rows = qt_ref.shape
    width = min(2 * (rows // GROUP), rows)
    return [(head, slice(start, start + width)) for head in range(kv_local) for start in range(0, rows, width)]


def attend(qt_ref, keys, values_t, old, new):
    high_ref, total_ref, accum_ref = new

    def second(block, scores):
        head, cols = block
        before = None if old is None else (old[0][head, :, cols], old[1][head, :, cols])
        weights, high, total, decay = soften(scores, before)
        accum = jnp.dot(values_t[head], weights, preferred_element_type=jnp.float32)
        if old is not None:
            accum = accum + old[2][head, :, cols] * decay
        high_ref[head, :, cols] = high
        total_ref[head, :, cols] = total
        accum_ref[head, :, cols] = accum

    walk(blocks_of(qt_ref), lambda block: scores_of(qt_ref, block[0], block[1], keys[block[0]]), second)


def hidden(seen):
    return jnp.where(seen, jnp.float32(0.0), jnp.float32(HIDDEN)).astype(jnp.bfloat16)


def stretch_mask(shard, own, tokens):
    place = lax.broadcasted_iota(jnp.int32, (tokens, tokens), 0)
    token = lax.broadcasted_iota(jnp.int32, (tokens, tokens), 1)
    return hidden(place - token <= (own - shard) * tokens)


def cache_mask(shard, limit, c_rows, tokens):
    place = lax.broadcasted_iota(jnp.int32, (c_rows, tokens), 0)
    return hidden(place < limit - shard * c_rows)


def slot_row(targets_ref, shard, own, tokens, pool):
    page = lax.broadcasted_iota(jnp.int32, (1, tokens), 1) // PAGE
    slots = jnp.full((1, tokens), -1, jnp.int32)
    for index in range(tokens // PAGE):
        target = targets_ref[shard * (tokens // PAGE) + index]
        slot = jnp.where(lax.div(target, P_DEV) == own, pool + lax.rem(target, P_DEV), -1)
        slots = jnp.where(page == index, slot, slots)
    return slots


def sent_pages(targets_ref, shard, owner, pages):
    one, two = jnp.int32(-1), jnp.int32(-1)
    for index in range(pages):
        hit = lax.div(targets_ref[shard * pages + index], P_DEV) == owner
        two = jnp.where(hit & (one >= 0) & (two < 0), index, two)
        one = jnp.where(hit & (one < 0), index, one)
    return one, two


def sent_slots(targets_ref, shard, owner, pages, pool):
    place = lax.broadcasted_iota(jnp.int32, (1, SEND_CAP * PAGE), 1)
    slots = []
    for index in sent_pages(targets_ref, shard, owner, pages):
        target = targets_ref[shard * pages + jnp.maximum(index, 0)]
        slots.append(jnp.where(index >= 0, pool + lax.rem(target, P_DEV), -1))
    return jnp.where(place < PAGE, slots[0], slots[1])


def length_column(length_ref):
    rows = length_ref.shape[0]
    place = lax.broadcasted_iota(jnp.int32, (rows, 1), 0)
    lengths = jnp.zeros((rows, 1), jnp.int32)
    for row in range(rows):
        lengths = jnp.where(place == row, length_ref[row], lengths)
    return lengths


def tally_of(lists, lengths, slot):
    rows, span = lists.shape
    tokens = slot.shape[1]
    slot = jnp.broadcast_to(slot, (rows, tokens))
    offset = lax.rem(lax.broadcasted_iota(jnp.int32, (rows, tokens), 1), PAGE)
    tally = jnp.zeros((rows, tokens), jnp.float32)
    for entry in range(span):
        hit = (slot == lists[:, entry : entry + 1]) & (offset < lengths - entry * PAGE)
        tally = tally + jnp.where(hit, jnp.float32(1.0), jnp.float32(0.0))
    return tally[None]


def shard_of(own, hop, count):
    return lax.rem(own + hop + count, count)


def wide_queries(q_ref, kv_local):
    heads = q_ref.shape[1] // HEAD_DIM
    queries = q_ref[...].astype(jnp.float32)
    stacked = []
    for head in range(heads):
        piece = queries[:, head * HEAD_DIM : (head + 1) * HEAD_DIM]
        blank = jnp.zeros_like(piece)
        stacked.append(
            jnp.concatenate([piece if kv == head // GROUP else blank for kv in range(kv_local)], axis=1)
        )
    return jnp.concatenate(stacked, axis=0).astype(jnp.bfloat16)


def decode_attend(queries, parts, state):
    done = []
    for keys, values, tally in parts:
        scores = lax.dot_general(
            queries, keys, (((1,), (1,)), ((), ())), preferred_element_type=jnp.float32
        ).reshape(-1, tally.shape[1], tally.shape[2])
        done.append((jnp.where(tally > 0, scores, jnp.float32(HIDDEN)), tally, values))
    highs = [jnp.max(scores, axis=-1, keepdims=True) for scores, _, _ in done]
    if state is not None:
        old_high, old_total, old_mixed = state
        highs.append(old_high)
    high = functools.reduce(jnp.maximum, highs)
    total, mixed = 0.0, 0.0
    if state is not None:
        decay = jnp.exp2((old_high - high) * EXP2_SCALE)
        total = old_total * decay
        mixed = old_mixed * decay
    for scores, tally, values in done:
        weights = jnp.exp2((scores - high) * EXP2_SCALE) * tally
        total = total + jnp.sum(weights, axis=-1, keepdims=True)
        mixed = mixed + jnp.dot(
            weights.reshape(queries.shape[0], -1).astype(jnp.bfloat16),
            values,
            preferred_element_type=jnp.float32,
        ).reshape(high.shape[0], high.shape[1], -1)
    return high, total, mixed


def features(head):
    return slice(head * HEAD_DIM, (head + 1) * HEAD_DIM)


def shard_parts(ref, tokens, c_rows):
    return slice(0, tokens + c_rows), slice(tokens + c_rows, 2 * (tokens + c_rows))


def own_kernel(
    count, hops, own_ref, limit_ref, targets_ref, q_ref, shard_ref,
    qt_ref, near_ref, far_ref, pick_ref, high_ref, total_ref, accum_ref,
):
    kv_local, _, rows = qt_ref.shape
    tokens = q_ref.shape[0]
    c_rows = far_ref.shape[1]
    own = own_ref[0]
    limit = limit_ref[0]
    place = lax.broadcasted_iota(jnp.int32, (tokens, tokens), 0)
    token = lax.broadcasted_iota(jnp.int32, (tokens, tokens), 1)
    pick = jnp.where(place == token, jnp.float32(1.0), jnp.float32(0.0)).astype(jnp.bfloat16)
    for head in range(kv_local):
        for sub in range(GROUP):
            cols = slice(sub * tokens, (sub + 1) * tokens)
            qt_ref[head, :HEAD_DIM, cols] = q_ref[:, features(head * GROUP + sub)].T
            qt_ref[head, HEAD_DIM:, cols] = pick
    for place, hop in enumerate(hops):
        shard = shard_of(own, hop, count)
        near_ref[place] = stretch_mask(shard, own, tokens)
        far_ref[place] = cache_mask(shard, limit, c_rows, tokens)
    onward = 1 if hops[-1] < 0 else -1
    pages = tokens // PAGE
    one, two = sent_pages(
        targets_ref, shard_of(own, hops[-1] + onward, count), shard_of(own, onward, count), pages
    )
    row = lax.broadcasted_iota(jnp.int32, pick_ref.shape, 0)
    token = lax.broadcasted_iota(jnp.int32, pick_ref.shape, 1)
    sent = ((row < PAGE) & (one >= 0) & (token == row + one * PAGE)) | (
        (row >= PAGE) & (two >= 0) & (token == row + (two - 1) * PAGE)
    )
    pick_ref[...] = jnp.where(sent, jnp.float32(1.0), jnp.float32(0.0)).astype(jnp.bfloat16)
    mask = jnp.concatenate([stretch_mask(own, own, tokens), cache_mask(own, limit, c_rows, tokens)], axis=0)
    key_rows, value_rows = shard_parts(shard_ref, tokens, c_rows)
    keys = [jnp.concatenate([shard_ref[key_rows, features(head)], mask], axis=1) for head in range(kv_local)]
    values_t = [shard_ref[value_rows, features(head)].T for head in range(kv_local)]
    attend(qt_ref, keys, values_t, None, (high_ref, total_ref, accum_ref))


def held_kernel(
    own_ref, targets_ref, length_ref, q_ref, lists_ref, pool_k, pool_v, rest_ref,
    wide_ref, high_ref, total_ref, mixed_ref,
):
    kv_width = rest_ref.shape[1]
    pool = pool_k.shape[0]
    held = pool * PAGE
    tokens = PAGE * P_DEV
    half = rest_ref.shape[0] // 2
    own = own_ref[0]
    lists = lists_ref[...]
    lengths = length_column(length_ref)
    wide_ref[...] = wide_queries(q_ref, kv_width // HEAD_DIM)
    held_slot = lax.broadcasted_iota(jnp.int32, (1, held), 1) // PAGE
    own_slot = slot_row(targets_ref, own, own, tokens, pool)
    parts = [
        (
            pool_k[...].reshape(held, kv_width),
            pool_v[...].reshape(held, kv_width),
            tally_of(lists, lengths, held_slot),
        ),
        (rest_ref[:tokens], rest_ref[half : half + tokens], tally_of(lists, lengths, own_slot)),
    ]
    high_ref[...], total_ref[...], mixed_ref[...] = decode_attend(wide_ref[...], parts, None)


def hop_kernel(places, qt_ref, near_ref, far_ref, high_in, total_in, accum_in, *refs):
    shard_refs, outs = refs[: len(places)], refs[len(places) :]
    tokens, c_rows = near_ref.shape[1], far_ref.shape[1]
    mask = jnp.concatenate([ref[place] for place in places for ref in (near_ref, far_ref)], axis=0)
    keys, values_t = [], []
    for head in range(qt_ref.shape[0]):
        pieces, values = [], []
        for ref in shard_refs:
            key_rows, value_rows = shard_parts(ref, tokens, c_rows)
            pieces.append(ref[key_rows, features(head)])
            values.append(ref[value_rows, features(head)])
        keys.append(jnp.concatenate([jnp.concatenate(pieces, axis=0), mask], axis=1))
        values_t.append(jnp.concatenate(values, axis=0).T)
    attend(qt_ref, keys, values_t, (high_in, total_in, accum_in), outs)


def split_kernel(pick_ref, shard_ref, keys_ref, stretch_ref, values_ref, pages_ref):
    tokens = pick_ref.shape[1]
    half = shard_ref.shape[0] // 2
    sent = pick_ref.shape[0]
    for place, start in enumerate((0, half)):
        stretch_ref[place * tokens : (place + 1) * tokens] = shard_ref[start : start + tokens]
        rows = jnp.dot(pick_ref[...], shard_ref[start : start + tokens], preferred_element_type=jnp.float32)
        pages_ref[place * sent : (place + 1) * sent] = rows.astype(jnp.bfloat16)
    keys_ref[...] = shard_ref[tokens:half]
    values_ref[...] = shard_ref[half + tokens :]


def pages_kernel(count, hops, tokens, pool, own_ref, targets_ref, length_ref, lists_ref, *refs):
    shard_refs, refs = refs[: len(hops) + 1], refs[len(hops) + 1 :]
    wide_ref, dec_high, dec_total, dec_mixed, dec_out = refs
    own = own_ref[0]
    pages = tokens // PAGE
    lists = lists_ref[...]
    lengths = length_column(length_ref)
    parts = []
    for hop, ref in zip(hops[:-1], shard_refs):
        half = ref.shape[0] // 2
        slot = slot_row(targets_ref, shard_of(own, hop, count), own, tokens, pool)
        parts.append((ref[:tokens], ref[half : half + tokens], tally_of(lists, lengths, slot)))
    stretch_ref, pages_ref = shard_refs[-2:]
    shard = shard_of(own, hops[-1], count)
    attended = shard < own
    slot = jnp.where(attended, slot_row(targets_ref, shard, own, tokens, pool), -1)
    parts.append((stretch_ref[:tokens], stretch_ref[tokens:], tally_of(lists, lengths, slot)))
    sent = pages_ref.shape[0] // 2
    slot = jnp.where(attended, -1, sent_slots(targets_ref, shard, own, pages, pool))
    parts.append((pages_ref[:sent], pages_ref[sent:], tally_of(lists, lengths, slot)))
    _, total, mixed = decode_attend(wide_ref[...], parts, (dec_high[...], dec_total[...], dec_mixed[...]))
    for head in range(dec_high.shape[0]):
        piece = mixed[head, :, features(head // GROUP)] / total[head]
        dec_out[:, features(head)] = piece.astype(jnp.bfloat16)


def score_kernel(
    final, qt_ref, near_ref, far_ref, high_in, total_in, accum_in, keys_ref, stretch_ref,
    weights_ref, total_ref, accum_ref,
):
    kv_local = qt_ref.shape[0]
    tokens, c_rows = near_ref.shape[1], far_ref.shape[1]
    mask = jnp.concatenate([near_ref[final], far_ref[final]], axis=0)
    keys, values_t = [], []
    for head in range(kv_local):
        pieces = [stretch_ref[:tokens, features(head)], keys_ref[:, features(head)]]
        keys.append(jnp.concatenate([jnp.concatenate(pieces, axis=0), mask], axis=1))
        values_t.append(stretch_ref[tokens:, features(head)].T)

    def second(block, scores):
        head, cols = block
        before = (high_in[head, :, cols], total_in[head, :, cols])
        weights, _, total, decay = soften(scores, before)
        weights_ref[head, :, cols] = weights[tokens:]
        total_ref[head, :, cols] = total
        accum_ref[head, :, cols] = accum_in[head, :, cols] * decay + jnp.dot(
            values_t[head], weights[:tokens], preferred_element_type=jnp.float32
        )

    walk(blocks_of(qt_ref), lambda block: scores_of(qt_ref, block[0], block[1], keys[block[0]]), second)


def last_kernel(weights_ref, total_ref, accum_ref, values_ref, out_ref, result_ref, sems):
    tokens = result_ref.shape[0]
    values_t = [values_ref[:, features(head)].T for head in range(weights_ref.shape[0])]
    copies = []

    def first(block):
        head, cols = block
        return jnp.dot(values_t[head], weights_ref[head, :, cols], preferred_element_type=jnp.float32)

    def second(block, mixed):
        head, cols = block
        mixed = mixed + accum_ref[head, :, cols]
        mixed = (mixed * (1.0 / total_ref[head, :, cols])).astype(jnp.bfloat16)
        start = (head * GROUP + cols.start // tokens) * HEAD_DIM
        pieces = (cols.stop - cols.start) // tokens
        for piece in range(pieces):
            col = start + piece * HEAD_DIM
            result_ref[:, col : col + HEAD_DIM] = mixed[:, piece * tokens : (piece + 1) * tokens].T
        span = pl.ds(start, pieces * HEAD_DIM)
        copy = pltpu.make_async_copy(result_ref.at[:, span], out_ref.at[:, span], sems.at[len(copies)])
        copy.start()
        copies.append(copy)

    walk(blocks_of(weights_ref), first, second)
    for copy in copies:
        copy.wait()


def per_device(
    count,
    queries,
    stretch_keys,
    stretch_values,
    cache_keys,
    cache_values,
    prefix_length,
    page_targets,
    pool_keys,
    pool_values,
    decode_queries,
    page_lists,
    context_length,
):
    own = lax.axis_index("ctx")
    own_array = jnp.full((1,), own, jnp.int32)
    tokens, width = queries.shape
    kv_width = stretch_keys.shape[1]
    kv_local = kv_width // HEAD_DIM
    rows = GROUP * tokens
    heads = kv_local * GROUP
    dec_rows = decode_queries.shape[0]
    c_rows = cache_keys.shape[0]
    pool = pool_keys.shape[0]
    f32, bf16 = jnp.float32, jnp.bfloat16
    shape = jax.ShapeDtypeStruct
    params = pltpu.CompilerParams(vmem_limit_bytes=VMEM_BYTES)
    up_pairs = [(i, (i + 1) % count) for i in range(count)]
    down_pairs = [(i, (i - 1) % count) for i in range(count)]
    hops = []
    for far in range(1, count // 2 + 1):
        hops += [-far, far] if far <= (count - 1) // 2 else [-far]

    def send(array, hop):
        return lax.ppermute(array, "ctx", up_pairs if hop < 0 else down_pairs)

    def cost(keys):
        pairs = kv_local * rows * keys
        return pl.CostEstimate(
            flops=4 * pairs * HEAD_DIM, bytes_accessed=4 * rows * kv_local * HEAD_DIM, transcendentals=pairs
        )

    half = tokens + c_rows
    low = jnp.array(-jnp.inf, bf16)
    spread, start = [], 0
    for part in (stretch_keys, cache_keys, stretch_values, cache_values):
        end = 2 * half - start - part.shape[0]
        spread.append(lax.pad(part, low, ((start, end, 0), (0, 0, 0))))
        start += part.shape[0]
    shard = {0: functools.reduce(jnp.maximum, spread)}
    shard[-1] = send(shard[0], -1)

    state_shapes = (
        shape((kv_local, 1, rows), f32),
        shape((kv_local, 1, rows), f32),
        shape((kv_local, HEAD_DIM, rows), f32),
    )
    qt, near, far, pick, *state = pl.pallas_call(
        functools.partial(own_kernel, count, hops),
        out_shape=(
            shape((kv_local, HEAD_DIM + tokens, rows), bf16),
            shape((count - 1, tokens, tokens), bf16),
            shape((count - 1, c_rows, tokens), bf16),
            shape((SEND_CAP * PAGE, tokens), bf16),
        )
        + state_shapes,
        in_specs=[SMEM] * 3 + [VMEM] * 2,
        out_specs=(VMEM,) * 7,
        compiler_params=params,
        cost_estimate=cost(tokens + c_rows),
        name="own_shard",
    )(own_array, prefix_length, page_targets, queries, shard[0])

    wide, *dec_state = pl.pallas_call(
        held_kernel,
        out_shape=(
            shape((heads * dec_rows, kv_width), bf16),
            shape((heads, dec_rows, 1), f32),
            shape((heads, dec_rows, 1), f32),
            shape((heads, dec_rows, kv_width), f32),
        ),
        in_specs=[SMEM] * 3 + [VMEM] * 5,
        out_specs=(VMEM,) * 4,
        compiler_params=params,
        cost_estimate=pl.CostEstimate(
            flops=4 * 128 * 2048 * 256, bytes_accessed=4 * pool_keys.size, transcendentals=128 * 2048
        ),
        name="decode_held_pages",
    )(own_array, page_targets, context_length, decode_queries, page_lists, pool_keys, pool_values, shard[0])

    if 1 in hops:
        sent_down, state, dec_state = lax.optimization_barrier((shard[0], state, dec_state))
        shard[1] = send(sent_down, 1)
    shard[-1], state, dec_state = lax.optimization_barrier((shard[-1], state, dec_state))
    for hop in hops[2:-1]:
        shard[hop] = send(shard[hop + 1 if hop < 0 else hop - 1], hop)
    hop = hops[-1]
    nearer = shard[hop + 1 if hop < 0 else hop - 1]
    pieces = pl.pallas_call(
        split_kernel,
        out_shape=(
            shape((c_rows, kv_width), bf16),
            shape((2 * tokens, kv_width), bf16),
            shape((c_rows, kv_width), bf16),
            shape((2 * SEND_CAP * PAGE, kv_width), bf16),
        ),
        in_specs=[VMEM] * 2,
        out_specs=(VMEM,) * 4,
        compiler_params=params,
        name="pieces_to_send_on",
    )(pick, nearer)
    last_keys = send(pieces[0], hop)
    attending, others = [], []
    for pair in up_pairs if hop < 0 else down_pairs:
        (attending if (pair[1] + hop) % count < pair[1] else others).append(pair)
    last_stretch = lax.ppermute(pieces[1], "ctx", attending)
    last_pages = lax.ppermute(pieces[3], "ctx", others)
    last_values = send(pieces[2], hop)

    last_pages, state = lax.optimization_barrier((last_pages, state))
    for first in range(len(hops) - 1):
        places = [first]
        state = pl.pallas_call(
            functools.partial(hop_kernel, places),
            out_shape=state_shapes,
            in_specs=[VMEM] * (6 + len(places)),
            out_specs=(VMEM,) * 3,
            compiler_params=params,
            cost_estimate=cost((c_rows + tokens) * len(places)),
            name="whole_shards_" + str(first),
        )(qt, near, far, *state, *[shard[hops[place]] for place in places])

    final = len(hops) - 1
    decoded = pl.pallas_call(
        functools.partial(pages_kernel, count, hops, tokens, pool),
        out_shape=shape(decode_queries.shape, bf16),
        in_specs=[SMEM] * 3 + [VMEM] * (6 + len(hops)),
        out_specs=VMEM,
        compiler_params=params,
        cost_estimate=cost(tokens),
        name="decode_new_pages",
    )(
        own_array, page_targets, context_length, page_lists, *[shard[hop] for hop in hops[:-1]], last_stretch, last_pages,
        wide, *dec_state,
    )

    decoded, state = lax.optimization_barrier((decoded, state))
    weights, total, accum = pl.pallas_call(
        functools.partial(score_kernel, final),
        out_shape=(shape((kv_local, c_rows, rows), bf16),) + state_shapes[1:],
        in_specs=[VMEM] * 8,
        out_specs=(VMEM,) * 3,
        compiler_params=params,
        cost_estimate=cost(half),
        name="last_scores",
    )(qt, near, far, *state, last_keys, last_stretch)

    prefill = pl.pallas_call(
        last_kernel,
        out_shape=shape((tokens, width), bf16),
        in_specs=[VMEM] * 4,
        out_specs=HBM,
        scratch_shapes=[
            pltpu.VMEM((tokens, width), bf16),
            pltpu.SemaphoreType.DMA((kv_local * max(GROUP // 2, 1),)),
        ],
        compiler_params=params,
        cost_estimate=cost(c_rows // 2),
        name="last_values",
    )(weights, total, accum, last_values)
    return (prefill, decoded)


def solution(mesh):
    in_specs = (
        P(("groups", "ctx"), "head"),
        P(("groups", "ctx"), "head"),
        P(("groups", "ctx"), "head"),
        P(("groups", "ctx"), "head"),
        P(("groups", "ctx"), "head"),
        P("groups"),
        P("groups"),
        P(("groups", "ctx"), None, "head"),
        P(("groups", "ctx"), None, "head"),
        P(("groups", "ctx"), "head"),
        P(("groups", "ctx"), None),
        P(("groups", "ctx")),
    )
    out_specs = (P(("groups", "ctx"), "head"), P(("groups", "ctx"), "head"))
    return jax.shard_map(
        functools.partial(per_device, mesh.shape["ctx"]),
        mesh=mesh,
        in_specs=in_specs,
        out_specs=out_specs,
        check_vma=False,
    )
```

```python
import functools

import jax
import jax.numpy as jnp
from jax import lax
from jax.experimental import pallas as pl
from jax.experimental.pallas import tpu as pltpu
from jax.sharding import PartitionSpec as P

HEADS = 64
KV_HEADS = 8
HEAD_DIM = 128
GROUP = HEADS // KV_HEADS
PAGE = 16
P_DEV = 8
SEND_CAP = 2
EXP2_SCALE = HEAD_DIM ** (-0.5) * 1.4426950408889634
HIDDEN = -1e30
VMEM_BYTES = 48 * 1024 * 1024

VMEM = pl.BlockSpec(memory_space=pltpu.VMEM)
SMEM = pl.BlockSpec(memory_space=pltpu.SMEM)
HBM = pl.BlockSpec(memory_space=pltpu.HBM)


def scores_of(qt_ref, head, cols, keys):
    return jnp.dot(keys, qt_ref[head, :, cols], preferred_element_type=jnp.float32)


def soften(scores, old):
    high = jnp.max(scores, axis=0, keepdims=True)
    if old is None:
        weights = jnp.exp2((scores - high) * EXP2_SCALE)
        return weights.astype(jnp.bfloat16), high, jnp.sum(weights, axis=0, keepdims=True), None
    old_high, old_total = old
    high = jnp.maximum(high, old_high)
    decay = jnp.exp2((old_high - high) * EXP2_SCALE)
    weights = jnp.exp2((scores - high) * EXP2_SCALE)
    total = old_total * decay + jnp.sum(weights, axis=0, keepdims=True)
    return weights.astype(jnp.bfloat16), high, total, decay


def walk(blocks, first, second):
    ahead = first(blocks[0])
    for place, block in enumerate(blocks):
        current = ahead
        if place + 1 < len(blocks):
            ahead = first(blocks[place + 1])
        second(block, current)


def blocks_of(qt_ref):
    kv_local, _, rows = qt_ref.shape
    width = min(2 * (rows // GROUP), rows)
    return [(head, slice(start, start + width)) for head in range(kv_local) for start in range(0, rows, width)]


def attend(qt_ref, keys, values_t, old, new):
    high_ref, total_ref, accum_ref = new

    def second(block, scores):
        head, cols = block
        before = None if old is None else (old[0][head, :, cols], old[1][head, :, cols])
        weights, high, total, decay = soften(scores, before)
        accum = jnp.dot(values_t[head], weights, preferred_element_type=jnp.float32)
        if old is not None:
            accum = accum + old[2][head, :, cols] * decay
        high_ref[head, :, cols] = high
        total_ref[head, :, cols] = total
        accum_ref[head, :, cols] = accum

    walk(blocks_of(qt_ref), lambda block: scores_of(qt_ref, block[0], block[1], keys[block[0]]), second)


def hidden(seen):
    return jnp.where(seen, jnp.float32(0.0), jnp.float32(HIDDEN)).astype(jnp.bfloat16)


def stretch_mask(shard, own, tokens):
    place = lax.broadcasted_iota(jnp.int32, (tokens, tokens), 0)
    token = lax.broadcasted_iota(jnp.int32, (tokens, tokens), 1)
    return hidden(place - token <= (own - shard) * tokens)


def cache_mask(shard, limit, c_rows, tokens):
    place = lax.broadcasted_iota(jnp.int32, (c_rows, tokens), 0)
    return hidden(place < limit - shard * c_rows)


def slot_row(targets_ref, shard, own, tokens, pool):
    page = lax.broadcasted_iota(jnp.int32, (1, tokens), 1) // PAGE
    slots = jnp.full((1, tokens), -1, jnp.int32)
    for index in range(tokens // PAGE):
        target = targets_ref[shard * (tokens // PAGE) + index]
        slot = jnp.where(lax.div(target, P_DEV) == own, pool + lax.rem(target, P_DEV), -1)
        slots = jnp.where(page == index, slot, slots)
    return slots


def sent_pages(targets_ref, shard, owner, pages):
    one, two = jnp.int32(-1), jnp.int32(-1)
    for index in range(pages):
        hit = lax.div(targets_ref[shard * pages + index], P_DEV) == owner
        two = jnp.where(hit & (one >= 0) & (two < 0), index, two)
        one = jnp.where(hit & (one < 0), index, one)
    return one, two


def sent_slots(targets_ref, shard, owner, pages, pool):
    place = lax.broadcasted_iota(jnp.int32, (1, SEND_CAP * PAGE), 1)
    slots = []
    for index in sent_pages(targets_ref, shard, owner, pages):
        target = targets_ref[shard * pages + jnp.maximum(index, 0)]
        slots.append(jnp.where(index >= 0, pool + lax.rem(target, P_DEV), -1))
    return jnp.where(place < PAGE, slots[0], slots[1])


def length_column(length_ref):
    rows = length_ref.shape[0]
    place = lax.broadcasted_iota(jnp.int32, (rows, 1), 0)
    lengths = jnp.zeros((rows, 1), jnp.int32)
    for row in range(rows):
        lengths = jnp.where(place == row, length_ref[row], lengths)
    return lengths


def tally_of(lists, lengths, slot):
    rows, span = lists.shape
    tokens = slot.shape[1]
    slot = jnp.broadcast_to(slot, (rows, tokens))
    offset = lax.rem(lax.broadcasted_iota(jnp.int32, (rows, tokens), 1), PAGE)
    tally = jnp.zeros((rows, tokens), jnp.float32)
    for entry in range(span):
        hit = (slot == lists[:, entry : entry + 1]) & (offset < lengths - entry * PAGE)
        tally = tally + jnp.where(hit, jnp.float32(1.0), jnp.float32(0.0))
    return tally[None]


def shard_of(own, hop, count):
    return lax.rem(own + hop + count, count)


def wide_queries(q_ref, kv_local):
    heads = q_ref.shape[1] // HEAD_DIM
    queries = q_ref[...].astype(jnp.float32)
    stacked = []
    for head in range(heads):
        piece = queries[:, head * HEAD_DIM : (head + 1) * HEAD_DIM]
        blank = jnp.zeros_like(piece)
        stacked.append(
            jnp.concatenate([piece if kv == head // GROUP else blank for kv in range(kv_local)], axis=1)
        )
    return jnp.concatenate(stacked, axis=0).astype(jnp.bfloat16)


def decode_attend(queries, parts, state):
    done = []
    for keys, values, tally in parts:
        scores = lax.dot_general(
            queries, keys, (((1,), (1,)), ((), ())), preferred_element_type=jnp.float32
        ).reshape(-1, tally.shape[1], tally.shape[2])
        done.append((jnp.where(tally > 0, scores, jnp.float32(HIDDEN)), tally, values))
    highs = [jnp.max(scores, axis=-1, keepdims=True) for scores, _, _ in done]
    if state is not None:
        old_high, old_total, old_mixed = state
        highs.append(old_high)
    high = functools.reduce(jnp.maximum, highs)
    total, mixed = 0.0, 0.0
    if state is not None:
        decay = jnp.exp2((old_high - high) * EXP2_SCALE)
        total = old_total * decay
        mixed = old_mixed * decay
    for scores, tally, values in done:
        weights = jnp.exp2((scores - high) * EXP2_SCALE) * tally
        total = total + jnp.sum(weights, axis=-1, keepdims=True)
        mixed = mixed + jnp.dot(
            weights.reshape(queries.shape[0], -1).astype(jnp.bfloat16),
            values,
            preferred_element_type=jnp.float32,
        ).reshape(high.shape[0], high.shape[1], -1)
    return high, total, mixed


def features(head):
    return slice(head * HEAD_DIM, (head + 1) * HEAD_DIM)


def shard_parts(ref, tokens, c_rows):
    return slice(0, tokens + c_rows), slice(tokens + c_rows, 2 * (tokens + c_rows))


def own_kernel(
    count, hops, own_ref, limit_ref, targets_ref, q_ref, shard_ref,
    qt_ref, near_ref, far_ref, pick_ref, high_ref, total_ref, accum_ref,
):
    kv_local, _, rows = qt_ref.shape
    tokens = q_ref.shape[0]
    c_rows = far_ref.shape[1]
    own = own_ref[0]
    limit = limit_ref[0]
    place = lax.broadcasted_iota(jnp.int32, (tokens, tokens), 0)
    token = lax.broadcasted_iota(jnp.int32, (tokens, tokens), 1)
    pick = jnp.where(place == token, jnp.float32(1.0), jnp.float32(0.0)).astype(jnp.bfloat16)
    for head in range(kv_local):
        for sub in range(GROUP):
            cols = slice(sub * tokens, (sub + 1) * tokens)
            qt_ref[head, :HEAD_DIM, cols] = q_ref[:, features(head * GROUP + sub)].T
            qt_ref[head, HEAD_DIM:, cols] = pick
    for place, hop in enumerate(hops):
        shard = shard_of(own, hop, count)
        near_ref[place] = stretch_mask(shard, own, tokens)
        far_ref[place] = cache_mask(shard, limit, c_rows, tokens)
    onward = 1 if hops[-1] < 0 else -1
    pages = tokens // PAGE
    one, two = sent_pages(
        targets_ref, shard_of(own, hops[-1] + onward, count), shard_of(own, onward, count), pages
    )
    row = lax.broadcasted_iota(jnp.int32, pick_ref.shape, 0)
    token = lax.broadcasted_iota(jnp.int32, pick_ref.shape, 1)
    sent = ((row < PAGE) & (one >= 0) & (token == row + one * PAGE)) | (
        (row >= PAGE) & (two >= 0) & (token == row + (two - 1) * PAGE)
    )
    pick_ref[...] = jnp.where(sent, jnp.float32(1.0), jnp.float32(0.0)).astype(jnp.bfloat16)
    mask = jnp.concatenate([stretch_mask(own, own, tokens), cache_mask(own, limit, c_rows, tokens)], axis=0)
    key_rows, value_rows = shard_parts(shard_ref, tokens, c_rows)
    keys = [jnp.concatenate([shard_ref[key_rows, features(head)], mask], axis=1) for head in range(kv_local)]
    values_t = [shard_ref[value_rows, features(head)].T for head in range(kv_local)]
    attend(qt_ref, keys, values_t, None, (high_ref, total_ref, accum_ref))


def held_kernel(
    own_ref, targets_ref, length_ref, q_ref, lists_ref, pool_k, pool_v, rest_ref,
    wide_ref, high_ref, total_ref, mixed_ref,
):
    kv_width = rest_ref.shape[1]
    pool = pool_k.shape[0]
    held = pool * PAGE
    tokens = PAGE * P_DEV
    half = rest_ref.shape[0] // 2
    own = own_ref[0]
    lists = lists_ref[...]
    lengths = length_column(length_ref)
    wide_ref[...] = wide_queries(q_ref, kv_width // HEAD_DIM)
    held_slot = lax.broadcasted_iota(jnp.int32, (1, held), 1) // PAGE
    own_slot = slot_row(targets_ref, own, own, tokens, pool)
    parts = [
        (
            pool_k[...].reshape(held, kv_width),
            pool_v[...].reshape(held, kv_width),
            tally_of(lists, lengths, held_slot),
        ),
        (rest_ref[:tokens], rest_ref[half : half + tokens], tally_of(lists, lengths, own_slot)),
    ]
    high_ref[...], total_ref[...], mixed_ref[...] = decode_attend(wide_ref[...], parts, None)


def hop_kernel(places, qt_ref, near_ref, far_ref, high_in, total_in, accum_in, *refs):
    shard_refs, outs = refs[: len(places)], refs[len(places) :]
    tokens, c_rows = near_ref.shape[1], far_ref.shape[1]
    mask = jnp.concatenate([ref[place] for place in places for ref in (near_ref, far_ref)], axis=0)
    keys, values_t = [], []
    for head in range(qt_ref.shape[0]):
        pieces, values = [], []
        for ref in shard_refs:
            key_rows, value_rows = shard_parts(ref, tokens, c_rows)
            pieces.append(ref[key_rows, features(head)])
            values.append(ref[value_rows, features(head)])
        keys.append(jnp.concatenate([jnp.concatenate(pieces, axis=0), mask], axis=1))
        values_t.append(jnp.concatenate(values, axis=0).T)
    attend(qt_ref, keys, values_t, (high_in, total_in, accum_in), outs)


def split_kernel(pick_ref, shard_ref, keys_ref, stretch_ref, values_ref, pages_ref):
    tokens = pick_ref.shape[1]
    half = shard_ref.shape[0] // 2
    sent = pick_ref.shape[0]
    for place, start in enumerate((0, half)):
        stretch_ref[place * tokens : (place + 1) * tokens] = shard_ref[start : start + tokens]
        rows = jnp.dot(pick_ref[...], shard_ref[start : start + tokens], preferred_element_type=jnp.float32)
        pages_ref[place * sent : (place + 1) * sent] = rows.astype(jnp.bfloat16)
    keys_ref[...] = shard_ref[tokens:half]
    values_ref[...] = shard_ref[half + tokens :]


def near_pages_kernel(count, hops, tokens, pool, own_ref, targets_ref, length_ref, lists_ref, *refs):
    shard_refs, refs = refs[: len(hops)], refs[len(hops) :]
    wide_ref, dec_high, dec_total, dec_mixed, high_ref, total_ref, mixed_ref = refs
    own = own_ref[0]
    lists = lists_ref[...]
    lengths = length_column(length_ref)
    parts = []
    for hop, ref in zip(hops, shard_refs):
        half = ref.shape[0] // 2
        slot = slot_row(targets_ref, shard_of(own, hop, count), own, tokens, pool)
        parts.append((ref[:tokens], ref[half : half + tokens], tally_of(lists, lengths, slot)))
    state = (dec_high[...], dec_total[...], dec_mixed[...])
    high_ref[...], total_ref[...], mixed_ref[...] = decode_attend(wide_ref[...], parts, state)


def last_pages_kernel(
    count, hop, pool, own_ref, targets_ref, length_ref, lists_ref, stretch_ref, pages_ref,
    wide_ref, dec_high, dec_total, dec_mixed, dec_out,
):
    own = own_ref[0]
    tokens = stretch_ref.shape[0] // 2
    sent = pages_ref.shape[0] // 2
    lists = lists_ref[...]
    lengths = length_column(length_ref)
    shard = shard_of(own, hop, count)
    attended = shard < own
    whole = jnp.where(attended, slot_row(targets_ref, shard, own, tokens, pool), -1)
    alone = jnp.where(attended, -1, sent_slots(targets_ref, shard, own, tokens // PAGE, pool))
    parts = [
        (stretch_ref[:tokens], stretch_ref[tokens:], tally_of(lists, lengths, whole)),
        (pages_ref[:sent], pages_ref[sent:], tally_of(lists, lengths, alone)),
    ]
    _, total, mixed = decode_attend(wide_ref[...], parts, (dec_high[...], dec_total[...], dec_mixed[...]))
    for head in range(dec_high.shape[0]):
        piece = mixed[head, :, features(head // GROUP)] / total[head]
        dec_out[:, features(head)] = piece.astype(jnp.bfloat16)


def score_kernel(
    final, qt_ref, near_ref, far_ref, high_in, total_in, accum_in, keys_ref, stretch_ref,
    weights_ref, total_ref, accum_ref,
):
    kv_local = qt_ref.shape[0]
    tokens, c_rows = near_ref.shape[1], far_ref.shape[1]
    mask = jnp.concatenate([near_ref[final], far_ref[final]], axis=0)
    keys, values_t = [], []
    for head in range(kv_local):
        pieces = [stretch_ref[:tokens, features(head)], keys_ref[:, features(head)]]
        keys.append(jnp.concatenate([jnp.concatenate(pieces, axis=0), mask], axis=1))
        values_t.append(stretch_ref[tokens:, features(head)].T)

    def second(block, scores):
        head, cols = block
        before = (high_in[head, :, cols], total_in[head, :, cols])
        weights, _, total, decay = soften(scores, before)
        weights_ref[head, :, cols] = weights[tokens:]
        total_ref[head, :, cols] = total
        accum_ref[head, :, cols] = accum_in[head, :, cols] * decay + jnp.dot(
            values_t[head], weights[:tokens], preferred_element_type=jnp.float32
        )

    walk(blocks_of(qt_ref), lambda block: scores_of(qt_ref, block[0], block[1], keys[block[0]]), second)


def last_kernel(weights_ref, total_ref, accum_ref, values_ref, out_ref, result_ref, sems):
    tokens = result_ref.shape[0]
    values_t = [values_ref[:, features(head)].T for head in range(weights_ref.shape[0])]
    copies = []

    def first(block):
        head, cols = block
        return jnp.dot(values_t[head], weights_ref[head, :, cols], preferred_element_type=jnp.float32)

    def second(block, mixed):
        head, cols = block
        mixed = mixed + accum_ref[head, :, cols]
        mixed = (mixed * (1.0 / total_ref[head, :, cols])).astype(jnp.bfloat16)
        start = (head * GROUP + cols.start // tokens) * HEAD_DIM
        pieces = (cols.stop - cols.start) // tokens
        for piece in range(pieces):
            col = start + piece * HEAD_DIM
            result_ref[:, col : col + HEAD_DIM] = mixed[:, piece * tokens : (piece + 1) * tokens].T
        span = pl.ds(start, pieces * HEAD_DIM)
        copy = pltpu.make_async_copy(result_ref.at[:, span], out_ref.at[:, span], sems.at[len(copies)])
        copy.start()
        copies.append(copy)

    walk(blocks_of(weights_ref), first, second)
    for copy in copies:
        copy.wait()


def per_device(
    count,
    queries,
    stretch_keys,
    stretch_values,
    cache_keys,
    cache_values,
    prefix_length,
    page_targets,
    pool_keys,
    pool_values,
    decode_queries,
    page_lists,
    context_length,
):
    own = lax.axis_index("ctx")
    own_array = jnp.full((1,), own, jnp.int32)
    tokens, width = queries.shape
    kv_width = stretch_keys.shape[1]
    kv_local = kv_width // HEAD_DIM
    rows = GROUP * tokens
    heads = kv_local * GROUP
    dec_rows = decode_queries.shape[0]
    c_rows = cache_keys.shape[0]
    pool = pool_keys.shape[0]
    f32, bf16 = jnp.float32, jnp.bfloat16
    shape = jax.ShapeDtypeStruct
    params = pltpu.CompilerParams(vmem_limit_bytes=VMEM_BYTES)
    up_pairs = [(i, (i + 1) % count) for i in range(count)]
    down_pairs = [(i, (i - 1) % count) for i in range(count)]
    hops = []
    for far in range(1, count // 2 + 1):
        hops += [-far, far] if far <= (count - 1) // 2 else [-far]

    def send(array, hop):
        return lax.ppermute(array, "ctx", up_pairs if hop < 0 else down_pairs)

    def cost(keys):
        pairs = kv_local * rows * keys
        return pl.CostEstimate(
            flops=4 * pairs * HEAD_DIM, bytes_accessed=4 * rows * kv_local * HEAD_DIM, transcendentals=pairs
        )

    half = tokens + c_rows
    low = jnp.array(-jnp.inf, bf16)
    spread, start = [], 0
    for part in (stretch_keys, cache_keys, stretch_values, cache_values):
        end = 2 * half - start - part.shape[0]
        spread.append(lax.pad(part, low, ((start, end, 0), (0, 0, 0))))
        start += part.shape[0]
    shard = {0: functools.reduce(jnp.maximum, spread)}
    shard[-1] = send(shard[0], -1)

    state_shapes = (
        shape((kv_local, 1, rows), f32),
        shape((kv_local, 1, rows), f32),
        shape((kv_local, HEAD_DIM, rows), f32),
    )
    qt, near, far, pick, *state = pl.pallas_call(
        functools.partial(own_kernel, count, hops),
        out_shape=(
            shape((kv_local, HEAD_DIM + tokens, rows), bf16),
            shape((count - 1, tokens, tokens), bf16),
            shape((count - 1, c_rows, tokens), bf16),
            shape((SEND_CAP * PAGE, tokens), bf16),
        )
        + state_shapes,
        in_specs=[SMEM] * 3 + [VMEM] * 2,
        out_specs=(VMEM,) * 7,
        compiler_params=params,
        cost_estimate=cost(tokens + c_rows),
        name="own_shard",
    )(own_array, prefix_length, page_targets, queries, shard[0])

    dec_shapes = (
        shape((heads, dec_rows, 1), f32),
        shape((heads, dec_rows, 1), f32),
        shape((heads, dec_rows, kv_width), f32),
    )
    wide, *dec_state = pl.pallas_call(
        held_kernel,
        out_shape=(shape((heads * dec_rows, kv_width), bf16),) + dec_shapes,
        in_specs=[SMEM] * 3 + [VMEM] * 5,
        out_specs=(VMEM,) * 4,
        compiler_params=params,
        cost_estimate=pl.CostEstimate(
            flops=4 * 128 * 2048 * 256, bytes_accessed=4 * pool_keys.size, transcendentals=128 * 2048
        ),
        name="decode_held_pages",
    )(own_array, page_targets, context_length, decode_queries, page_lists, pool_keys, pool_values, shard[0])

    if 1 in hops:
        sent_down, state, dec_state = lax.optimization_barrier((shard[0], state, dec_state))
        shard[1] = send(sent_down, 1)
    shard[-1], state, dec_state = lax.optimization_barrier((shard[-1], state, dec_state))
    for hop in hops[2:-1]:
        shard[hop] = send(shard[hop + 1 if hop < 0 else hop - 1], hop)
    hop = hops[-1]
    nearer = shard[hop + 1 if hop < 0 else hop - 1]
    pieces = pl.pallas_call(
        split_kernel,
        out_shape=(
            shape((c_rows, kv_width), bf16),
            shape((2 * tokens, kv_width), bf16),
            shape((c_rows, kv_width), bf16),
            shape((2 * SEND_CAP * PAGE, kv_width), bf16),
        ),
        in_specs=[VMEM] * 2,
        out_specs=(VMEM,) * 4,
        compiler_params=params,
        name="pieces_to_send_on",
    )(pick, nearer)
    last_keys = send(pieces[0], hop)
    attending, others = [], []
    for pair in up_pairs if hop < 0 else down_pairs:
        (attending if (pair[1] + hop) % count < pair[1] else others).append(pair)
    last_stretch = lax.ppermute(pieces[1], "ctx", attending)
    last_pages = lax.ppermute(pieces[3], "ctx", others)
    last_values = send(pieces[2], hop)

    for first in range(len(hops) - 1):
        places = [first]
        state = pl.pallas_call(
            functools.partial(hop_kernel, places),
            out_shape=state_shapes,
            in_specs=[VMEM] * (6 + len(places)),
            out_specs=(VMEM,) * 3,
            compiler_params=params,
            cost_estimate=cost((c_rows + tokens) * len(places)),
            name="whole_shards_" + str(first),
        )(qt, near, far, *state, *[shard[hops[place]] for place in places])

    final = len(hops) - 1
    dec_state, state = lax.optimization_barrier((dec_state, state))
    near_hops = hops[:-1]
    dec_state = pl.pallas_call(
        functools.partial(near_pages_kernel, count, near_hops, tokens, pool),
        out_shape=dec_shapes,
        in_specs=[SMEM] * 3 + [VMEM] * (5 + len(near_hops)),
        out_specs=(VMEM,) * 3,
        compiler_params=params,
        cost_estimate=cost(tokens),
        name="decode_near_pages",
    )(
        own_array, page_targets, context_length, page_lists, *[shard[hop] for hop in near_hops],
        wide, *dec_state,
    )
    dec_state, state = lax.optimization_barrier((dec_state, state))

    weights, total, accum = pl.pallas_call(
        functools.partial(score_kernel, final),
        out_shape=(shape((kv_local, c_rows, rows), bf16),) + state_shapes[1:],
        in_specs=[VMEM] * 8,
        out_specs=(VMEM,) * 3,
        compiler_params=params,
        cost_estimate=cost(half),
        name="last_scores",
    )(qt, near, far, *state, last_keys, last_stretch)

    prefill = pl.pallas_call(
        last_kernel,
        out_shape=shape((tokens, width), bf16),
        in_specs=[VMEM] * 4,
        out_specs=HBM,
        scratch_shapes=[
            pltpu.VMEM((tokens, width), bf16),
            pltpu.SemaphoreType.DMA((kv_local * max(GROUP // 2, 1),)),
        ],
        compiler_params=params,
        cost_estimate=cost(c_rows // 2),
        name="last_values",
    )(weights, total, accum, last_values)

    prefill, dec_state = lax.optimization_barrier((prefill, dec_state))
    decoded = pl.pallas_call(
        functools.partial(last_pages_kernel, count, hops[-1], pool),
        out_shape=shape(decode_queries.shape, bf16),
        in_specs=[SMEM] * 3 + [VMEM] * 7,
        out_specs=VMEM,
        compiler_params=params,
        cost_estimate=cost(tokens // 2),
        name="decode_last_pages",
    )(
        own_array, page_targets, context_length, page_lists, last_stretch, last_pages, wide, *dec_state
    )
    return (prefill, decoded)


def solution(mesh):
    in_specs = (
        P(("groups", "ctx"), "head"),
        P(("groups", "ctx"), "head"),
        P(("groups", "ctx"), "head"),
        P(("groups", "ctx"), "head"),
        P(("groups", "ctx"), "head"),
        P("groups"),
        P("groups"),
        P(("groups", "ctx"), None, "head"),
        P(("groups", "ctx"), None, "head"),
        P(("groups", "ctx"), "head"),
        P(("groups", "ctx"), None),
        P(("groups", "ctx")),
    )
    out_specs = (P(("groups", "ctx"), "head"), P(("groups", "ctx"), "head"))
    return jax.shard_map(
        functools.partial(per_device, mesh.shape["ctx"]),
        mesh=mesh,
        in_specs=in_specs,
        out_specs=out_specs,
        check_vma=False,
    )
```

```python
import functools

import jax
import jax.numpy as jnp
from jax import lax
from jax.experimental import pallas as pl
from jax.experimental.pallas import tpu as pltpu
from jax.sharding import PartitionSpec as P

HEADS = 64
KV_HEADS = 8
HEAD_DIM = 128
GROUP = HEADS // KV_HEADS
PAGE = 16
P_DEV = 8
SEND_CAP = 2
EXP2_SCALE = HEAD_DIM ** (-0.5) * 1.4426950408889634
HIDDEN = -1e30
VMEM_BYTES = 48 * 1024 * 1024

VMEM = pl.BlockSpec(memory_space=pltpu.VMEM)
SMEM = pl.BlockSpec(memory_space=pltpu.SMEM)
HBM = pl.BlockSpec(memory_space=pltpu.HBM)


def scores_of(qt_ref, head, cols, keys):
    return jnp.dot(keys, qt_ref[head, :, cols], preferred_element_type=jnp.float32)


def soften(scores, old):
    high = jnp.max(scores, axis=0, keepdims=True)
    if old is None:
        weights = jnp.exp2((scores - high) * EXP2_SCALE)
        return weights.astype(jnp.bfloat16), high, jnp.sum(weights, axis=0, keepdims=True), None
    old_high, old_total = old
    high = jnp.maximum(high, old_high)
    decay = jnp.exp2((old_high - high) * EXP2_SCALE)
    weights = jnp.exp2((scores - high) * EXP2_SCALE)
    total = old_total * decay + jnp.sum(weights, axis=0, keepdims=True)
    return weights.astype(jnp.bfloat16), high, total, decay


def walk(blocks, first, second):
    ahead = first(blocks[0])
    for place, block in enumerate(blocks):
        current = ahead
        if place + 1 < len(blocks):
            ahead = first(blocks[place + 1])
        second(block, current)


def blocks_of(qt_ref):
    kv_local, _, rows = qt_ref.shape
    width = min(2 * (rows // GROUP), rows)
    return [(head, slice(start, start + width)) for head in range(kv_local) for start in range(0, rows, width)]


def attend(qt_ref, keys, values_t, old, new):
    high_ref, total_ref, accum_ref = new

    def second(block, scores):
        head, cols = block
        before = None if old is None else (old[0][head, :, cols], old[1][head, :, cols])
        weights, high, total, decay = soften(scores, before)
        accum = jnp.dot(values_t[head], weights, preferred_element_type=jnp.float32)
        if old is not None:
            accum = accum + old[2][head, :, cols] * decay
        high_ref[head, :, cols] = high
        total_ref[head, :, cols] = total
        accum_ref[head, :, cols] = accum

    walk(blocks_of(qt_ref), lambda block: scores_of(qt_ref, block[0], block[1], keys[block[0]]), second)


def hidden(seen):
    return jnp.where(seen, jnp.float32(0.0), jnp.float32(HIDDEN)).astype(jnp.bfloat16)


def stretch_mask(shard, own, tokens):
    place = lax.broadcasted_iota(jnp.int32, (tokens, tokens), 0)
    token = lax.broadcasted_iota(jnp.int32, (tokens, tokens), 1)
    return hidden(place - token <= (own - shard) * tokens)


def cache_mask(shard, limit, c_rows, tokens):
    place = lax.broadcasted_iota(jnp.int32, (c_rows, tokens), 0)
    return hidden(place < limit - shard * c_rows)


def slot_row(targets_ref, shard, own, tokens, pool):
    page = lax.broadcasted_iota(jnp.int32, (1, tokens), 1) // PAGE
    slots = jnp.full((1, tokens), -1, jnp.int32)
    for index in range(tokens // PAGE):
        target = targets_ref[shard * (tokens // PAGE) + index]
        slot = jnp.where(lax.div(target, P_DEV) == own, pool + lax.rem(target, P_DEV), -1)
        slots = jnp.where(page == index, slot, slots)
    return slots


def sent_pages(targets_ref, shard, owner, pages):
    one, two = jnp.int32(-1), jnp.int32(-1)
    for index in range(pages):
        hit = lax.div(targets_ref[shard * pages + index], P_DEV) == owner
        two = jnp.where(hit & (one >= 0) & (two < 0), index, two)
        one = jnp.where(hit & (one < 0), index, one)
    return one, two


def sent_slots(targets_ref, shard, owner, pages, pool):
    place = lax.broadcasted_iota(jnp.int32, (1, SEND_CAP * PAGE), 1)
    slots = []
    for index in sent_pages(targets_ref, shard, owner, pages):
        target = targets_ref[shard * pages + jnp.maximum(index, 0)]
        slots.append(jnp.where(index >= 0, pool + lax.rem(target, P_DEV), -1))
    return jnp.where(place < PAGE, slots[0], slots[1])


def length_column(length_ref):
    rows = length_ref.shape[0]
    place = lax.broadcasted_iota(jnp.int32, (rows, 1), 0)
    lengths = jnp.zeros((rows, 1), jnp.int32)
    for row in range(rows):
        lengths = jnp.where(place == row, length_ref[row], lengths)
    return lengths


def tally_of(lists, lengths, slot):
    rows, span = lists.shape
    tokens = slot.shape[1]
    slot = jnp.broadcast_to(slot, (rows, tokens))
    offset = lax.rem(lax.broadcasted_iota(jnp.int32, (rows, tokens), 1), PAGE)
    tally = jnp.zeros((rows, tokens), jnp.float32)
    for entry in range(span):
        hit = (slot == lists[:, entry : entry + 1]) & (offset < lengths - entry * PAGE)
        tally = tally + jnp.where(hit, jnp.float32(1.0), jnp.float32(0.0))
    return tally[None]


def shard_of(own, hop, count):
    return lax.rem(own + hop + count, count)


def wide_queries(q_ref, kv_local):
    heads = q_ref.shape[1] // HEAD_DIM
    queries = q_ref[...].astype(jnp.float32)
    stacked = []
    for head in range(heads):
        piece = queries[:, head * HEAD_DIM : (head + 1) * HEAD_DIM]
        blank = jnp.zeros_like(piece)
        stacked.append(
            jnp.concatenate([piece if kv == head // GROUP else blank for kv in range(kv_local)], axis=1)
        )
    return jnp.concatenate(stacked, axis=0).astype(jnp.bfloat16)


def decode_attend(queries, parts, state):
    done = []
    for keys, values, tally in parts:
        scores = lax.dot_general(
            queries, keys, (((1,), (1,)), ((), ())), preferred_element_type=jnp.float32
        ).reshape(-1, tally.shape[1], tally.shape[2])
        done.append((jnp.where(tally > 0, scores, jnp.float32(HIDDEN)), tally, values))
    highs = [jnp.max(scores, axis=-1, keepdims=True) for scores, _, _ in done]
    if state is not None:
        old_high, old_total, old_mixed = state
        highs.append(old_high)
    high = functools.reduce(jnp.maximum, highs)
    total, mixed = 0.0, 0.0
    if state is not None:
        decay = jnp.exp2((old_high - high) * EXP2_SCALE)
        total = old_total * decay
        mixed = old_mixed * decay
    for scores, tally, values in done:
        weights = jnp.exp2((scores - high) * EXP2_SCALE) * tally
        total = total + jnp.sum(weights, axis=-1, keepdims=True)
        mixed = mixed + jnp.dot(
            weights.reshape(queries.shape[0], -1).astype(jnp.bfloat16),
            values,
            preferred_element_type=jnp.float32,
        ).reshape(high.shape[0], high.shape[1], -1)
    return high, total, mixed


def features(head):
    return slice(head * HEAD_DIM, (head + 1) * HEAD_DIM)


def shard_parts(ref, tokens, c_rows):
    return slice(0, tokens + c_rows), slice(tokens + c_rows, 2 * (tokens + c_rows))


def own_kernel(
    count, hops, own_ref, limit_ref, targets_ref, q_ref, shard_ref,
    qt_ref, near_ref, far_ref, pick_ref, high_ref, total_ref, accum_ref,
):
    kv_local, _, rows = qt_ref.shape
    tokens = q_ref.shape[0]
    c_rows = far_ref.shape[1]
    own = own_ref[0]
    limit = limit_ref[0]
    place = lax.broadcasted_iota(jnp.int32, (tokens, tokens), 0)
    token = lax.broadcasted_iota(jnp.int32, (tokens, tokens), 1)
    pick = jnp.where(place == token, jnp.float32(1.0), jnp.float32(0.0)).astype(jnp.bfloat16)
    for head in range(kv_local):
        for sub in range(GROUP):
            cols = slice(sub * tokens, (sub + 1) * tokens)
            qt_ref[head, :HEAD_DIM, cols] = q_ref[:, features(head * GROUP + sub)].T
            qt_ref[head, HEAD_DIM:, cols] = pick
    for place, hop in enumerate(hops):
        shard = shard_of(own, hop, count)
        near_ref[place] = stretch_mask(shard, own, tokens)
        far_ref[place] = cache_mask(shard, limit, c_rows, tokens)
    onward = 1 if hops[-1] < 0 else -1
    pages = tokens // PAGE
    one, two = sent_pages(
        targets_ref, shard_of(own, hops[-1] + onward, count), shard_of(own, onward, count), pages
    )
    row = lax.broadcasted_iota(jnp.int32, pick_ref.shape, 0)
    token = lax.broadcasted_iota(jnp.int32, pick_ref.shape, 1)
    sent = ((row < PAGE) & (one >= 0) & (token == row + one * PAGE)) | (
        (row >= PAGE) & (two >= 0) & (token == row + (two - 1) * PAGE)
    )
    pick_ref[...] = jnp.where(sent, jnp.float32(1.0), jnp.float32(0.0)).astype(jnp.bfloat16)
    mask = jnp.concatenate([stretch_mask(own, own, tokens), cache_mask(own, limit, c_rows, tokens)], axis=0)
    key_rows, value_rows = shard_parts(shard_ref, tokens, c_rows)
    keys = [jnp.concatenate([shard_ref[key_rows, features(head)], mask], axis=1) for head in range(kv_local)]
    values_t = [shard_ref[value_rows, features(head)].T for head in range(kv_local)]
    attend(qt_ref, keys, values_t, None, (high_ref, total_ref, accum_ref))


def held_kernel(
    own_ref, targets_ref, length_ref, q_ref, lists_ref, pool_k, pool_v, rest_ref,
    wide_ref, high_ref, total_ref, mixed_ref,
):
    kv_width = rest_ref.shape[1]
    pool = pool_k.shape[0]
    held = pool * PAGE
    tokens = PAGE * P_DEV
    half = rest_ref.shape[0] // 2
    own = own_ref[0]
    lists = lists_ref[...]
    lengths = length_column(length_ref)
    wide_ref[...] = wide_queries(q_ref, kv_width // HEAD_DIM)
    held_slot = lax.broadcasted_iota(jnp.int32, (1, held), 1) // PAGE
    own_slot = slot_row(targets_ref, own, own, tokens, pool)
    parts = [
        (
            pool_k[...].reshape(held, kv_width),
            pool_v[...].reshape(held, kv_width),
            tally_of(lists, lengths, held_slot),
        ),
        (rest_ref[:tokens], rest_ref[half : half + tokens], tally_of(lists, lengths, own_slot)),
    ]
    high_ref[...], total_ref[...], mixed_ref[...] = decode_attend(wide_ref[...], parts, None)


def hop_kernel(places, qt_ref, near_ref, far_ref, high_in, total_in, accum_in, *refs):
    shard_refs, outs = refs[: len(places)], refs[len(places) :]
    tokens, c_rows = near_ref.shape[1], far_ref.shape[1]
    mask = jnp.concatenate([ref[place] for place in places for ref in (near_ref, far_ref)], axis=0)
    keys, values_t = [], []
    for head in range(qt_ref.shape[0]):
        pieces, values = [], []
        for ref in shard_refs:
            key_rows, value_rows = shard_parts(ref, tokens, c_rows)
            pieces.append(ref[key_rows, features(head)])
            values.append(ref[value_rows, features(head)])
        keys.append(jnp.concatenate([jnp.concatenate(pieces, axis=0), mask], axis=1))
        values_t.append(jnp.concatenate(values, axis=0).T)
    attend(qt_ref, keys, values_t, (high_in, total_in, accum_in), outs)


def split_kernel(pick_ref, shard_ref, keys_ref, stretch_ref, values_ref, pages_ref):
    tokens = pick_ref.shape[1]
    half = shard_ref.shape[0] // 2
    sent = pick_ref.shape[0]
    for place, start in enumerate((0, half)):
        stretch_ref[place * tokens : (place + 1) * tokens] = shard_ref[start : start + tokens]
        rows = jnp.dot(pick_ref[...], shard_ref[start : start + tokens], preferred_element_type=jnp.float32)
        pages_ref[place * sent : (place + 1) * sent] = rows.astype(jnp.bfloat16)
    keys_ref[...] = shard_ref[tokens:half]
    values_ref[...] = shard_ref[half + tokens :]


def near_pages_kernel(count, hops, tokens, pool, own_ref, targets_ref, length_ref, lists_ref, *refs):
    shard_refs, refs = refs[: len(hops) - 1], refs[len(hops) - 1 :]
    wide_ref, dec_high, dec_total, dec_mixed, high_ref, total_ref, mixed_ref, whole_ref, alone_ref = refs
    own = own_ref[0]
    lists = lists_ref[...]
    lengths = length_column(length_ref)
    parts = []
    for hop, ref in zip(hops, shard_refs):
        half = ref.shape[0] // 2
        slot = slot_row(targets_ref, shard_of(own, hop, count), own, tokens, pool)
        parts.append((ref[:tokens], ref[half : half + tokens], tally_of(lists, lengths, slot)))
    state = (dec_high[...], dec_total[...], dec_mixed[...])
    high_ref[...], total_ref[...], mixed_ref[...] = decode_attend(wide_ref[...], parts, state)
    shard = shard_of(own, hops[-1], count)
    attended = shard < own
    whole = jnp.where(attended, slot_row(targets_ref, shard, own, tokens, pool), -1)
    alone = jnp.where(attended, -1, sent_slots(targets_ref, shard, own, tokens // PAGE, pool))
    whole_ref[...] = tally_of(lists, lengths, whole)
    alone_ref[...] = tally_of(lists, lengths, alone)


def score_kernel(
    final, qt_ref, near_ref, far_ref, high_in, total_in, accum_in, keys_ref, stretch_ref,
    weights_ref, total_ref, accum_ref,
):
    kv_local = qt_ref.shape[0]
    tokens, c_rows = near_ref.shape[1], far_ref.shape[1]
    mask = jnp.concatenate([near_ref[final], far_ref[final]], axis=0)
    keys, values_t = [], []
    for head in range(kv_local):
        pieces = [stretch_ref[:tokens, features(head)], keys_ref[:, features(head)]]
        keys.append(jnp.concatenate([jnp.concatenate(pieces, axis=0), mask], axis=1))
        values_t.append(stretch_ref[tokens:, features(head)].T)

    def second(block, scores):
        head, cols = block
        before = (high_in[head, :, cols], total_in[head, :, cols])
        weights, _, total, decay = soften(scores, before)
        weights_ref[head, :, cols] = weights[tokens:]
        total_ref[head, :, cols] = total
        accum_ref[head, :, cols] = accum_in[head, :, cols] * decay + jnp.dot(
            values_t[head], weights[:tokens], preferred_element_type=jnp.float32
        )

    walk(blocks_of(qt_ref), lambda block: scores_of(qt_ref, block[0], block[1], keys[block[0]]), second)


def last_kernel(
    weights_ref, total_ref, accum_ref, values_ref, stretch_ref, pages_ref, whole_ref, alone_ref,
    wide_ref, dec_high, dec_total, dec_mixed, out_ref, dec_out, result_ref, sems,
):
    tokens = result_ref.shape[0]
    sent = pages_ref.shape[0] // 2
    parts = [
        (stretch_ref[:tokens], stretch_ref[tokens:], whole_ref[...]),
        (pages_ref[:sent], pages_ref[sent:], alone_ref[...]),
    ]
    _, total, mixed = decode_attend(wide_ref[...], parts, (dec_high[...], dec_total[...], dec_mixed[...]))
    for head in range(dec_high.shape[0]):
        piece = mixed[head, :, features(head // GROUP)] / total[head]
        dec_out[:, features(head)] = piece.astype(jnp.bfloat16)
    values_t = [values_ref[:, features(head)].T for head in range(weights_ref.shape[0])]
    copies = []

    def first(block):
        head, cols = block
        return jnp.dot(values_t[head], weights_ref[head, :, cols], preferred_element_type=jnp.float32)

    def second(block, mixed):
        head, cols = block
        mixed = mixed + accum_ref[head, :, cols]
        mixed = (mixed * (1.0 / total_ref[head, :, cols])).astype(jnp.bfloat16)
        start = (head * GROUP + cols.start // tokens) * HEAD_DIM
        pieces = (cols.stop - cols.start) // tokens
        for piece in range(pieces):
            col = start + piece * HEAD_DIM
            result_ref[:, col : col + HEAD_DIM] = mixed[:, piece * tokens : (piece + 1) * tokens].T
        span = pl.ds(start, pieces * HEAD_DIM)
        copy = pltpu.make_async_copy(result_ref.at[:, span], out_ref.at[:, span], sems.at[len(copies)])
        copy.start()
        copies.append(copy)

    walk(blocks_of(weights_ref), first, second)
    for copy in copies:
        copy.wait()


def per_device(
    count,
    queries,
    stretch_keys,
    stretch_values,
    cache_keys,
    cache_values,
    prefix_length,
    page_targets,
    pool_keys,
    pool_values,
    decode_queries,
    page_lists,
    context_length,
):
    own = lax.axis_index("ctx")
    own_array = jnp.full((1,), own, jnp.int32)
    tokens, width = queries.shape
    kv_width = stretch_keys.shape[1]
    kv_local = kv_width // HEAD_DIM
    rows = GROUP * tokens
    heads = kv_local * GROUP
    dec_rows = decode_queries.shape[0]
    c_rows = cache_keys.shape[0]
    pool = pool_keys.shape[0]
    f32, bf16 = jnp.float32, jnp.bfloat16
    shape = jax.ShapeDtypeStruct
    params = pltpu.CompilerParams(vmem_limit_bytes=VMEM_BYTES)
    up_pairs = [(i, (i + 1) % count) for i in range(count)]
    down_pairs = [(i, (i - 1) % count) for i in range(count)]
    hops = []
    for far in range(1, count // 2 + 1):
        hops += [-far, far] if far <= (count - 1) // 2 else [-far]

    def send(array, hop):
        return lax.ppermute(array, "ctx", up_pairs if hop < 0 else down_pairs)

    def cost(keys):
        pairs = kv_local * rows * keys
        return pl.CostEstimate(
            flops=4 * pairs * HEAD_DIM, bytes_accessed=4 * rows * kv_local * HEAD_DIM, transcendentals=pairs
        )

    half = tokens + c_rows
    low = jnp.array(-jnp.inf, bf16)
    spread, start = [], 0
    for part in (stretch_keys, cache_keys, stretch_values, cache_values):
        end = 2 * half - start - part.shape[0]
        spread.append(lax.pad(part, low, ((start, end, 0), (0, 0, 0))))
        start += part.shape[0]
    shard = {0: functools.reduce(jnp.maximum, spread)}
    shard[-1] = send(shard[0], -1)

    state_shapes = (
        shape((kv_local, 1, rows), f32),
        shape((kv_local, 1, rows), f32),
        shape((kv_local, HEAD_DIM, rows), f32),
    )
    qt, near, far, pick, *state = pl.pallas_call(
        functools.partial(own_kernel, count, hops),
        out_shape=(
            shape((kv_local, HEAD_DIM + tokens, rows), bf16),
            shape((count - 1, tokens, tokens), bf16),
            shape((count - 1, c_rows, tokens), bf16),
            shape((SEND_CAP * PAGE, tokens), bf16),
        )
        + state_shapes,
        in_specs=[SMEM] * 3 + [VMEM] * 2,
        out_specs=(VMEM,) * 7,
        compiler_params=params,
        cost_estimate=cost(tokens + c_rows),
        name="own_shard",
    )(own_array, prefix_length, page_targets, queries, shard[0])

    dec_shapes = (
        shape((heads, dec_rows, 1), f32),
        shape((heads, dec_rows, 1), f32),
        shape((heads, dec_rows, kv_width), f32),
    )
    wide, *dec_state = pl.pallas_call(
        held_kernel,
        out_shape=(shape((heads * dec_rows, kv_width), bf16),) + dec_shapes,
        in_specs=[SMEM] * 3 + [VMEM] * 5,
        out_specs=(VMEM,) * 4,
        compiler_params=params,
        cost_estimate=pl.CostEstimate(
            flops=4 * 128 * 2048 * 256, bytes_accessed=4 * pool_keys.size, transcendentals=128 * 2048
        ),
        name="decode_held_pages",
    )(own_array, page_targets, context_length, decode_queries, page_lists, pool_keys, pool_values, shard[0])

    if 1 in hops:
        sent_down, state, dec_state = lax.optimization_barrier((shard[0], state, dec_state))
        shard[1] = send(sent_down, 1)
    shard[-1], state, dec_state = lax.optimization_barrier((shard[-1], state, dec_state))
    for hop in hops[2:-1]:
        shard[hop] = send(shard[hop + 1 if hop < 0 else hop - 1], hop)
    hop = hops[-1]
    nearer = shard[hop + 1 if hop < 0 else hop - 1]
    pieces = pl.pallas_call(
        split_kernel,
        out_shape=(
            shape((c_rows, kv_width), bf16),
            shape((2 * tokens, kv_width), bf16),
            shape((c_rows, kv_width), bf16),
            shape((2 * SEND_CAP * PAGE, kv_width), bf16),
        ),
        in_specs=[VMEM] * 2,
        out_specs=(VMEM,) * 4,
        compiler_params=params,
        name="pieces_to_send_on",
    )(pick, nearer)
    last_keys = send(pieces[0], hop)
    attending, others = [], []
    for pair in up_pairs if hop < 0 else down_pairs:
        (attending if (pair[1] + hop) % count < pair[1] else others).append(pair)
    last_stretch = lax.ppermute(pieces[1], "ctx", attending)
    last_pages = lax.ppermute(pieces[3], "ctx", others)
    last_values = send(pieces[2], hop)

    for first in range(len(hops) - 1):
        places = [first]
        state = pl.pallas_call(
            functools.partial(hop_kernel, places),
            out_shape=state_shapes,
            in_specs=[VMEM] * (6 + len(places)),
            out_specs=(VMEM,) * 3,
            compiler_params=params,
            cost_estimate=cost((c_rows + tokens) * len(places)),
            name="whole_shards_" + str(first),
        )(qt, near, far, *state, *[shard[hops[place]] for place in places])

    final = len(hops) - 1
    dec_state, state = lax.optimization_barrier((dec_state, state))
    near_hops = hops[:-1]
    *dec_state, whole, alone = pl.pallas_call(
        functools.partial(near_pages_kernel, count, hops, tokens, pool),
        out_shape=dec_shapes
        + (shape((1, dec_rows, tokens), f32), shape((1, dec_rows, SEND_CAP * PAGE), f32)),
        in_specs=[SMEM] * 3 + [VMEM] * (5 + len(near_hops)),
        out_specs=(VMEM,) * 5,
        compiler_params=params,
        cost_estimate=cost(tokens),
        name="decode_near_pages",
    )(
        own_array, page_targets, context_length, page_lists, *[shard[hop] for hop in near_hops],
        wide, *dec_state,
    )
    dec_state, state = lax.optimization_barrier((dec_state, state))

    weights, total, accum = pl.pallas_call(
        functools.partial(score_kernel, final),
        out_shape=(shape((kv_local, c_rows, rows), bf16),) + state_shapes[1:],
        in_specs=[VMEM] * 8,
        out_specs=(VMEM,) * 3,
        compiler_params=params,
        cost_estimate=cost(half),
        name="last_scores",
    )(qt, near, far, *state, last_keys, last_stretch)

    prefill, decoded = pl.pallas_call(
        last_kernel,
        out_shape=(shape((tokens, width), bf16), shape(decode_queries.shape, bf16)),
        in_specs=[VMEM] * 12,
        out_specs=(HBM, VMEM),
        scratch_shapes=[
            pltpu.VMEM((tokens, width), bf16),
            pltpu.SemaphoreType.DMA((kv_local * max(GROUP // 2, 1),)),
        ],
        compiler_params=params,
        cost_estimate=cost(c_rows // 2),
        name="last_values_and_pages",
    )(weights, total, accum, last_values, last_stretch, last_pages, whole, alone, wide, *dec_state)
    return (prefill, decoded)


def solution(mesh):
    in_specs = (
        P(("groups", "ctx"), "head"),
        P(("groups", "ctx"), "head"),
        P(("groups", "ctx"), "head"),
        P(("groups", "ctx"), "head"),
        P(("groups", "ctx"), "head"),
        P("groups"),
        P("groups"),
        P(("groups", "ctx"), None, "head"),
        P(("groups", "ctx"), None, "head"),
        P(("groups", "ctx"), "head"),
        P(("groups", "ctx"), None),
        P(("groups", "ctx")),
    )
    out_specs = (P(("groups", "ctx"), "head"), P(("groups", "ctx"), "head"))
    return jax.shard_map(
        functools.partial(per_device, mesh.shape["ctx"]),
        mesh=mesh,
        in_specs=in_specs,
        out_specs=out_specs,
        check_vma=False,
    )
```

```python
import functools

import jax
import jax.numpy as jnp
from jax import lax
from jax.experimental import pallas as pl
from jax.experimental.pallas import tpu as pltpu
from jax.sharding import PartitionSpec as P

HEADS = 64
KV_HEADS = 8
HEAD_DIM = 128
GROUP = HEADS // KV_HEADS
PAGE = 16
P_DEV = 8
SEND_CAP = 2
EXP2_SCALE = HEAD_DIM ** (-0.5) * 1.4426950408889634
HIDDEN = -1e30
VMEM_BYTES = 48 * 1024 * 1024

VMEM = pl.BlockSpec(memory_space=pltpu.VMEM)
SMEM = pl.BlockSpec(memory_space=pltpu.SMEM)
HBM = pl.BlockSpec(memory_space=pltpu.HBM)


def scores_of(qt_ref, head, cols, keys):
    return jnp.dot(keys, qt_ref[head, :, cols], preferred_element_type=jnp.float32)


def soften(scores, old):
    high = jnp.max(scores, axis=0, keepdims=True)
    if old is None:
        weights = jnp.exp2((scores - high) * EXP2_SCALE)
        return weights.astype(jnp.bfloat16), high, jnp.sum(weights, axis=0, keepdims=True), None
    old_high, old_total = old
    high = jnp.maximum(high, old_high)
    decay = jnp.exp2((old_high - high) * EXP2_SCALE)
    weights = jnp.exp2((scores - high) * EXP2_SCALE)
    total = old_total * decay + jnp.sum(weights, axis=0, keepdims=True)
    return weights.astype(jnp.bfloat16), high, total, decay


def walk(blocks, first, second):
    ahead = first(blocks[0])
    for place, block in enumerate(blocks):
        current = ahead
        if place + 1 < len(blocks):
            ahead = first(blocks[place + 1])
        second(block, current)


def blocks_of(qt_ref):
    kv_local, _, rows = qt_ref.shape
    width = min(2 * (rows // GROUP), rows)
    return [(head, slice(start, start + width)) for head in range(kv_local) for start in range(0, rows, width)]


def attend(qt_ref, keys, values_t, old, new):
    high_ref, total_ref, accum_ref = new

    def second(block, scores):
        head, cols = block
        before = None if old is None else (old[0][head, :, cols], old[1][head, :, cols])
        weights, high, total, decay = soften(scores, before)
        accum = jnp.dot(values_t[head], weights, preferred_element_type=jnp.float32)
        if old is not None:
            accum = accum + old[2][head, :, cols] * decay
        high_ref[head, :, cols] = high
        total_ref[head, :, cols] = total
        accum_ref[head, :, cols] = accum

    walk(blocks_of(qt_ref), lambda block: scores_of(qt_ref, block[0], block[1], keys[block[0]]), second)


def hidden(seen):
    return jnp.where(seen, jnp.float32(0.0), jnp.float32(HIDDEN)).astype(jnp.bfloat16)


def stretch_mask(shard, own, tokens):
    place = lax.broadcasted_iota(jnp.int32, (tokens, tokens), 0)
    token = lax.broadcasted_iota(jnp.int32, (tokens, tokens), 1)
    return hidden(place - token <= (own - shard) * tokens)


def cache_mask(shard, limit, c_rows, tokens):
    place = lax.broadcasted_iota(jnp.int32, (c_rows, tokens), 0)
    return hidden(place < limit - shard * c_rows)


def slot_row(targets_ref, shard, own, tokens, pool):
    page = lax.broadcasted_iota(jnp.int32, (1, tokens), 1) // PAGE
    slots = jnp.full((1, tokens), -1, jnp.int32)
    for index in range(tokens // PAGE):
        target = targets_ref[shard * (tokens // PAGE) + index]
        slot = jnp.where(lax.div(target, P_DEV) == own, pool + lax.rem(target, P_DEV), -1)
        slots = jnp.where(page == index, slot, slots)
    return slots


def sent_pages(targets_ref, shard, owner, pages):
    one, two = jnp.int32(-1), jnp.int32(-1)
    for index in range(pages):
        hit = lax.div(targets_ref[shard * pages + index], P_DEV) == owner
        two = jnp.where(hit & (one >= 0) & (two < 0), index, two)
        one = jnp.where(hit & (one < 0), index, one)
    return one, two


def sent_slots(targets_ref, shard, owner, pages, pool):
    place = lax.broadcasted_iota(jnp.int32, (1, SEND_CAP * PAGE), 1)
    slots = []
    for index in sent_pages(targets_ref, shard, owner, pages):
        target = targets_ref[shard * pages + jnp.maximum(index, 0)]
        slots.append(jnp.where(index >= 0, pool + lax.rem(target, P_DEV), -1))
    return jnp.where(place < PAGE, slots[0], slots[1])


def length_column(length_ref):
    rows = length_ref.shape[0]
    place = lax.broadcasted_iota(jnp.int32, (rows, 1), 0)
    lengths = jnp.zeros((rows, 1), jnp.int32)
    for row in range(rows):
        lengths = jnp.where(place == row, length_ref[row], lengths)
    return lengths


def tally_of(lists, lengths, slot):
    rows, span = lists.shape
    tokens = slot.shape[1]
    slot = jnp.broadcast_to(slot, (rows, tokens))
    offset = lax.rem(lax.broadcasted_iota(jnp.int32, (rows, tokens), 1), PAGE)
    tally = jnp.zeros((rows, tokens), jnp.float32)
    for entry in range(span):
        hit = (slot == lists[:, entry : entry + 1]) & (offset < lengths - entry * PAGE)
        tally = tally + jnp.where(hit, jnp.float32(1.0), jnp.float32(0.0))
    return tally[None]


def shard_of(own, hop, count):
    return lax.rem(own + hop + count, count)


def wide_queries(q_ref, kv_local):
    heads = q_ref.shape[1] // HEAD_DIM
    queries = q_ref[...].astype(jnp.float32)
    stacked = []
    for head in range(heads):
        piece = queries[:, head * HEAD_DIM : (head + 1) * HEAD_DIM]
        blank = jnp.zeros_like(piece)
        stacked.append(
            jnp.concatenate([piece if kv == head // GROUP else blank for kv in range(kv_local)], axis=1)
        )
    return jnp.concatenate(stacked, axis=0).astype(jnp.bfloat16)


def decode_attend(queries, parts, state):
    done = []
    for keys, values, tally in parts:
        scores = lax.dot_general(
            queries, keys, (((1,), (1,)), ((), ())), preferred_element_type=jnp.float32
        ).reshape(-1, tally.shape[1], tally.shape[2])
        done.append((jnp.where(tally > 0, scores, jnp.float32(HIDDEN)), tally, values))
    highs = [jnp.max(scores, axis=-1, keepdims=True) for scores, _, _ in done]
    if state is not None:
        old_high, old_total, old_mixed = state
        highs.append(old_high)
    high = functools.reduce(jnp.maximum, highs)
    total, mixed = 0.0, 0.0
    if state is not None:
        decay = jnp.exp2((old_high - high) * EXP2_SCALE)
        total = old_total * decay
        mixed = old_mixed * decay
    for scores, tally, values in done:
        weights = jnp.exp2((scores - high) * EXP2_SCALE) * tally
        total = total + jnp.sum(weights, axis=-1, keepdims=True)
        mixed = mixed + jnp.dot(
            weights.reshape(queries.shape[0], -1).astype(jnp.bfloat16),
            values,
            preferred_element_type=jnp.float32,
        ).reshape(high.shape[0], high.shape[1], -1)
    return high, total, mixed


def features(head):
    return slice(head * HEAD_DIM, (head + 1) * HEAD_DIM)


def shard_parts(ref, tokens, c_rows):
    return slice(0, tokens + c_rows), slice(tokens + c_rows, 2 * (tokens + c_rows))


def own_kernel(
    count, hops, own_ref, limit_ref, targets_ref, q_ref, shard_ref,
    qt_ref, near_ref, far_ref, pick_ref, high_ref, total_ref, accum_ref,
):
    kv_local, _, rows = qt_ref.shape
    tokens = q_ref.shape[0]
    c_rows = far_ref.shape[1]
    own = own_ref[0]
    limit = limit_ref[0]
    place = lax.broadcasted_iota(jnp.int32, (tokens, tokens), 0)
    token = lax.broadcasted_iota(jnp.int32, (tokens, tokens), 1)
    pick = jnp.where(place == token, jnp.float32(1.0), jnp.float32(0.0)).astype(jnp.bfloat16)
    for head in range(kv_local):
        for sub in range(GROUP):
            cols = slice(sub * tokens, (sub + 1) * tokens)
            qt_ref[head, :HEAD_DIM, cols] = q_ref[:, features(head * GROUP + sub)].T
            qt_ref[head, HEAD_DIM:, cols] = pick
    for place, hop in enumerate(hops):
        shard = shard_of(own, hop, count)
        near_ref[place] = stretch_mask(shard, own, tokens)
        far_ref[place] = cache_mask(shard, limit, c_rows, tokens)
    onward = 1 if hops[-1] < 0 else -1
    pages = tokens // PAGE
    one, two = sent_pages(
        targets_ref, shard_of(own, hops[-1] + onward, count), shard_of(own, onward, count), pages
    )
    row = lax.broadcasted_iota(jnp.int32, pick_ref.shape, 0)
    token = lax.broadcasted_iota(jnp.int32, pick_ref.shape, 1)
    sent = ((row < PAGE) & (one >= 0) & (token == row + one * PAGE)) | (
        (row >= PAGE) & (two >= 0) & (token == row + (two - 1) * PAGE)
    )
    pick_ref[...] = jnp.where(sent, jnp.float32(1.0), jnp.float32(0.0)).astype(jnp.bfloat16)
    mask = jnp.concatenate([stretch_mask(own, own, tokens), cache_mask(own, limit, c_rows, tokens)], axis=0)
    key_rows, value_rows = shard_parts(shard_ref, tokens, c_rows)
    keys = [jnp.concatenate([shard_ref[key_rows, features(head)], mask], axis=1) for head in range(kv_local)]
    values_t = [shard_ref[value_rows, features(head)].T for head in range(kv_local)]
    attend(qt_ref, keys, values_t, None, (high_ref, total_ref, accum_ref))


def held_kernel(
    own_ref, targets_ref, length_ref, q_ref, lists_ref, pool_k, pool_v, rest_ref,
    wide_ref, high_ref, total_ref, mixed_ref,
):
    kv_width = rest_ref.shape[1]
    pool = pool_k.shape[0]
    held = pool * PAGE
    tokens = PAGE * P_DEV
    half = rest_ref.shape[0] // 2
    own = own_ref[0]
    lists = lists_ref[...]
    lengths = length_column(length_ref)
    wide_ref[...] = wide_queries(q_ref, kv_width // HEAD_DIM)
    held_slot = lax.broadcasted_iota(jnp.int32, (1, held), 1) // PAGE
    own_slot = slot_row(targets_ref, own, own, tokens, pool)
    parts = [
        (
            pool_k[...].reshape(held, kv_width),
            pool_v[...].reshape(held, kv_width),
            tally_of(lists, lengths, held_slot),
        ),
        (rest_ref[:tokens], rest_ref[half : half + tokens], tally_of(lists, lengths, own_slot)),
    ]
    high_ref[...], total_ref[...], mixed_ref[...] = decode_attend(wide_ref[...], parts, None)


def hop_kernel(places, qt_ref, near_ref, far_ref, high_in, total_in, accum_in, *refs):
    shard_refs, outs = refs[: len(places)], refs[len(places) :]
    tokens, c_rows = near_ref.shape[1], far_ref.shape[1]
    mask = jnp.concatenate([ref[place] for place in places for ref in (near_ref, far_ref)], axis=0)
    keys, values_t = [], []
    for head in range(qt_ref.shape[0]):
        pieces, values = [], []
        for ref in shard_refs:
            key_rows, value_rows = shard_parts(ref, tokens, c_rows)
            pieces.append(ref[key_rows, features(head)])
            values.append(ref[value_rows, features(head)])
        keys.append(jnp.concatenate([jnp.concatenate(pieces, axis=0), mask], axis=1))
        values_t.append(jnp.concatenate(values, axis=0).T)
    attend(qt_ref, keys, values_t, (high_in, total_in, accum_in), outs)


def split_kernel(pick_ref, shard_ref, keys_ref, stretch_ref, values_ref, pages_ref):
    tokens = pick_ref.shape[1]
    half = shard_ref.shape[0] // 2
    sent = pick_ref.shape[0]
    for place, start in enumerate((0, half)):
        stretch_ref[place * tokens : (place + 1) * tokens] = shard_ref[start : start + tokens]
        rows = jnp.dot(pick_ref[...], shard_ref[start : start + tokens], preferred_element_type=jnp.float32)
        pages_ref[place * sent : (place + 1) * sent] = rows.astype(jnp.bfloat16)
    keys_ref[...] = shard_ref[tokens:half]
    values_ref[...] = shard_ref[half + tokens :]


def near_pages_kernel(count, hops, tokens, pool, own_ref, targets_ref, length_ref, lists_ref, *refs):
    shard_refs, refs = refs[: len(hops) - 1], refs[len(hops) - 1 :]
    wide_ref, dec_high, dec_total, dec_mixed, high_ref, total_ref, mixed_ref, tally_ref = refs
    own = own_ref[0]
    lists = lists_ref[...]
    lengths = length_column(length_ref)
    parts = []
    for hop, ref in zip(hops, shard_refs):
        half = ref.shape[0] // 2
        slot = slot_row(targets_ref, shard_of(own, hop, count), own, tokens, pool)
        parts.append((ref[:tokens], ref[half : half + tokens], tally_of(lists, lengths, slot)))
    state = (dec_high[...], dec_total[...], dec_mixed[...])
    high_ref[...], total_ref[...], mixed_ref[...] = decode_attend(wide_ref[...], parts, state)
    shard = shard_of(own, hops[-1], count)
    attended = shard < own
    whole = jnp.where(attended, slot_row(targets_ref, shard, own, tokens, pool), -1)
    alone = jnp.where(attended, -1, sent_slots(targets_ref, shard, own, tokens // PAGE, pool))
    tally_ref[:, :, :tokens] = tally_of(lists, lengths, whole)
    tally_ref[:, :, tokens:] = tally_of(lists, lengths, alone)


def score_kernel(
    final, qt_ref, near_ref, far_ref, high_in, total_in, accum_in, keys_ref, stretch_ref,
    weights_ref, total_ref, accum_ref,
):
    kv_local = qt_ref.shape[0]
    tokens, c_rows = near_ref.shape[1], far_ref.shape[1]
    mask = jnp.concatenate([near_ref[final], far_ref[final]], axis=0)
    keys, values_t = [], []
    for head in range(kv_local):
        pieces = [stretch_ref[:tokens, features(head)], keys_ref[:, features(head)]]
        keys.append(jnp.concatenate([jnp.concatenate(pieces, axis=0), mask], axis=1))
        values_t.append(stretch_ref[tokens:, features(head)].T)

    def second(block, scores):
        head, cols = block
        before = (high_in[head, :, cols], total_in[head, :, cols])
        weights, _, total, decay = soften(scores, before)
        weights_ref[head, :, cols] = weights[tokens:]
        total_ref[head, :, cols] = total
        accum_ref[head, :, cols] = accum_in[head, :, cols] * decay + jnp.dot(
            values_t[head], weights[:tokens], preferred_element_type=jnp.float32
        )

    walk(blocks_of(qt_ref), lambda block: scores_of(qt_ref, block[0], block[1], keys[block[0]]), second)


def last_kernel(
    weights_ref, total_ref, accum_ref, values_ref, stretch_ref, pages_ref, tally_ref,
    wide_ref, dec_high, dec_total, dec_mixed, out_ref, dec_out, result_ref, sems,
):
    tokens = result_ref.shape[0]
    values_t = [values_ref[:, features(head)].T for head in range(weights_ref.shape[0])]
    copies = []

    def first(block):
        head, cols = block
        return jnp.dot(values_t[head], weights_ref[head, :, cols], preferred_element_type=jnp.float32)

    def second(block, mixed):
        head, cols = block
        mixed = mixed + accum_ref[head, :, cols]
        mixed = (mixed * (1.0 / total_ref[head, :, cols])).astype(jnp.bfloat16)
        start = (head * GROUP + cols.start // tokens) * HEAD_DIM
        pieces = (cols.stop - cols.start) // tokens
        for piece in range(pieces):
            col = start + piece * HEAD_DIM
            result_ref[:, col : col + HEAD_DIM] = mixed[:, piece * tokens : (piece + 1) * tokens].T
        span = pl.ds(start, pieces * HEAD_DIM)
        copy = pltpu.make_async_copy(result_ref.at[:, span], out_ref.at[:, span], sems.at[len(copies)])
        copy.start()
        copies.append(copy)

    walk(blocks_of(weights_ref), first, second)

    sent = pages_ref.shape[0] // 2
    keys = jnp.concatenate([stretch_ref[:tokens], pages_ref[:sent]], axis=0)
    values = jnp.concatenate([stretch_ref[tokens:], pages_ref[sent:]], axis=0)
    state = (dec_high[...], dec_total[...], dec_mixed[...])
    _, total, mixed = decode_attend(wide_ref[...], [(keys, values, tally_ref[...])], state)
    share = 1.0 / total
    for head in range(dec_high.shape[0]):
        piece = mixed[head, :, features(head // GROUP)] * share[head]
        dec_out[:, features(head)] = piece.astype(jnp.bfloat16)
    for copy in copies:
        copy.wait()


def per_device(
    count,
    queries,
    stretch_keys,
    stretch_values,
    cache_keys,
    cache_values,
    prefix_length,
    page_targets,
    pool_keys,
    pool_values,
    decode_queries,
    page_lists,
    context_length,
):
    own = lax.axis_index("ctx")
    own_array = jnp.full((1,), own, jnp.int32)
    tokens, width = queries.shape
    kv_width = stretch_keys.shape[1]
    kv_local = kv_width // HEAD_DIM
    rows = GROUP * tokens
    heads = kv_local * GROUP
    dec_rows = decode_queries.shape[0]
    c_rows = cache_keys.shape[0]
    pool = pool_keys.shape[0]
    f32, bf16 = jnp.float32, jnp.bfloat16
    shape = jax.ShapeDtypeStruct
    params = pltpu.CompilerParams(vmem_limit_bytes=VMEM_BYTES)
    up_pairs = [(i, (i + 1) % count) for i in range(count)]
    down_pairs = [(i, (i - 1) % count) for i in range(count)]
    hops = []
    for far in range(1, count // 2 + 1):
        hops += [-far, far] if far <= (count - 1) // 2 else [-far]

    def send(array, hop):
        return lax.ppermute(array, "ctx", up_pairs if hop < 0 else down_pairs)

    def cost(keys):
        pairs = kv_local * rows * keys
        return pl.CostEstimate(
            flops=4 * pairs * HEAD_DIM, bytes_accessed=4 * rows * kv_local * HEAD_DIM, transcendentals=pairs
        )

    half = tokens + c_rows
    low = jnp.array(-jnp.inf, bf16)
    spread, start = [], 0
    for part in (stretch_keys, cache_keys, stretch_values, cache_values):
        end = 2 * half - start - part.shape[0]
        spread.append(lax.pad(part, low, ((start, end, 0), (0, 0, 0))))
        start += part.shape[0]
    shard = {0: functools.reduce(jnp.maximum, spread)}
    shard[-1] = send(shard[0], -1)

    state_shapes = (
        shape((kv_local, 1, rows), f32),
        shape((kv_local, 1, rows), f32),
        shape((kv_local, HEAD_DIM, rows), f32),
    )
    qt, near, far, pick, *state = pl.pallas_call(
        functools.partial(own_kernel, count, hops),
        out_shape=(
            shape((kv_local, HEAD_DIM + tokens, rows), bf16),
            shape((count - 1, tokens, tokens), bf16),
            shape((count - 1, c_rows, tokens), bf16),
            shape((SEND_CAP * PAGE, tokens), bf16),
        )
        + state_shapes,
        in_specs=[SMEM] * 3 + [VMEM] * 2,
        out_specs=(VMEM,) * 7,
        compiler_params=params,
        cost_estimate=cost(tokens + c_rows),
        name="own_shard",
    )(own_array, prefix_length, page_targets, queries, shard[0])

    dec_shapes = (
        shape((heads, dec_rows, 1), f32),
        shape((heads, dec_rows, 1), f32),
        shape((heads, dec_rows, kv_width), f32),
    )
    wide, *dec_state = pl.pallas_call(
        held_kernel,
        out_shape=(shape((heads * dec_rows, kv_width), bf16),) + dec_shapes,
        in_specs=[SMEM] * 3 + [VMEM] * 5,
        out_specs=(VMEM,) * 4,
        compiler_params=params,
        cost_estimate=pl.CostEstimate(
            flops=4 * 128 * 2048 * 256, bytes_accessed=4 * pool_keys.size, transcendentals=128 * 2048
        ),
        name="decode_held_pages",
    )(own_array, page_targets, context_length, decode_queries, page_lists, pool_keys, pool_values, shard[0])

    if 1 in hops:
        sent_down, state, dec_state = lax.optimization_barrier((shard[0], state, dec_state))
        shard[1] = send(sent_down, 1)
    shard[-1], state, dec_state = lax.optimization_barrier((shard[-1], state, dec_state))
    for hop in hops[2:-1]:
        shard[hop] = send(shard[hop + 1 if hop < 0 else hop - 1], hop)
    hop = hops[-1]
    nearer = shard[hop + 1 if hop < 0 else hop - 1]
    pieces = pl.pallas_call(
        split_kernel,
        out_shape=(
            shape((c_rows, kv_width), bf16),
            shape((2 * tokens, kv_width), bf16),
            shape((c_rows, kv_width), bf16),
            shape((2 * SEND_CAP * PAGE, kv_width), bf16),
        ),
        in_specs=[VMEM] * 2,
        out_specs=(VMEM,) * 4,
        compiler_params=params,
        name="pieces_to_send_on",
    )(pick, nearer)
    last_keys = send(pieces[0], hop)
    attending, others = [], []
    for pair in up_pairs if hop < 0 else down_pairs:
        (attending if (pair[1] + hop) % count < pair[1] else others).append(pair)
    last_stretch = lax.ppermute(pieces[1], "ctx", attending)
    last_pages = lax.ppermute(pieces[3], "ctx", others)
    last_values = send(pieces[2], hop)

    for first in range(len(hops) - 1):
        places = [first]
        state = pl.pallas_call(
            functools.partial(hop_kernel, places),
            out_shape=state_shapes,
            in_specs=[VMEM] * (6 + len(places)),
            out_specs=(VMEM,) * 3,
            compiler_params=params,
            cost_estimate=cost((c_rows + tokens) * len(places)),
            name="whole_shards_" + str(first),
        )(qt, near, far, *state, *[shard[hops[place]] for place in places])

    final = len(hops) - 1
    dec_state, state = lax.optimization_barrier((dec_state, state))
    near_hops = hops[:-1]
    *dec_state, tally = pl.pallas_call(
        functools.partial(near_pages_kernel, count, hops, tokens, pool),
        out_shape=dec_shapes
        + (shape((1, dec_rows, tokens + SEND_CAP * PAGE), f32),),
        in_specs=[SMEM] * 3 + [VMEM] * (5 + len(near_hops)),
        out_specs=(VMEM,) * 4,
        compiler_params=params,
        cost_estimate=cost(tokens),
        name="decode_near_pages",
    )(
        own_array, page_targets, context_length, page_lists, *[shard[hop] for hop in near_hops],
        wide, *dec_state,
    )
    dec_state, state = lax.optimization_barrier((dec_state, state))

    weights, total, accum = pl.pallas_call(
        functools.partial(score_kernel, final),
        out_shape=(shape((kv_local, c_rows, rows), bf16),) + state_shapes[1:],
        in_specs=[VMEM] * 8,
        out_specs=(VMEM,) * 3,
        compiler_params=params,
        cost_estimate=cost(half),
        name="last_scores",
    )(qt, near, far, *state, last_keys, last_stretch)

    prefill, decoded = pl.pallas_call(
        last_kernel,
        out_shape=(shape((tokens, width), bf16), shape(decode_queries.shape, bf16)),
        in_specs=[VMEM] * 11,
        out_specs=(HBM, VMEM),
        scratch_shapes=[
            pltpu.VMEM((tokens, width), bf16),
            pltpu.SemaphoreType.DMA((kv_local * max(GROUP // 2, 1),)),
        ],
        compiler_params=params,
        cost_estimate=cost(c_rows // 2),
        name="last_values_and_pages",
    )(weights, total, accum, last_values, last_stretch, last_pages, tally, wide, *dec_state)
    return (prefill, decoded)


def solution(mesh):
    in_specs = (
        P(("groups", "ctx"), "head"),
        P(("groups", "ctx"), "head"),
        P(("groups", "ctx"), "head"),
        P(("groups", "ctx"), "head"),
        P(("groups", "ctx"), "head"),
        P("groups"),
        P("groups"),
        P(("groups", "ctx"), None, "head"),
        P(("groups", "ctx"), None, "head"),
        P(("groups", "ctx"), "head"),
        P(("groups", "ctx"), None),
        P(("groups", "ctx")),
    )
    out_specs = (P(("groups", "ctx"), "head"), P(("groups", "ctx"), "head"))
    return jax.shard_map(
        functools.partial(per_device, mesh.shape["ctx"]),
        mesh=mesh,
        in_specs=in_specs,
        out_specs=out_specs,
        check_vma=False,
    )
```

```python
import functools

import jax
import jax.numpy as jnp
from jax import lax
from jax.experimental import pallas as pl
from jax.experimental.pallas import tpu as pltpu
from jax.sharding import PartitionSpec as P

HEADS = 64
KV_HEADS = 8
HEAD_DIM = 128
GROUP = HEADS // KV_HEADS
PAGE = 16
P_DEV = 8
SEND_CAP = 2
EXP2_SCALE = HEAD_DIM ** (-0.5) * 1.4426950408889634
HIDDEN = -1e30
VMEM_BYTES = 48 * 1024 * 1024

VMEM = pl.BlockSpec(memory_space=pltpu.VMEM)
SMEM = pl.BlockSpec(memory_space=pltpu.SMEM)
HBM = pl.BlockSpec(memory_space=pltpu.HBM)


def scores_of(qt_ref, head, cols, keys):
    return jnp.dot(keys, qt_ref[head, :, cols], preferred_element_type=jnp.float32)


def soften(scores, old):
    high = jnp.max(scores, axis=0, keepdims=True)
    if old is None:
        weights = jnp.exp2((scores - high) * EXP2_SCALE)
        return weights.astype(jnp.bfloat16), high, jnp.sum(weights, axis=0, keepdims=True), None
    old_high, old_total = old
    high = jnp.maximum(high, old_high)
    decay = jnp.exp2((old_high - high) * EXP2_SCALE)
    weights = jnp.exp2((scores - high) * EXP2_SCALE)
    total = old_total * decay + jnp.sum(weights, axis=0, keepdims=True)
    return weights.astype(jnp.bfloat16), high, total, decay


def walk(blocks, first, second):
    ahead = first(blocks[0])
    for place, block in enumerate(blocks):
        current = ahead
        if place + 1 < len(blocks):
            ahead = first(blocks[place + 1])
        second(block, current)


def blocks_of(qt_ref):
    kv_local, _, rows = qt_ref.shape
    width = min(2 * (rows // GROUP), rows)
    return [(head, slice(start, start + width)) for head in range(kv_local) for start in range(0, rows, width)]


def attend(qt_ref, keys, values_t, old, new):
    high_ref, total_ref, accum_ref = new

    def second(block, scores):
        head, cols = block
        before = None if old is None else (old[0][head, :, cols], old[1][head, :, cols])
        weights, high, total, decay = soften(scores, before)
        accum = jnp.dot(values_t[head], weights, preferred_element_type=jnp.float32)
        if old is not None:
            accum = accum + old[2][head, :, cols] * decay
        high_ref[head, :, cols] = high
        total_ref[head, :, cols] = total
        accum_ref[head, :, cols] = accum

    walk(blocks_of(qt_ref), lambda block: scores_of(qt_ref, block[0], block[1], keys[block[0]]), second)


def hidden(seen):
    return jnp.where(seen, jnp.float32(0.0), jnp.float32(HIDDEN)).astype(jnp.bfloat16)


def stretch_mask(shard, own, tokens):
    place = lax.broadcasted_iota(jnp.int32, (tokens, tokens), 0)
    token = lax.broadcasted_iota(jnp.int32, (tokens, tokens), 1)
    return hidden(place - token <= (own - shard) * tokens)


def cache_mask(shard, limit, c_rows, tokens):
    place = lax.broadcasted_iota(jnp.int32, (c_rows, tokens), 0)
    return hidden(place < limit - shard * c_rows)


def slot_row(targets_ref, shard, own, tokens, pool):
    page = lax.broadcasted_iota(jnp.int32, (1, tokens), 1) // PAGE
    slots = jnp.full((1, tokens), -1, jnp.int32)
    for index in range(tokens // PAGE):
        target = targets_ref[shard * (tokens // PAGE) + index]
        slot = jnp.where(lax.div(target, P_DEV) == own, pool + lax.rem(target, P_DEV), -1)
        slots = jnp.where(page == index, slot, slots)
    return slots


def sent_pages(targets_ref, shard, owner, pages):
    one, two = jnp.int32(-1), jnp.int32(-1)
    for index in range(pages):
        hit = lax.div(targets_ref[shard * pages + index], P_DEV) == owner
        two = jnp.where(hit & (one >= 0) & (two < 0), index, two)
        one = jnp.where(hit & (one < 0), index, one)
    return one, two


def sent_slots(targets_ref, shard, owner, pages, pool):
    place = lax.broadcasted_iota(jnp.int32, (1, SEND_CAP * PAGE), 1)
    slots = []
    for index in sent_pages(targets_ref, shard, owner, pages):
        target = targets_ref[shard * pages + jnp.maximum(index, 0)]
        slots.append(jnp.where(index >= 0, pool + lax.rem(target, P_DEV), -1))
    return jnp.where(place < PAGE, slots[0], slots[1])


def length_column(length_ref):
    rows = length_ref.shape[0]
    place = lax.broadcasted_iota(jnp.int32, (rows, 1), 0)
    lengths = jnp.zeros((rows, 1), jnp.int32)
    for row in range(rows):
        lengths = jnp.where(place == row, length_ref[row], lengths)
    return lengths


def tally_of(lists, lengths, slot):
    rows, span = lists.shape
    tokens = slot.shape[1]
    slot = jnp.broadcast_to(slot, (rows, tokens))
    offset = lax.rem(lax.broadcasted_iota(jnp.int32, (rows, tokens), 1), PAGE)
    tally = jnp.zeros((rows, tokens), jnp.float32)
    for entry in range(span):
        hit = (slot == lists[:, entry : entry + 1]) & (offset < lengths - entry * PAGE)
        tally = tally + jnp.where(hit, jnp.float32(1.0), jnp.float32(0.0))
    return tally[None]


def shard_of(own, hop, count):
    return lax.rem(own + hop + count, count)


def wide_queries(q_ref, kv_local):
    heads = q_ref.shape[1] // HEAD_DIM
    queries = q_ref[...].astype(jnp.float32)
    stacked = []
    for head in range(heads):
        piece = queries[:, head * HEAD_DIM : (head + 1) * HEAD_DIM]
        blank = jnp.zeros_like(piece)
        stacked.append(
            jnp.concatenate([piece if kv == head // GROUP else blank for kv in range(kv_local)], axis=1)
        )
    return jnp.concatenate(stacked, axis=0).astype(jnp.bfloat16)


def decode_attend(queries, parts, state):
    done = []
    for keys, values, tally in parts:
        scores = lax.dot_general(
            queries, keys, (((1,), (1,)), ((), ())), preferred_element_type=jnp.float32
        ).reshape(-1, tally.shape[1], tally.shape[2])
        done.append((jnp.where(tally > 0, scores, jnp.float32(HIDDEN)), tally, values))
    highs = [jnp.max(scores, axis=-1, keepdims=True) for scores, _, _ in done]
    if state is not None:
        old_high, old_total, old_mixed = state
        highs.append(old_high)
    high = functools.reduce(jnp.maximum, highs)
    total, mixed = 0.0, 0.0
    if state is not None:
        decay = jnp.exp2((old_high - high) * EXP2_SCALE)
        total = old_total * decay
        mixed = old_mixed * decay
    for scores, tally, values in done:
        weights = jnp.exp2((scores - high) * EXP2_SCALE) * tally
        total = total + jnp.sum(weights, axis=-1, keepdims=True)
        mixed = mixed + jnp.dot(
            weights.reshape(queries.shape[0], -1).astype(jnp.bfloat16),
            values,
            preferred_element_type=jnp.float32,
        ).reshape(high.shape[0], high.shape[1], -1)
    return high, total, mixed


def features(head):
    return slice(head * HEAD_DIM, (head + 1) * HEAD_DIM)


def shard_parts(ref, tokens, c_rows):
    return slice(0, tokens + c_rows), slice(tokens + c_rows, 2 * (tokens + c_rows))


def own_kernel(
    count, hops, own_ref, limit_ref, targets_ref, q_ref, shard_ref,
    qt_ref, near_ref, far_ref, pick_ref, high_ref, total_ref, accum_ref,
):
    kv_local, _, rows = qt_ref.shape
    tokens = q_ref.shape[0]
    c_rows = far_ref.shape[1]
    own = own_ref[0]
    limit = limit_ref[0]
    place = lax.broadcasted_iota(jnp.int32, (tokens, tokens), 0)
    token = lax.broadcasted_iota(jnp.int32, (tokens, tokens), 1)
    pick = jnp.where(place == token, jnp.float32(1.0), jnp.float32(0.0)).astype(jnp.bfloat16)
    for head in range(kv_local):
        for sub in range(GROUP):
            cols = slice(sub * tokens, (sub + 1) * tokens)
            qt_ref[head, :HEAD_DIM, cols] = q_ref[:, features(head * GROUP + sub)].T
            qt_ref[head, HEAD_DIM:, cols] = pick
    for place, hop in enumerate(hops):
        shard = shard_of(own, hop, count)
        near_ref[place] = stretch_mask(shard, own, tokens)
        far_ref[place] = cache_mask(shard, limit, c_rows, tokens)
    onward = 1 if hops[-1] < 0 else -1
    pages = tokens // PAGE
    one, two = sent_pages(
        targets_ref, shard_of(own, hops[-1] + onward, count), shard_of(own, onward, count), pages
    )
    row = lax.broadcasted_iota(jnp.int32, pick_ref.shape, 0)
    token = lax.broadcasted_iota(jnp.int32, pick_ref.shape, 1)
    sent = ((row < PAGE) & (one >= 0) & (token == row + one * PAGE)) | (
        (row >= PAGE) & (two >= 0) & (token == row + (two - 1) * PAGE)
    )
    pick_ref[...] = jnp.where(sent, jnp.float32(1.0), jnp.float32(0.0)).astype(jnp.bfloat16)
    mask = jnp.concatenate([stretch_mask(own, own, tokens), cache_mask(own, limit, c_rows, tokens)], axis=0)
    key_rows, value_rows = shard_parts(shard_ref, tokens, c_rows)
    keys = [jnp.concatenate([shard_ref[key_rows, features(head)], mask], axis=1) for head in range(kv_local)]
    values_t = [shard_ref[value_rows, features(head)].T for head in range(kv_local)]
    attend(qt_ref, keys, values_t, None, (high_ref, total_ref, accum_ref))


def held_kernel(
    own_ref, targets_ref, length_ref, q_ref, lists_ref, pool_k, pool_v, rest_ref,
    wide_ref, high_ref, total_ref, mixed_ref,
):
    kv_width = rest_ref.shape[1]
    pool = pool_k.shape[0]
    held = pool * PAGE
    tokens = PAGE * P_DEV
    half = rest_ref.shape[0] // 2
    own = own_ref[0]
    lists = lists_ref[...]
    lengths = length_column(length_ref)
    wide_ref[...] = wide_queries(q_ref, kv_width // HEAD_DIM)
    held_slot = lax.broadcasted_iota(jnp.int32, (1, held), 1) // PAGE
    own_slot = slot_row(targets_ref, own, own, tokens, pool)
    parts = [
        (
            pool_k[...].reshape(held, kv_width),
            pool_v[...].reshape(held, kv_width),
            tally_of(lists, lengths, held_slot),
        ),
        (rest_ref[:tokens], rest_ref[half : half + tokens], tally_of(lists, lengths, own_slot)),
    ]
    high_ref[...], total_ref[...], mixed_ref[...] = decode_attend(wide_ref[...], parts, None)


def hop_kernel(places, qt_ref, near_ref, far_ref, high_in, total_in, accum_in, *refs):
    shard_refs, outs = refs[: len(places)], refs[len(places) :]
    tokens, c_rows = near_ref.shape[1], far_ref.shape[1]
    mask = jnp.concatenate([ref[place] for place in places for ref in (near_ref, far_ref)], axis=0)
    keys, values_t = [], []
    for head in range(qt_ref.shape[0]):
        pieces, values = [], []
        for ref in shard_refs:
            key_rows, value_rows = shard_parts(ref, tokens, c_rows)
            pieces.append(ref[key_rows, features(head)])
            values.append(ref[value_rows, features(head)])
        keys.append(jnp.concatenate([jnp.concatenate(pieces, axis=0), mask], axis=1))
        values_t.append(jnp.concatenate(values, axis=0).T)
    attend(qt_ref, keys, values_t, (high_in, total_in, accum_in), outs)


def split_kernel(pick_ref, shard_ref, keys_ref, stretch_ref, values_ref, pages_ref):
    tokens = pick_ref.shape[1]
    half = shard_ref.shape[0] // 2
    sent = pick_ref.shape[0]
    for place, start in enumerate((0, half)):
        stretch_ref[place * tokens : (place + 1) * tokens] = shard_ref[start : start + tokens]
        rows = jnp.dot(pick_ref[...], shard_ref[start : start + tokens], preferred_element_type=jnp.float32)
        pages_ref[place * sent : (place + 1) * sent] = rows.astype(jnp.bfloat16)
    keys_ref[...] = shard_ref[tokens:half]
    values_ref[...] = shard_ref[half + tokens :]


def near_pages_kernel(count, hops, tokens, pool, own_ref, targets_ref, length_ref, lists_ref, *refs):
    shard_refs, refs = refs[: len(hops) - 1], refs[len(hops) - 1 :]
    wide_ref, dec_high, dec_total, dec_mixed, high_ref, total_ref, mixed_ref, tally_ref = refs
    own = own_ref[0]
    lists = lists_ref[...]
    lengths = length_column(length_ref)
    parts = []
    for hop, ref in zip(hops, shard_refs):
        half = ref.shape[0] // 2
        slot = slot_row(targets_ref, shard_of(own, hop, count), own, tokens, pool)
        parts.append((ref[:tokens], ref[half : half + tokens], tally_of(lists, lengths, slot)))
    state = (dec_high[...], dec_total[...], dec_mixed[...])
    high_ref[...], total_ref[...], mixed_ref[...] = decode_attend(wide_ref[...], parts, state)
    shard = shard_of(own, hops[-1], count)
    attended = shard < own
    whole = jnp.where(attended, slot_row(targets_ref, shard, own, tokens, pool), -1)
    alone = jnp.where(attended, -1, sent_slots(targets_ref, shard, own, tokens // PAGE, pool))
    tally_ref[:, :, :tokens] = tally_of(lists, lengths, whole)
    tally_ref[:, :, tokens:] = tally_of(lists, lengths, alone)


def score_kernel(
    final, qt_ref, near_ref, far_ref, high_in, total_in, accum_in, keys_ref, stretch_ref,
    weights_ref, total_ref, accum_ref,
):
    kv_local = qt_ref.shape[0]
    tokens, c_rows = near_ref.shape[1], far_ref.shape[1]
    mask = jnp.concatenate([near_ref[final], far_ref[final]], axis=0)
    keys, values_t = [], []
    for head in range(kv_local):
        pieces = [stretch_ref[:tokens, features(head)], keys_ref[:, features(head)]]
        keys.append(jnp.concatenate([jnp.concatenate(pieces, axis=0), mask], axis=1))
        values_t.append(stretch_ref[tokens:, features(head)].T)

    def second(block, scores):
        head, cols = block
        before = (high_in[head, :, cols], total_in[head, :, cols])
        weights, _, total, decay = soften(scores, before)
        weights_ref[head, :, cols] = weights[tokens:]
        total_ref[head, :, cols] = total
        accum_ref[head, :, cols] = accum_in[head, :, cols] * decay + jnp.dot(
            values_t[head], weights[:tokens], preferred_element_type=jnp.float32
        )

    walk(blocks_of(qt_ref), lambda block: scores_of(qt_ref, block[0], block[1], keys[block[0]]), second)


def last_pages_kernel(
    stretch_ref, pages_ref, tally_ref, wide_ref, dec_high, dec_total, dec_mixed, dec_out
):
    tokens = stretch_ref.shape[0] // 2
    sent = pages_ref.shape[0] // 2
    keys = jnp.concatenate([stretch_ref[:tokens], pages_ref[:sent]], axis=0)
    values = jnp.concatenate([stretch_ref[tokens:], pages_ref[sent:]], axis=0)
    state = (dec_high[...], dec_total[...], dec_mixed[...])
    _, total, mixed = decode_attend(wide_ref[...], [(keys, values, tally_ref[...])], state)
    share = 1.0 / total
    for head in range(dec_high.shape[0]):
        piece = mixed[head, :, features(head // GROUP)] * share[head]
        dec_out[:, features(head)] = piece.astype(jnp.bfloat16)


def last_kernel(weights_ref, total_ref, accum_ref, values_ref, out_ref, result_ref, sems):
    tokens = result_ref.shape[0]
    values_t = [values_ref[:, features(head)].T for head in range(weights_ref.shape[0])]
    copies = []

    def first(block):
        head, cols = block
        return jnp.dot(values_t[head], weights_ref[head, :, cols], preferred_element_type=jnp.float32)

    def second(block, mixed):
        head, cols = block
        mixed = mixed + accum_ref[head, :, cols]
        mixed = (mixed * (1.0 / total_ref[head, :, cols])).astype(jnp.bfloat16)
        start = (head * GROUP + cols.start // tokens) * HEAD_DIM
        pieces = (cols.stop - cols.start) // tokens
        for piece in range(pieces):
            col = start + piece * HEAD_DIM
            result_ref[:, col : col + HEAD_DIM] = mixed[:, piece * tokens : (piece + 1) * tokens].T
        span = pl.ds(start, pieces * HEAD_DIM)
        copy = pltpu.make_async_copy(result_ref.at[:, span], out_ref.at[:, span], sems.at[len(copies)])
        copy.start()
        copies.append(copy)

    walk(blocks_of(weights_ref), first, second)

    for copy in copies:
        copy.wait()


def per_device(
    count,
    queries,
    stretch_keys,
    stretch_values,
    cache_keys,
    cache_values,
    prefix_length,
    page_targets,
    pool_keys,
    pool_values,
    decode_queries,
    page_lists,
    context_length,
):
    own = lax.axis_index("ctx")
    own_array = jnp.full((1,), own, jnp.int32)
    tokens, width = queries.shape
    kv_width = stretch_keys.shape[1]
    kv_local = kv_width // HEAD_DIM
    rows = GROUP * tokens
    heads = kv_local * GROUP
    dec_rows = decode_queries.shape[0]
    c_rows = cache_keys.shape[0]
    pool = pool_keys.shape[0]
    f32, bf16 = jnp.float32, jnp.bfloat16
    shape = jax.ShapeDtypeStruct
    params = pltpu.CompilerParams(vmem_limit_bytes=VMEM_BYTES)
    up_pairs = [(i, (i + 1) % count) for i in range(count)]
    down_pairs = [(i, (i - 1) % count) for i in range(count)]
    hops = []
    for far in range(1, count // 2 + 1):
        hops += [-far, far] if far <= (count - 1) // 2 else [-far]

    def send(array, hop):
        return lax.ppermute(array, "ctx", up_pairs if hop < 0 else down_pairs)

    def cost(keys):
        pairs = kv_local * rows * keys
        return pl.CostEstimate(
            flops=4 * pairs * HEAD_DIM, bytes_accessed=4 * rows * kv_local * HEAD_DIM, transcendentals=pairs
        )

    half = tokens + c_rows
    low = jnp.array(-jnp.inf, bf16)
    spread, start = [], 0
    for part in (stretch_keys, cache_keys, stretch_values, cache_values):
        end = 2 * half - start - part.shape[0]
        spread.append(lax.pad(part, low, ((start, end, 0), (0, 0, 0))))
        start += part.shape[0]
    shard = {0: functools.reduce(jnp.maximum, spread)}
    shard[-1] = send(shard[0], -1)

    state_shapes = (
        shape((kv_local, 1, rows), f32),
        shape((kv_local, 1, rows), f32),
        shape((kv_local, HEAD_DIM, rows), f32),
    )
    qt, near, far, pick, *state = pl.pallas_call(
        functools.partial(own_kernel, count, hops),
        out_shape=(
            shape((kv_local, HEAD_DIM + tokens, rows), bf16),
            shape((count - 1, tokens, tokens), bf16),
            shape((count - 1, c_rows, tokens), bf16),
            shape((SEND_CAP * PAGE, tokens), bf16),
        )
        + state_shapes,
        in_specs=[SMEM] * 3 + [VMEM] * 2,
        out_specs=(VMEM,) * 7,
        compiler_params=params,
        cost_estimate=cost(tokens + c_rows),
        name="own_shard",
    )(own_array, prefix_length, page_targets, queries, shard[0])

    dec_shapes = (
        shape((heads, dec_rows, 1), f32),
        shape((heads, dec_rows, 1), f32),
        shape((heads, dec_rows, kv_width), f32),
    )
    wide, *dec_state = pl.pallas_call(
        held_kernel,
        out_shape=(shape((heads * dec_rows, kv_width), bf16),) + dec_shapes,
        in_specs=[SMEM] * 3 + [VMEM] * 5,
        out_specs=(VMEM,) * 4,
        compiler_params=params,
        cost_estimate=pl.CostEstimate(
            flops=4 * 128 * 2048 * 256, bytes_accessed=4 * pool_keys.size, transcendentals=128 * 2048
        ),
        name="decode_held_pages",
    )(own_array, page_targets, context_length, decode_queries, page_lists, pool_keys, pool_values, shard[0])

    if 1 in hops:
        sent_down, state, dec_state = lax.optimization_barrier((shard[0], state, dec_state))
        shard[1] = send(sent_down, 1)
    shard[-1], state, dec_state = lax.optimization_barrier((shard[-1], state, dec_state))
    for hop in hops[2:-1]:
        shard[hop] = send(shard[hop + 1 if hop < 0 else hop - 1], hop)
    hop = hops[-1]
    nearer = shard[hop + 1 if hop < 0 else hop - 1]
    pieces = pl.pallas_call(
        split_kernel,
        out_shape=(
            shape((c_rows, kv_width), bf16),
            shape((2 * tokens, kv_width), bf16),
            shape((c_rows, kv_width), bf16),
            shape((2 * SEND_CAP * PAGE, kv_width), bf16),
        ),
        in_specs=[VMEM] * 2,
        out_specs=(VMEM,) * 4,
        compiler_params=params,
        name="pieces_to_send_on",
    )(pick, nearer)
    last_keys = send(pieces[0], hop)
    attending, others = [], []
    for pair in up_pairs if hop < 0 else down_pairs:
        (attending if (pair[1] + hop) % count < pair[1] else others).append(pair)
    last_stretch = lax.ppermute(pieces[1], "ctx", attending)
    last_pages = lax.ppermute(pieces[3], "ctx", others)
    last_values = send(pieces[2], hop)

    for first in range(len(hops) - 1):
        places = [first]
        state = pl.pallas_call(
            functools.partial(hop_kernel, places),
            out_shape=state_shapes,
            in_specs=[VMEM] * (6 + len(places)),
            out_specs=(VMEM,) * 3,
            compiler_params=params,
            cost_estimate=cost((c_rows + tokens) * len(places)),
            name="whole_shards_" + str(first),
        )(qt, near, far, *state, *[shard[hops[place]] for place in places])

    final = len(hops) - 1
    dec_state, state = lax.optimization_barrier((dec_state, state))
    near_hops = hops[:-1]
    *dec_state, tally = pl.pallas_call(
        functools.partial(near_pages_kernel, count, hops, tokens, pool),
        out_shape=dec_shapes
        + (shape((1, dec_rows, tokens + SEND_CAP * PAGE), f32),),
        in_specs=[SMEM] * 3 + [VMEM] * (5 + len(near_hops)),
        out_specs=(VMEM,) * 4,
        compiler_params=params,
        cost_estimate=cost(tokens),
        name="decode_near_pages",
    )(
        own_array, page_targets, context_length, page_lists, *[shard[hop] for hop in near_hops],
        wide, *dec_state,
    )
    dec_state, state = lax.optimization_barrier((dec_state, state))

    weights, total, accum = pl.pallas_call(
        functools.partial(score_kernel, final),
        out_shape=(shape((kv_local, c_rows, rows), bf16),) + state_shapes[1:],
        in_specs=[VMEM] * 8,
        out_specs=(VMEM,) * 3,
        compiler_params=params,
        cost_estimate=cost(half),
        name="last_scores",
    )(qt, near, far, *state, last_keys, last_stretch)

    dec_state, total = lax.optimization_barrier((dec_state, total))
    decoded = pl.pallas_call(
        last_pages_kernel,
        out_shape=shape(decode_queries.shape, bf16),
        in_specs=[VMEM] * 7,
        out_specs=VMEM,
        compiler_params=params,
        cost_estimate=cost(tokens // 2),
        name="decode_last_pages",
    )(last_stretch, last_pages, tally, wide, *dec_state)
    decoded, total = lax.optimization_barrier((decoded, total))

    prefill = pl.pallas_call(
        last_kernel,
        out_shape=shape((tokens, width), bf16),
        in_specs=[VMEM] * 4,
        out_specs=HBM,
        scratch_shapes=[
            pltpu.VMEM((tokens, width), bf16),
            pltpu.SemaphoreType.DMA((kv_local * max(GROUP // 2, 1),)),
        ],
        compiler_params=params,
        cost_estimate=cost(c_rows // 2),
        name="last_values",
    )(weights, total, accum, last_values)
    return (prefill, decoded)


def solution(mesh):
    in_specs = (
        P(("groups", "ctx"), "head"),
        P(("groups", "ctx"), "head"),
        P(("groups", "ctx"), "head"),
        P(("groups", "ctx"), "head"),
        P(("groups", "ctx"), "head"),
        P("groups"),
        P("groups"),
        P(("groups", "ctx"), None, "head"),
        P(("groups", "ctx"), None, "head"),
        P(("groups", "ctx"), "head"),
        P(("groups", "ctx"), None),
        P(("groups", "ctx")),
    )
    out_specs = (P(("groups", "ctx"), "head"), P(("groups", "ctx"), "head"))
    return jax.shard_map(
        functools.partial(per_device, mesh.shape["ctx"]),
        mesh=mesh,
        in_specs=in_specs,
        out_specs=out_specs,
        check_vma=False,
    )
```

```python
import functools

import jax
import jax.numpy as jnp
from jax import lax
from jax.experimental import pallas as pl
from jax.experimental.pallas import tpu as pltpu
from jax.sharding import PartitionSpec as P

HEADS = 64
KV_HEADS = 8
HEAD_DIM = 128
GROUP = HEADS // KV_HEADS
PAGE = 16
P_DEV = 8
SEND_CAP = 2
EXP2_SCALE = HEAD_DIM ** (-0.5) * 1.4426950408889634
HIDDEN = -1e30
VMEM_BYTES = 48 * 1024 * 1024

VMEM = pl.BlockSpec(memory_space=pltpu.VMEM)
SMEM = pl.BlockSpec(memory_space=pltpu.SMEM)
HBM = pl.BlockSpec(memory_space=pltpu.HBM)


def scores_of(qt_ref, head, cols, keys):
    return jnp.dot(keys, qt_ref[head, :, cols], preferred_element_type=jnp.float32)


def soften(scores, old):
    high = jnp.max(scores, axis=0, keepdims=True)
    if old is None:
        weights = jnp.exp2((scores - high) * EXP2_SCALE)
        return weights.astype(jnp.bfloat16), high, jnp.sum(weights, axis=0, keepdims=True), None
    old_high, old_total = old
    high = jnp.maximum(high, old_high)
    decay = jnp.exp2((old_high - high) * EXP2_SCALE)
    weights = jnp.exp2((scores - high) * EXP2_SCALE)
    total = old_total * decay + jnp.sum(weights, axis=0, keepdims=True)
    return weights.astype(jnp.bfloat16), high, total, decay


def walk(blocks, first, second):
    ahead = first(blocks[0])
    for place, block in enumerate(blocks):
        current = ahead
        if place + 1 < len(blocks):
            ahead = first(blocks[place + 1])
        second(block, current)


def blocks_of(qt_ref):
    kv_local, _, rows = qt_ref.shape
    width = min(2 * (rows // GROUP), rows)
    return [(head, slice(start, start + width)) for head in range(kv_local) for start in range(0, rows, width)]


def attend(qt_ref, keys, values_t, old, new):
    high_ref, total_ref, accum_ref = new

    def second(block, scores):
        head, cols = block
        before = None if old is None else (old[0][head, :, cols], old[1][head, :, cols])
        weights, high, total, decay = soften(scores, before)
        accum = jnp.dot(values_t[head], weights, preferred_element_type=jnp.float32)
        if old is not None:
            accum = accum + old[2][head, :, cols] * decay
        high_ref[head, :, cols] = high
        total_ref[head, :, cols] = total
        accum_ref[head, :, cols] = accum

    walk(blocks_of(qt_ref), lambda block: scores_of(qt_ref, block[0], block[1], keys[block[0]]), second)


def hidden(seen):
    return jnp.where(seen, jnp.float32(0.0), jnp.float32(HIDDEN)).astype(jnp.bfloat16)


def stretch_mask(shard, own, tokens):
    place = lax.broadcasted_iota(jnp.int32, (tokens, tokens), 0)
    token = lax.broadcasted_iota(jnp.int32, (tokens, tokens), 1)
    return hidden(place - token <= (own - shard) * tokens)


def cache_mask(shard, limit, c_rows, tokens):
    place = lax.broadcasted_iota(jnp.int32, (c_rows, tokens), 0)
    return hidden(place < limit - shard * c_rows)


def slot_row(targets_ref, shard, own, tokens, pool):
    page = lax.broadcasted_iota(jnp.int32, (1, tokens), 1) // PAGE
    slots = jnp.full((1, tokens), -1, jnp.int32)
    for index in range(tokens // PAGE):
        target = targets_ref[shard * (tokens // PAGE) + index]
        slot = jnp.where(lax.div(target, P_DEV) == own, pool + lax.rem(target, P_DEV), -1)
        slots = jnp.where(page == index, slot, slots)
    return slots


def sent_pages(targets_ref, shard, owner, pages):
    one, two = jnp.int32(-1), jnp.int32(-1)
    for index in range(pages):
        hit = lax.div(targets_ref[shard * pages + index], P_DEV) == owner
        two = jnp.where(hit & (one >= 0) & (two < 0), index, two)
        one = jnp.where(hit & (one < 0), index, one)
    return one, two


def pick_pages(targets_ref, shard, owner, dims):
    one, two = sent_pages(targets_ref, shard, owner, dims[1] // PAGE)
    row = lax.broadcasted_iota(jnp.int32, dims, 0)
    token = lax.broadcasted_iota(jnp.int32, dims, 1)
    sent = ((row < PAGE) & (one >= 0) & (token == row + one * PAGE)) | (
        (row >= PAGE) & (two >= 0) & (token == row + (two - 1) * PAGE)
    )
    return jnp.where(sent, jnp.float32(1.0), jnp.float32(0.0)).astype(jnp.bfloat16)


def sent_slots(targets_ref, shard, owner, pages, pool):
    place = lax.broadcasted_iota(jnp.int32, (1, SEND_CAP * PAGE), 1)
    slots = []
    for index in sent_pages(targets_ref, shard, owner, pages):
        target = targets_ref[shard * pages + jnp.maximum(index, 0)]
        slots.append(jnp.where(index >= 0, pool + lax.rem(target, P_DEV), -1))
    return jnp.where(place < PAGE, slots[0], slots[1])


def length_column(length_ref):
    rows = length_ref.shape[0]
    place = lax.broadcasted_iota(jnp.int32, (rows, 1), 0)
    lengths = jnp.zeros((rows, 1), jnp.int32)
    for row in range(rows):
        lengths = jnp.where(place == row, length_ref[row], lengths)
    return lengths


def tally_of(lists, lengths, slot):
    rows, span = lists.shape
    tokens = slot.shape[1]
    slot = jnp.broadcast_to(slot, (rows, tokens))
    offset = lax.rem(lax.broadcasted_iota(jnp.int32, (rows, tokens), 1), PAGE)
    tally = jnp.zeros((rows, tokens), jnp.float32)
    for entry in range(span):
        hit = (slot == lists[:, entry : entry + 1]) & (offset < lengths - entry * PAGE)
        tally = tally + jnp.where(hit, jnp.float32(1.0), jnp.float32(0.0))
    return tally[None]


def shard_of(own, hop, count):
    return lax.rem(own + hop + count, count)


def wide_queries(q_ref, kv_local):
    heads = q_ref.shape[1] // HEAD_DIM
    queries = q_ref[...].astype(jnp.float32)
    stacked = []
    for head in range(heads):
        piece = queries[:, head * HEAD_DIM : (head + 1) * HEAD_DIM]
        blank = jnp.zeros_like(piece)
        stacked.append(
            jnp.concatenate([piece if kv == head // GROUP else blank for kv in range(kv_local)], axis=1)
        )
    return jnp.concatenate(stacked, axis=0).astype(jnp.bfloat16)


def decode_attend(queries, parts, state):
    done = []
    for keys, values, tally in parts:
        scores = lax.dot_general(
            queries, keys, (((1,), (1,)), ((), ())), preferred_element_type=jnp.float32
        ).reshape(-1, tally.shape[1], tally.shape[2])
        done.append((jnp.where(tally > 0, scores, jnp.float32(HIDDEN)), tally, values))
    highs = [jnp.max(scores, axis=-1, keepdims=True) for scores, _, _ in done]
    if state is not None:
        old_high, old_total, old_mixed = state
        highs.append(old_high)
    high = functools.reduce(jnp.maximum, highs)
    total, mixed = 0.0, 0.0
    if state is not None:
        decay = jnp.exp2((old_high - high) * EXP2_SCALE)
        total = old_total * decay
        mixed = old_mixed * decay
    for scores, tally, values in done:
        weights = jnp.exp2((scores - high) * EXP2_SCALE) * tally
        total = total + jnp.sum(weights, axis=-1, keepdims=True)
        mixed = mixed + jnp.dot(
            weights.reshape(queries.shape[0], -1).astype(jnp.bfloat16),
            values,
            preferred_element_type=jnp.float32,
        ).reshape(high.shape[0], high.shape[1], -1)
    return high, total, mixed


def features(head):
    return slice(head * HEAD_DIM, (head + 1) * HEAD_DIM)


def shard_parts(ref, tokens, c_rows):
    return slice(0, tokens + c_rows), slice(tokens + c_rows, 2 * (tokens + c_rows))


def own_kernel(
    count, hops, own_ref, limit_ref, targets_ref, q_ref, shard_ref,
    qt_ref, near_ref, far_ref, pick_ref, below_ref, high_ref, total_ref, accum_ref,
):
    kv_local, _, rows = qt_ref.shape
    tokens = q_ref.shape[0]
    c_rows = far_ref.shape[1]
    own = own_ref[0]
    limit = limit_ref[0]
    place = lax.broadcasted_iota(jnp.int32, (tokens, tokens), 0)
    token = lax.broadcasted_iota(jnp.int32, (tokens, tokens), 1)
    pick = jnp.where(place == token, jnp.float32(1.0), jnp.float32(0.0)).astype(jnp.bfloat16)
    for head in range(kv_local):
        for sub in range(GROUP):
            cols = slice(sub * tokens, (sub + 1) * tokens)
            qt_ref[head, :HEAD_DIM, cols] = q_ref[:, features(head * GROUP + sub)].T
            qt_ref[head, HEAD_DIM:, cols] = pick
    for place, hop in enumerate(hops):
        shard = shard_of(own, hop, count)
        near_ref[place] = stretch_mask(shard, own, tokens)
        far_ref[place] = cache_mask(shard, limit, c_rows, tokens)
    onward = 1 if hops[-1] < 0 else -1
    pick_ref[...] = pick_pages(
        targets_ref, shard_of(own, hops[-1] + onward, count), shard_of(own, onward, count), pick_ref.shape
    )
    below_ref[...] = pick_pages(targets_ref, own, own - 1, below_ref.shape)
    mask = jnp.concatenate([stretch_mask(own, own, tokens), cache_mask(own, limit, c_rows, tokens)], axis=0)
    key_rows, value_rows = shard_parts(shard_ref, tokens, c_rows)
    keys = [jnp.concatenate([shard_ref[key_rows, features(head)], mask], axis=1) for head in range(kv_local)]
    values_t = [shard_ref[value_rows, features(head)].T for head in range(kv_local)]
    attend(qt_ref, keys, values_t, None, (high_ref, total_ref, accum_ref))


def held_kernel(
    own_ref, targets_ref, length_ref, q_ref, lists_ref, pool_k, pool_v, rest_ref,
    wide_ref, high_ref, total_ref, mixed_ref,
):
    kv_width = rest_ref.shape[1]
    pool = pool_k.shape[0]
    held = pool * PAGE
    tokens = PAGE * P_DEV
    half = rest_ref.shape[0] // 2
    own = own_ref[0]
    lists = lists_ref[...]
    lengths = length_column(length_ref)
    wide_ref[...] = wide_queries(q_ref, kv_width // HEAD_DIM)
    held_slot = lax.broadcasted_iota(jnp.int32, (1, held), 1) // PAGE
    own_slot = slot_row(targets_ref, own, own, tokens, pool)
    parts = [
        (
            pool_k[...].reshape(held, kv_width),
            pool_v[...].reshape(held, kv_width),
            tally_of(lists, lengths, held_slot),
        ),
        (rest_ref[:tokens], rest_ref[half : half + tokens], tally_of(lists, lengths, own_slot)),
    ]
    high_ref[...], total_ref[...], mixed_ref[...] = decode_attend(wide_ref[...], parts, None)


def hop_kernel(place, qt_ref, near_ref, far_ref, high_in, total_in, accum_in, shard_ref, *refs):
    extra, outs = refs[:-3], refs[-3:]
    tokens, c_rows = near_ref.shape[1], far_ref.shape[1]
    key_rows, value_rows = shard_parts(shard_ref, tokens, c_rows)
    mask = jnp.concatenate([near_ref[place], far_ref[place]], axis=0)
    keys, values_t = [], []
    for head in range(qt_ref.shape[0]):
        parts = [shard_ref[key_rows, features(head)], shard_ref[value_rows, features(head)]]
        for ref in extra:
            for index in range(2):
                cached = ref[index * c_rows : (index + 1) * c_rows, features(head)]
                part = parts[index]
                parts[index] = jnp.concatenate([part[:tokens], part[tokens:] + cached], axis=0)
        keys.append(jnp.concatenate([parts[0], mask], axis=1))
        values_t.append(parts[1].T)
    attend(qt_ref, keys, values_t, (high_in, total_in, accum_in), outs)


def down_kernel(pick_ref, shard_ref, out_ref):
    sent, tokens = pick_ref.shape
    half = shard_ref.shape[0] // 2
    c_rows = half - tokens
    for place, start in enumerate((0, half)):
        out_ref[place * c_rows : (place + 1) * c_rows] = shard_ref[start + tokens : start + half]
        rows = jnp.dot(pick_ref[...], shard_ref[start : start + tokens], preferred_element_type=jnp.float32)
        out_ref[2 * c_rows + place * sent : 2 * c_rows + (place + 1) * sent] = rows.astype(jnp.bfloat16)


def split_kernel(pick_ref, shard_ref, keys_ref, stretch_ref, values_ref, pages_ref):
    tokens = pick_ref.shape[1]
    half = shard_ref.shape[0] // 2
    sent = pick_ref.shape[0]
    for place, start in enumerate((0, half)):
        stretch_ref[place * tokens : (place + 1) * tokens] = shard_ref[start : start + tokens]
        rows = jnp.dot(pick_ref[...], shard_ref[start : start + tokens], preferred_element_type=jnp.float32)
        pages_ref[place * sent : (place + 1) * sent] = rows.astype(jnp.bfloat16)
    keys_ref[...] = shard_ref[tokens:half]
    values_ref[...] = shard_ref[half + tokens :]


def near_pages_kernel(count, hops, tokens, pool, own_ref, targets_ref, length_ref, lists_ref, *refs):
    shard_refs, refs = refs[: len(hops) - 1], refs[len(hops) - 1 :]
    extra, refs = refs[:-8], refs[-8:]
    wide_ref, dec_high, dec_total, dec_mixed, high_ref, total_ref, mixed_ref, tally_ref = refs
    own = own_ref[0]
    lists = lists_ref[...]
    lengths = length_column(length_ref)
    parts = []
    for hop, ref in zip(hops, shard_refs):
        half = ref.shape[0] // 2
        slot = slot_row(targets_ref, shard_of(own, hop, count), own, tokens, pool)
        if extra and hop == 1:
            slot = jnp.where(own + 1 < count, -1, slot)
        parts.append((ref[:tokens], ref[half : half + tokens], tally_of(lists, lengths, slot)))
    for ref in extra:
        sent = SEND_CAP * PAGE
        first = ref.shape[0] - 2 * sent
        slot = sent_slots(targets_ref, shard_of(own, 1, count), own, tokens // PAGE, pool)
        slot = jnp.where(own + 1 < count, slot, -1)
        parts.append((ref[first : first + sent], ref[first + sent :], tally_of(lists, lengths, slot)))
    state = (dec_high[...], dec_total[...], dec_mixed[...])
    high_ref[...], total_ref[...], mixed_ref[...] = decode_attend(wide_ref[...], parts, state)
    shard = shard_of(own, hops[-1], count)
    attended = shard < own
    whole = jnp.where(attended, slot_row(targets_ref, shard, own, tokens, pool), -1)
    alone = jnp.where(attended, -1, sent_slots(targets_ref, shard, own, tokens // PAGE, pool))
    tally_ref[:, :, :tokens] = tally_of(lists, lengths, whole)
    tally_ref[:, :, tokens:] = tally_of(lists, lengths, alone)


def score_kernel(
    final, qt_ref, near_ref, far_ref, high_in, total_in, accum_in, keys_ref, stretch_ref,
    weights_ref, total_ref, accum_ref,
):
    kv_local = qt_ref.shape[0]
    tokens, c_rows = near_ref.shape[1], far_ref.shape[1]
    mask = jnp.concatenate([near_ref[final], far_ref[final]], axis=0)
    keys, values_t = [], []
    for head in range(kv_local):
        pieces = [stretch_ref[:tokens, features(head)], keys_ref[:, features(head)]]
        keys.append(jnp.concatenate([jnp.concatenate(pieces, axis=0), mask], axis=1))
        values_t.append(stretch_ref[tokens:, features(head)].T)

    def second(block, scores):
        head, cols = block
        before = (high_in[head, :, cols], total_in[head, :, cols])
        weights, _, total, decay = soften(scores, before)
        weights_ref[head, :, cols] = weights[tokens:]
        total_ref[head, :, cols] = total
        accum_ref[head, :, cols] = accum_in[head, :, cols] * decay + jnp.dot(
            values_t[head], weights[:tokens], preferred_element_type=jnp.float32
        )

    walk(blocks_of(qt_ref), lambda block: scores_of(qt_ref, block[0], block[1], keys[block[0]]), second)


def last_pages_kernel(
    stretch_ref, pages_ref, tally_ref, wide_ref, dec_high, dec_total, dec_mixed, dec_out
):
    tokens = stretch_ref.shape[0] // 2
    sent = pages_ref.shape[0] // 2
    keys = jnp.concatenate([stretch_ref[:tokens], pages_ref[:sent]], axis=0)
    values = jnp.concatenate([stretch_ref[tokens:], pages_ref[sent:]], axis=0)
    state = (dec_high[...], dec_total[...], dec_mixed[...])
    _, total, mixed = decode_attend(wide_ref[...], [(keys, values, tally_ref[...])], state)
    share = 1.0 / total
    for head in range(dec_high.shape[0]):
        piece = mixed[head, :, features(head // GROUP)] * share[head]
        dec_out[:, features(head)] = piece.astype(jnp.bfloat16)


def last_kernel(weights_ref, total_ref, accum_ref, values_ref, out_ref, result_ref, sems):
    tokens = result_ref.shape[0]
    values_t = [values_ref[:, features(head)].T for head in range(weights_ref.shape[0])]
    copies = []

    def first(block):
        head, cols = block
        return jnp.dot(values_t[head], weights_ref[head, :, cols], preferred_element_type=jnp.float32)

    def second(block, mixed):
        head, cols = block
        mixed = mixed + accum_ref[head, :, cols]
        mixed = (mixed * (1.0 / total_ref[head, :, cols])).astype(jnp.bfloat16)
        start = (head * GROUP + cols.start // tokens) * HEAD_DIM
        pieces = (cols.stop - cols.start) // tokens
        for piece in range(pieces):
            col = start + piece * HEAD_DIM
            result_ref[:, col : col + HEAD_DIM] = mixed[:, piece * tokens : (piece + 1) * tokens].T
        span = pl.ds(start, pieces * HEAD_DIM)
        copy = pltpu.make_async_copy(result_ref.at[:, span], out_ref.at[:, span], sems.at[len(copies)])
        copy.start()
        copies.append(copy)

    walk(blocks_of(weights_ref), first, second)

    for copy in copies:
        copy.wait()


def per_device(
    count,
    queries,
    stretch_keys,
    stretch_values,
    cache_keys,
    cache_values,
    prefix_length,
    page_targets,
    pool_keys,
    pool_values,
    decode_queries,
    page_lists,
    context_length,
):
    own = lax.axis_index("ctx")
    own_array = jnp.full((1,), own, jnp.int32)
    tokens, width = queries.shape
    kv_width = stretch_keys.shape[1]
    kv_local = kv_width // HEAD_DIM
    rows = GROUP * tokens
    heads = kv_local * GROUP
    dec_rows = decode_queries.shape[0]
    c_rows = cache_keys.shape[0]
    pool = pool_keys.shape[0]
    f32, bf16 = jnp.float32, jnp.bfloat16
    shape = jax.ShapeDtypeStruct
    params = pltpu.CompilerParams(vmem_limit_bytes=VMEM_BYTES)
    up_pairs = [(i, (i + 1) % count) for i in range(count)]
    down_pairs = [(i, (i - 1) % count) for i in range(count)]
    hops = []
    for far in range(1, count // 2 + 1):
        hops += [-far, far] if far <= (count - 1) // 2 else [-far]

    def send(array, hop):
        return lax.ppermute(array, "ctx", up_pairs if hop < 0 else down_pairs)

    def cost(keys):
        pairs = kv_local * rows * keys
        return pl.CostEstimate(
            flops=4 * pairs * HEAD_DIM, bytes_accessed=4 * rows * kv_local * HEAD_DIM, transcendentals=pairs
        )

    half = tokens + c_rows
    low = jnp.array(-jnp.inf, bf16)
    spread, start = [], 0
    for part in (stretch_keys, cache_keys, stretch_values, cache_values):
        end = 2 * half - start - part.shape[0]
        spread.append(lax.pad(part, low, ((start, end, 0), (0, 0, 0))))
        start += part.shape[0]
    shard = {0: functools.reduce(jnp.maximum, spread)}
    shard[-1] = send(shard[0], -1)

    state_shapes = (
        shape((kv_local, 1, rows), f32),
        shape((kv_local, 1, rows), f32),
        shape((kv_local, HEAD_DIM, rows), f32),
    )
    qt, near, far, pick, below, *state = pl.pallas_call(
        functools.partial(own_kernel, count, hops),
        out_shape=(
            shape((kv_local, HEAD_DIM + tokens, rows), bf16),
            shape((count - 1, tokens, tokens), bf16),
            shape((count - 1, c_rows, tokens), bf16),
            shape((SEND_CAP * PAGE, tokens), bf16),
            shape((SEND_CAP * PAGE, tokens), bf16),
        )
        + state_shapes,
        in_specs=[SMEM] * 3 + [VMEM] * 2,
        out_specs=(VMEM,) * 8,
        compiler_params=params,
        cost_estimate=cost(tokens + c_rows),
        name="own_shard",
    )(own_array, prefix_length, page_targets, queries, shard[0])

    dec_shapes = (
        shape((heads, dec_rows, 1), f32),
        shape((heads, dec_rows, 1), f32),
        shape((heads, dec_rows, kv_width), f32),
    )
    wide, *dec_state = pl.pallas_call(
        held_kernel,
        out_shape=(shape((heads * dec_rows, kv_width), bf16),) + dec_shapes,
        in_specs=[SMEM] * 3 + [VMEM] * 5,
        out_specs=(VMEM,) * 4,
        compiler_params=params,
        cost_estimate=pl.CostEstimate(
            flops=4 * 128 * 2048 * 256, bytes_accessed=4 * pool_keys.size, transcendentals=128 * 2048
        ),
        name="decode_held_pages",
    )(own_array, page_targets, context_length, decode_queries, page_lists, pool_keys, pool_values, shard[0])

    extra = []
    if hops == [-1, 1, -2]:
        down = pl.pallas_call(
            down_kernel,
            out_shape=shape((2 * (c_rows + SEND_CAP * PAGE), kv_width), bf16),
            in_specs=[VMEM] * 2,
            out_specs=VMEM,
            compiler_params=params,
            name="rows_to_send_down",
        )(below, shard[0])
        down, straight, state, dec_state = lax.optimization_barrier((down, shard[0], state, dec_state))
        extra = [lax.ppermute(down, "ctx", down_pairs[1:])]
        shard[1] = lax.ppermute(straight, "ctx", down_pairs[:1])
    elif 1 in hops:
        sent_down, state, dec_state = lax.optimization_barrier((shard[0], state, dec_state))
        shard[1] = send(sent_down, 1)
    shard[-1], state, dec_state = lax.optimization_barrier((shard[-1], state, dec_state))
    for hop in hops[2:-1]:
        shard[hop] = send(shard[hop + 1 if hop < 0 else hop - 1], hop)
    hop = hops[-1]
    nearer = shard[hop + 1 if hop < 0 else hop - 1]
    pieces = pl.pallas_call(
        split_kernel,
        out_shape=(
            shape((c_rows, kv_width), bf16),
            shape((2 * tokens, kv_width), bf16),
            shape((c_rows, kv_width), bf16),
            shape((2 * SEND_CAP * PAGE, kv_width), bf16),
        ),
        in_specs=[VMEM] * 2,
        out_specs=(VMEM,) * 4,
        compiler_params=params,
        name="pieces_to_send_on",
    )(pick, nearer)
    last_keys = send(pieces[0], hop)
    attending, others = [], []
    for pair in up_pairs if hop < 0 else down_pairs:
        (attending if (pair[1] + hop) % count < pair[1] else others).append(pair)
    last_stretch = lax.ppermute(pieces[1], "ctx", attending)
    last_pages = lax.ppermute(pieces[3], "ctx", others)

    for place, hop in enumerate(hops[:-1]):
        received = [shard[hop]] + (extra if hop == 1 else [])
        state = pl.pallas_call(
            functools.partial(hop_kernel, place),
            out_shape=state_shapes,
            in_specs=[VMEM] * (6 + len(received)),
            out_specs=(VMEM,) * 3,
            compiler_params=params,
            cost_estimate=cost(half),
            name="whole_shards_" + str(place),
        )(qt, near, far, *state, *received)
        if place == 0:
            last_piece, shard[1], extra, state = lax.optimization_barrier((pieces[2], shard[1], extra, state))
            last_values = send(last_piece, hops[-1])

    final = len(hops) - 1
    dec_state, state = lax.optimization_barrier((dec_state, state))
    last_pages, dec_state = lax.optimization_barrier((last_pages, dec_state))
    near_hops = hops[:-1]
    *dec_state, tally = pl.pallas_call(
        functools.partial(near_pages_kernel, count, hops, tokens, pool),
        out_shape=dec_shapes
        + (shape((1, dec_rows, tokens + SEND_CAP * PAGE), f32),),
        in_specs=[SMEM] * 3 + [VMEM] * (5 + len(near_hops) + len(extra)),
        out_specs=(VMEM,) * 4,
        compiler_params=params,
        cost_estimate=cost(tokens),
        name="decode_near_pages",
    )(
        own_array, page_targets, context_length, page_lists, *[shard[hop] for hop in near_hops], *extra,
        wide, *dec_state,
    )
    dec_state, state = lax.optimization_barrier((dec_state, state))

    weights, total, accum = pl.pallas_call(
        functools.partial(score_kernel, final),
        out_shape=(shape((kv_local, c_rows, rows), bf16),) + state_shapes[1:],
        in_specs=[VMEM] * 8,
        out_specs=(VMEM,) * 3,
        compiler_params=params,
        cost_estimate=cost(half),
        name="last_scores",
    )(qt, near, far, *state, last_keys, last_stretch)

    dec_state, total = lax.optimization_barrier((dec_state, total))
    decoded = pl.pallas_call(
        last_pages_kernel,
        out_shape=shape(decode_queries.shape, bf16),
        in_specs=[VMEM] * 7,
        out_specs=VMEM,
        compiler_params=params,
        cost_estimate=cost(tokens // 2),
        name="decode_last_pages",
    )(last_stretch, last_pages, tally, wide, *dec_state)
    decoded, total = lax.optimization_barrier((decoded, total))

    prefill = pl.pallas_call(
        last_kernel,
        out_shape=shape((tokens, width), bf16),
        in_specs=[VMEM] * 4,
        out_specs=HBM,
        scratch_shapes=[
            pltpu.VMEM((tokens, width), bf16),
            pltpu.SemaphoreType.DMA((kv_local * max(GROUP // 2, 1),)),
        ],
        compiler_params=params,
        cost_estimate=cost(c_rows // 2),
        name="last_values",
    )(weights, total, accum, last_values)
    return (prefill, decoded)


def solution(mesh):
    in_specs = (
        P(("groups", "ctx"), "head"),
        P(("groups", "ctx"), "head"),
        P(("groups", "ctx"), "head"),
        P(("groups", "ctx"), "head"),
        P(("groups", "ctx"), "head"),
        P("groups"),
        P("groups"),
        P(("groups", "ctx"), None, "head"),
        P(("groups", "ctx"), None, "head"),
        P(("groups", "ctx"), "head"),
        P(("groups", "ctx"), None),
        P(("groups", "ctx")),
    )
    out_specs = (P(("groups", "ctx"), "head"), P(("groups", "ctx"), "head"))
    return jax.shard_map(
        functools.partial(per_device, mesh.shape["ctx"]),
        mesh=mesh,
        in_specs=in_specs,
        out_specs=out_specs,
        check_vma=False,
    )
```

```python
import functools

import jax
import jax.numpy as jnp
from jax import lax
from jax.experimental import pallas as pl
from jax.experimental.pallas import tpu as pltpu
from jax.sharding import PartitionSpec as P

HEADS = 64
KV_HEADS = 8
HEAD_DIM = 128
GROUP = HEADS // KV_HEADS
PAGE = 16
P_DEV = 8
SEND_CAP = 2
EXP2_SCALE = HEAD_DIM ** (-0.5) * 1.4426950408889634
HIDDEN = -1e30
VMEM_BYTES = 48 * 1024 * 1024

VMEM = pl.BlockSpec(memory_space=pltpu.VMEM)
SMEM = pl.BlockSpec(memory_space=pltpu.SMEM)
HBM = pl.BlockSpec(memory_space=pltpu.HBM)


def scores_of(qt_ref, head, cols, keys):
    return jnp.dot(keys, qt_ref[head, :, cols], preferred_element_type=jnp.float32)


def soften(scores, old):
    high = jnp.max(scores, axis=0, keepdims=True)
    if old is None:
        weights = jnp.exp2((scores - high) * EXP2_SCALE)
        return weights.astype(jnp.bfloat16), high, jnp.sum(weights, axis=0, keepdims=True), None
    old_high, old_total = old
    high = jnp.maximum(high, old_high)
    decay = jnp.exp2((old_high - high) * EXP2_SCALE)
    weights = jnp.exp2((scores - high) * EXP2_SCALE)
    total = old_total * decay + jnp.sum(weights, axis=0, keepdims=True)
    return weights.astype(jnp.bfloat16), high, total, decay


def walk(blocks, first, second):
    ahead = first(blocks[0])
    for place, block in enumerate(blocks):
        current = ahead
        if place + 1 < len(blocks):
            ahead = first(blocks[place + 1])
        second(block, current)


def blocks_of(qt_ref):
    kv_local, _, rows = qt_ref.shape
    width = min(2 * (rows // GROUP), rows)
    return [(head, slice(start, start + width)) for head in range(kv_local) for start in range(0, rows, width)]


def attend(qt_ref, keys, values_t, old, new):
    high_ref, total_ref, accum_ref = new

    def second(block, scores):
        head, cols = block
        before = None if old is None else (old[0][head, :, cols], old[1][head, :, cols])
        weights, high, total, decay = soften(scores, before)
        accum = jnp.dot(values_t[head], weights, preferred_element_type=jnp.float32)
        if old is not None:
            accum = accum + old[2][head, :, cols] * decay
        high_ref[head, :, cols] = high
        total_ref[head, :, cols] = total
        accum_ref[head, :, cols] = accum

    walk(blocks_of(qt_ref), lambda block: scores_of(qt_ref, block[0], block[1], keys[block[0]]), second)


def hidden(seen):
    return jnp.where(seen, jnp.float32(0.0), jnp.float32(HIDDEN)).astype(jnp.bfloat16)


def stretch_mask(shard, own, tokens):
    place = lax.broadcasted_iota(jnp.int32, (tokens, tokens), 0)
    token = lax.broadcasted_iota(jnp.int32, (tokens, tokens), 1)
    return hidden(place - token <= (own - shard) * tokens)


def cache_mask(shard, limit, c_rows, tokens):
    place = lax.broadcasted_iota(jnp.int32, (c_rows, tokens), 0)
    return hidden(place < limit - shard * c_rows)


def slot_row(targets_ref, shard, own, tokens, pool):
    page = lax.broadcasted_iota(jnp.int32, (1, tokens), 1) // PAGE
    slots = jnp.full((1, tokens), -1, jnp.int32)
    for index in range(tokens // PAGE):
        target = targets_ref[shard * (tokens // PAGE) + index]
        slot = jnp.where(lax.div(target, P_DEV) == own, pool + lax.rem(target, P_DEV), -1)
        slots = jnp.where(page == index, slot, slots)
    return slots


def sent_pages(targets_ref, shard, owner, pages):
    one, two = jnp.int32(-1), jnp.int32(-1)
    for index in range(pages):
        hit = lax.div(targets_ref[shard * pages + index], P_DEV) == owner
        two = jnp.where(hit & (one >= 0) & (two < 0), index, two)
        one = jnp.where(hit & (one < 0), index, one)
    return one, two


def sent_slots(targets_ref, shard, owner, pages, pool):
    place = lax.broadcasted_iota(jnp.int32, (1, SEND_CAP * PAGE), 1)
    slots = []
    for index in sent_pages(targets_ref, shard, owner, pages):
        target = targets_ref[shard * pages + jnp.maximum(index, 0)]
        slots.append(jnp.where(index >= 0, pool + lax.rem(target, P_DEV), -1))
    return jnp.where(place < PAGE, slots[0], slots[1])


def length_column(length_ref):
    rows = length_ref.shape[0]
    place = lax.broadcasted_iota(jnp.int32, (rows, 1), 0)
    lengths = jnp.zeros((rows, 1), jnp.int32)
    for row in range(rows):
        lengths = jnp.where(place == row, length_ref[row], lengths)
    return lengths


def tally_of(lists, lengths, slot):
    rows, span = lists.shape
    tokens = slot.shape[1]
    slot = jnp.broadcast_to(slot, (rows, tokens))
    offset = lax.rem(lax.broadcasted_iota(jnp.int32, (rows, tokens), 1), PAGE)
    tally = jnp.zeros((rows, tokens), jnp.float32)
    for entry in range(span):
        hit = (slot == lists[:, entry : entry + 1]) & (offset < lengths - entry * PAGE)
        tally = tally + jnp.where(hit, jnp.float32(1.0), jnp.float32(0.0))
    return tally[None]


def shard_of(own, hop, count):
    return lax.rem(own + hop + count, count)


def wide_queries(q_ref, kv_local):
    heads = q_ref.shape[1] // HEAD_DIM
    queries = q_ref[...].astype(jnp.float32)
    stacked = []
    for head in range(heads):
        piece = queries[:, head * HEAD_DIM : (head + 1) * HEAD_DIM]
        blank = jnp.zeros_like(piece)
        stacked.append(
            jnp.concatenate([piece if kv == head // GROUP else blank for kv in range(kv_local)], axis=1)
        )
    return jnp.concatenate(stacked, axis=0).astype(jnp.bfloat16)


def decode_attend(queries, parts, state):
    done = []
    for keys, values, tally in parts:
        scores = lax.dot_general(
            queries, keys, (((1,), (1,)), ((), ())), preferred_element_type=jnp.float32
        ).reshape(-1, tally.shape[1], tally.shape[2])
        done.append((jnp.where(tally > 0, scores, jnp.float32(HIDDEN)), tally, values))
    highs = [jnp.max(scores, axis=-1, keepdims=True) for scores, _, _ in done]
    if state is not None:
        old_high, old_total, old_mixed = state
        highs.append(old_high)
    high = functools.reduce(jnp.maximum, highs)
    total, mixed = 0.0, 0.0
    if state is not None:
        decay = jnp.exp2((old_high - high) * EXP2_SCALE)
        total = old_total * decay
        mixed = old_mixed * decay
    for scores, tally, values in done:
        weights = jnp.exp2((scores - high) * EXP2_SCALE) * tally
        total = total + jnp.sum(weights, axis=-1, keepdims=True)
        mixed = mixed + jnp.dot(
            weights.reshape(queries.shape[0], -1).astype(jnp.bfloat16),
            values,
            preferred_element_type=jnp.float32,
        ).reshape(high.shape[0], high.shape[1], -1)
    return high, total, mixed


def features(head):
    return slice(head * HEAD_DIM, (head + 1) * HEAD_DIM)


def shard_parts(ref, tokens, c_rows):
    return slice(0, tokens + c_rows), slice(tokens + c_rows, 2 * (tokens + c_rows))


def own_kernel(
    count, hops, own_ref, limit_ref, targets_ref, q_ref, shard_ref,
    qt_ref, near_ref, far_ref, pick_ref, high_ref, total_ref, accum_ref,
):
    kv_local, _, rows = qt_ref.shape
    tokens = q_ref.shape[0]
    c_rows = far_ref.shape[1]
    own = own_ref[0]
    limit = limit_ref[0]
    place = lax.broadcasted_iota(jnp.int32, (tokens, tokens), 0)
    token = lax.broadcasted_iota(jnp.int32, (tokens, tokens), 1)
    pick = jnp.where(place == token, jnp.float32(1.0), jnp.float32(0.0)).astype(jnp.bfloat16)
    for head in range(kv_local):
        for sub in range(GROUP):
            cols = slice(sub * tokens, (sub + 1) * tokens)
            qt_ref[head, :HEAD_DIM, cols] = q_ref[:, features(head * GROUP + sub)].T
            qt_ref[head, HEAD_DIM:, cols] = pick
    for place, hop in enumerate(hops):
        shard = shard_of(own, hop, count)
        near_ref[place] = stretch_mask(shard, own, tokens)
        far_ref[place] = cache_mask(shard, limit, c_rows, tokens)
    one, two = sent_pages(targets_ref, own, shard_of(own, -hops[-1], count), tokens // PAGE)
    row = lax.broadcasted_iota(jnp.int32, pick_ref.shape, 0)
    token = lax.broadcasted_iota(jnp.int32, pick_ref.shape, 1)
    sent = ((row < PAGE) & (one >= 0) & (token == row + one * PAGE)) | (
        (row >= PAGE) & (two >= 0) & (token == row + (two - 1) * PAGE)
    )
    pick_ref[...] = jnp.where(sent, jnp.float32(1.0), jnp.float32(0.0)).astype(jnp.bfloat16)
    mask = jnp.concatenate([stretch_mask(own, own, tokens), cache_mask(own, limit, c_rows, tokens)], axis=0)
    key_rows, value_rows = shard_parts(shard_ref, tokens, c_rows)
    keys = [jnp.concatenate([shard_ref[key_rows, features(head)], mask], axis=1) for head in range(kv_local)]
    values_t = [shard_ref[value_rows, features(head)].T for head in range(kv_local)]
    attend(qt_ref, keys, values_t, None, (high_ref, total_ref, accum_ref))


def held_kernel(
    own_ref, targets_ref, length_ref, q_ref, lists_ref, pool_k, pool_v, rest_ref,
    wide_ref, high_ref, total_ref, mixed_ref,
):
    kv_width = rest_ref.shape[1]
    pool = pool_k.shape[0]
    held = pool * PAGE
    tokens = PAGE * P_DEV
    half = rest_ref.shape[0] // 2
    own = own_ref[0]
    lists = lists_ref[...]
    lengths = length_column(length_ref)
    wide_ref[...] = wide_queries(q_ref, kv_width // HEAD_DIM)
    held_slot = lax.broadcasted_iota(jnp.int32, (1, held), 1) // PAGE
    own_slot = slot_row(targets_ref, own, own, tokens, pool)
    parts = [
        (
            pool_k[...].reshape(held, kv_width),
            pool_v[...].reshape(held, kv_width),
            tally_of(lists, lengths, held_slot),
        ),
        (rest_ref[:tokens], rest_ref[half : half + tokens], tally_of(lists, lengths, own_slot)),
    ]
    high_ref[...], total_ref[...], mixed_ref[...] = decode_attend(wide_ref[...], parts, None)


def hop_kernel(places, qt_ref, near_ref, far_ref, high_in, total_in, accum_in, *refs):
    shard_refs, outs = refs[: len(places)], refs[len(places) :]
    tokens, c_rows = near_ref.shape[1], far_ref.shape[1]
    mask = jnp.concatenate([ref[place] for place in places for ref in (near_ref, far_ref)], axis=0)
    keys, values_t = [], []
    for head in range(qt_ref.shape[0]):
        pieces, values = [], []
        for ref in shard_refs:
            key_rows, value_rows = shard_parts(ref, tokens, c_rows)
            pieces.append(ref[key_rows, features(head)])
            values.append(ref[value_rows, features(head)])
        keys.append(jnp.concatenate([jnp.concatenate(pieces, axis=0), mask], axis=1))
        values_t.append(jnp.concatenate(values, axis=0).T)
    attend(qt_ref, keys, values_t, (high_in, total_in, accum_in), outs)


def pick_kernel(pick_ref, shard_ref, pages_ref):
    tokens = pick_ref.shape[1]
    sent = pick_ref.shape[0]
    for place, start in enumerate((0, shard_ref.shape[0] // 2)):
        rows = jnp.dot(pick_ref[...], shard_ref[start : start + tokens], preferred_element_type=jnp.float32)
        pages_ref[place * sent : (place + 1) * sent] = rows.astype(jnp.bfloat16)


def split_kernel(shard_ref, keys_ref, stretch_ref, values_ref):
    c_rows = keys_ref.shape[0]
    tokens = stretch_ref.shape[0] // 2
    half = tokens + c_rows
    for place, start in enumerate((0, half)):
        stretch_ref[place * tokens : (place + 1) * tokens] = shard_ref[start : start + tokens]
    keys_ref[...] = shard_ref[tokens:half]
    values_ref[...] = shard_ref[half + tokens :]


def new_pages_kernel(count, hops, tokens, pool, own_ref, targets_ref, length_ref, lists_ref, *refs):
    shard_refs, refs = refs[: len(hops) - 1], refs[len(hops) - 1 :]
    pages_ref, wide_ref, dec_high, dec_total, dec_mixed, dec_out = refs
    own = own_ref[0]
    lists = lists_ref[...]
    lengths = length_column(length_ref)
    parts = []
    for hop, ref in zip(hops, shard_refs):
        half = ref.shape[0] // 2
        slot = slot_row(targets_ref, shard_of(own, hop, count), own, tokens, pool)
        parts.append((ref[:tokens], ref[half : half + tokens], tally_of(lists, lengths, slot)))
    sent = pages_ref.shape[0] // 2
    slot = sent_slots(targets_ref, shard_of(own, hops[-1], count), own, tokens // PAGE, pool)
    parts.append((pages_ref[:sent], pages_ref[sent:], tally_of(lists, lengths, slot)))
    _, total, mixed = decode_attend(wide_ref[...], parts, (dec_high[...], dec_total[...], dec_mixed[...]))
    share = 1.0 / total
    for head in range(dec_high.shape[0]):
        piece = mixed[head, :, features(head // GROUP)] * share[head]
        dec_out[:, features(head)] = piece.astype(jnp.bfloat16)


def score_kernel(
    final, qt_ref, near_ref, far_ref, high_in, total_in, accum_in, keys_ref, stretch_ref,
    weights_ref, total_ref, accum_ref,
):
    kv_local = qt_ref.shape[0]
    tokens, c_rows = near_ref.shape[1], far_ref.shape[1]
    mask = jnp.concatenate([near_ref[final], far_ref[final]], axis=0)
    keys, values_t = [], []
    for head in range(kv_local):
        pieces = [stretch_ref[:tokens, features(head)], keys_ref[:, features(head)]]
        keys.append(jnp.concatenate([jnp.concatenate(pieces, axis=0), mask], axis=1))
        values_t.append(stretch_ref[tokens:, features(head)].T)

    def second(block, scores):
        head, cols = block
        before = (high_in[head, :, cols], total_in[head, :, cols])
        weights, _, total, decay = soften(scores, before)
        weights_ref[head, :, cols] = weights[tokens:]
        total_ref[head, :, cols] = total
        accum_ref[head, :, cols] = accum_in[head, :, cols] * decay + jnp.dot(
            values_t[head], weights[:tokens], preferred_element_type=jnp.float32
        )

    walk(blocks_of(qt_ref), lambda block: scores_of(qt_ref, block[0], block[1], keys[block[0]]), second)


def last_kernel(weights_ref, total_ref, accum_ref, values_ref, out_ref, result_ref, sems):
    tokens = result_ref.shape[0]
    values_t = [values_ref[:, features(head)].T for head in range(weights_ref.shape[0])]
    copies = []

    def first(block):
        head, cols = block
        return jnp.dot(values_t[head], weights_ref[head, :, cols], preferred_element_type=jnp.float32)

    def second(block, mixed):
        head, cols = block
        mixed = mixed + accum_ref[head, :, cols]
        mixed = (mixed * (1.0 / total_ref[head, :, cols])).astype(jnp.bfloat16)
        start = (head * GROUP + cols.start // tokens) * HEAD_DIM
        pieces = (cols.stop - cols.start) // tokens
        for piece in range(pieces):
            col = start + piece * HEAD_DIM
            result_ref[:, col : col + HEAD_DIM] = mixed[:, piece * tokens : (piece + 1) * tokens].T
        span = pl.ds(start, pieces * HEAD_DIM)
        copy = pltpu.make_async_copy(result_ref.at[:, span], out_ref.at[:, span], sems.at[len(copies)])
        copy.start()
        copies.append(copy)

    walk(blocks_of(weights_ref), first, second)

    for copy in copies:
        copy.wait()


def per_device(
    count,
    queries,
    stretch_keys,
    stretch_values,
    cache_keys,
    cache_values,
    prefix_length,
    page_targets,
    pool_keys,
    pool_values,
    decode_queries,
    page_lists,
    context_length,
):
    own = lax.axis_index("ctx")
    own_array = jnp.full((1,), own, jnp.int32)
    tokens, width = queries.shape
    kv_width = stretch_keys.shape[1]
    kv_local = kv_width // HEAD_DIM
    rows = GROUP * tokens
    heads = kv_local * GROUP
    dec_rows = decode_queries.shape[0]
    c_rows = cache_keys.shape[0]
    pool = pool_keys.shape[0]
    f32, bf16 = jnp.float32, jnp.bfloat16
    shape = jax.ShapeDtypeStruct
    params = pltpu.CompilerParams(vmem_limit_bytes=VMEM_BYTES)
    up_pairs = [(i, (i + 1) % count) for i in range(count)]
    down_pairs = [(i, (i - 1) % count) for i in range(count)]
    hops = []
    for far in range(1, count // 2 + 1):
        hops += [-far, far] if far <= (count - 1) // 2 else [-far]

    def send(array, hop):
        return lax.ppermute(array, "ctx", up_pairs if hop < 0 else down_pairs)

    def cost(keys):
        pairs = kv_local * rows * keys
        return pl.CostEstimate(
            flops=4 * pairs * HEAD_DIM, bytes_accessed=4 * rows * kv_local * HEAD_DIM, transcendentals=pairs
        )

    half = tokens + c_rows
    low = jnp.array(-jnp.inf, bf16)
    spread, start = [], 0
    for part in (stretch_keys, cache_keys, stretch_values, cache_values):
        end = 2 * half - start - part.shape[0]
        spread.append(lax.pad(part, low, ((start, end, 0), (0, 0, 0))))
        start += part.shape[0]
    shard = {0: functools.reduce(jnp.maximum, spread)}
    shard[-1] = send(shard[0], -1)

    state_shapes = (
        shape((kv_local, 1, rows), f32),
        shape((kv_local, 1, rows), f32),
        shape((kv_local, HEAD_DIM, rows), f32),
    )
    qt, near, far, pick, *state = pl.pallas_call(
        functools.partial(own_kernel, count, hops),
        out_shape=(
            shape((kv_local, HEAD_DIM + tokens, rows), bf16),
            shape((count - 1, tokens, tokens), bf16),
            shape((count - 1, c_rows, tokens), bf16),
            shape((SEND_CAP * PAGE, tokens), bf16),
        )
        + state_shapes,
        in_specs=[SMEM] * 3 + [VMEM] * 2,
        out_specs=(VMEM,) * 7,
        compiler_params=params,
        cost_estimate=cost(tokens + c_rows),
        name="own_shard",
    )(own_array, prefix_length, page_targets, queries, shard[0])

    dec_shapes = (
        shape((heads, dec_rows, 1), f32),
        shape((heads, dec_rows, 1), f32),
        shape((heads, dec_rows, kv_width), f32),
    )
    wide, *dec_state = pl.pallas_call(
        held_kernel,
        out_shape=(shape((heads * dec_rows, kv_width), bf16),) + dec_shapes,
        in_specs=[SMEM] * 3 + [VMEM] * 5,
        out_specs=(VMEM,) * 4,
        compiler_params=params,
        cost_estimate=pl.CostEstimate(
            flops=4 * 128 * 2048 * 256, bytes_accessed=4 * pool_keys.size, transcendentals=128 * 2048
        ),
        name="decode_held_pages",
    )(own_array, page_targets, context_length, decode_queries, page_lists, pool_keys, pool_values, shard[0])

    if 1 in hops:
        sent_down, state, dec_state = lax.optimization_barrier((shard[0], state, dec_state))
        shard[1] = send(sent_down, 1)
    shard[-1], state, dec_state = lax.optimization_barrier((shard[-1], state, dec_state))
    for hop in hops[2:-1]:
        shard[hop] = send(shard[hop + 1 if hop < 0 else hop - 1], hop)
    hop = hops[-1]
    nearer = shard[hop + 1 if hop < 0 else hop - 1]
    pieces = pl.pallas_call(
        split_kernel,
        out_shape=(
            shape((c_rows, kv_width), bf16),
            shape((2 * tokens, kv_width), bf16),
            shape((c_rows, kv_width), bf16),
        ),
        in_specs=[VMEM],
        out_specs=(VMEM,) * 3,
        compiler_params=params,
        name="pieces_to_send_on",
    )(nearer)
    far_pages = pl.pallas_call(
        pick_kernel,
        out_shape=shape((2 * SEND_CAP * PAGE, kv_width), bf16),
        in_specs=[VMEM] * 2,
        out_specs=VMEM,
        compiler_params=params,
        name="pages_to_send",
    )(pick, shard[0])
    far_pages = lax.ppermute(far_pages, "ctx", [(i, (i - hop) % count) for i in range(count)])
    last_keys = send(pieces[0], hop)
    attending = [pair for pair in (up_pairs if hop < 0 else down_pairs) if (pair[1] + hop) % count < pair[1]]
    last_stretch = lax.ppermute(pieces[1], "ctx", attending)

    for place, hop in enumerate(hops[:-1]):
        if place == 1:
            last_piece, far_pages, state = lax.optimization_barrier((pieces[2], far_pages, state))
            last_values = send(last_piece, hops[-1])
        state = pl.pallas_call(
            functools.partial(hop_kernel, [place]),
            out_shape=state_shapes,
            in_specs=[VMEM] * 7,
            out_specs=(VMEM,) * 3,
            compiler_params=params,
            cost_estimate=cost(half),
            name="whole_shards_" + str(place),
        )(qt, near, far, *state, shard[hop])

    final = len(hops) - 1
    dec_state, state = lax.optimization_barrier((dec_state, state))
    decoded = pl.pallas_call(
        functools.partial(new_pages_kernel, count, hops, tokens, pool),
        out_shape=shape(decode_queries.shape, bf16),
        in_specs=[SMEM] * 3 + [VMEM] * (6 + len(hops) - 1),
        out_specs=VMEM,
        compiler_params=params,
        cost_estimate=cost(tokens),
        name="decode_new_pages",
    )(
        own_array, page_targets, context_length, page_lists, *[shard[hop] for hop in hops[:-1]], far_pages,
        wide, *dec_state,
    )
    decoded, state = lax.optimization_barrier((decoded, state))

    weights, total, accum = pl.pallas_call(
        functools.partial(score_kernel, final),
        out_shape=(shape((kv_local, c_rows, rows), bf16),) + state_shapes[1:],
        in_specs=[VMEM] * 8,
        out_specs=(VMEM,) * 3,
        compiler_params=params,
        cost_estimate=cost(half),
        name="last_scores",
    )(qt, near, far, *state, last_keys, last_stretch)

    prefill = pl.pallas_call(
        last_kernel,
        out_shape=shape((tokens, width), bf16),
        in_specs=[VMEM] * 4,
        out_specs=HBM,
        scratch_shapes=[
            pltpu.VMEM((tokens, width), bf16),
            pltpu.SemaphoreType.DMA((kv_local * max(GROUP // 2, 1),)),
        ],
        compiler_params=params,
        cost_estimate=cost(c_rows // 2),
        name="last_values",
    )(weights, total, accum, last_values)
    return (prefill, decoded)


def solution(mesh):
    in_specs = (
        P(("groups", "ctx"), "head"),
        P(("groups", "ctx"), "head"),
        P(("groups", "ctx"), "head"),
        P(("groups", "ctx"), "head"),
        P(("groups", "ctx"), "head"),
        P("groups"),
        P("groups"),
        P(("groups", "ctx"), None, "head"),
        P(("groups", "ctx"), None, "head"),
        P(("groups", "ctx"), "head"),
        P(("groups", "ctx"), None),
        P(("groups", "ctx")),
    )
    out_specs = (P(("groups", "ctx"), "head"), P(("groups", "ctx"), "head"))
    return jax.shard_map(
        functools.partial(per_device, mesh.shape["ctx"]),
        mesh=mesh,
        in_specs=in_specs,
        out_specs=out_specs,
        check_vma=False,
    )
```

```python
import functools

import jax
import jax.numpy as jnp
from jax import lax
from jax.experimental import pallas as pl
from jax.experimental.pallas import tpu as pltpu
from jax.sharding import PartitionSpec as P

HEADS = 64
KV_HEADS = 8
HEAD_DIM = 128
GROUP = HEADS // KV_HEADS
PAGE = 16
P_DEV = 8
SEND_CAP = 2
EXP2_SCALE = HEAD_DIM ** (-0.5) * 1.4426950408889634
HIDDEN = -1e30
VMEM_BYTES = 48 * 1024 * 1024

VMEM = pl.BlockSpec(memory_space=pltpu.VMEM)
SMEM = pl.BlockSpec(memory_space=pltpu.SMEM)
HBM = pl.BlockSpec(memory_space=pltpu.HBM)


def scores_of(qt_ref, head, cols, keys):
    return jnp.dot(keys, qt_ref[head, :, cols], preferred_element_type=jnp.float32)


def soften(scores, old):
    high = jnp.max(scores, axis=0, keepdims=True)
    if old is None:
        weights = jnp.exp2((scores - high) * EXP2_SCALE)
        return weights.astype(jnp.bfloat16), high, jnp.sum(weights, axis=0, keepdims=True), None
    old_high, old_total = old
    high = jnp.maximum(high, old_high)
    decay = jnp.exp2((old_high - high) * EXP2_SCALE)
    weights = jnp.exp2((scores - high) * EXP2_SCALE)
    total = old_total * decay + jnp.sum(weights, axis=0, keepdims=True)
    return weights.astype(jnp.bfloat16), high, total, decay


def walk(blocks, first, second):
    ahead = first(blocks[0])
    for place, block in enumerate(blocks):
        current = ahead
        if place + 1 < len(blocks):
            ahead = first(blocks[place + 1])
        second(block, current)


def blocks_of(qt_ref):
    kv_local, _, rows = qt_ref.shape
    width = min(2 * (rows // GROUP), rows)
    return [(head, slice(start, start + width)) for head in range(kv_local) for start in range(0, rows, width)]


def attend(qt_ref, keys, values_t, old, new):
    high_ref, total_ref, accum_ref = new

    def second(block, scores):
        head, cols = block
        before = None if old is None else (old[0][head, :, cols], old[1][head, :, cols])
        weights, high, total, decay = soften(scores, before)
        accum = jnp.dot(values_t[head], weights, preferred_element_type=jnp.float32)
        if old is not None:
            accum = accum + old[2][head, :, cols] * decay
        high_ref[head, :, cols] = high
        total_ref[head, :, cols] = total
        accum_ref[head, :, cols] = accum

    walk(blocks_of(qt_ref), lambda block: scores_of(qt_ref, block[0], block[1], keys[block[0]]), second)


def hidden(seen):
    return jnp.where(seen, jnp.float32(0.0), jnp.float32(HIDDEN)).astype(jnp.bfloat16)


def stretch_mask(shard, own, tokens):
    place = lax.broadcasted_iota(jnp.int32, (tokens, tokens), 0)
    token = lax.broadcasted_iota(jnp.int32, (tokens, tokens), 1)
    return hidden(place - token <= (own - shard) * tokens)


def cache_mask(shard, limit, c_rows, tokens):
    place = lax.broadcasted_iota(jnp.int32, (c_rows, tokens), 0)
    return hidden(place < limit - shard * c_rows)


def slot_row(targets_ref, shard, own, tokens, pool):
    page = lax.broadcasted_iota(jnp.int32, (1, tokens), 1) // PAGE
    slots = jnp.full((1, tokens), -1, jnp.int32)
    for index in range(tokens // PAGE):
        target = targets_ref[shard * (tokens // PAGE) + index]
        slot = jnp.where(lax.div(target, P_DEV) == own, pool + lax.rem(target, P_DEV), -1)
        slots = jnp.where(page == index, slot, slots)
    return slots


def sent_pages(targets_ref, shard, owner, pages):
    one, two = jnp.int32(-1), jnp.int32(-1)
    for index in range(pages):
        hit = lax.div(targets_ref[shard * pages + index], P_DEV) == owner
        two = jnp.where(hit & (one >= 0) & (two < 0), index, two)
        one = jnp.where(hit & (one < 0), index, one)
    return one, two


def sent_slots(targets_ref, shard, owner, pages, pool):
    place = lax.broadcasted_iota(jnp.int32, (1, SEND_CAP * PAGE), 1)
    slots = []
    for index in sent_pages(targets_ref, shard, owner, pages):
        target = targets_ref[shard * pages + jnp.maximum(index, 0)]
        slots.append(jnp.where(index >= 0, pool + lax.rem(target, P_DEV), -1))
    return jnp.where(place < PAGE, slots[0], slots[1])


def length_column(length_ref):
    rows = length_ref.shape[0]
    place = lax.broadcasted_iota(jnp.int32, (rows, 1), 0)
    lengths = jnp.zeros((rows, 1), jnp.int32)
    for row in range(rows):
        lengths = jnp.where(place == row, length_ref[row], lengths)
    return lengths


def tally_of(lists, lengths, slot):
    rows, span = lists.shape
    tokens = slot.shape[1]
    slot = jnp.broadcast_to(slot, (rows, tokens))
    offset = lax.rem(lax.broadcasted_iota(jnp.int32, (rows, tokens), 1), PAGE)
    tally = jnp.zeros((rows, tokens), jnp.float32)
    for entry in range(span):
        hit = (slot == lists[:, entry : entry + 1]) & (offset < lengths - entry * PAGE)
        tally = tally + jnp.where(hit, jnp.float32(1.0), jnp.float32(0.0))
    return tally[None]


def shard_of(own, hop, count):
    return lax.rem(own + hop + count, count)


def wide_queries(q_ref, kv_local):
    heads = q_ref.shape[1] // HEAD_DIM
    queries = q_ref[...].astype(jnp.float32)
    stacked = []
    for head in range(heads):
        piece = queries[:, head * HEAD_DIM : (head + 1) * HEAD_DIM]
        blank = jnp.zeros_like(piece)
        stacked.append(
            jnp.concatenate([piece if kv == head // GROUP else blank for kv in range(kv_local)], axis=1)
        )
    return jnp.concatenate(stacked, axis=0).astype(jnp.bfloat16)


def decode_attend(queries, parts, state):
    done = []
    for keys, values, tally in parts:
        scores = lax.dot_general(
            queries, keys, (((1,), (1,)), ((), ())), preferred_element_type=jnp.float32
        ).reshape(-1, tally.shape[1], tally.shape[2])
        done.append((jnp.where(tally > 0, scores, jnp.float32(HIDDEN)), tally, values))
    highs = [jnp.max(scores, axis=-1, keepdims=True) for scores, _, _ in done]
    if state is not None:
        old_high, old_total, old_mixed = state
        highs.append(old_high)
    high = functools.reduce(jnp.maximum, highs)
    total, mixed = 0.0, 0.0
    if state is not None:
        decay = jnp.exp2((old_high - high) * EXP2_SCALE)
        total = old_total * decay
        mixed = old_mixed * decay
    for scores, tally, values in done:
        weights = jnp.exp2((scores - high) * EXP2_SCALE) * tally
        total = total + jnp.sum(weights, axis=-1, keepdims=True)
        mixed = mixed + jnp.dot(
            weights.reshape(queries.shape[0], -1).astype(jnp.bfloat16),
            values,
            preferred_element_type=jnp.float32,
        ).reshape(high.shape[0], high.shape[1], -1)
    return high, total, mixed


def features(head):
    return slice(head * HEAD_DIM, (head + 1) * HEAD_DIM)


def shard_parts(ref, tokens, c_rows):
    return slice(0, tokens + c_rows), slice(tokens + c_rows, 2 * (tokens + c_rows))


def own_kernel(
    count, hops, own_ref, limit_ref, targets_ref, q_ref, shard_ref,
    qt_ref, near_ref, far_ref, pick_ref, high_ref, total_ref, accum_ref,
):
    kv_local, _, rows = qt_ref.shape
    tokens = q_ref.shape[0]
    c_rows = far_ref.shape[1]
    own = own_ref[0]
    limit = limit_ref[0]
    place = lax.broadcasted_iota(jnp.int32, (tokens, tokens), 0)
    token = lax.broadcasted_iota(jnp.int32, (tokens, tokens), 1)
    pick = jnp.where(place == token, jnp.float32(1.0), jnp.float32(0.0)).astype(jnp.bfloat16)
    for head in range(kv_local):
        for sub in range(GROUP):
            cols = slice(sub * tokens, (sub + 1) * tokens)
            qt_ref[head, :HEAD_DIM, cols] = q_ref[:, features(head * GROUP + sub)].T
            qt_ref[head, HEAD_DIM:, cols] = pick
    for place, hop in enumerate(hops):
        shard = shard_of(own, hop, count)
        near_ref[place] = stretch_mask(shard, own, tokens)
        far_ref[place] = cache_mask(shard, limit, c_rows, tokens)
    one, two = sent_pages(targets_ref, own, shard_of(own, -hops[-1], count), tokens // PAGE)
    row = lax.broadcasted_iota(jnp.int32, pick_ref.shape, 0)
    token = lax.broadcasted_iota(jnp.int32, pick_ref.shape, 1)
    sent = ((row < PAGE) & (one >= 0) & (token == row + one * PAGE)) | (
        (row >= PAGE) & (two >= 0) & (token == row + (two - 1) * PAGE)
    )
    pick_ref[...] = jnp.where(sent, jnp.float32(1.0), jnp.float32(0.0)).astype(jnp.bfloat16)
    mask = jnp.concatenate([stretch_mask(own, own, tokens), cache_mask(own, limit, c_rows, tokens)], axis=0)
    key_rows, value_rows = shard_parts(shard_ref, tokens, c_rows)
    keys = [jnp.concatenate([shard_ref[key_rows, features(head)], mask], axis=1) for head in range(kv_local)]
    values_t = [shard_ref[value_rows, features(head)].T for head in range(kv_local)]
    attend(qt_ref, keys, values_t, None, (high_ref, total_ref, accum_ref))


def held_kernel(
    own_ref, targets_ref, length_ref, q_ref, lists_ref, pool_k, pool_v, rest_ref,
    wide_ref, high_ref, total_ref, mixed_ref,
):
    kv_width = rest_ref.shape[1]
    pool = pool_k.shape[0]
    held = pool * PAGE
    tokens = PAGE * P_DEV
    half = rest_ref.shape[0] // 2
    own = own_ref[0]
    lists = lists_ref[...]
    lengths = length_column(length_ref)
    wide_ref[...] = wide_queries(q_ref, kv_width // HEAD_DIM)
    held_slot = lax.broadcasted_iota(jnp.int32, (1, held), 1) // PAGE
    own_slot = slot_row(targets_ref, own, own, tokens, pool)
    parts = [
        (
            pool_k[...].reshape(held, kv_width),
            pool_v[...].reshape(held, kv_width),
            tally_of(lists, lengths, held_slot),
        ),
        (rest_ref[:tokens], rest_ref[half : half + tokens], tally_of(lists, lengths, own_slot)),
    ]
    high_ref[...], total_ref[...], mixed_ref[...] = decode_attend(wide_ref[...], parts, None)


def hop_kernel(places, qt_ref, near_ref, far_ref, high_in, total_in, accum_in, *refs):
    shard_refs, outs = refs[: len(places)], refs[len(places) :]
    tokens, c_rows = near_ref.shape[1], far_ref.shape[1]
    mask = jnp.concatenate([ref[place] for place in places for ref in (near_ref, far_ref)], axis=0)
    keys, values_t = [], []
    for head in range(qt_ref.shape[0]):
        pieces, values = [], []
        for ref in shard_refs:
            key_rows, value_rows = shard_parts(ref, tokens, c_rows)
            pieces.append(ref[key_rows, features(head)])
            values.append(ref[value_rows, features(head)])
        keys.append(jnp.concatenate([jnp.concatenate(pieces, axis=0), mask], axis=1))
        values_t.append(jnp.concatenate(values, axis=0).T)
    attend(qt_ref, keys, values_t, (high_in, total_in, accum_in), outs)


def pick_kernel(pick_ref, shard_ref, pages_ref):
    tokens = pick_ref.shape[1]
    sent = pick_ref.shape[0]
    for place, start in enumerate((0, shard_ref.shape[0] // 2)):
        rows = jnp.dot(pick_ref[...], shard_ref[start : start + tokens], preferred_element_type=jnp.float32)
        pages_ref[place * sent : (place + 1) * sent] = rows.astype(jnp.bfloat16)


def split_kernel(shard_ref, keys_ref, stretch_ref, values_ref):
    c_rows = keys_ref.shape[0]
    tokens = stretch_ref.shape[0] // 2
    half = tokens + c_rows
    for place, start in enumerate((0, half)):
        stretch_ref[place * tokens : (place + 1) * tokens] = shard_ref[start : start + tokens]
    keys_ref[...] = shard_ref[tokens:half]
    values_ref[...] = shard_ref[half + tokens :]


def near_pages_kernel(count, hops, tokens, pool, own_ref, targets_ref, length_ref, lists_ref, *refs):
    shard_refs, refs = refs[: len(hops) - 1], refs[len(hops) - 1 :]
    wide_ref, dec_high, dec_total, dec_mixed, high_ref, total_ref, mixed_ref, tally_ref = refs
    own = own_ref[0]
    lists = lists_ref[...]
    lengths = length_column(length_ref)
    parts = []
    for hop, ref in zip(hops, shard_refs):
        half = ref.shape[0] // 2
        slot = slot_row(targets_ref, shard_of(own, hop, count), own, tokens, pool)
        parts.append((ref[:tokens], ref[half : half + tokens], tally_of(lists, lengths, slot)))
    state = (dec_high[...], dec_total[...], dec_mixed[...])
    high_ref[...], total_ref[...], mixed_ref[...] = decode_attend(wide_ref[...], parts, state)
    shard = shard_of(own, hops[-1], count)
    attended = shard < own
    whole = jnp.where(attended, slot_row(targets_ref, shard, own, tokens, pool), -1)
    alone = jnp.where(attended, -1, sent_slots(targets_ref, shard, own, tokens // PAGE, pool))
    tally_ref[:, :, :tokens] = tally_of(lists, lengths, whole)
    tally_ref[:, :, tokens:] = tally_of(lists, lengths, alone)


def score_kernel(
    final, qt_ref, near_ref, far_ref, high_in, total_in, accum_in, keys_ref, stretch_ref,
    weights_ref, total_ref, accum_ref,
):
    kv_local = qt_ref.shape[0]
    tokens, c_rows = near_ref.shape[1], far_ref.shape[1]
    mask = jnp.concatenate([near_ref[final], far_ref[final]], axis=0)
    keys, values_t = [], []
    for head in range(kv_local):
        pieces = [stretch_ref[:tokens, features(head)], keys_ref[:, features(head)]]
        keys.append(jnp.concatenate([jnp.concatenate(pieces, axis=0), mask], axis=1))
        values_t.append(stretch_ref[tokens:, features(head)].T)

    def second(block, scores):
        head, cols = block
        before = (high_in[head, :, cols], total_in[head, :, cols])
        weights, _, total, decay = soften(scores, before)
        weights_ref[head, :, cols] = weights[tokens:]
        total_ref[head, :, cols] = total
        accum_ref[head, :, cols] = accum_in[head, :, cols] * decay + jnp.dot(
            values_t[head], weights[:tokens], preferred_element_type=jnp.float32
        )

    walk(blocks_of(qt_ref), lambda block: scores_of(qt_ref, block[0], block[1], keys[block[0]]), second)


def last_pages_kernel(
    stretch_ref, pages_ref, tally_ref, wide_ref, dec_high, dec_total, dec_mixed, dec_out
):
    tokens = stretch_ref.shape[0] // 2
    sent = pages_ref.shape[0] // 2
    keys = jnp.concatenate([stretch_ref[:tokens], pages_ref[:sent]], axis=0)
    values = jnp.concatenate([stretch_ref[tokens:], pages_ref[sent:]], axis=0)
    state = (dec_high[...], dec_total[...], dec_mixed[...])
    _, total, mixed = decode_attend(wide_ref[...], [(keys, values, tally_ref[...])], state)
    share = 1.0 / total
    for head in range(dec_high.shape[0]):
        piece = mixed[head, :, features(head // GROUP)] * share[head]
        dec_out[:, features(head)] = piece.astype(jnp.bfloat16)


def last_kernel(weights_ref, total_ref, accum_ref, values_ref, out_ref, result_ref, sems):
    tokens = result_ref.shape[0]
    values_t = [values_ref[:, features(head)].T for head in range(weights_ref.shape[0])]
    copies = []

    def first(block):
        head, cols = block
        return jnp.dot(values_t[head], weights_ref[head, :, cols], preferred_element_type=jnp.float32)

    def second(block, mixed):
        head, cols = block
        mixed = mixed + accum_ref[head, :, cols]
        mixed = (mixed * (1.0 / total_ref[head, :, cols])).astype(jnp.bfloat16)
        start = (head * GROUP + cols.start // tokens) * HEAD_DIM
        pieces = (cols.stop - cols.start) // tokens
        for piece in range(pieces):
            col = start + piece * HEAD_DIM
            result_ref[:, col : col + HEAD_DIM] = mixed[:, piece * tokens : (piece + 1) * tokens].T
        span = pl.ds(start, pieces * HEAD_DIM)
        copy = pltpu.make_async_copy(result_ref.at[:, span], out_ref.at[:, span], sems.at[len(copies)])
        copy.start()
        copies.append(copy)

    walk(blocks_of(weights_ref), first, second)

    for copy in copies:
        copy.wait()


def per_device(
    count,
    queries,
    stretch_keys,
    stretch_values,
    cache_keys,
    cache_values,
    prefix_length,
    page_targets,
    pool_keys,
    pool_values,
    decode_queries,
    page_lists,
    context_length,
):
    own = lax.axis_index("ctx")
    own_array = jnp.full((1,), own, jnp.int32)
    tokens, width = queries.shape
    kv_width = stretch_keys.shape[1]
    kv_local = kv_width // HEAD_DIM
    rows = GROUP * tokens
    heads = kv_local * GROUP
    dec_rows = decode_queries.shape[0]
    c_rows = cache_keys.shape[0]
    pool = pool_keys.shape[0]
    f32, bf16 = jnp.float32, jnp.bfloat16
    shape = jax.ShapeDtypeStruct
    params = pltpu.CompilerParams(vmem_limit_bytes=VMEM_BYTES)
    up_pairs = [(i, (i + 1) % count) for i in range(count)]
    down_pairs = [(i, (i - 1) % count) for i in range(count)]
    hops = []
    for far in range(1, count // 2 + 1):
        hops += [-far, far] if far <= (count - 1) // 2 else [-far]

    def send(array, hop):
        return lax.ppermute(array, "ctx", up_pairs if hop < 0 else down_pairs)

    def cost(keys):
        pairs = kv_local * rows * keys
        return pl.CostEstimate(
            flops=4 * pairs * HEAD_DIM, bytes_accessed=4 * rows * kv_local * HEAD_DIM, transcendentals=pairs
        )

    half = tokens + c_rows
    low = jnp.array(-jnp.inf, bf16)
    spread, start = [], 0
    for part in (stretch_keys, cache_keys, stretch_values, cache_values):
        end = 2 * half - start - part.shape[0]
        spread.append(lax.pad(part, low, ((start, end, 0), (0, 0, 0))))
        start += part.shape[0]
    shard = {0: functools.reduce(jnp.maximum, spread)}
    shard[-1] = send(shard[0], -1)

    state_shapes = (
        shape((kv_local, 1, rows), f32),
        shape((kv_local, 1, rows), f32),
        shape((kv_local, HEAD_DIM, rows), f32),
    )
    qt, near, far, pick, *state = pl.pallas_call(
        functools.partial(own_kernel, count, hops),
        out_shape=(
            shape((kv_local, HEAD_DIM + tokens, rows), bf16),
            shape((count - 1, tokens, tokens), bf16),
            shape((count - 1, c_rows, tokens), bf16),
            shape((SEND_CAP * PAGE, tokens), bf16),
        )
        + state_shapes,
        in_specs=[SMEM] * 3 + [VMEM] * 2,
        out_specs=(VMEM,) * 7,
        compiler_params=params,
        cost_estimate=cost(tokens + c_rows),
        name="own_shard",
    )(own_array, prefix_length, page_targets, queries, shard[0])

    dec_shapes = (
        shape((heads, dec_rows, 1), f32),
        shape((heads, dec_rows, 1), f32),
        shape((heads, dec_rows, kv_width), f32),
    )
    wide, *dec_state = pl.pallas_call(
        held_kernel,
        out_shape=(shape((heads * dec_rows, kv_width), bf16),) + dec_shapes,
        in_specs=[SMEM] * 3 + [VMEM] * 5,
        out_specs=(VMEM,) * 4,
        compiler_params=params,
        cost_estimate=pl.CostEstimate(
            flops=4 * 128 * 2048 * 256, bytes_accessed=4 * pool_keys.size, transcendentals=128 * 2048
        ),
        name="decode_held_pages",
    )(own_array, page_targets, context_length, decode_queries, page_lists, pool_keys, pool_values, shard[0])

    if 1 in hops:
        sent_down, state, dec_state = lax.optimization_barrier((shard[0], state, dec_state))
        shard[1] = send(sent_down, 1)
    shard[-1], state, dec_state = lax.optimization_barrier((shard[-1], state, dec_state))
    for hop in hops[2:-1]:
        shard[hop] = send(shard[hop + 1 if hop < 0 else hop - 1], hop)
    hop = hops[-1]
    nearer = shard[hop + 1 if hop < 0 else hop - 1]
    pieces = pl.pallas_call(
        split_kernel,
        out_shape=(
            shape((c_rows, kv_width), bf16),
            shape((2 * tokens, kv_width), bf16),
            shape((c_rows, kv_width), bf16),
        ),
        in_specs=[VMEM],
        out_specs=(VMEM,) * 3,
        compiler_params=params,
        name="pieces_to_send_on",
    )(nearer)
    far_pages = pl.pallas_call(
        pick_kernel,
        out_shape=shape((2 * SEND_CAP * PAGE, kv_width), bf16),
        in_specs=[VMEM] * 2,
        out_specs=VMEM,
        compiler_params=params,
        name="pages_to_send",
    )(pick, shard[0])
    straight = [(i, (i - hop) % count) for i in range(count) if i > (i - hop) % count]
    last_pages = lax.ppermute(far_pages, "ctx", straight)
    last_keys = send(pieces[0], hop)
    attending = [pair for pair in (up_pairs if hop < 0 else down_pairs) if (pair[1] + hop) % count < pair[1]]
    last_stretch = lax.ppermute(pieces[1], "ctx", attending)

    for first in range(len(hops) - 1):
        places = [first]
        state = pl.pallas_call(
            functools.partial(hop_kernel, places),
            out_shape=state_shapes,
            in_specs=[VMEM] * (6 + len(places)),
            out_specs=(VMEM,) * 3,
            compiler_params=params,
            cost_estimate=cost((c_rows + tokens) * len(places)),
            name="whole_shards_" + str(first),
        )(qt, near, far, *state, *[shard[hops[place]] for place in places])

    last_piece, last_pages, state = lax.optimization_barrier((pieces[2], last_pages, state))
    last_values = send(last_piece, hops[-1])

    final = len(hops) - 1
    dec_state, state = lax.optimization_barrier((dec_state, state))
    near_hops = hops[:-1]
    *dec_state, tally = pl.pallas_call(
        functools.partial(near_pages_kernel, count, hops, tokens, pool),
        out_shape=dec_shapes
        + (shape((1, dec_rows, tokens + SEND_CAP * PAGE), f32),),
        in_specs=[SMEM] * 3 + [VMEM] * (5 + len(near_hops)),
        out_specs=(VMEM,) * 4,
        compiler_params=params,
        cost_estimate=cost(tokens),
        name="decode_near_pages",
    )(
        own_array, page_targets, context_length, page_lists, *[shard[hop] for hop in near_hops],
        wide, *dec_state,
    )
    dec_state, state = lax.optimization_barrier((dec_state, state))

    decoded = pl.pallas_call(
        last_pages_kernel,
        out_shape=shape(decode_queries.shape, bf16),
        in_specs=[VMEM] * 7,
        out_specs=VMEM,
        compiler_params=params,
        cost_estimate=cost(tokens // 2),
        name="decode_last_pages",
    )(last_stretch, last_pages, tally, wide, *dec_state)
    decoded, state = lax.optimization_barrier((decoded, state))

    weights, total, accum = pl.pallas_call(
        functools.partial(score_kernel, final),
        out_shape=(shape((kv_local, c_rows, rows), bf16),) + state_shapes[1:],
        in_specs=[VMEM] * 8,
        out_specs=(VMEM,) * 3,
        compiler_params=params,
        cost_estimate=cost(half),
        name="last_scores",
    )(qt, near, far, *state, last_keys, last_stretch)

    prefill = pl.pallas_call(
        last_kernel,
        out_shape=shape((tokens, width), bf16),
        in_specs=[VMEM] * 4,
        out_specs=HBM,
        scratch_shapes=[
            pltpu.VMEM((tokens, width), bf16),
            pltpu.SemaphoreType.DMA((kv_local * max(GROUP // 2, 1),)),
        ],
        compiler_params=params,
        cost_estimate=cost(c_rows // 2),
        name="last_values",
    )(weights, total, accum, last_values)
    return (prefill, decoded)


def solution(mesh):
    in_specs = (
        P(("groups", "ctx"), "head"),
        P(("groups", "ctx"), "head"),
        P(("groups", "ctx"), "head"),
        P(("groups", "ctx"), "head"),
        P(("groups", "ctx"), "head"),
        P("groups"),
        P("groups"),
        P(("groups", "ctx"), None, "head"),
        P(("groups", "ctx"), None, "head"),
        P(("groups", "ctx"), "head"),
        P(("groups", "ctx"), None),
        P(("groups", "ctx")),
    )
    out_specs = (P(("groups", "ctx"), "head"), P(("groups", "ctx"), "head"))
    return jax.shard_map(
        functools.partial(per_device, mesh.shape["ctx"]),
        mesh=mesh,
        in_specs=in_specs,
        out_specs=out_specs,
        check_vma=False,
    )
```

```python
import functools

import jax
import jax.numpy as jnp
from jax import lax
from jax.experimental import pallas as pl
from jax.experimental.pallas import tpu as pltpu
from jax.sharding import PartitionSpec as P

HEADS = 64
KV_HEADS = 8
HEAD_DIM = 128
GROUP = HEADS // KV_HEADS
PAGE = 16
P_DEV = 8
SEND_CAP = 2
EXP2_SCALE = HEAD_DIM ** (-0.5) * 1.4426950408889634
HIDDEN = -1e30
VMEM_BYTES = 48 * 1024 * 1024

VMEM = pl.BlockSpec(memory_space=pltpu.VMEM)
SMEM = pl.BlockSpec(memory_space=pltpu.SMEM)
HBM = pl.BlockSpec(memory_space=pltpu.HBM)


def scores_of(qt_ref, head, cols, keys):
    return jnp.dot(keys, qt_ref[head, :, cols], preferred_element_type=jnp.float32)


def soften(scores, old):
    high = jnp.max(scores, axis=0, keepdims=True)
    if old is None:
        weights = jnp.exp2((scores - high) * EXP2_SCALE)
        return weights.astype(jnp.bfloat16), high, jnp.sum(weights, axis=0, keepdims=True), None
    old_high, old_total = old
    high = jnp.maximum(high, old_high)
    decay = jnp.exp2((old_high - high) * EXP2_SCALE)
    weights = jnp.exp2((scores - high) * EXP2_SCALE)
    total = old_total * decay + jnp.sum(weights, axis=0, keepdims=True)
    return weights.astype(jnp.bfloat16), high, total, decay


def walk(blocks, first, second):
    ahead = first(blocks[0])
    for place, block in enumerate(blocks):
        current = ahead
        if place + 1 < len(blocks):
            ahead = first(blocks[place + 1])
        second(block, current)


def blocks_of(qt_ref):
    kv_local, _, rows = qt_ref.shape
    width = min(2 * (rows // GROUP), rows)
    return [(head, slice(start, start + width)) for head in range(kv_local) for start in range(0, rows, width)]


def attend(qt_ref, keys, values_t, old, new):
    high_ref, total_ref, accum_ref = new

    def second(block, scores):
        head, cols = block
        before = None if old is None else (old[0][head, :, cols], old[1][head, :, cols])
        weights, high, total, decay = soften(scores, before)
        accum = jnp.dot(values_t[head], weights, preferred_element_type=jnp.float32)
        if old is not None:
            accum = accum + old[2][head, :, cols] * decay
        high_ref[head, :, cols] = high
        total_ref[head, :, cols] = total
        accum_ref[head, :, cols] = accum

    walk(blocks_of(qt_ref), lambda block: scores_of(qt_ref, block[0], block[1], keys[block[0]]), second)


def hidden(seen):
    return jnp.where(seen, jnp.float32(0.0), jnp.float32(HIDDEN)).astype(jnp.bfloat16)


def stretch_mask(shard, own, tokens):
    place = lax.broadcasted_iota(jnp.int32, (tokens, tokens), 0)
    token = lax.broadcasted_iota(jnp.int32, (tokens, tokens), 1)
    return hidden(place - token <= (own - shard) * tokens)


def cache_mask(shard, limit, c_rows, tokens):
    place = lax.broadcasted_iota(jnp.int32, (c_rows, tokens), 0)
    return hidden(place < limit - shard * c_rows)


def slot_row(targets_ref, shard, own, tokens, pool):
    page = lax.broadcasted_iota(jnp.int32, (1, tokens), 1) // PAGE
    slots = jnp.full((1, tokens), -1, jnp.int32)
    for index in range(tokens // PAGE):
        target = targets_ref[shard * (tokens // PAGE) + index]
        slot = jnp.where(lax.div(target, P_DEV) == own, pool + lax.rem(target, P_DEV), -1)
        slots = jnp.where(page == index, slot, slots)
    return slots


def sent_pages(targets_ref, shard, owner, pages):
    one, two = jnp.int32(-1), jnp.int32(-1)
    for index in range(pages):
        hit = lax.div(targets_ref[shard * pages + index], P_DEV) == owner
        two = jnp.where(hit & (one >= 0) & (two < 0), index, two)
        one = jnp.where(hit & (one < 0), index, one)
    return one, two


def sent_slots(targets_ref, shard, owner, pages, pool):
    place = lax.broadcasted_iota(jnp.int32, (1, SEND_CAP * PAGE), 1)
    slots = []
    for index in sent_pages(targets_ref, shard, owner, pages):
        target = targets_ref[shard * pages + jnp.maximum(index, 0)]
        slots.append(jnp.where(index >= 0, pool + lax.rem(target, P_DEV), -1))
    return jnp.where(place < PAGE, slots[0], slots[1])


def length_column(length_ref):
    rows = length_ref.shape[0]
    place = lax.broadcasted_iota(jnp.int32, (rows, 1), 0)
    lengths = jnp.zeros((rows, 1), jnp.int32)
    for row in range(rows):
        lengths = jnp.where(place == row, length_ref[row], lengths)
    return lengths


def tally_of(lists, lengths, slot):
    rows, span = lists.shape
    tokens = slot.shape[1]
    slot = jnp.broadcast_to(slot, (rows, tokens))
    offset = lax.rem(lax.broadcasted_iota(jnp.int32, (rows, tokens), 1), PAGE)
    tally = jnp.zeros((rows, tokens), jnp.float32)
    for entry in range(span):
        hit = (slot == lists[:, entry : entry + 1]) & (offset < lengths - entry * PAGE)
        tally = tally + jnp.where(hit, jnp.float32(1.0), jnp.float32(0.0))
    return tally[None]


def shard_of(own, hop, count):
    return lax.rem(own + hop + count, count)


def wide_queries(q_ref, kv_local):
    heads = q_ref.shape[1] // HEAD_DIM
    queries = q_ref[...].astype(jnp.float32)
    stacked = []
    for head in range(heads):
        piece = queries[:, head * HEAD_DIM : (head + 1) * HEAD_DIM]
        blank = jnp.zeros_like(piece)
        stacked.append(
            jnp.concatenate([piece if kv == head // GROUP else blank for kv in range(kv_local)], axis=1)
        )
    return jnp.concatenate(stacked, axis=0).astype(jnp.bfloat16)


def decode_attend(queries, parts, state):
    done = []
    for keys, values, tally in parts:
        scores = lax.dot_general(
            queries, keys, (((1,), (1,)), ((), ())), preferred_element_type=jnp.float32
        ).reshape(-1, tally.shape[1], tally.shape[2])
        done.append((jnp.where(tally > 0, scores, jnp.float32(HIDDEN)), tally, values))
    highs = [jnp.max(scores, axis=-1, keepdims=True) for scores, _, _ in done]
    if state is not None:
        old_high, old_total, old_mixed = state
        highs.append(old_high)
    high = functools.reduce(jnp.maximum, highs)
    total, mixed = 0.0, 0.0
    if state is not None:
        decay = jnp.exp2((old_high - high) * EXP2_SCALE)
        total = old_total * decay
        mixed = old_mixed * decay
    for scores, tally, values in done:
        weights = jnp.exp2((scores - high) * EXP2_SCALE) * tally
        total = total + jnp.sum(weights, axis=-1, keepdims=True)
        mixed = mixed + jnp.dot(
            weights.reshape(queries.shape[0], -1).astype(jnp.bfloat16),
            values,
            preferred_element_type=jnp.float32,
        ).reshape(high.shape[0], high.shape[1], -1)
    return high, total, mixed


def features(head):
    return slice(head * HEAD_DIM, (head + 1) * HEAD_DIM)


def shard_parts(ref, tokens, c_rows):
    return slice(0, tokens + c_rows), slice(tokens + c_rows, 2 * (tokens + c_rows))


def own_kernel(
    count, hops, own_ref, limit_ref, targets_ref, q_ref, shard_ref,
    qt_ref, near_ref, far_ref, pick_ref, high_ref, total_ref, accum_ref,
):
    kv_local, _, rows = qt_ref.shape
    tokens = q_ref.shape[0]
    c_rows = far_ref.shape[1]
    own = own_ref[0]
    limit = limit_ref[0]
    place = lax.broadcasted_iota(jnp.int32, (tokens, tokens), 0)
    token = lax.broadcasted_iota(jnp.int32, (tokens, tokens), 1)
    pick = jnp.where(place == token, jnp.float32(1.0), jnp.float32(0.0)).astype(jnp.bfloat16)
    for head in range(kv_local):
        for sub in range(GROUP):
            cols = slice(sub * tokens, (sub + 1) * tokens)
            qt_ref[head, :HEAD_DIM, cols] = q_ref[:, features(head * GROUP + sub)].T
            qt_ref[head, HEAD_DIM:, cols] = pick
    for place, hop in enumerate(hops):
        shard = shard_of(own, hop, count)
        near_ref[place] = stretch_mask(shard, own, tokens)
        far_ref[place] = cache_mask(shard, limit, c_rows, tokens)
    one, two = sent_pages(targets_ref, own, shard_of(own, -hops[-1], count), tokens // PAGE)
    row = lax.broadcasted_iota(jnp.int32, pick_ref.shape, 0)
    token = lax.broadcasted_iota(jnp.int32, pick_ref.shape, 1)
    sent = ((row < PAGE) & (one >= 0) & (token == row + one * PAGE)) | (
        (row >= PAGE) & (two >= 0) & (token == row + (two - 1) * PAGE)
    )
    pick_ref[...] = jnp.where(sent, jnp.float32(1.0), jnp.float32(0.0)).astype(jnp.bfloat16)
    mask = jnp.concatenate([stretch_mask(own, own, tokens), cache_mask(own, limit, c_rows, tokens)], axis=0)
    key_rows, value_rows = shard_parts(shard_ref, tokens, c_rows)
    keys = [jnp.concatenate([shard_ref[key_rows, features(head)], mask], axis=1) for head in range(kv_local)]
    values_t = [shard_ref[value_rows, features(head)].T for head in range(kv_local)]
    attend(qt_ref, keys, values_t, None, (high_ref, total_ref, accum_ref))


def held_kernel(
    own_ref, targets_ref, length_ref, q_ref, lists_ref, pool_k, pool_v, rest_ref,
    wide_ref, high_ref, total_ref, mixed_ref,
):
    kv_width = rest_ref.shape[1]
    pool = pool_k.shape[0]
    held = pool * PAGE
    tokens = PAGE * P_DEV
    half = rest_ref.shape[0] // 2
    own = own_ref[0]
    lists = lists_ref[...]
    lengths = length_column(length_ref)
    wide_ref[...] = wide_queries(q_ref, kv_width // HEAD_DIM)
    held_slot = lax.broadcasted_iota(jnp.int32, (1, held), 1) // PAGE
    own_slot = slot_row(targets_ref, own, own, tokens, pool)
    parts = [
        (
            pool_k[...].reshape(held, kv_width),
            pool_v[...].reshape(held, kv_width),
            tally_of(lists, lengths, held_slot),
        ),
        (rest_ref[:tokens], rest_ref[half : half + tokens], tally_of(lists, lengths, own_slot)),
    ]
    high_ref[...], total_ref[...], mixed_ref[...] = decode_attend(wide_ref[...], parts, None)


def hop_kernel(places, qt_ref, near_ref, far_ref, high_in, total_in, accum_in, *refs):
    shard_refs, outs = refs[: len(places)], refs[len(places) :]
    tokens, c_rows = near_ref.shape[1], far_ref.shape[1]
    mask = jnp.concatenate([ref[place] for place in places for ref in (near_ref, far_ref)], axis=0)
    keys, values_t = [], []
    for head in range(qt_ref.shape[0]):
        pieces, values = [], []
        for ref in shard_refs:
            key_rows, value_rows = shard_parts(ref, tokens, c_rows)
            pieces.append(ref[key_rows, features(head)])
            values.append(ref[value_rows, features(head)])
        keys.append(jnp.concatenate([jnp.concatenate(pieces, axis=0), mask], axis=1))
        values_t.append(jnp.concatenate(values, axis=0).T)
    attend(qt_ref, keys, values_t, (high_in, total_in, accum_in), outs)


def pick_kernel(pick_ref, shard_ref, pages_ref):
    tokens = pick_ref.shape[1]
    sent = pick_ref.shape[0]
    for place, start in enumerate((0, shard_ref.shape[0] // 2)):
        rows = jnp.dot(pick_ref[...], shard_ref[start : start + tokens], preferred_element_type=jnp.float32)
        pages_ref[place * sent : (place + 1) * sent] = rows.astype(jnp.bfloat16)


def split_kernel(shard_ref, keys_ref, stretch_ref, values_ref):
    c_rows = keys_ref.shape[0]
    tokens = stretch_ref.shape[0] // 2
    half = tokens + c_rows
    for place, start in enumerate((0, half)):
        stretch_ref[place * tokens : (place + 1) * tokens] = shard_ref[start : start + tokens]
    keys_ref[...] = shard_ref[tokens:half]
    values_ref[...] = shard_ref[half + tokens :]


def near_pages_kernel(count, hops, tokens, pool, own_ref, targets_ref, length_ref, lists_ref, *refs):
    shard_refs, refs = refs[: len(hops) - 1], refs[len(hops) - 1 :]
    wide_ref, dec_high, dec_total, dec_mixed, high_ref, total_ref, mixed_ref, tally_ref = refs
    own = own_ref[0]
    lists = lists_ref[...]
    lengths = length_column(length_ref)
    parts = []
    for hop, ref in zip(hops, shard_refs):
        half = ref.shape[0] // 2
        slot = slot_row(targets_ref, shard_of(own, hop, count), own, tokens, pool)
        parts.append((ref[:tokens], ref[half : half + tokens], tally_of(lists, lengths, slot)))
    state = (dec_high[...], dec_total[...], dec_mixed[...])
    high_ref[...], total_ref[...], mixed_ref[...] = decode_attend(wide_ref[...], parts, state)
    shard = shard_of(own, hops[-1], count)
    attended = shard < own
    whole = jnp.where(attended, slot_row(targets_ref, shard, own, tokens, pool), -1)
    alone = jnp.where(attended, -1, sent_slots(targets_ref, shard, own, tokens // PAGE, pool))
    tally_ref[:, :, :tokens] = tally_of(lists, lengths, whole)
    tally_ref[:, :, tokens:] = tally_of(lists, lengths, alone)


def score_kernel(
    final, qt_ref, near_ref, far_ref, high_in, total_in, accum_in, keys_ref, stretch_ref,
    weights_ref, total_ref, accum_ref,
):
    kv_local = qt_ref.shape[0]
    tokens, c_rows = near_ref.shape[1], far_ref.shape[1]
    mask = jnp.concatenate([near_ref[final], far_ref[final]], axis=0)
    keys, values_t = [], []
    for head in range(kv_local):
        pieces = [stretch_ref[:tokens, features(head)], keys_ref[:, features(head)]]
        keys.append(jnp.concatenate([jnp.concatenate(pieces, axis=0), mask], axis=1))
        values_t.append(stretch_ref[tokens:, features(head)].T)

    def second(block, scores):
        head, cols = block
        before = (high_in[head, :, cols], total_in[head, :, cols])
        weights, _, total, decay = soften(scores, before)
        weights_ref[head, :, cols] = weights[tokens:]
        total_ref[head, :, cols] = total
        accum_ref[head, :, cols] = accum_in[head, :, cols] * decay + jnp.dot(
            values_t[head], weights[:tokens], preferred_element_type=jnp.float32
        )

    walk(blocks_of(qt_ref), lambda block: scores_of(qt_ref, block[0], block[1], keys[block[0]]), second)


def last_pages_kernel(
    stretch_ref, pages_ref, tally_ref, wide_ref, dec_high, dec_total, dec_mixed, dec_out
):
    tokens = stretch_ref.shape[0] // 2
    sent = pages_ref.shape[0] // 2
    keys = jnp.concatenate([stretch_ref[:tokens], pages_ref[:sent]], axis=0)
    values = jnp.concatenate([stretch_ref[tokens:], pages_ref[sent:]], axis=0)
    state = (dec_high[...], dec_total[...], dec_mixed[...])
    _, total, mixed = decode_attend(wide_ref[...], [(keys, values, tally_ref[...])], state)
    share = 1.0 / total
    for head in range(dec_high.shape[0]):
        piece = mixed[head, :, features(head // GROUP)] * share[head]
        dec_out[:, features(head)] = piece.astype(jnp.bfloat16)


def last_kernel(weights_ref, total_ref, accum_ref, values_ref, out_ref, result_ref, sems):
    tokens = result_ref.shape[0]
    values_t = [values_ref[:, features(head)].T for head in range(weights_ref.shape[0])]
    copies = []

    def first(block):
        head, cols = block
        return jnp.dot(values_t[head], weights_ref[head, :, cols], preferred_element_type=jnp.float32)

    def second(block, mixed):
        head, cols = block
        mixed = mixed + accum_ref[head, :, cols]
        mixed = (mixed * (1.0 / total_ref[head, :, cols])).astype(jnp.bfloat16)
        start = (head * GROUP + cols.start // tokens) * HEAD_DIM
        pieces = (cols.stop - cols.start) // tokens
        for piece in range(pieces):
            col = start + piece * HEAD_DIM
            result_ref[:, col : col + HEAD_DIM] = mixed[:, piece * tokens : (piece + 1) * tokens].T
        span = pl.ds(start, pieces * HEAD_DIM)
        copy = pltpu.make_async_copy(result_ref.at[:, span], out_ref.at[:, span], sems.at[len(copies)])
        copy.start()
        copies.append(copy)

    walk(blocks_of(weights_ref), first, second)

    for copy in copies:
        copy.wait()


def per_device(
    count,
    queries,
    stretch_keys,
    stretch_values,
    cache_keys,
    cache_values,
    prefix_length,
    page_targets,
    pool_keys,
    pool_values,
    decode_queries,
    page_lists,
    context_length,
):
    own = lax.axis_index("ctx")
    own_array = jnp.full((1,), own, jnp.int32)
    tokens, width = queries.shape
    kv_width = stretch_keys.shape[1]
    kv_local = kv_width // HEAD_DIM
    rows = GROUP * tokens
    heads = kv_local * GROUP
    dec_rows = decode_queries.shape[0]
    c_rows = cache_keys.shape[0]
    pool = pool_keys.shape[0]
    f32, bf16 = jnp.float32, jnp.bfloat16
    shape = jax.ShapeDtypeStruct
    params = pltpu.CompilerParams(vmem_limit_bytes=VMEM_BYTES)
    up_pairs = [(i, (i + 1) % count) for i in range(count)]
    down_pairs = [(i, (i - 1) % count) for i in range(count)]
    hops = []
    for far in range(1, count // 2 + 1):
        hops += [-far, far] if far <= (count - 1) // 2 else [-far]

    def send(array, hop):
        return lax.ppermute(array, "ctx", up_pairs if hop < 0 else down_pairs)

    def cost(keys):
        pairs = kv_local * rows * keys
        return pl.CostEstimate(
            flops=4 * pairs * HEAD_DIM, bytes_accessed=4 * rows * kv_local * HEAD_DIM, transcendentals=pairs
        )

    half = tokens + c_rows
    low = jnp.array(-jnp.inf, bf16)
    spread, start = [], 0
    for part in (stretch_keys, cache_keys, stretch_values, cache_values):
        end = 2 * half - start - part.shape[0]
        spread.append(lax.pad(part, low, ((start, end, 0), (0, 0, 0))))
        start += part.shape[0]
    shard = {0: functools.reduce(jnp.maximum, spread)}
    shard[-1] = send(shard[0], -1)

    state_shapes = (
        shape((kv_local, 1, rows), f32),
        shape((kv_local, 1, rows), f32),
        shape((kv_local, HEAD_DIM, rows), f32),
    )
    qt, near, far, pick, *state = pl.pallas_call(
        functools.partial(own_kernel, count, hops),
        out_shape=(
            shape((kv_local, HEAD_DIM + tokens, rows), bf16),
            shape((count - 1, tokens, tokens), bf16),
            shape((count - 1, c_rows, tokens), bf16),
            shape((SEND_CAP * PAGE, tokens), bf16),
        )
        + state_shapes,
        in_specs=[SMEM] * 3 + [VMEM] * 2,
        out_specs=(VMEM,) * 7,
        compiler_params=params,
        cost_estimate=cost(tokens + c_rows),
        name="own_shard",
    )(own_array, prefix_length, page_targets, queries, shard[0])

    dec_shapes = (
        shape((heads, dec_rows, 1), f32),
        shape((heads, dec_rows, 1), f32),
        shape((heads, dec_rows, kv_width), f32),
    )
    wide, *dec_state = pl.pallas_call(
        held_kernel,
        out_shape=(shape((heads * dec_rows, kv_width), bf16),) + dec_shapes,
        in_specs=[SMEM] * 3 + [VMEM] * 5,
        out_specs=(VMEM,) * 4,
        compiler_params=params,
        cost_estimate=pl.CostEstimate(
            flops=4 * 128 * 2048 * 256, bytes_accessed=4 * pool_keys.size, transcendentals=128 * 2048
        ),
        name="decode_held_pages",
    )(own_array, page_targets, context_length, decode_queries, page_lists, pool_keys, pool_values, shard[0])

    if 1 in hops:
        sent_down, state, dec_state = lax.optimization_barrier((shard[0], state, dec_state))
        shard[1] = send(sent_down, 1)
    shard[-1], state, dec_state = lax.optimization_barrier((shard[-1], state, dec_state))
    for hop in hops[2:-1]:
        shard[hop] = send(shard[hop + 1 if hop < 0 else hop - 1], hop)
    hop = hops[-1]
    nearer = shard[hop + 1 if hop < 0 else hop - 1]
    pieces = pl.pallas_call(
        split_kernel,
        out_shape=(
            shape((c_rows, kv_width), bf16),
            shape((2 * tokens, kv_width), bf16),
            shape((c_rows, kv_width), bf16),
        ),
        in_specs=[VMEM],
        out_specs=(VMEM,) * 3,
        compiler_params=params,
        name="pieces_to_send_on",
    )(nearer)
    far_pages = pl.pallas_call(
        pick_kernel,
        out_shape=shape((2 * SEND_CAP * PAGE, kv_width), bf16),
        in_specs=[VMEM] * 2,
        out_specs=VMEM,
        compiler_params=params,
        name="pages_to_send",
    )(pick, shard[0])
    straight = [(i, (i - hop) % count) for i in range(count) if i > (i - hop) % count]
    last_pages = lax.ppermute(far_pages, "ctx", straight)
    last_keys = send(pieces[0], hop)
    attending = [pair for pair in (up_pairs if hop < 0 else down_pairs) if (pair[1] + hop) % count < pair[1]]
    last_stretch = lax.ppermute(pieces[1], "ctx", attending)

    for first in range(len(hops) - 1):
        places = [first]
        state = pl.pallas_call(
            functools.partial(hop_kernel, places),
            out_shape=state_shapes,
            in_specs=[VMEM] * (6 + len(places)),
            out_specs=(VMEM,) * 3,
            compiler_params=params,
            cost_estimate=cost((c_rows + tokens) * len(places)),
            name="whole_shards_" + str(first),
        )(qt, near, far, *state, *[shard[hops[place]] for place in places])
        if first == 0:
            last_piece, last_pages, state = lax.optimization_barrier((pieces[2], last_pages, state))
            last_values = send(last_piece, hops[-1])

    final = len(hops) - 1
    dec_state, state = lax.optimization_barrier((dec_state, state))
    near_hops = hops[:-1]
    *dec_state, tally = pl.pallas_call(
        functools.partial(near_pages_kernel, count, hops, tokens, pool),
        out_shape=dec_shapes
        + (shape((1, dec_rows, tokens + SEND_CAP * PAGE), f32),),
        in_specs=[SMEM] * 3 + [VMEM] * (5 + len(near_hops)),
        out_specs=(VMEM,) * 4,
        compiler_params=params,
        cost_estimate=cost(tokens),
        name="decode_near_pages",
    )(
        own_array, page_targets, context_length, page_lists, *[shard[hop] for hop in near_hops],
        wide, *dec_state,
    )
    dec_state, state = lax.optimization_barrier((dec_state, state))

    decoded = pl.pallas_call(
        last_pages_kernel,
        out_shape=shape(decode_queries.shape, bf16),
        in_specs=[VMEM] * 7,
        out_specs=VMEM,
        compiler_params=params,
        cost_estimate=cost(tokens // 2),
        name="decode_last_pages",
    )(last_stretch, last_pages, tally, wide, *dec_state)
    decoded, state = lax.optimization_barrier((decoded, state))

    weights, total, accum = pl.pallas_call(
        functools.partial(score_kernel, final),
        out_shape=(shape((kv_local, c_rows, rows), bf16),) + state_shapes[1:],
        in_specs=[VMEM] * 8,
        out_specs=(VMEM,) * 3,
        compiler_params=params,
        cost_estimate=cost(half),
        name="last_scores",
    )(qt, near, far, *state, last_keys, last_stretch)

    prefill = pl.pallas_call(
        last_kernel,
        out_shape=shape((tokens, width), bf16),
        in_specs=[VMEM] * 4,
        out_specs=HBM,
        scratch_shapes=[
            pltpu.VMEM((tokens, width), bf16),
            pltpu.SemaphoreType.DMA((kv_local * max(GROUP // 2, 1),)),
        ],
        compiler_params=params,
        cost_estimate=cost(c_rows // 2),
        name="last_values",
    )(weights, total, accum, last_values)
    return (prefill, decoded)


def solution(mesh):
    in_specs = (
        P(("groups", "ctx"), "head"),
        P(("groups", "ctx"), "head"),
        P(("groups", "ctx"), "head"),
        P(("groups", "ctx"), "head"),
        P(("groups", "ctx"), "head"),
        P("groups"),
        P("groups"),
        P(("groups", "ctx"), None, "head"),
        P(("groups", "ctx"), None, "head"),
        P(("groups", "ctx"), "head"),
        P(("groups", "ctx"), None),
        P(("groups", "ctx")),
    )
    out_specs = (P(("groups", "ctx"), "head"), P(("groups", "ctx"), "head"))
    return jax.shard_map(
        functools.partial(per_device, mesh.shape["ctx"]),
        mesh=mesh,
        in_specs=in_specs,
        out_specs=out_specs,
        check_vma=False,
    )
```

```python
import functools

import jax
import jax.numpy as jnp
from jax import lax
from jax.experimental import pallas as pl
from jax.experimental.pallas import tpu as pltpu
from jax.sharding import PartitionSpec as P

HEADS = 64
KV_HEADS = 8
HEAD_DIM = 128
GROUP = HEADS // KV_HEADS
PAGE = 16
P_DEV = 8
SEND_CAP = 2
EXP2_SCALE = HEAD_DIM ** (-0.5) * 1.4426950408889634
HIDDEN = -1e30
VMEM_BYTES = 48 * 1024 * 1024

VMEM = pl.BlockSpec(memory_space=pltpu.VMEM)
SMEM = pl.BlockSpec(memory_space=pltpu.SMEM)
HBM = pl.BlockSpec(memory_space=pltpu.HBM)


def scores_of(qt_ref, head, cols, keys):
    return jnp.dot(keys, qt_ref[head, :, cols], preferred_element_type=jnp.float32)


def soften(scores, old):
    high = jnp.max(scores, axis=0, keepdims=True)
    if old is None:
        weights = jnp.exp2((scores - high) * EXP2_SCALE)
        return weights.astype(jnp.bfloat16), high, jnp.sum(weights, axis=0, keepdims=True), None
    old_high, old_total = old
    high = jnp.maximum(high, old_high)
    decay = jnp.exp2((old_high - high) * EXP2_SCALE)
    weights = jnp.exp2((scores - high) * EXP2_SCALE)
    total = old_total * decay + jnp.sum(weights, axis=0, keepdims=True)
    return weights.astype(jnp.bfloat16), high, total, decay


def walk(blocks, first, second):
    ahead = first(blocks[0])
    for place, block in enumerate(blocks):
        current = ahead
        if place + 1 < len(blocks):
            ahead = first(blocks[place + 1])
        second(block, current)


def blocks_of(qt_ref):
    kv_local, _, rows = qt_ref.shape
    width = min(2 * (rows // GROUP), rows)
    return [(head, slice(start, start + width)) for head in range(kv_local) for start in range(0, rows, width)]


def attend(qt_ref, keys, values_t, old, new):
    high_ref, total_ref, accum_ref = new

    def second(block, scores):
        head, cols = block
        before = None if old is None else (old[0][head, :, cols], old[1][head, :, cols])
        weights, high, total, decay = soften(scores, before)
        accum = jnp.dot(values_t[head], weights, preferred_element_type=jnp.float32)
        if old is not None:
            accum = accum + old[2][head, :, cols] * decay
        high_ref[head, :, cols] = high
        total_ref[head, :, cols] = total
        accum_ref[head, :, cols] = accum

    walk(blocks_of(qt_ref), lambda block: scores_of(qt_ref, block[0], block[1], keys[block[0]]), second)


def hidden(seen):
    return jnp.where(seen, jnp.float32(0.0), jnp.float32(HIDDEN)).astype(jnp.bfloat16)


def stretch_mask(shard, own, tokens):
    place = lax.broadcasted_iota(jnp.int32, (tokens, tokens), 0)
    token = lax.broadcasted_iota(jnp.int32, (tokens, tokens), 1)
    return hidden(place - token <= (own - shard) * tokens)


def cache_mask(shard, limit, c_rows, tokens):
    place = lax.broadcasted_iota(jnp.int32, (c_rows, tokens), 0)
    return hidden(place < limit - shard * c_rows)


def slot_row(targets_ref, shard, own, tokens, pool):
    page = lax.broadcasted_iota(jnp.int32, (1, tokens), 1) // PAGE
    slots = jnp.full((1, tokens), -1, jnp.int32)
    for index in range(tokens // PAGE):
        target = targets_ref[shard * (tokens // PAGE) + index]
        slot = jnp.where(lax.div(target, P_DEV) == own, pool + lax.rem(target, P_DEV), -1)
        slots = jnp.where(page == index, slot, slots)
    return slots


def sent_pages(targets_ref, shard, owner, pages):
    one, two = jnp.int32(-1), jnp.int32(-1)
    for index in range(pages):
        hit = lax.div(targets_ref[shard * pages + index], P_DEV) == owner
        two = jnp.where(hit & (one >= 0) & (two < 0), index, two)
        one = jnp.where(hit & (one < 0), index, one)
    return one, two


def sent_slots(targets_ref, shard, owner, tokens, pool):
    page = lax.broadcasted_iota(jnp.int32, (1, tokens), 1) // PAGE
    row = jnp.full((1, tokens), -1, jnp.int32)
    for place, index in enumerate(sent_pages(targets_ref, shard, owner, tokens // PAGE)):
        target = targets_ref[shard * (tokens // PAGE) + jnp.maximum(index, 0)]
        slot = jnp.where(index >= 0, pool + lax.rem(target, P_DEV), -1)
        row = jnp.where(page == place, slot, row)
    return row


def length_column(length_ref):
    rows = length_ref.shape[0]
    place = lax.broadcasted_iota(jnp.int32, (rows, 1), 0)
    lengths = jnp.zeros((rows, 1), jnp.int32)
    for row in range(rows):
        lengths = jnp.where(place == row, length_ref[row], lengths)
    return lengths


def tally_of(lists, lengths, slot):
    rows, span = lists.shape
    tokens = slot.shape[1]
    slot = jnp.broadcast_to(slot, (rows, tokens))
    offset = lax.rem(lax.broadcasted_iota(jnp.int32, (rows, tokens), 1), PAGE)
    tally = jnp.zeros((rows, tokens), jnp.float32)
    for entry in range(span):
        hit = (slot == lists[:, entry : entry + 1]) & (offset < lengths - entry * PAGE)
        tally = tally + jnp.where(hit, jnp.float32(1.0), jnp.float32(0.0))
    return tally[None]


def shard_of(own, hop, count):
    return lax.rem(own + hop + count, count)


def wide_queries(q_ref, kv_local):
    heads = q_ref.shape[1] // HEAD_DIM
    queries = q_ref[...].astype(jnp.float32)
    stacked = []
    for head in range(heads):
        piece = queries[:, head * HEAD_DIM : (head + 1) * HEAD_DIM]
        blank = jnp.zeros_like(piece)
        stacked.append(
            jnp.concatenate([piece if kv == head // GROUP else blank for kv in range(kv_local)], axis=1)
        )
    return jnp.concatenate(stacked, axis=0).astype(jnp.bfloat16)


def decode_attend(queries, parts, state):
    done = []
    for keys, values, tally in parts:
        scores = lax.dot_general(
            queries, keys, (((1,), (1,)), ((), ())), preferred_element_type=jnp.float32
        ).reshape(-1, tally.shape[1], tally.shape[2])
        done.append((jnp.where(tally > 0, scores, jnp.float32(HIDDEN)), tally, values))
    highs = [jnp.max(scores, axis=-1, keepdims=True) for scores, _, _ in done]
    if state is not None:
        old_high, old_total, old_mixed = state
        highs.append(old_high)
    high = functools.reduce(jnp.maximum, highs)
    total, mixed = 0.0, 0.0
    if state is not None:
        decay = jnp.exp2((old_high - high) * EXP2_SCALE)
        total = old_total * decay
        mixed = old_mixed * decay
    for scores, tally, values in done:
        weights = jnp.exp2((scores - high) * EXP2_SCALE) * tally
        total = total + jnp.sum(weights, axis=-1, keepdims=True)
        mixed = mixed + jnp.dot(
            weights.reshape(queries.shape[0], -1).astype(jnp.bfloat16),
            values,
            preferred_element_type=jnp.float32,
        ).reshape(high.shape[0], high.shape[1], -1)
    return high, total, mixed


def features(head):
    return slice(head * HEAD_DIM, (head + 1) * HEAD_DIM)


def shard_parts(ref, tokens, c_rows):
    return slice(0, tokens + c_rows), slice(tokens + c_rows, 2 * (tokens + c_rows))


def own_kernel(
    count, hops, own_ref, limit_ref, targets_ref, q_ref, shard_ref,
    qt_ref, near_ref, far_ref, pick_ref, high_ref, total_ref, accum_ref,
):
    kv_local, _, rows = qt_ref.shape
    tokens = q_ref.shape[0]
    c_rows = far_ref.shape[1]
    own = own_ref[0]
    limit = limit_ref[0]
    place = lax.broadcasted_iota(jnp.int32, (tokens, tokens), 0)
    token = lax.broadcasted_iota(jnp.int32, (tokens, tokens), 1)
    pick = jnp.where(place == token, jnp.float32(1.0), jnp.float32(0.0)).astype(jnp.bfloat16)
    for head in range(kv_local):
        for sub in range(GROUP):
            cols = slice(sub * tokens, (sub + 1) * tokens)
            qt_ref[head, :HEAD_DIM, cols] = q_ref[:, features(head * GROUP + sub)].T
            qt_ref[head, HEAD_DIM:, cols] = pick
    for place, hop in enumerate(hops):
        shard = shard_of(own, hop, count)
        near_ref[place] = stretch_mask(shard, own, tokens)
        far_ref[place] = cache_mask(shard, limit, c_rows, tokens)
    onward = 1 if hops[-1] < 0 else -1
    pages = tokens // PAGE
    one, two = sent_pages(
        targets_ref, shard_of(own, hops[-1] + onward, count), shard_of(own, onward, count), pages
    )
    row = lax.broadcasted_iota(jnp.int32, pick_ref.shape, 0)
    token = lax.broadcasted_iota(jnp.int32, pick_ref.shape, 1)
    sent = ((row < PAGE) & (one >= 0) & (token == row + one * PAGE)) | (
        (row >= PAGE) & (two >= 0) & (token == row + (two - 1) * PAGE)
    )
    pick_ref[...] = jnp.where(sent, jnp.float32(1.0), jnp.float32(0.0)).astype(jnp.bfloat16)
    mask = jnp.concatenate([stretch_mask(own, own, tokens), cache_mask(own, limit, c_rows, tokens)], axis=0)
    key_rows, value_rows = shard_parts(shard_ref, tokens, c_rows)
    keys = [jnp.concatenate([shard_ref[key_rows, features(head)], mask], axis=1) for head in range(kv_local)]
    values_t = [shard_ref[value_rows, features(head)].T for head in range(kv_local)]
    attend(qt_ref, keys, values_t, None, (high_ref, total_ref, accum_ref))


def held_kernel(
    own_ref, targets_ref, length_ref, q_ref, lists_ref, pool_k, pool_v, rest_ref,
    wide_ref, high_ref, total_ref, mixed_ref,
):
    kv_width = rest_ref.shape[1]
    pool = pool_k.shape[0]
    held = pool * PAGE
    tokens = PAGE * P_DEV
    half = rest_ref.shape[0] // 2
    own = own_ref[0]
    lists = lists_ref[...]
    lengths = length_column(length_ref)
    wide_ref[...] = wide_queries(q_ref, kv_width // HEAD_DIM)
    held_slot = lax.broadcasted_iota(jnp.int32, (1, held), 1) // PAGE
    own_slot = slot_row(targets_ref, own, own, tokens, pool)
    parts = [
        (
            pool_k[...].reshape(held, kv_width),
            pool_v[...].reshape(held, kv_width),
            tally_of(lists, lengths, held_slot),
        ),
        (rest_ref[:tokens], rest_ref[half : half + tokens], tally_of(lists, lengths, own_slot)),
    ]
    high_ref[...], total_ref[...], mixed_ref[...] = decode_attend(wide_ref[...], parts, None)


def hop_kernel(places, qt_ref, near_ref, far_ref, high_in, total_in, accum_in, *refs):
    shard_refs, outs = refs[: len(places)], refs[len(places) :]
    tokens, c_rows = near_ref.shape[1], far_ref.shape[1]
    mask = jnp.concatenate([ref[place] for place in places for ref in (near_ref, far_ref)], axis=0)
    keys, values_t = [], []
    for head in range(qt_ref.shape[0]):
        pieces, values = [], []
        for ref in shard_refs:
            key_rows, value_rows = shard_parts(ref, tokens, c_rows)
            pieces.append(ref[key_rows, features(head)])
            values.append(ref[value_rows, features(head)])
        keys.append(jnp.concatenate([jnp.concatenate(pieces, axis=0), mask], axis=1))
        values_t.append(jnp.concatenate(values, axis=0).T)
    attend(qt_ref, keys, values_t, (high_in, total_in, accum_in), outs)


def split_kernel(pick_ref, shard_ref, keys_ref, stretch_ref, values_ref, pages_ref):
    tokens = pick_ref.shape[1]
    half = shard_ref.shape[0] // 2
    sent = pick_ref.shape[0]
    for place, start in enumerate((0, half)):
        stretch_ref[place * tokens : (place + 1) * tokens] = shard_ref[start : start + tokens]
        rows = jnp.dot(pick_ref[...], shard_ref[start : start + tokens], preferred_element_type=jnp.float32)
        pages_ref[place * sent : (place + 1) * sent] = rows.astype(jnp.bfloat16)
    keys_ref[...] = shard_ref[tokens:half]
    values_ref[...] = shard_ref[half + tokens :]


def near_pages_kernel(count, hops, tokens, pool, own_ref, targets_ref, length_ref, lists_ref, *refs):
    shard_refs, refs = refs[: len(hops) - 1], refs[len(hops) - 1 :]
    wide_ref, dec_high, dec_total, dec_mixed, high_ref, total_ref, mixed_ref, tally_ref = refs
    own = own_ref[0]
    lists = lists_ref[...]
    lengths = length_column(length_ref)
    parts = []
    for hop, ref in zip(hops, shard_refs):
        half = ref.shape[0] // 2
        slot = slot_row(targets_ref, shard_of(own, hop, count), own, tokens, pool)
        parts.append((ref[:tokens], ref[half : half + tokens], tally_of(lists, lengths, slot)))
    state = (dec_high[...], dec_total[...], dec_mixed[...])
    high_ref[...], total_ref[...], mixed_ref[...] = decode_attend(wide_ref[...], parts, state)
    shard = shard_of(own, hops[-1], count)
    attended = shard < own
    whole = slot_row(targets_ref, shard, own, tokens, pool)
    alone = sent_slots(targets_ref, shard, own, tokens, pool)
    tally_ref[...] = tally_of(lists, lengths, jnp.where(attended, whole, alone))


def score_kernel(
    final, qt_ref, near_ref, far_ref, high_in, total_in, accum_in, keys_ref, stretch_ref,
    weights_ref, total_ref, accum_ref,
):
    kv_local = qt_ref.shape[0]
    tokens, c_rows = near_ref.shape[1], far_ref.shape[1]
    def run(attended):
        mask = far_ref[final]
        if attended:
            mask = jnp.concatenate([near_ref[final], mask], axis=0)
        keys, values_t = [], []
        for head in range(kv_local):
            rows = keys_ref[:, features(head)]
            if attended:
                rows = jnp.concatenate([stretch_ref[:tokens, features(head)], rows], axis=0)
                values_t.append(stretch_ref[tokens:, features(head)].T)
            keys.append(jnp.concatenate([rows, mask], axis=1))

        def second(block, scores):
            head, cols = block
            before = (high_in[head, :, cols], total_in[head, :, cols])
            weights, _, total, decay = soften(scores, before)
            weights_ref[head, :, cols] = weights[-c_rows:]
            total_ref[head, :, cols] = total
            accum = accum_in[head, :, cols] * decay
            if attended:
                accum = accum + jnp.dot(values_t[head], weights[:tokens], preferred_element_type=jnp.float32)
            accum_ref[head, :, cols] = accum

        walk(blocks_of(qt_ref), lambda block: scores_of(qt_ref, block[0], block[1], keys[block[0]]), second)

    attended = jnp.max(near_ref[final].astype(jnp.float32)) > HIDDEN / 2
    pl.when(attended)(functools.partial(run, True))
    pl.when(jnp.logical_not(attended))(functools.partial(run, False))


def last_pages_kernel(
    stretch_ref, pages_ref, tally_ref, wide_ref, dec_high, dec_total, dec_mixed, dec_out
):
    tokens = stretch_ref.shape[0] // 2
    sent = pages_ref.shape[0] // 2
    keys = jnp.concatenate([stretch_ref[:sent] + pages_ref[:sent], stretch_ref[sent:tokens]], axis=0)
    values = jnp.concatenate(
        [stretch_ref[tokens : tokens + sent] + pages_ref[sent:], stretch_ref[tokens + sent :]], axis=0
    )
    state = (dec_high[...], dec_total[...], dec_mixed[...])
    _, total, mixed = decode_attend(wide_ref[...], [(keys, values, tally_ref[...])], state)
    share = 1.0 / total
    for head in range(dec_high.shape[0]):
        piece = mixed[head, :, features(head // GROUP)] * share[head]
        dec_out[:, features(head)] = piece.astype(jnp.bfloat16)


def last_kernel(weights_ref, total_ref, accum_ref, values_ref, out_ref, result_ref, sems):
    tokens = result_ref.shape[0]
    values_t = [values_ref[:, features(head)].T for head in range(weights_ref.shape[0])]
    copies = []

    def first(block):
        head, cols = block
        return jnp.dot(values_t[head], weights_ref[head, :, cols], preferred_element_type=jnp.float32)

    def second(block, mixed):
        head, cols = block
        mixed = mixed + accum_ref[head, :, cols]
        mixed = (mixed * (1.0 / total_ref[head, :, cols])).astype(jnp.bfloat16)
        start = (head * GROUP + cols.start // tokens) * HEAD_DIM
        pieces = (cols.stop - cols.start) // tokens
        for piece in range(pieces):
            col = start + piece * HEAD_DIM
            result_ref[:, col : col + HEAD_DIM] = mixed[:, piece * tokens : (piece + 1) * tokens].T
        span = pl.ds(start, pieces * HEAD_DIM)
        copy = pltpu.make_async_copy(result_ref.at[:, span], out_ref.at[:, span], sems.at[len(copies)])
        copy.start()
        copies.append(copy)

    walk(blocks_of(weights_ref), first, second)

    for copy in copies:
        copy.wait()


def per_device(
    count,
    queries,
    stretch_keys,
    stretch_values,
    cache_keys,
    cache_values,
    prefix_length,
    page_targets,
    pool_keys,
    pool_values,
    decode_queries,
    page_lists,
    context_length,
):
    own = lax.axis_index("ctx")
    own_array = jnp.full((1,), own, jnp.int32)
    tokens, width = queries.shape
    kv_width = stretch_keys.shape[1]
    kv_local = kv_width // HEAD_DIM
    rows = GROUP * tokens
    heads = kv_local * GROUP
    dec_rows = decode_queries.shape[0]
    c_rows = cache_keys.shape[0]
    pool = pool_keys.shape[0]
    f32, bf16 = jnp.float32, jnp.bfloat16
    shape = jax.ShapeDtypeStruct
    params = pltpu.CompilerParams(vmem_limit_bytes=VMEM_BYTES)
    up_pairs = [(i, (i + 1) % count) for i in range(count)]
    down_pairs = [(i, (i - 1) % count) for i in range(count)]
    hops = []
    for far in range(1, count // 2 + 1):
        hops += [-far, far] if far <= (count - 1) // 2 else [-far]

    def send(array, hop):
        return lax.ppermute(array, "ctx", up_pairs if hop < 0 else down_pairs)

    def cost(keys):
        pairs = kv_local * rows * keys
        return pl.CostEstimate(
            flops=4 * pairs * HEAD_DIM, bytes_accessed=4 * rows * kv_local * HEAD_DIM, transcendentals=pairs
        )

    half = tokens + c_rows
    low = jnp.array(-jnp.inf, bf16)
    spread, start = [], 0
    for part in (stretch_keys, cache_keys, stretch_values, cache_values):
        end = 2 * half - start - part.shape[0]
        spread.append(lax.pad(part, low, ((start, end, 0), (0, 0, 0))))
        start += part.shape[0]
    shard = {0: functools.reduce(jnp.maximum, spread)}
    shard[-1] = send(shard[0], -1)

    state_shapes = (
        shape((kv_local, 1, rows), f32),
        shape((kv_local, 1, rows), f32),
        shape((kv_local, HEAD_DIM, rows), f32),
    )
    qt, near, far, pick, *state = pl.pallas_call(
        functools.partial(own_kernel, count, hops),
        out_shape=(
            shape((kv_local, HEAD_DIM + tokens, rows), bf16),
            shape((count - 1, tokens, tokens), bf16),
            shape((count - 1, c_rows, tokens), bf16),
            shape((SEND_CAP * PAGE, tokens), bf16),
        )
        + state_shapes,
        in_specs=[SMEM] * 3 + [VMEM] * 2,
        out_specs=(VMEM,) * 7,
        compiler_params=params,
        cost_estimate=cost(tokens + c_rows),
        name="own_shard",
    )(own_array, prefix_length, page_targets, queries, shard[0])

    dec_shapes = (
        shape((heads, dec_rows, 1), f32),
        shape((heads, dec_rows, 1), f32),
        shape((heads, dec_rows, kv_width), f32),
    )
    wide, *dec_state = pl.pallas_call(
        held_kernel,
        out_shape=(shape((heads * dec_rows, kv_width), bf16),) + dec_shapes,
        in_specs=[SMEM] * 3 + [VMEM] * 5,
        out_specs=(VMEM,) * 4,
        compiler_params=params,
        cost_estimate=pl.CostEstimate(
            flops=4 * 128 * 2048 * 256, bytes_accessed=4 * pool_keys.size, transcendentals=128 * 2048
        ),
        name="decode_held_pages",
    )(own_array, page_targets, context_length, decode_queries, page_lists, pool_keys, pool_values, shard[0])

    if 1 in hops:
        sent_down, state, dec_state = lax.optimization_barrier((shard[0], state, dec_state))
        shard[1] = send(sent_down, 1)
    shard[-1], state, dec_state = lax.optimization_barrier((shard[-1], state, dec_state))
    for hop in hops[2:-1]:
        shard[hop] = send(shard[hop + 1 if hop < 0 else hop - 1], hop)
    hop = hops[-1]
    nearer = shard[hop + 1 if hop < 0 else hop - 1]
    pieces = pl.pallas_call(
        split_kernel,
        out_shape=(
            shape((c_rows, kv_width), bf16),
            shape((2 * tokens, kv_width), bf16),
            shape((c_rows, kv_width), bf16),
            shape((2 * SEND_CAP * PAGE, kv_width), bf16),
        ),
        in_specs=[VMEM] * 2,
        out_specs=(VMEM,) * 4,
        compiler_params=params,
        name="pieces_to_send_on",
    )(pick, nearer)
    last_keys = send(pieces[0], hop)
    attending, others = [], []
    for pair in up_pairs if hop < 0 else down_pairs:
        (attending if (pair[1] + hop) % count < pair[1] else others).append(pair)
    last_stretch = lax.ppermute(pieces[1], "ctx", attending)
    last_pages = lax.ppermute(pieces[3], "ctx", others)
    last_values = send(pieces[2], hop)

    for first in range(len(hops) - 1):
        places = [first]
        state = pl.pallas_call(
            functools.partial(hop_kernel, places),
            out_shape=state_shapes,
            in_specs=[VMEM] * (6 + len(places)),
            out_specs=(VMEM,) * 3,
            compiler_params=params,
            cost_estimate=cost((c_rows + tokens) * len(places)),
            name="whole_shards_" + str(first),
        )(qt, near, far, *state, *[shard[hops[place]] for place in places])

    final = len(hops) - 1
    dec_state, state = lax.optimization_barrier((dec_state, state))
    near_hops = hops[:-1]
    *dec_state, tally = pl.pallas_call(
        functools.partial(near_pages_kernel, count, hops, tokens, pool),
        out_shape=dec_shapes
        + (shape((1, dec_rows, tokens), f32),),
        in_specs=[SMEM] * 3 + [VMEM] * (5 + len(near_hops)),
        out_specs=(VMEM,) * 4,
        compiler_params=params,
        cost_estimate=cost(tokens),
        name="decode_near_pages",
    )(
        own_array, page_targets, context_length, page_lists, *[shard[hop] for hop in near_hops],
        wide, *dec_state,
    )
    dec_state, state = lax.optimization_barrier((dec_state, state))

    weights, total, accum = pl.pallas_call(
        functools.partial(score_kernel, final),
        out_shape=(shape((kv_local, c_rows, rows), bf16),) + state_shapes[1:],
        in_specs=[VMEM] * 8,
        out_specs=(VMEM,) * 3,
        compiler_params=params,
        cost_estimate=cost(half),
        name="last_scores",
    )(qt, near, far, *state, last_keys, last_stretch)

    dec_state, total = lax.optimization_barrier((dec_state, total))
    decoded = pl.pallas_call(
        last_pages_kernel,
        out_shape=shape(decode_queries.shape, bf16),
        in_specs=[VMEM] * 7,
        out_specs=VMEM,
        compiler_params=params,
        cost_estimate=cost(tokens // 2),
        name="decode_last_pages",
    )(last_stretch, last_pages, tally, wide, *dec_state)
    decoded, total = lax.optimization_barrier((decoded, total))

    prefill = pl.pallas_call(
        last_kernel,
        out_shape=shape((tokens, width), bf16),
        in_specs=[VMEM] * 4,
        out_specs=HBM,
        scratch_shapes=[
            pltpu.VMEM((tokens, width), bf16),
            pltpu.SemaphoreType.DMA((kv_local * max(GROUP // 2, 1),)),
        ],
        compiler_params=params,
        cost_estimate=cost(c_rows // 2),
        name="last_values",
    )(weights, total, accum, last_values)
    return (prefill, decoded)


def solution(mesh):
    in_specs = (
        P(("groups", "ctx"), "head"),
        P(("groups", "ctx"), "head"),
        P(("groups", "ctx"), "head"),
        P(("groups", "ctx"), "head"),
        P(("groups", "ctx"), "head"),
        P("groups"),
        P("groups"),
        P(("groups", "ctx"), None, "head"),
        P(("groups", "ctx"), None, "head"),
        P(("groups", "ctx"), "head"),
        P(("groups", "ctx"), None),
        P(("groups", "ctx")),
    )
    out_specs = (P(("groups", "ctx"), "head"), P(("groups", "ctx"), "head"))
    return jax.shard_map(
        functools.partial(per_device, mesh.shape["ctx"]),
        mesh=mesh,
        in_specs=in_specs,
        out_specs=out_specs,
        check_vma=False,
    )
```

```python
import functools

import jax
import jax.numpy as jnp
from jax import lax
from jax.experimental import pallas as pl
from jax.experimental.pallas import tpu as pltpu
from jax.sharding import PartitionSpec as P

HEADS = 64
KV_HEADS = 8
HEAD_DIM = 128
GROUP = HEADS // KV_HEADS
PAGE = 16
P_DEV = 8
SEND_CAP = 2
EXP2_SCALE = HEAD_DIM ** (-0.5) * 1.4426950408889634
HIDDEN = -1e30
VMEM_BYTES = 48 * 1024 * 1024

VMEM = pl.BlockSpec(memory_space=pltpu.VMEM)
SMEM = pl.BlockSpec(memory_space=pltpu.SMEM)
HBM = pl.BlockSpec(memory_space=pltpu.HBM)


def scores_of(qt_ref, head, cols, keys):
    return jnp.dot(keys, qt_ref[head, :, cols], preferred_element_type=jnp.float32)


def soften(scores, old):
    high = jnp.max(scores, axis=0, keepdims=True)
    if old is None:
        weights = jnp.exp2((scores - high) * EXP2_SCALE)
        return weights.astype(jnp.bfloat16), high, jnp.sum(weights, axis=0, keepdims=True), None
    old_high, old_total = old
    high = jnp.maximum(high, old_high)
    decay = jnp.exp2((old_high - high) * EXP2_SCALE)
    weights = jnp.exp2((scores - high) * EXP2_SCALE)
    total = old_total * decay + jnp.sum(weights, axis=0, keepdims=True)
    return weights.astype(jnp.bfloat16), high, total, decay


def walk(blocks, first, second):
    ahead = first(blocks[0])
    for place, block in enumerate(blocks):
        current = ahead
        if place + 1 < len(blocks):
            ahead = first(blocks[place + 1])
        second(block, current)


def blocks_of(qt_ref):
    kv_local, _, rows = qt_ref.shape
    width = min(4 * (rows // GROUP), rows)
    return [(head, slice(start, start + width)) for head in range(kv_local) for start in range(0, rows, width)]


def attend(qt_ref, keys, values_t, old, new):
    high_ref, total_ref, accum_ref = new

    def second(block, scores):
        head, cols = block
        before = None if old is None else (old[0][head, :, cols], old[1][head, :, cols])
        weights, high, total, decay = soften(scores, before)
        accum = jnp.dot(values_t[head], weights, preferred_element_type=jnp.float32)
        if old is not None:
            accum = accum + old[2][head, :, cols] * decay
        high_ref[head, :, cols] = high
        total_ref[head, :, cols] = total
        accum_ref[head, :, cols] = accum

    walk(blocks_of(qt_ref), lambda block: scores_of(qt_ref, block[0], block[1], keys[block[0]]), second)


def hidden(seen):
    return jnp.where(seen, jnp.float32(0.0), jnp.float32(HIDDEN)).astype(jnp.bfloat16)


def stretch_mask(shard, own, tokens):
    place = lax.broadcasted_iota(jnp.int32, (tokens, tokens), 0)
    token = lax.broadcasted_iota(jnp.int32, (tokens, tokens), 1)
    return hidden(place - token <= (own - shard) * tokens)


def cache_mask(shard, limit, c_rows, tokens):
    place = lax.broadcasted_iota(jnp.int32, (c_rows, tokens), 0)
    return hidden(place < limit - shard * c_rows)


def slot_row(targets_ref, shard, own, tokens, pool):
    page = lax.broadcasted_iota(jnp.int32, (1, tokens), 1) // PAGE
    slots = jnp.full((1, tokens), -1, jnp.int32)
    for index in range(tokens // PAGE):
        target = targets_ref[shard * (tokens // PAGE) + index]
        slot = jnp.where(lax.div(target, P_DEV) == own, pool + lax.rem(target, P_DEV), -1)
        slots = jnp.where(page == index, slot, slots)
    return slots


def sent_pages(targets_ref, shard, owner, pages):
    one, two = jnp.int32(-1), jnp.int32(-1)
    for index in range(pages):
        hit = lax.div(targets_ref[shard * pages + index], P_DEV) == owner
        two = jnp.where(hit & (one >= 0) & (two < 0), index, two)
        one = jnp.where(hit & (one < 0), index, one)
    return one, two


def sent_slots(targets_ref, shard, owner, tokens, pool):
    page = lax.broadcasted_iota(jnp.int32, (1, tokens), 1) // PAGE
    row = jnp.full((1, tokens), -1, jnp.int32)
    for place, index in enumerate(sent_pages(targets_ref, shard, owner, tokens // PAGE)):
        target = targets_ref[shard * (tokens // PAGE) + jnp.maximum(index, 0)]
        slot = jnp.where(index >= 0, pool + lax.rem(target, P_DEV), -1)
        row = jnp.where(page == place, slot, row)
    return row


def length_column(length_ref):
    rows = length_ref.shape[0]
    place = lax.broadcasted_iota(jnp.int32, (rows, 1), 0)
    lengths = jnp.zeros((rows, 1), jnp.int32)
    for row in range(rows):
        lengths = jnp.where(place == row, length_ref[row], lengths)
    return lengths


def tally_of(lists, lengths, slot):
    rows, span = lists.shape
    tokens = slot.shape[1]
    slot = jnp.broadcast_to(slot, (rows, tokens))
    offset = lax.rem(lax.broadcasted_iota(jnp.int32, (rows, tokens), 1), PAGE)
    tally = jnp.zeros((rows, tokens), jnp.float32)
    for entry in range(span):
        hit = (slot == lists[:, entry : entry + 1]) & (offset < lengths - entry * PAGE)
        tally = tally + jnp.where(hit, jnp.float32(1.0), jnp.float32(0.0))
    return tally[None]


def shard_of(own, hop, count):
    return lax.rem(own + hop + count, count)


def wide_queries(q_ref, kv_local):
    heads = q_ref.shape[1] // HEAD_DIM
    queries = q_ref[...].astype(jnp.float32)
    stacked = []
    for head in range(heads):
        piece = queries[:, head * HEAD_DIM : (head + 1) * HEAD_DIM]
        blank = jnp.zeros_like(piece)
        stacked.append(
            jnp.concatenate([piece if kv == head // GROUP else blank for kv in range(kv_local)], axis=1)
        )
    return jnp.concatenate(stacked, axis=0).astype(jnp.bfloat16)


def decode_attend(queries, parts, state):
    done = []
    for keys, values, tally in parts:
        scores = lax.dot_general(
            queries, keys, (((1,), (1,)), ((), ())), preferred_element_type=jnp.float32
        ).reshape(-1, tally.shape[1], tally.shape[2])
        done.append((jnp.where(tally > 0, scores, jnp.float32(HIDDEN)), tally, values))
    highs = [jnp.max(scores, axis=-1, keepdims=True) for scores, _, _ in done]
    if state is not None:
        old_high, old_total, old_mixed = state
        highs.append(old_high)
    high = functools.reduce(jnp.maximum, highs)
    total, mixed = 0.0, 0.0
    if state is not None:
        decay = jnp.exp2((old_high - high) * EXP2_SCALE)
        total = old_total * decay
        mixed = old_mixed * decay
    for scores, tally, values in done:
        weights = jnp.exp2((scores - high) * EXP2_SCALE) * tally
        total = total + jnp.sum(weights, axis=-1, keepdims=True)
        mixed = mixed + jnp.dot(
            weights.reshape(queries.shape[0], -1).astype(jnp.bfloat16),
            values,
            preferred_element_type=jnp.float32,
        ).reshape(high.shape[0], high.shape[1], -1)
    return high, total, mixed


def features(head):
    return slice(head * HEAD_DIM, (head + 1) * HEAD_DIM)


def shard_parts(ref, tokens, c_rows):
    return slice(0, tokens + c_rows), slice(tokens + c_rows, 2 * (tokens + c_rows))


def own_kernel(
    count, hops, own_ref, limit_ref, targets_ref, q_ref, shard_ref,
    qt_ref, near_ref, far_ref, pick_ref, high_ref, total_ref, accum_ref,
):
    kv_local, _, rows = qt_ref.shape
    tokens = q_ref.shape[0]
    c_rows = far_ref.shape[1]
    own = own_ref[0]
    limit = limit_ref[0]
    place = lax.broadcasted_iota(jnp.int32, (tokens, tokens), 0)
    token = lax.broadcasted_iota(jnp.int32, (tokens, tokens), 1)
    pick = jnp.where(place == token, jnp.float32(1.0), jnp.float32(0.0)).astype(jnp.bfloat16)
    for head in range(kv_local):
        for sub in range(GROUP):
            cols = slice(sub * tokens, (sub + 1) * tokens)
            qt_ref[head, :HEAD_DIM, cols] = q_ref[:, features(head * GROUP + sub)].T
            qt_ref[head, HEAD_DIM:, cols] = pick
    for place, hop in enumerate(hops):
        shard = shard_of(own, hop, count)
        near_ref[place] = stretch_mask(shard, own, tokens)
        far_ref[place] = cache_mask(shard, limit, c_rows, tokens)
    onward = 1 if hops[-1] < 0 else -1
    pages = tokens // PAGE
    one, two = sent_pages(
        targets_ref, shard_of(own, hops[-1] + onward, count), shard_of(own, onward, count), pages
    )
    row = lax.broadcasted_iota(jnp.int32, pick_ref.shape, 0)
    token = lax.broadcasted_iota(jnp.int32, pick_ref.shape, 1)
    sent = ((row < PAGE) & (one >= 0) & (token == row + one * PAGE)) | (
        (row >= PAGE) & (two >= 0) & (token == row + (two - 1) * PAGE)
    )
    pick_ref[...] = jnp.where(sent, jnp.float32(1.0), jnp.float32(0.0)).astype(jnp.bfloat16)
    mask = jnp.concatenate([stretch_mask(own, own, tokens), cache_mask(own, limit, c_rows, tokens)], axis=0)
    key_rows, value_rows = shard_parts(shard_ref, tokens, c_rows)
    keys = [jnp.concatenate([shard_ref[key_rows, features(head)], mask], axis=1) for head in range(kv_local)]
    values_t = [shard_ref[value_rows, features(head)].T for head in range(kv_local)]
    attend(qt_ref, keys, values_t, None, (high_ref, total_ref, accum_ref))


def held_kernel(
    own_ref, targets_ref, length_ref, q_ref, lists_ref, pool_k, pool_v, rest_ref,
    wide_ref, high_ref, total_ref, mixed_ref,
):
    kv_width = rest_ref.shape[1]
    pool = pool_k.shape[0]
    held = pool * PAGE
    tokens = PAGE * P_DEV
    half = rest_ref.shape[0] // 2
    own = own_ref[0]
    lists = lists_ref[...]
    lengths = length_column(length_ref)
    wide_ref[...] = wide_queries(q_ref, kv_width // HEAD_DIM)
    held_slot = lax.broadcasted_iota(jnp.int32, (1, held), 1) // PAGE
    own_slot = slot_row(targets_ref, own, own, tokens, pool)
    parts = [
        (
            pool_k[...].reshape(held, kv_width),
            pool_v[...].reshape(held, kv_width),
            tally_of(lists, lengths, held_slot),
        ),
        (rest_ref[:tokens], rest_ref[half : half + tokens], tally_of(lists, lengths, own_slot)),
    ]
    high_ref[...], total_ref[...], mixed_ref[...] = decode_attend(wide_ref[...], parts, None)


def hop_kernel(places, qt_ref, near_ref, far_ref, high_in, total_in, accum_in, *refs):
    shard_refs, outs = refs[: len(places)], refs[len(places) :]
    tokens, c_rows = near_ref.shape[1], far_ref.shape[1]
    mask = jnp.concatenate([ref[place] for place in places for ref in (near_ref, far_ref)], axis=0)
    keys, values_t = [], []
    for head in range(qt_ref.shape[0]):
        pieces, values = [], []
        for ref in shard_refs:
            key_rows, value_rows = shard_parts(ref, tokens, c_rows)
            pieces.append(ref[key_rows, features(head)])
            values.append(ref[value_rows, features(head)])
        keys.append(jnp.concatenate([jnp.concatenate(pieces, axis=0), mask], axis=1))
        values_t.append(jnp.concatenate(values, axis=0).T)
    attend(qt_ref, keys, values_t, (high_in, total_in, accum_in), outs)


def split_kernel(pick_ref, shard_ref, keys_ref, stretch_ref, values_ref, pages_ref):
    tokens = pick_ref.shape[1]
    half = shard_ref.shape[0] // 2
    sent = pick_ref.shape[0]
    for place, start in enumerate((0, half)):
        stretch_ref[place * tokens : (place + 1) * tokens] = shard_ref[start : start + tokens]
        rows = jnp.dot(pick_ref[...], shard_ref[start : start + tokens], preferred_element_type=jnp.float32)
        pages_ref[place * sent : (place + 1) * sent] = rows.astype(jnp.bfloat16)
    keys_ref[...] = shard_ref[tokens:half]
    values_ref[...] = shard_ref[half + tokens :]


def near_pages_kernel(count, hops, tokens, pool, own_ref, targets_ref, length_ref, lists_ref, *refs):
    shard_refs, refs = refs[: len(hops) - 1], refs[len(hops) - 1 :]
    wide_ref, dec_high, dec_total, dec_mixed, high_ref, total_ref, mixed_ref, tally_ref = refs
    own = own_ref[0]
    lists = lists_ref[...]
    lengths = length_column(length_ref)
    parts = []
    for hop, ref in zip(hops, shard_refs):
        half = ref.shape[0] // 2
        slot = slot_row(targets_ref, shard_of(own, hop, count), own, tokens, pool)
        parts.append((ref[:tokens], ref[half : half + tokens], tally_of(lists, lengths, slot)))
    state = (dec_high[...], dec_total[...], dec_mixed[...])
    high_ref[...], total_ref[...], mixed_ref[...] = decode_attend(wide_ref[...], parts, state)
    shard = shard_of(own, hops[-1], count)
    attended = shard < own
    whole = slot_row(targets_ref, shard, own, tokens, pool)
    alone = sent_slots(targets_ref, shard, own, tokens, pool)
    tally_ref[...] = tally_of(lists, lengths, jnp.where(attended, whole, alone))


def score_kernel(
    final, qt_ref, near_ref, far_ref, high_in, total_in, accum_in, keys_ref, stretch_ref,
    weights_ref, total_ref, accum_ref,
):
    kv_local = qt_ref.shape[0]
    tokens, c_rows = near_ref.shape[1], far_ref.shape[1]
    def run(attended):
        mask = far_ref[final]
        if attended:
            mask = jnp.concatenate([near_ref[final], mask], axis=0)
        keys, values_t = [], []
        for head in range(kv_local):
            rows = keys_ref[:, features(head)]
            if attended:
                rows = jnp.concatenate([stretch_ref[:tokens, features(head)], rows], axis=0)
                values_t.append(stretch_ref[tokens:, features(head)].T)
            keys.append(jnp.concatenate([rows, mask], axis=1))

        def second(block, scores):
            head, cols = block
            before = (high_in[head, :, cols], total_in[head, :, cols])
            weights, _, total, decay = soften(scores, before)
            weights_ref[head, :, cols] = weights[-c_rows:]
            total_ref[head, :, cols] = total
            accum = accum_in[head, :, cols] * decay
            if attended:
                accum = accum + jnp.dot(values_t[head], weights[:tokens], preferred_element_type=jnp.float32)
            accum_ref[head, :, cols] = accum

        walk(blocks_of(qt_ref), lambda block: scores_of(qt_ref, block[0], block[1], keys[block[0]]), second)

    attended = jnp.max(near_ref[final].astype(jnp.float32)) > HIDDEN / 2
    pl.when(attended)(functools.partial(run, True))
    pl.when(jnp.logical_not(attended))(functools.partial(run, False))


def last_pages_kernel(
    stretch_ref, pages_ref, tally_ref, wide_ref, dec_high, dec_total, dec_mixed, dec_out
):
    tokens = stretch_ref.shape[0] // 2
    sent = pages_ref.shape[0] // 2
    keys = jnp.concatenate([stretch_ref[:sent] + pages_ref[:sent], stretch_ref[sent:tokens]], axis=0)
    values = jnp.concatenate(
        [stretch_ref[tokens : tokens + sent] + pages_ref[sent:], stretch_ref[tokens + sent :]], axis=0
    )
    state = (dec_high[...], dec_total[...], dec_mixed[...])
    _, total, mixed = decode_attend(wide_ref[...], [(keys, values, tally_ref[...])], state)
    share = 1.0 / total
    for head in range(dec_high.shape[0]):
        piece = mixed[head, :, features(head // GROUP)] * share[head]
        dec_out[:, features(head)] = piece.astype(jnp.bfloat16)


def last_kernel(weights_ref, total_ref, accum_ref, values_ref, out_ref, result_ref, sems):
    tokens = result_ref.shape[0]
    values_t = [values_ref[:, features(head)].T for head in range(weights_ref.shape[0])]
    copies = []

    def first(block):
        head, cols = block
        return jnp.dot(values_t[head], weights_ref[head, :, cols], preferred_element_type=jnp.float32)

    def second(block, mixed):
        head, cols = block
        mixed = mixed + accum_ref[head, :, cols]
        mixed = (mixed * (1.0 / total_ref[head, :, cols])).astype(jnp.bfloat16)
        start = (head * GROUP + cols.start // tokens) * HEAD_DIM
        pieces = (cols.stop - cols.start) // tokens
        for piece in range(pieces):
            col = start + piece * HEAD_DIM
            result_ref[:, col : col + HEAD_DIM] = mixed[:, piece * tokens : (piece + 1) * tokens].T
        span = pl.ds(start, pieces * HEAD_DIM)
        copy = pltpu.make_async_copy(result_ref.at[:, span], out_ref.at[:, span], sems.at[len(copies)])
        copy.start()
        copies.append(copy)

    walk(blocks_of(weights_ref), first, second)

    for copy in copies:
        copy.wait()


def per_device(
    count,
    queries,
    stretch_keys,
    stretch_values,
    cache_keys,
    cache_values,
    prefix_length,
    page_targets,
    pool_keys,
    pool_values,
    decode_queries,
    page_lists,
    context_length,
):
    own = lax.axis_index("ctx")
    own_array = jnp.full((1,), own, jnp.int32)
    tokens, width = queries.shape
    kv_width = stretch_keys.shape[1]
    kv_local = kv_width // HEAD_DIM
    rows = GROUP * tokens
    heads = kv_local * GROUP
    dec_rows = decode_queries.shape[0]
    c_rows = cache_keys.shape[0]
    pool = pool_keys.shape[0]
    f32, bf16 = jnp.float32, jnp.bfloat16
    shape = jax.ShapeDtypeStruct
    params = pltpu.CompilerParams(vmem_limit_bytes=VMEM_BYTES)
    up_pairs = [(i, (i + 1) % count) for i in range(count)]
    down_pairs = [(i, (i - 1) % count) for i in range(count)]
    hops = []
    for far in range(1, count // 2 + 1):
        hops += [-far, far] if far <= (count - 1) // 2 else [-far]

    def send(array, hop):
        return lax.ppermute(array, "ctx", up_pairs if hop < 0 else down_pairs)

    def cost(keys):
        pairs = kv_local * rows * keys
        return pl.CostEstimate(
            flops=4 * pairs * HEAD_DIM, bytes_accessed=4 * rows * kv_local * HEAD_DIM, transcendentals=pairs
        )

    half = tokens + c_rows
    low = jnp.array(-jnp.inf, bf16)
    spread, start = [], 0
    for part in (stretch_keys, cache_keys, stretch_values, cache_values):
        end = 2 * half - start - part.shape[0]
        spread.append(lax.pad(part, low, ((start, end, 0), (0, 0, 0))))
        start += part.shape[0]
    shard = {0: functools.reduce(jnp.maximum, spread)}
    shard[-1] = send(shard[0], -1)

    state_shapes = (
        shape((kv_local, 1, rows), f32),
        shape((kv_local, 1, rows), f32),
        shape((kv_local, HEAD_DIM, rows), f32),
    )
    qt, near, far, pick, *state = pl.pallas_call(
        functools.partial(own_kernel, count, hops),
        out_shape=(
            shape((kv_local, HEAD_DIM + tokens, rows), bf16),
            shape((count - 1, tokens, tokens), bf16),
            shape((count - 1, c_rows, tokens), bf16),
            shape((SEND_CAP * PAGE, tokens), bf16),
        )
        + state_shapes,
        in_specs=[SMEM] * 3 + [VMEM] * 2,
        out_specs=(VMEM,) * 7,
        compiler_params=params,
        cost_estimate=cost(tokens + c_rows),
        name="own_shard",
    )(own_array, prefix_length, page_targets, queries, shard[0])

    dec_shapes = (
        shape((heads, dec_rows, 1), f32),
        shape((heads, dec_rows, 1), f32),
        shape((heads, dec_rows, kv_width), f32),
    )
    wide, *dec_state = pl.pallas_call(
        held_kernel,
        out_shape=(shape((heads * dec_rows, kv_width), bf16),) + dec_shapes,
        in_specs=[SMEM] * 3 + [VMEM] * 5,
        out_specs=(VMEM,) * 4,
        compiler_params=params,
        cost_estimate=pl.CostEstimate(
            flops=4 * 128 * 2048 * 256, bytes_accessed=4 * pool_keys.size, transcendentals=128 * 2048
        ),
        name="decode_held_pages",
    )(own_array, page_targets, context_length, decode_queries, page_lists, pool_keys, pool_values, shard[0])

    if 1 in hops:
        sent_down, state, dec_state = lax.optimization_barrier((shard[0], state, dec_state))
        shard[1] = send(sent_down, 1)
    shard[-1], state, dec_state = lax.optimization_barrier((shard[-1], state, dec_state))
    for hop in hops[2:-1]:
        shard[hop] = send(shard[hop + 1 if hop < 0 else hop - 1], hop)
    hop = hops[-1]
    nearer = shard[hop + 1 if hop < 0 else hop - 1]
    pieces = pl.pallas_call(
        split_kernel,
        out_shape=(
            shape((c_rows, kv_width), bf16),
            shape((2 * tokens, kv_width), bf16),
            shape((c_rows, kv_width), bf16),
            shape((2 * SEND_CAP * PAGE, kv_width), bf16),
        ),
        in_specs=[VMEM] * 2,
        out_specs=(VMEM,) * 4,
        compiler_params=params,
        name="pieces_to_send_on",
    )(pick, nearer)
    last_keys = send(pieces[0], hop)
    attending, others = [], []
    for pair in up_pairs if hop < 0 else down_pairs:
        (attending if (pair[1] + hop) % count < pair[1] else others).append(pair)
    last_stretch = lax.ppermute(pieces[1], "ctx", attending)
    last_pages = lax.ppermute(pieces[3], "ctx", others)
    last_values = send(pieces[2], hop)

    for first in range(len(hops) - 1):
        places = [first]
        state = pl.pallas_call(
            functools.partial(hop_kernel, places),
            out_shape=state_shapes,
            in_specs=[VMEM] * (6 + len(places)),
            out_specs=(VMEM,) * 3,
            compiler_params=params,
            cost_estimate=cost((c_rows + tokens) * len(places)),
            name="whole_shards_" + str(first),
        )(qt, near, far, *state, *[shard[hops[place]] for place in places])

    final = len(hops) - 1
    dec_state, state = lax.optimization_barrier((dec_state, state))
    near_hops = hops[:-1]
    *dec_state, tally = pl.pallas_call(
        functools.partial(near_pages_kernel, count, hops, tokens, pool),
        out_shape=dec_shapes
        + (shape((1, dec_rows, tokens), f32),),
        in_specs=[SMEM] * 3 + [VMEM] * (5 + len(near_hops)),
        out_specs=(VMEM,) * 4,
        compiler_params=params,
        cost_estimate=cost(tokens),
        name="decode_near_pages",
    )(
        own_array, page_targets, context_length, page_lists, *[shard[hop] for hop in near_hops],
        wide, *dec_state,
    )
    dec_state, state = lax.optimization_barrier((dec_state, state))

    weights, total, accum = pl.pallas_call(
        functools.partial(score_kernel, final),
        out_shape=(shape((kv_local, c_rows, rows), bf16),) + state_shapes[1:],
        in_specs=[VMEM] * 8,
        out_specs=(VMEM,) * 3,
        compiler_params=params,
        cost_estimate=cost(half),
        name="last_scores",
    )(qt, near, far, *state, last_keys, last_stretch)

    dec_state, total = lax.optimization_barrier((dec_state, total))
    decoded = pl.pallas_call(
        last_pages_kernel,
        out_shape=shape(decode_queries.shape, bf16),
        in_specs=[VMEM] * 7,
        out_specs=VMEM,
        compiler_params=params,
        cost_estimate=cost(tokens // 2),
        name="decode_last_pages",
    )(last_stretch, last_pages, tally, wide, *dec_state)
    decoded, total = lax.optimization_barrier((decoded, total))

    prefill = pl.pallas_call(
        last_kernel,
        out_shape=shape((tokens, width), bf16),
        in_specs=[VMEM] * 4,
        out_specs=HBM,
        scratch_shapes=[
            pltpu.VMEM((tokens, width), bf16),
            pltpu.SemaphoreType.DMA((kv_local * max(GROUP // 2, 1),)),
        ],
        compiler_params=params,
        cost_estimate=cost(c_rows // 2),
        name="last_values",
    )(weights, total, accum, last_values)
    return (prefill, decoded)


def solution(mesh):
    in_specs = (
        P(("groups", "ctx"), "head"),
        P(("groups", "ctx"), "head"),
        P(("groups", "ctx"), "head"),
        P(("groups", "ctx"), "head"),
        P(("groups", "ctx"), "head"),
        P("groups"),
        P("groups"),
        P(("groups", "ctx"), None, "head"),
        P(("groups", "ctx"), None, "head"),
        P(("groups", "ctx"), "head"),
        P(("groups", "ctx"), None),
        P(("groups", "ctx")),
    )
    out_specs = (P(("groups", "ctx"), "head"), P(("groups", "ctx"), "head"))
    return jax.shard_map(
        functools.partial(per_device, mesh.shape["ctx"]),
        mesh=mesh,
        in_specs=in_specs,
        out_specs=out_specs,
        check_vma=False,
    )
```

```python
import functools

import jax
import jax.numpy as jnp
from jax import lax
from jax.experimental import pallas as pl
from jax.experimental.pallas import tpu as pltpu
from jax.sharding import PartitionSpec as P

HEADS = 64
KV_HEADS = 8
HEAD_DIM = 128
GROUP = HEADS // KV_HEADS
PAGE = 16
P_DEV = 8
SEND_CAP = 2
EXP2_SCALE = HEAD_DIM ** (-0.5) * 1.4426950408889634
HIDDEN = -1e30
VMEM_BYTES = 48 * 1024 * 1024

VMEM = pl.BlockSpec(memory_space=pltpu.VMEM)
SMEM = pl.BlockSpec(memory_space=pltpu.SMEM)
HBM = pl.BlockSpec(memory_space=pltpu.HBM)


def scores_of(qt_ref, head, cols, keys):
    return jnp.dot(keys, qt_ref[head, :, cols], preferred_element_type=jnp.float32)


def soften(scores, old):
    high = jnp.max(scores, axis=0, keepdims=True)
    if old is None:
        weights = jnp.exp2((scores - high) * EXP2_SCALE)
        return weights.astype(jnp.bfloat16), high, jnp.sum(weights, axis=0, keepdims=True), None
    old_high, old_total = old
    high = jnp.maximum(high, old_high)
    decay = jnp.exp2((old_high - high) * EXP2_SCALE)
    weights = jnp.exp2((scores - high) * EXP2_SCALE)
    total = old_total * decay + jnp.sum(weights, axis=0, keepdims=True)
    return weights.astype(jnp.bfloat16), high, total, decay


def walk(blocks, first, second):
    ahead = first(blocks[0])
    for place, block in enumerate(blocks):
        current = ahead
        if place + 1 < len(blocks):
            ahead = first(blocks[place + 1])
        second(block, current)


def blocks_of(ref, groups=GROUP):
    kv_local, _, rows = ref.shape
    width = groups * (rows // GROUP)
    return [(head, slice(start, start + width)) for head in range(kv_local) for start in range(0, rows, width)]


def attend(qt_ref, keys, values_t, old, new):
    high_ref, total_ref, accum_ref = new

    def second(block, scores):
        head, cols = block
        before = None if old is None else (old[0][head, :, cols], old[1][head, :, cols])
        weights, high, total, decay = soften(scores, before)
        accum = jnp.dot(values_t[head], weights, preferred_element_type=jnp.float32)
        if old is not None:
            accum = accum + old[2][head, :, cols] * decay
        high_ref[head, :, cols] = high
        total_ref[head, :, cols] = total
        accum_ref[head, :, cols] = accum

    walk(blocks_of(qt_ref), lambda block: scores_of(qt_ref, block[0], block[1], keys[block[0]]), second)


def hidden(seen):
    return jnp.where(seen, jnp.float32(0.0), jnp.float32(HIDDEN)).astype(jnp.bfloat16)


def stretch_mask(shard, own, tokens):
    place = lax.broadcasted_iota(jnp.int32, (tokens, tokens), 0)
    token = lax.broadcasted_iota(jnp.int32, (tokens, tokens), 1)
    return hidden(place - token <= (own - shard) * tokens)


def cache_mask(shard, limit, c_rows, tokens):
    place = lax.broadcasted_iota(jnp.int32, (c_rows, tokens), 0)
    return hidden(place < limit - shard * c_rows)


def slot_row(targets_ref, shard, own, tokens, pool):
    page = lax.broadcasted_iota(jnp.int32, (1, tokens), 1) // PAGE
    slots = jnp.full((1, tokens), -1, jnp.int32)
    for index in range(tokens // PAGE):
        target = targets_ref[shard * (tokens // PAGE) + index]
        slot = jnp.where(lax.div(target, P_DEV) == own, pool + lax.rem(target, P_DEV), -1)
        slots = jnp.where(page == index, slot, slots)
    return slots


def sent_pages(targets_ref, shard, owner, pages):
    one, two = jnp.int32(-1), jnp.int32(-1)
    for index in range(pages):
        hit = lax.div(targets_ref[shard * pages + index], P_DEV) == owner
        two = jnp.where(hit & (one >= 0) & (two < 0), index, two)
        one = jnp.where(hit & (one < 0), index, one)
    return one, two


def sent_slots(targets_ref, shard, owner, tokens, pool):
    page = lax.broadcasted_iota(jnp.int32, (1, tokens), 1) // PAGE
    row = jnp.full((1, tokens), -1, jnp.int32)
    for place, index in enumerate(sent_pages(targets_ref, shard, owner, tokens // PAGE)):
        target = targets_ref[shard * (tokens // PAGE) + jnp.maximum(index, 0)]
        slot = jnp.where(index >= 0, pool + lax.rem(target, P_DEV), -1)
        row = jnp.where(page == place, slot, row)
    return row


def length_column(length_ref):
    rows = length_ref.shape[0]
    place = lax.broadcasted_iota(jnp.int32, (rows, 1), 0)
    lengths = jnp.zeros((rows, 1), jnp.int32)
    for row in range(rows):
        lengths = jnp.where(place == row, length_ref[row], lengths)
    return lengths


def tally_of(lists, lengths, slot):
    rows, span = lists.shape
    tokens = slot.shape[1]
    slot = jnp.broadcast_to(slot, (rows, tokens))
    offset = lax.rem(lax.broadcasted_iota(jnp.int32, (rows, tokens), 1), PAGE)
    tally = jnp.zeros((rows, tokens), jnp.float32)
    for entry in range(span):
        hit = (slot == lists[:, entry : entry + 1]) & (offset < lengths - entry * PAGE)
        tally = tally + jnp.where(hit, jnp.float32(1.0), jnp.float32(0.0))
    return tally[None]


def shard_of(own, hop, count):
    return lax.rem(own + hop + count, count)


def wide_queries(q_ref, kv_local):
    heads = q_ref.shape[1] // HEAD_DIM
    queries = q_ref[...].astype(jnp.float32)
    stacked = []
    for head in range(heads):
        piece = queries[:, head * HEAD_DIM : (head + 1) * HEAD_DIM]
        blank = jnp.zeros_like(piece)
        stacked.append(
            jnp.concatenate([piece if kv == head // GROUP else blank for kv in range(kv_local)], axis=1)
        )
    return jnp.concatenate(stacked, axis=0).astype(jnp.bfloat16)


def decode_attend(queries, parts, state):
    done = []
    for keys, values, tally in parts:
        scores = lax.dot_general(
            queries, keys, (((1,), (1,)), ((), ())), preferred_element_type=jnp.float32
        ).reshape(-1, tally.shape[1], tally.shape[2])
        done.append((jnp.where(tally > 0, scores, jnp.float32(HIDDEN)), tally, values))
    highs = [jnp.max(scores, axis=-1, keepdims=True) for scores, _, _ in done]
    if state is not None:
        old_high, old_total, old_mixed = state
        highs.append(old_high)
    high = functools.reduce(jnp.maximum, highs)
    total, mixed = 0.0, 0.0
    if state is not None:
        decay = jnp.exp2((old_high - high) * EXP2_SCALE)
        total = old_total * decay
        mixed = old_mixed * decay
    for scores, tally, values in done:
        weights = jnp.exp2((scores - high) * EXP2_SCALE) * tally
        total = total + jnp.sum(weights, axis=-1, keepdims=True)
        mixed = mixed + jnp.dot(
            weights.reshape(queries.shape[0], -1).astype(jnp.bfloat16),
            values,
            preferred_element_type=jnp.float32,
        ).reshape(high.shape[0], high.shape[1], -1)
    return high, total, mixed


def features(head):
    return slice(head * HEAD_DIM, (head + 1) * HEAD_DIM)


def shard_parts(ref, tokens, c_rows):
    return slice(0, tokens + c_rows), slice(tokens + c_rows, 2 * (tokens + c_rows))


def own_kernel(
    count, hops, own_ref, limit_ref, targets_ref, q_ref, shard_ref,
    qt_ref, near_ref, far_ref, pick_ref, high_ref, total_ref, accum_ref,
):
    kv_local, _, rows = qt_ref.shape
    tokens = q_ref.shape[0]
    c_rows = far_ref.shape[1]
    own = own_ref[0]
    limit = limit_ref[0]
    place = lax.broadcasted_iota(jnp.int32, (tokens, tokens), 0)
    token = lax.broadcasted_iota(jnp.int32, (tokens, tokens), 1)
    pick = jnp.where(place == token, jnp.float32(1.0), jnp.float32(0.0)).astype(jnp.bfloat16)
    for head in range(kv_local):
        for sub in range(GROUP):
            cols = slice(sub * tokens, (sub + 1) * tokens)
            qt_ref[head, :HEAD_DIM, cols] = q_ref[:, features(head * GROUP + sub)].T
            qt_ref[head, HEAD_DIM:, cols] = pick
    for place, hop in enumerate(hops):
        shard = shard_of(own, hop, count)
        near_ref[place] = stretch_mask(shard, own, tokens)
        far_ref[place] = cache_mask(shard, limit, c_rows, tokens)
    onward = 1 if hops[-1] < 0 else -1
    pages = tokens // PAGE
    one, two = sent_pages(
        targets_ref, shard_of(own, hops[-1] + onward, count), shard_of(own, onward, count), pages
    )
    row = lax.broadcasted_iota(jnp.int32, pick_ref.shape, 0)
    token = lax.broadcasted_iota(jnp.int32, pick_ref.shape, 1)
    sent = ((row < PAGE) & (one >= 0) & (token == row + one * PAGE)) | (
        (row >= PAGE) & (two >= 0) & (token == row + (two - 1) * PAGE)
    )
    pick_ref[...] = jnp.where(sent, jnp.float32(1.0), jnp.float32(0.0)).astype(jnp.bfloat16)
    mask = jnp.concatenate([stretch_mask(own, own, tokens), cache_mask(own, limit, c_rows, tokens)], axis=0)
    key_rows, value_rows = shard_parts(shard_ref, tokens, c_rows)
    keys = [jnp.concatenate([shard_ref[key_rows, features(head)], mask], axis=1) for head in range(kv_local)]
    values_t = [shard_ref[value_rows, features(head)].T for head in range(kv_local)]
    attend(qt_ref, keys, values_t, None, (high_ref, total_ref, accum_ref))


def held_kernel(
    own_ref, targets_ref, length_ref, q_ref, lists_ref, pool_k, pool_v, rest_ref,
    wide_ref, high_ref, total_ref, mixed_ref,
):
    kv_width = rest_ref.shape[1]
    pool = pool_k.shape[0]
    held = pool * PAGE
    tokens = PAGE * P_DEV
    half = rest_ref.shape[0] // 2
    own = own_ref[0]
    lists = lists_ref[...]
    lengths = length_column(length_ref)
    wide_ref[...] = wide_queries(q_ref, kv_width // HEAD_DIM)
    held_slot = lax.broadcasted_iota(jnp.int32, (1, held), 1) // PAGE
    own_slot = slot_row(targets_ref, own, own, tokens, pool)
    parts = [
        (
            pool_k[...].reshape(held, kv_width),
            pool_v[...].reshape(held, kv_width),
            tally_of(lists, lengths, held_slot),
        ),
        (rest_ref[:tokens], rest_ref[half : half + tokens], tally_of(lists, lengths, own_slot)),
    ]
    high_ref[...], total_ref[...], mixed_ref[...] = decode_attend(wide_ref[...], parts, None)


def hop_kernel(places, qt_ref, near_ref, far_ref, high_in, total_in, accum_in, *refs):
    shard_refs, outs = refs[: len(places)], refs[len(places) :]
    tokens, c_rows = near_ref.shape[1], far_ref.shape[1]
    mask = jnp.concatenate([ref[place] for place in places for ref in (near_ref, far_ref)], axis=0)
    keys, values_t = [], []
    for head in range(qt_ref.shape[0]):
        pieces, values = [], []
        for ref in shard_refs:
            key_rows, value_rows = shard_parts(ref, tokens, c_rows)
            pieces.append(ref[key_rows, features(head)])
            values.append(ref[value_rows, features(head)])
        keys.append(jnp.concatenate([jnp.concatenate(pieces, axis=0), mask], axis=1))
        values_t.append(jnp.concatenate(values, axis=0).T)
    attend(qt_ref, keys, values_t, (high_in, total_in, accum_in), outs)


def split_kernel(pick_ref, shard_ref, keys_ref, stretch_ref, values_ref, pages_ref):
    tokens = pick_ref.shape[1]
    half = shard_ref.shape[0] // 2
    sent = pick_ref.shape[0]
    for place, start in enumerate((0, half)):
        stretch_ref[place * tokens : (place + 1) * tokens] = shard_ref[start : start + tokens]
        rows = jnp.dot(pick_ref[...], shard_ref[start : start + tokens], preferred_element_type=jnp.float32)
        pages_ref[place * sent : (place + 1) * sent] = rows.astype(jnp.bfloat16)
    keys_ref[...] = shard_ref[tokens:half]
    values_ref[...] = shard_ref[half + tokens :]


def near_pages_kernel(count, hops, tokens, pool, own_ref, targets_ref, length_ref, lists_ref, *refs):
    shard_refs, refs = refs[: len(hops) - 1], refs[len(hops) - 1 :]
    wide_ref, dec_high, dec_total, dec_mixed, high_ref, total_ref, mixed_ref, tally_ref = refs
    own = own_ref[0]
    lists = lists_ref[...]
    lengths = length_column(length_ref)
    parts = []
    for hop, ref in zip(hops, shard_refs):
        half = ref.shape[0] // 2
        slot = slot_row(targets_ref, shard_of(own, hop, count), own, tokens, pool)
        parts.append((ref[:tokens], ref[half : half + tokens], tally_of(lists, lengths, slot)))
    state = (dec_high[...], dec_total[...], dec_mixed[...])
    high_ref[...], total_ref[...], mixed_ref[...] = decode_attend(wide_ref[...], parts, state)
    shard = shard_of(own, hops[-1], count)
    attended = shard < own
    whole = slot_row(targets_ref, shard, own, tokens, pool)
    alone = sent_slots(targets_ref, shard, own, tokens, pool)
    tally_ref[...] = tally_of(lists, lengths, jnp.where(attended, whole, alone))


def score_kernel(
    final, qt_ref, near_ref, far_ref, high_in, total_in, accum_in, keys_ref, stretch_ref,
    weights_ref, total_ref, accum_ref,
):
    kv_local = qt_ref.shape[0]
    tokens, c_rows = near_ref.shape[1], far_ref.shape[1]
    def run(attended):
        mask = far_ref[final]
        if attended:
            mask = jnp.concatenate([near_ref[final], mask], axis=0)
        keys, values_t = [], []
        for head in range(kv_local):
            rows = keys_ref[:, features(head)]
            if attended:
                rows = jnp.concatenate([stretch_ref[:tokens, features(head)], rows], axis=0)
                values_t.append(stretch_ref[tokens:, features(head)].T)
            keys.append(jnp.concatenate([rows, mask], axis=1))

        def second(block, scores):
            head, cols = block
            before = (high_in[head, :, cols], total_in[head, :, cols])
            weights, _, total, decay = soften(scores, before)
            weights_ref[head, :, cols] = weights[-c_rows:]
            total_ref[head, :, cols] = total
            accum = accum_in[head, :, cols] * decay
            if attended:
                accum = accum + jnp.dot(values_t[head], weights[:tokens], preferred_element_type=jnp.float32)
            accum_ref[head, :, cols] = accum

        walk(blocks_of(qt_ref), lambda block: scores_of(qt_ref, block[0], block[1], keys[block[0]]), second)

    attended = jnp.max(near_ref[final].astype(jnp.float32)) > HIDDEN / 2
    pl.when(attended)(functools.partial(run, True))
    pl.when(jnp.logical_not(attended))(functools.partial(run, False))


def last_pages_kernel(
    stretch_ref, pages_ref, tally_ref, wide_ref, dec_high, dec_total, dec_mixed, dec_out
):
    tokens = stretch_ref.shape[0] // 2
    sent = pages_ref.shape[0] // 2
    keys = jnp.concatenate([stretch_ref[:sent] + pages_ref[:sent], stretch_ref[sent:tokens]], axis=0)
    values = jnp.concatenate(
        [stretch_ref[tokens : tokens + sent] + pages_ref[sent:], stretch_ref[tokens + sent :]], axis=0
    )
    state = (dec_high[...], dec_total[...], dec_mixed[...])
    _, total, mixed = decode_attend(wide_ref[...], [(keys, values, tally_ref[...])], state)
    share = 1.0 / total
    for head in range(dec_high.shape[0]):
        piece = mixed[head, :, features(head // GROUP)] * share[head]
        dec_out[:, features(head)] = piece.astype(jnp.bfloat16)


def last_kernel(weights_ref, total_ref, accum_ref, values_ref, out_ref, result_ref, sems):
    tokens = result_ref.shape[0]
    values_t = [values_ref[:, features(head)].T for head in range(weights_ref.shape[0])]
    copies = []

    def first(block):
        head, cols = block
        return jnp.dot(values_t[head], weights_ref[head, :, cols], preferred_element_type=jnp.float32)

    def second(block, mixed):
        head, cols = block
        mixed = mixed + accum_ref[head, :, cols]
        mixed = (mixed * (1.0 / total_ref[head, :, cols])).astype(jnp.bfloat16)
        start = (head * GROUP + cols.start // tokens) * HEAD_DIM
        pieces = (cols.stop - cols.start) // tokens
        for piece in range(pieces):
            col = start + piece * HEAD_DIM
            result_ref[:, col : col + HEAD_DIM] = mixed[:, piece * tokens : (piece + 1) * tokens].T
        span = pl.ds(start, pieces * HEAD_DIM)
        copy = pltpu.make_async_copy(result_ref.at[:, span], out_ref.at[:, span], sems.at[len(copies)])
        copy.start()
        copies.append(copy)

    walk(blocks_of(weights_ref, 2), first, second)

    for copy in copies:
        copy.wait()


def per_device(
    count,
    queries,
    stretch_keys,
    stretch_values,
    cache_keys,
    cache_values,
    prefix_length,
    page_targets,
    pool_keys,
    pool_values,
    decode_queries,
    page_lists,
    context_length,
):
    own = lax.axis_index("ctx")
    own_array = jnp.full((1,), own, jnp.int32)
    tokens, width = queries.shape
    kv_width = stretch_keys.shape[1]
    kv_local = kv_width // HEAD_DIM
    rows = GROUP * tokens
    heads = kv_local * GROUP
    dec_rows = decode_queries.shape[0]
    c_rows = cache_keys.shape[0]
    pool = pool_keys.shape[0]
    f32, bf16 = jnp.float32, jnp.bfloat16
    shape = jax.ShapeDtypeStruct
    params = pltpu.CompilerParams(vmem_limit_bytes=VMEM_BYTES)
    up_pairs = [(i, (i + 1) % count) for i in range(count)]
    down_pairs = [(i, (i - 1) % count) for i in range(count)]
    hops = []
    for far in range(1, count // 2 + 1):
        hops += [-far, far] if far <= (count - 1) // 2 else [-far]

    def send(array, hop):
        return lax.ppermute(array, "ctx", up_pairs if hop < 0 else down_pairs)

    def cost(keys):
        pairs = kv_local * rows * keys
        return pl.CostEstimate(
            flops=4 * pairs * HEAD_DIM, bytes_accessed=4 * rows * kv_local * HEAD_DIM, transcendentals=pairs
        )

    half = tokens + c_rows
    low = jnp.array(-jnp.inf, bf16)
    spread, start = [], 0
    for part in (stretch_keys, cache_keys, stretch_values, cache_values):
        end = 2 * half - start - part.shape[0]
        spread.append(lax.pad(part, low, ((start, end, 0), (0, 0, 0))))
        start += part.shape[0]
    shard = {0: functools.reduce(jnp.maximum, spread)}
    shard[-1] = send(shard[0], -1)

    state_shapes = (
        shape((kv_local, 1, rows), f32),
        shape((kv_local, 1, rows), f32),
        shape((kv_local, HEAD_DIM, rows), f32),
    )
    qt, near, far, pick, *state = pl.pallas_call(
        functools.partial(own_kernel, count, hops),
        out_shape=(
            shape((kv_local, HEAD_DIM + tokens, rows), bf16),
            shape((count - 1, tokens, tokens), bf16),
            shape((count - 1, c_rows, tokens), bf16),
            shape((SEND_CAP * PAGE, tokens), bf16),
        )
        + state_shapes,
        in_specs=[SMEM] * 3 + [VMEM] * 2,
        out_specs=(VMEM,) * 7,
        compiler_params=params,
        cost_estimate=cost(tokens + c_rows),
        name="own_shard",
    )(own_array, prefix_length, page_targets, queries, shard[0])

    dec_shapes = (
        shape((heads, dec_rows, 1), f32),
        shape((heads, dec_rows, 1), f32),
        shape((heads, dec_rows, kv_width), f32),
    )
    wide, *dec_state = pl.pallas_call(
        held_kernel,
        out_shape=(shape((heads * dec_rows, kv_width), bf16),) + dec_shapes,
        in_specs=[SMEM] * 3 + [VMEM] * 5,
        out_specs=(VMEM,) * 4,
        compiler_params=params,
        cost_estimate=pl.CostEstimate(
            flops=4 * 128 * 2048 * 256, bytes_accessed=4 * pool_keys.size, transcendentals=128 * 2048
        ),
        name="decode_held_pages",
    )(own_array, page_targets, context_length, decode_queries, page_lists, pool_keys, pool_values, shard[0])

    if 1 in hops:
        sent_down, state, dec_state = lax.optimization_barrier((shard[0], state, dec_state))
        shard[1] = send(sent_down, 1)
    shard[-1], state, dec_state = lax.optimization_barrier((shard[-1], state, dec_state))
    for hop in hops[2:-1]:
        shard[hop] = send(shard[hop + 1 if hop < 0 else hop - 1], hop)
    hop = hops[-1]
    nearer = shard[hop + 1 if hop < 0 else hop - 1]
    pieces = pl.pallas_call(
        split_kernel,
        out_shape=(
            shape((c_rows, kv_width), bf16),
            shape((2 * tokens, kv_width), bf16),
            shape((c_rows, kv_width), bf16),
            shape((2 * SEND_CAP * PAGE, kv_width), bf16),
        ),
        in_specs=[VMEM] * 2,
        out_specs=(VMEM,) * 4,
        compiler_params=params,
        name="pieces_to_send_on",
    )(pick, nearer)
    last_keys = send(pieces[0], hop)
    attending, others = [], []
    for pair in up_pairs if hop < 0 else down_pairs:
        (attending if (pair[1] + hop) % count < pair[1] else others).append(pair)
    last_stretch = lax.ppermute(pieces[1], "ctx", attending)
    last_pages = lax.ppermute(pieces[3], "ctx", others)
    last_values = send(pieces[2], hop)

    for first in range(len(hops) - 1):
        places = [first]
        state = pl.pallas_call(
            functools.partial(hop_kernel, places),
            out_shape=state_shapes,
            in_specs=[VMEM] * (6 + len(places)),
            out_specs=(VMEM,) * 3,
            compiler_params=params,
            cost_estimate=cost((c_rows + tokens) * len(places)),
            name="whole_shards_" + str(first),
        )(qt, near, far, *state, *[shard[hops[place]] for place in places])

    final = len(hops) - 1
    dec_state, state = lax.optimization_barrier((dec_state, state))
    near_hops = hops[:-1]
    *dec_state, tally = pl.pallas_call(
        functools.partial(near_pages_kernel, count, hops, tokens, pool),
        out_shape=dec_shapes
        + (shape((1, dec_rows, tokens), f32),),
        in_specs=[SMEM] * 3 + [VMEM] * (5 + len(near_hops)),
        out_specs=(VMEM,) * 4,
        compiler_params=params,
        cost_estimate=cost(tokens),
        name="decode_near_pages",
    )(
        own_array, page_targets, context_length, page_lists, *[shard[hop] for hop in near_hops],
        wide, *dec_state,
    )
    dec_state, state = lax.optimization_barrier((dec_state, state))

    weights, total, accum = pl.pallas_call(
        functools.partial(score_kernel, final),
        out_shape=(shape((kv_local, c_rows, rows), bf16),) + state_shapes[1:],
        in_specs=[VMEM] * 8,
        out_specs=(VMEM,) * 3,
        compiler_params=params,
        cost_estimate=cost(half),
        name="last_scores",
    )(qt, near, far, *state, last_keys, last_stretch)

    dec_state, total = lax.optimization_barrier((dec_state, total))
    decoded = pl.pallas_call(
        last_pages_kernel,
        out_shape=shape(decode_queries.shape, bf16),
        in_specs=[VMEM] * 7,
        out_specs=VMEM,
        compiler_params=params,
        cost_estimate=cost(tokens // 2),
        name="decode_last_pages",
    )(last_stretch, last_pages, tally, wide, *dec_state)
    decoded, total = lax.optimization_barrier((decoded, total))

    prefill = pl.pallas_call(
        last_kernel,
        out_shape=shape((tokens, width), bf16),
        in_specs=[VMEM] * 4,
        out_specs=HBM,
        scratch_shapes=[
            pltpu.VMEM((tokens, width), bf16),
            pltpu.SemaphoreType.DMA((kv_local * GROUP // 2,)),
        ],
        compiler_params=params,
        cost_estimate=cost(c_rows // 2),
        name="last_values",
    )(weights, total, accum, last_values)
    return (prefill, decoded)


def solution(mesh):
    in_specs = (
        P(("groups", "ctx"), "head"),
        P(("groups", "ctx"), "head"),
        P(("groups", "ctx"), "head"),
        P(("groups", "ctx"), "head"),
        P(("groups", "ctx"), "head"),
        P("groups"),
        P("groups"),
        P(("groups", "ctx"), None, "head"),
        P(("groups", "ctx"), None, "head"),
        P(("groups", "ctx"), "head"),
        P(("groups", "ctx"), None),
        P(("groups", "ctx")),
    )
    out_specs = (P(("groups", "ctx"), "head"), P(("groups", "ctx"), "head"))
    return jax.shard_map(
        functools.partial(per_device, mesh.shape["ctx"]),
        mesh=mesh,
        in_specs=in_specs,
        out_specs=out_specs,
        check_vma=False,
    )
```

```python
import functools

import jax
import jax.numpy as jnp
from jax import lax
from jax.experimental import pallas as pl
from jax.experimental.pallas import tpu as pltpu
from jax.sharding import PartitionSpec as P

HEADS = 64
KV_HEADS = 8
HEAD_DIM = 128
GROUP = HEADS // KV_HEADS
PAGE = 16
P_DEV = 8
SEND_CAP = 2
EXP2_SCALE = HEAD_DIM ** (-0.5) * 1.4426950408889634
HIDDEN = -1e30
VMEM_BYTES = 48 * 1024 * 1024

VMEM = pl.BlockSpec(memory_space=pltpu.VMEM)
SMEM = pl.BlockSpec(memory_space=pltpu.SMEM)
HBM = pl.BlockSpec(memory_space=pltpu.HBM)


def scores_of(qt_ref, head, cols, keys):
    return jnp.dot(keys, qt_ref[head, :, cols], preferred_element_type=jnp.float32)


def soften(scores, old):
    high = jnp.max(scores, axis=0, keepdims=True)
    if old is None:
        weights = jnp.exp2((scores - high) * EXP2_SCALE)
        return weights.astype(jnp.bfloat16), high, jnp.sum(weights, axis=0, keepdims=True), None
    old_high, old_total = old
    high = jnp.maximum(high, old_high)
    decay = jnp.exp2((old_high - high) * EXP2_SCALE)
    weights = jnp.exp2((scores - high) * EXP2_SCALE)
    total = old_total * decay + jnp.sum(weights, axis=0, keepdims=True)
    return weights.astype(jnp.bfloat16), high, total, decay


def walk(blocks, first, second):
    ahead = first(blocks[0])
    for place, block in enumerate(blocks):
        current = ahead
        if place + 1 < len(blocks):
            ahead = first(blocks[place + 1])
        second(block, current)


def blocks_of(ref, groups=GROUP // 2):
    kv_local, _, rows = ref.shape
    width = groups * (rows // GROUP)
    return [(head, slice(start, start + width)) for head in range(kv_local) for start in range(0, rows, width)]


def attend(qt_ref, keys, values_t, old, new):
    high_ref, total_ref, accum_ref = new

    def second(block, scores):
        head, cols = block
        before = None if old is None else (old[0][head, :, cols], old[1][head, :, cols])
        weights, high, total, decay = soften(scores, before)
        accum = jnp.dot(values_t[head], weights, preferred_element_type=jnp.float32)
        if old is not None:
            accum = accum + old[2][head, :, cols] * decay
        high_ref[head, :, cols] = high
        total_ref[head, :, cols] = total
        accum_ref[head, :, cols] = accum

    walk(blocks_of(qt_ref), lambda block: scores_of(qt_ref, block[0], block[1], keys[block[0]]), second)


def hidden(seen):
    return jnp.where(seen, jnp.float32(0.0), jnp.float32(HIDDEN)).astype(jnp.bfloat16)


def stretch_mask(shard, own, tokens):
    place = lax.broadcasted_iota(jnp.int32, (tokens, tokens), 0)
    token = lax.broadcasted_iota(jnp.int32, (tokens, tokens), 1)
    return hidden(place - token <= (own - shard) * tokens)


def cache_mask(shard, limit, c_rows, tokens):
    place = lax.broadcasted_iota(jnp.int32, (c_rows, tokens), 0)
    return hidden(place < limit - shard * c_rows)


def slot_row(targets_ref, shard, own, tokens, pool):
    page = lax.broadcasted_iota(jnp.int32, (1, tokens), 1) // PAGE
    slots = jnp.full((1, tokens), -1, jnp.int32)
    for index in range(tokens // PAGE):
        target = targets_ref[shard * (tokens // PAGE) + index]
        slot = jnp.where(lax.div(target, P_DEV) == own, pool + lax.rem(target, P_DEV), -1)
        slots = jnp.where(page == index, slot, slots)
    return slots


def sent_pages(targets_ref, shard, owner, pages):
    one, two = jnp.int32(-1), jnp.int32(-1)
    for index in range(pages):
        hit = lax.div(targets_ref[shard * pages + index], P_DEV) == owner
        two = jnp.where(hit & (one >= 0) & (two < 0), index, two)
        one = jnp.where(hit & (one < 0), index, one)
    return one, two


def sent_slots(targets_ref, shard, owner, tokens, pool):
    page = lax.broadcasted_iota(jnp.int32, (1, tokens), 1) // PAGE
    row = jnp.full((1, tokens), -1, jnp.int32)
    for place, index in enumerate(sent_pages(targets_ref, shard, owner, tokens // PAGE)):
        target = targets_ref[shard * (tokens // PAGE) + jnp.maximum(index, 0)]
        slot = jnp.where(index >= 0, pool + lax.rem(target, P_DEV), -1)
        row = jnp.where(page == place, slot, row)
    return row


def length_column(length_ref):
    rows = length_ref.shape[0]
    place = lax.broadcasted_iota(jnp.int32, (rows, 1), 0)
    lengths = jnp.zeros((rows, 1), jnp.int32)
    for row in range(rows):
        lengths = jnp.where(place == row, length_ref[row], lengths)
    return lengths


def tally_of(lists, lengths, slot):
    rows, span = lists.shape
    tokens = slot.shape[1]
    slot = jnp.broadcast_to(slot, (rows, tokens))
    offset = lax.rem(lax.broadcasted_iota(jnp.int32, (rows, tokens), 1), PAGE)
    tally = jnp.zeros((rows, tokens), jnp.float32)
    for entry in range(span):
        hit = (slot == lists[:, entry : entry + 1]) & (offset < lengths - entry * PAGE)
        tally = tally + jnp.where(hit, jnp.float32(1.0), jnp.float32(0.0))
    return tally[None]


def shard_of(own, hop, count):
    return lax.rem(own + hop + count, count)


def wide_queries(q_ref, kv_local):
    heads = q_ref.shape[1] // HEAD_DIM
    queries = q_ref[...].astype(jnp.float32)
    stacked = []
    for head in range(heads):
        piece = queries[:, head * HEAD_DIM : (head + 1) * HEAD_DIM]
        blank = jnp.zeros_like(piece)
        stacked.append(
            jnp.concatenate([piece if kv == head // GROUP else blank for kv in range(kv_local)], axis=1)
        )
    return jnp.concatenate(stacked, axis=0).astype(jnp.bfloat16)


def decode_attend(queries, parts, state):
    done = []
    for keys, values, tally in parts:
        scores = lax.dot_general(
            queries, keys, (((1,), (1,)), ((), ())), preferred_element_type=jnp.float32
        ).reshape(-1, tally.shape[1], tally.shape[2])
        done.append((jnp.where(tally > 0, scores, jnp.float32(HIDDEN)), tally, values))
    highs = [jnp.max(scores, axis=-1, keepdims=True) for scores, _, _ in done]
    if state is not None:
        old_high, old_total, old_mixed = state
        highs.append(old_high)
    high = functools.reduce(jnp.maximum, highs)
    total, mixed = 0.0, 0.0
    if state is not None:
        decay = jnp.exp2((old_high - high) * EXP2_SCALE)
        total = old_total * decay
        mixed = old_mixed * decay
    for scores, tally, values in done:
        weights = jnp.exp2((scores - high) * EXP2_SCALE) * tally
        total = total + jnp.sum(weights, axis=-1, keepdims=True)
        mixed = mixed + jnp.dot(
            weights.reshape(queries.shape[0], -1).astype(jnp.bfloat16),
            values,
            preferred_element_type=jnp.float32,
        ).reshape(high.shape[0], high.shape[1], -1)
    return high, total, mixed


def features(head):
    return slice(head * HEAD_DIM, (head + 1) * HEAD_DIM)


def shard_parts(ref, tokens, c_rows):
    return slice(0, tokens + c_rows), slice(tokens + c_rows, 2 * (tokens + c_rows))


def own_kernel(
    count, hops, own_ref, limit_ref, targets_ref, q_ref, shard_ref,
    qt_ref, near_ref, far_ref, pick_ref, high_ref, total_ref, accum_ref,
):
    kv_local, _, rows = qt_ref.shape
    tokens = q_ref.shape[0]
    c_rows = far_ref.shape[1]
    own = own_ref[0]
    limit = limit_ref[0]
    place = lax.broadcasted_iota(jnp.int32, (tokens, tokens), 0)
    token = lax.broadcasted_iota(jnp.int32, (tokens, tokens), 1)
    pick = jnp.where(place == token, jnp.float32(1.0), jnp.float32(0.0)).astype(jnp.bfloat16)
    for head in range(kv_local):
        for sub in range(GROUP):
            cols = slice(sub * tokens, (sub + 1) * tokens)
            qt_ref[head, :HEAD_DIM, cols] = q_ref[:, features(head * GROUP + sub)].T
            qt_ref[head, HEAD_DIM:, cols] = pick
    for place, hop in enumerate(hops):
        shard = shard_of(own, hop, count)
        near_ref[place] = stretch_mask(shard, own, tokens)
        far_ref[place] = cache_mask(shard, limit, c_rows, tokens)
    onward = 1 if hops[-1] < 0 else -1
    pages = tokens // PAGE
    one, two = sent_pages(
        targets_ref, shard_of(own, hops[-1] + onward, count), shard_of(own, onward, count), pages
    )
    row = lax.broadcasted_iota(jnp.int32, pick_ref.shape, 0)
    token = lax.broadcasted_iota(jnp.int32, pick_ref.shape, 1)
    sent = ((row < PAGE) & (one >= 0) & (token == row + one * PAGE)) | (
        (row >= PAGE) & (two >= 0) & (token == row + (two - 1) * PAGE)
    )
    pick_ref[...] = jnp.where(sent, jnp.float32(1.0), jnp.float32(0.0)).astype(jnp.bfloat16)
    mask = jnp.concatenate([stretch_mask(own, own, tokens), cache_mask(own, limit, c_rows, tokens)], axis=0)
    key_rows, value_rows = shard_parts(shard_ref, tokens, c_rows)
    keys = [jnp.concatenate([shard_ref[key_rows, features(head)], mask], axis=1) for head in range(kv_local)]
    values_t = [shard_ref[value_rows, features(head)].T for head in range(kv_local)]
    attend(qt_ref, keys, values_t, None, (high_ref, total_ref, accum_ref))


def held_kernel(
    own_ref, targets_ref, length_ref, q_ref, lists_ref, pool_k, pool_v, rest_ref,
    wide_ref, high_ref, total_ref, mixed_ref,
):
    kv_width = rest_ref.shape[1]
    pool = pool_k.shape[0]
    held = pool * PAGE
    tokens = PAGE * P_DEV
    half = rest_ref.shape[0] // 2
    own = own_ref[0]
    lists = lists_ref[...]
    lengths = length_column(length_ref)
    wide_ref[...] = wide_queries(q_ref, kv_width // HEAD_DIM)
    held_slot = lax.broadcasted_iota(jnp.int32, (1, held), 1) // PAGE
    own_slot = slot_row(targets_ref, own, own, tokens, pool)
    parts = [
        (
            pool_k[...].reshape(held, kv_width),
            pool_v[...].reshape(held, kv_width),
            tally_of(lists, lengths, held_slot),
        ),
        (rest_ref[:tokens], rest_ref[half : half + tokens], tally_of(lists, lengths, own_slot)),
    ]
    high_ref[...], total_ref[...], mixed_ref[...] = decode_attend(wide_ref[...], parts, None)


def hop_kernel(places, qt_ref, near_ref, far_ref, high_in, total_in, accum_in, *refs):
    shard_refs, outs = refs[: len(places)], refs[len(places) :]
    tokens, c_rows = near_ref.shape[1], far_ref.shape[1]
    mask = jnp.concatenate([ref[place] for place in places for ref in (near_ref, far_ref)], axis=0)
    keys, values_t = [], []
    for head in range(qt_ref.shape[0]):
        pieces, values = [], []
        for ref in shard_refs:
            key_rows, value_rows = shard_parts(ref, tokens, c_rows)
            pieces.append(ref[key_rows, features(head)])
            values.append(ref[value_rows, features(head)])
        keys.append(jnp.concatenate([jnp.concatenate(pieces, axis=0), mask], axis=1))
        values_t.append(jnp.concatenate(values, axis=0).T)
    attend(qt_ref, keys, values_t, (high_in, total_in, accum_in), outs)


def split_kernel(pick_ref, shard_ref, keys_ref, stretch_ref, values_ref, pages_ref):
    tokens = pick_ref.shape[1]
    half = shard_ref.shape[0] // 2
    sent = pick_ref.shape[0]
    for place, start in enumerate((0, half)):
        stretch_ref[place * tokens : (place + 1) * tokens] = shard_ref[start : start + tokens]
        rows = jnp.dot(pick_ref[...], shard_ref[start : start + tokens], preferred_element_type=jnp.float32)
        pages_ref[place * sent : (place + 1) * sent] = rows.astype(jnp.bfloat16)
    keys_ref[...] = shard_ref[tokens:half]
    values_ref[...] = shard_ref[half + tokens :]


def near_pages_kernel(count, hops, tokens, pool, own_ref, targets_ref, length_ref, lists_ref, *refs):
    shard_refs, refs = refs[: len(hops) - 1], refs[len(hops) - 1 :]
    wide_ref, dec_high, dec_total, dec_mixed, high_ref, total_ref, mixed_ref, tally_ref = refs
    own = own_ref[0]
    lists = lists_ref[...]
    lengths = length_column(length_ref)
    parts = []
    for hop, ref in zip(hops, shard_refs):
        half = ref.shape[0] // 2
        slot = slot_row(targets_ref, shard_of(own, hop, count), own, tokens, pool)
        parts.append((ref[:tokens], ref[half : half + tokens], tally_of(lists, lengths, slot)))
    state = (dec_high[...], dec_total[...], dec_mixed[...])
    high_ref[...], total_ref[...], mixed_ref[...] = decode_attend(wide_ref[...], parts, state)
    shard = shard_of(own, hops[-1], count)
    attended = shard < own
    whole = slot_row(targets_ref, shard, own, tokens, pool)
    alone = sent_slots(targets_ref, shard, own, tokens, pool)
    tally_ref[...] = tally_of(lists, lengths, jnp.where(attended, whole, alone))


def score_kernel(
    final, qt_ref, near_ref, far_ref, high_in, total_in, accum_in, keys_ref, stretch_ref,
    weights_ref, total_ref, accum_ref,
):
    kv_local = qt_ref.shape[0]
    tokens, c_rows = near_ref.shape[1], far_ref.shape[1]
    def run(attended):
        mask = far_ref[final]
        if attended:
            mask = jnp.concatenate([near_ref[final], mask], axis=0)
        keys, values_t = [], []
        for head in range(kv_local):
            rows = keys_ref[:, features(head)]
            if attended:
                rows = jnp.concatenate([stretch_ref[:tokens, features(head)], rows], axis=0)
                values_t.append(stretch_ref[tokens:, features(head)].T)
            keys.append(jnp.concatenate([rows, mask], axis=1))

        def second(block, scores):
            head, cols = block
            before = (high_in[head, :, cols], total_in[head, :, cols])
            weights, _, total, decay = soften(scores, before)
            weights_ref[head, :, cols] = weights[-c_rows:]
            total_ref[head, :, cols] = total
            accum = accum_in[head, :, cols] * decay
            if attended:
                accum = accum + jnp.dot(values_t[head], weights[:tokens], preferred_element_type=jnp.float32)
            accum_ref[head, :, cols] = accum

        walk(blocks_of(qt_ref), lambda block: scores_of(qt_ref, block[0], block[1], keys[block[0]]), second)

    attended = jnp.max(near_ref[final].astype(jnp.float32)) > HIDDEN / 2
    pl.when(attended)(functools.partial(run, True))
    pl.when(jnp.logical_not(attended))(functools.partial(run, False))


def last_pages_kernel(
    stretch_ref, pages_ref, tally_ref, wide_ref, dec_high, dec_total, dec_mixed, dec_out
):
    tokens = stretch_ref.shape[0] // 2
    sent = pages_ref.shape[0] // 2
    keys = jnp.concatenate([stretch_ref[:sent] + pages_ref[:sent], stretch_ref[sent:tokens]], axis=0)
    values = jnp.concatenate(
        [stretch_ref[tokens : tokens + sent] + pages_ref[sent:], stretch_ref[tokens + sent :]], axis=0
    )
    state = (dec_high[...], dec_total[...], dec_mixed[...])
    _, total, mixed = decode_attend(wide_ref[...], [(keys, values, tally_ref[...])], state)
    share = 1.0 / total
    for head in range(dec_high.shape[0]):
        piece = mixed[head, :, features(head // GROUP)] * share[head]
        dec_out[:, features(head)] = piece.astype(jnp.bfloat16)


def last_kernel(weights_ref, total_ref, accum_ref, values_ref, out_ref, result_ref, sems):
    tokens = result_ref.shape[0]
    values_t = [values_ref[:, features(head)].T for head in range(weights_ref.shape[0])]
    copies = []

    def first(block):
        head, cols = block
        return jnp.dot(values_t[head], weights_ref[head, :, cols], preferred_element_type=jnp.float32)

    def second(block, mixed):
        head, cols = block
        mixed = mixed + accum_ref[head, :, cols]
        mixed = (mixed * (1.0 / total_ref[head, :, cols])).astype(jnp.bfloat16)
        start = (head * GROUP + cols.start // tokens) * HEAD_DIM
        pieces = (cols.stop - cols.start) // tokens
        for piece in range(pieces):
            col = start + piece * HEAD_DIM
            result_ref[:, col : col + HEAD_DIM] = mixed[:, piece * tokens : (piece + 1) * tokens].T
        span = pl.ds(start, pieces * HEAD_DIM)
        copy = pltpu.make_async_copy(result_ref.at[:, span], out_ref.at[:, span], sems.at[len(copies)])
        copy.start()
        copies.append(copy)

    walk(blocks_of(weights_ref, 2), first, second)

    for copy in copies:
        copy.wait()


def per_device(
    count,
    queries,
    stretch_keys,
    stretch_values,
    cache_keys,
    cache_values,
    prefix_length,
    page_targets,
    pool_keys,
    pool_values,
    decode_queries,
    page_lists,
    context_length,
):
    own = lax.axis_index("ctx")
    own_array = jnp.full((1,), own, jnp.int32)
    tokens, width = queries.shape
    kv_width = stretch_keys.shape[1]
    kv_local = kv_width // HEAD_DIM
    rows = GROUP * tokens
    heads = kv_local * GROUP
    dec_rows = decode_queries.shape[0]
    c_rows = cache_keys.shape[0]
    pool = pool_keys.shape[0]
    f32, bf16 = jnp.float32, jnp.bfloat16
    shape = jax.ShapeDtypeStruct
    params = pltpu.CompilerParams(vmem_limit_bytes=VMEM_BYTES)
    up_pairs = [(i, (i + 1) % count) for i in range(count)]
    down_pairs = [(i, (i - 1) % count) for i in range(count)]
    hops = []
    for far in range(1, count // 2 + 1):
        hops += [-far, far] if far <= (count - 1) // 2 else [-far]

    def send(array, hop):
        return lax.ppermute(array, "ctx", up_pairs if hop < 0 else down_pairs)

    def cost(keys):
        pairs = kv_local * rows * keys
        return pl.CostEstimate(
            flops=4 * pairs * HEAD_DIM, bytes_accessed=4 * rows * kv_local * HEAD_DIM, transcendentals=pairs
        )

    half = tokens + c_rows
    low = jnp.array(-jnp.inf, bf16)
    spread, start = [], 0
    for part in (stretch_keys, cache_keys, stretch_values, cache_values):
        end = 2 * half - start - part.shape[0]
        spread.append(lax.pad(part, low, ((start, end, 0), (0, 0, 0))))
        start += part.shape[0]
    shard = {0: functools.reduce(jnp.maximum, spread)}
    shard[-1] = send(shard[0], -1)

    state_shapes = (
        shape((kv_local, 1, rows), f32),
        shape((kv_local, 1, rows), f32),
        shape((kv_local, HEAD_DIM, rows), f32),
    )
    qt, near, far, pick, *state = pl.pallas_call(
        functools.partial(own_kernel, count, hops),
        out_shape=(
            shape((kv_local, HEAD_DIM + tokens, rows), bf16),
            shape((count - 1, tokens, tokens), bf16),
            shape((count - 1, c_rows, tokens), bf16),
            shape((SEND_CAP * PAGE, tokens), bf16),
        )
        + state_shapes,
        in_specs=[SMEM] * 3 + [VMEM] * 2,
        out_specs=(VMEM,) * 7,
        compiler_params=params,
        cost_estimate=cost(tokens + c_rows),
        name="own_shard",
    )(own_array, prefix_length, page_targets, queries, shard[0])

    dec_shapes = (
        shape((heads, dec_rows, 1), f32),
        shape((heads, dec_rows, 1), f32),
        shape((heads, dec_rows, kv_width), f32),
    )
    wide, *dec_state = pl.pallas_call(
        held_kernel,
        out_shape=(shape((heads * dec_rows, kv_width), bf16),) + dec_shapes,
        in_specs=[SMEM] * 3 + [VMEM] * 5,
        out_specs=(VMEM,) * 4,
        compiler_params=params,
        cost_estimate=pl.CostEstimate(
            flops=4 * 128 * 2048 * 256, bytes_accessed=4 * pool_keys.size, transcendentals=128 * 2048
        ),
        name="decode_held_pages",
    )(own_array, page_targets, context_length, decode_queries, page_lists, pool_keys, pool_values, shard[0])

    if 1 in hops:
        sent_down, state, dec_state = lax.optimization_barrier((shard[0], state, dec_state))
        shard[1] = send(sent_down, 1)
    shard[-1], state, dec_state = lax.optimization_barrier((shard[-1], state, dec_state))
    for hop in hops[2:-1]:
        shard[hop] = send(shard[hop + 1 if hop < 0 else hop - 1], hop)
    hop = hops[-1]
    nearer = shard[hop + 1 if hop < 0 else hop - 1]
    pieces = pl.pallas_call(
        split_kernel,
        out_shape=(
            shape((c_rows, kv_width), bf16),
            shape((2 * tokens, kv_width), bf16),
            shape((c_rows, kv_width), bf16),
            shape((2 * SEND_CAP * PAGE, kv_width), bf16),
        ),
        in_specs=[VMEM] * 2,
        out_specs=(VMEM,) * 4,
        compiler_params=params,
        name="pieces_to_send_on",
    )(pick, nearer)
    last_keys = send(pieces[0], hop)
    attending, others = [], []
    for pair in up_pairs if hop < 0 else down_pairs:
        (attending if (pair[1] + hop) % count < pair[1] else others).append(pair)
    last_stretch = lax.ppermute(pieces[1], "ctx", attending)
    last_pages = lax.ppermute(pieces[3], "ctx", others)
    last_values = send(pieces[2], hop)

    for first in range(len(hops) - 1):
        places = [first]
        state = pl.pallas_call(
            functools.partial(hop_kernel, places),
            out_shape=state_shapes,
            in_specs=[VMEM] * (6 + len(places)),
            out_specs=(VMEM,) * 3,
            compiler_params=params,
            cost_estimate=cost((c_rows + tokens) * len(places)),
            name="whole_shards_" + str(first),
        )(qt, near, far, *state, *[shard[hops[place]] for place in places])

    final = len(hops) - 1
    dec_state, state = lax.optimization_barrier((dec_state, state))
    near_hops = hops[:-1]
    *dec_state, tally = pl.pallas_call(
        functools.partial(near_pages_kernel, count, hops, tokens, pool),
        out_shape=dec_shapes
        + (shape((1, dec_rows, tokens), f32),),
        in_specs=[SMEM] * 3 + [VMEM] * (5 + len(near_hops)),
        out_specs=(VMEM,) * 4,
        compiler_params=params,
        cost_estimate=cost(tokens),
        name="decode_near_pages",
    )(
        own_array, page_targets, context_length, page_lists, *[shard[hop] for hop in near_hops],
        wide, *dec_state,
    )
    dec_state, state = lax.optimization_barrier((dec_state, state))

    weights, total, accum = pl.pallas_call(
        functools.partial(score_kernel, final),
        out_shape=(shape((kv_local, c_rows, rows), bf16),) + state_shapes[1:],
        in_specs=[VMEM] * 8,
        out_specs=(VMEM,) * 3,
        compiler_params=params,
        cost_estimate=cost(half),
        name="last_scores",
    )(qt, near, far, *state, last_keys, last_stretch)

    dec_state, total = lax.optimization_barrier((dec_state, total))
    decoded = pl.pallas_call(
        last_pages_kernel,
        out_shape=shape(decode_queries.shape, bf16),
        in_specs=[VMEM] * 7,
        out_specs=VMEM,
        compiler_params=params,
        cost_estimate=cost(tokens // 2),
        name="decode_last_pages",
    )(last_stretch, last_pages, tally, wide, *dec_state)
    decoded, total = lax.optimization_barrier((decoded, total))

    prefill = pl.pallas_call(
        last_kernel,
        out_shape=shape((tokens, width), bf16),
        in_specs=[VMEM] * 4,
        out_specs=HBM,
        scratch_shapes=[
            pltpu.VMEM((tokens, width), bf16),
            pltpu.SemaphoreType.DMA((kv_local * GROUP // 2,)),
        ],
        compiler_params=params,
        cost_estimate=cost(c_rows // 2),
        name="last_values",
    )(weights, total, accum, last_values)
    return (prefill, decoded)


def solution(mesh):
    in_specs = (
        P(("groups", "ctx"), "head"),
        P(("groups", "ctx"), "head"),
        P(("groups", "ctx"), "head"),
        P(("groups", "ctx"), "head"),
        P(("groups", "ctx"), "head"),
        P("groups"),
        P("groups"),
        P(("groups", "ctx"), None, "head"),
        P(("groups", "ctx"), None, "head"),
        P(("groups", "ctx"), "head"),
        P(("groups", "ctx"), None),
        P(("groups", "ctx")),
    )
    out_specs = (P(("groups", "ctx"), "head"), P(("groups", "ctx"), "head"))
    return jax.shard_map(
        functools.partial(per_device, mesh.shape["ctx"]),
        mesh=mesh,
        in_specs=in_specs,
        out_specs=out_specs,
        check_vma=False,
    )
```
